32 devices in a mesh: pipe: 2 (over x), dp: 8 (over z, y), tensor: 2 (over core).
Axes of the slice: x: 2, y: 2, z: 4, core: 2. Of those that a mesh axis runs over, the one named last changes fastest.
Arguments:
- inputs: bfloat16 [4096, 768], P(('dp', 'tensor')), may hold values from -6 to 6
- cotangent: bfloat16 [4096, 768], P(('dp', 'tensor')), may hold values from -6 to 6
- dealing: int32 [4096], P(('dp', 'tensor')), may hold values from 0 to 4095, as said below
- routes: int32 [4096, 1], P(('dp', 'tensor')), may hold values from 0 to 3
- slot_order: int32 [4096], P(('dp', 'tensor')), may hold values from 0 to 4095, each once
- doc_lengths: int32 [16, 2], P('dp'), may hold values from 1 to 255, as said below
- attn_weight: bfloat16 [2, 768, 3, 768], P('pipe', 'dp', None, 'tensor'), may hold values from -0.21875 to 0.21875
- attn_out_weight: bfloat16 [2, 768, 768], P('pipe', ('tensor', 'dp')), may hold values from -0.875 to 0.875
- expert_in_weight: bfloat16 [2, 4, 768, 3072], P('pipe', None, 'dp', 'tensor'), may hold values from -0.21875 to 0.21875
- expert_out_weight: bfloat16 [2, 4, 3072, 768], P('pipe', None, ('tensor', 'dp')), may hold values from -0.4375 to 0.4375
- norm_gains: float32 [2, 2, 768], P('pipe', None, ('dp', 'tensor')), may hold values from 0.25 to 1.75
- router_weight: float32 [2, 768, 4], P('pipe', ('dp', 'tensor')), may hold values from -0.15625 to 0.15625
Outputs:
- activations: bfloat16 [2, 4096, 768], P('pipe', ('dp', 'tensor'))
- input_grads: bfloat16 [2, 4096, 768], P('pipe', ('dp', 'tensor'))
- grad_attn: float32 [2, 768, 3, 768], P('pipe', 'dp', None, 'tensor')
- grad_attn_out: float32 [2, 768, 768], P('pipe', ('tensor', 'dp'))
- grad_expert_in: float32 [2, 4, 768, 3072], P('pipe', None, 'dp', 'tensor')
- grad_expert_out: float32 [2, 4, 3072, 768], P('pipe', None, ('tensor', 'dp'))
- grad_gains: float32 [2, 2, 768], P('pipe', None, ('dp', 'tensor'))
- grad_router: float32 [2, 768, 4], P('pipe', ('dp', 'tensor'))
The draws below stay inside these ranges and needn't reach their ends.
Inputs may be any that keep to these rules, and one draw needn't show every extreme that they name: dealing is a permutation of the 4096 places; the 256 arriving rows of each device send exactly 16 rows to the 256 places of each device. `doc_lengths`: each row holds 2 lengths that add up to 256; in every row one document covers positions on both sides of the pack's middle; some row has a document of exactly 255.
All inputs are finite; a program needn't handle non-finite values.
Results may differ from the reference program's by a relative error of at most 0.03.
Values may be sent and summed in bfloat16 or wider, within the bound.
No kernel may reach another device: no remote copies, remote signals or barrier semaphores. Data moves between devices by JAX's collectives and lax.ppermute only.
A program may use at most 192 MiB of HBM per device.

```python
import jax
import jax.numpy as jnp
from jax import lax

D = 768
HEADS = 12
HEAD_DIM = 64
FF = 3072
EXPERTS = 4
MB = 2
TOK_MB = 128
TOK_DEV = 256
SHARDS = 16
TOKENS = 4096
PER_PEER = 16
PACK = 256
PACKS = 16
CAP = 64
N_DP = 8
N_TENSOR = 2


def draw_dealing(key, part):
    key = jax.random.fold_in(key, 7)
    pick_key, shuffle_key = jax.random.split(key)
    owners = jax.vmap(lambda each_key: jax.random.permutation(each_key, SHARDS))(jax.random.split(pick_key, SHARDS))
    targets = jnp.arange(TOK_DEV) // PER_PEER
    within = jnp.arange(TOK_DEV) % PER_PEER

    def one_source(source_index, source_key):
        values = targets * TOK_DEV + owners[targets, source_index] * PER_PEER + within
        return values[jax.random.permutation(source_key, TOK_DEV)]
    rows_all = jax.vmap(one_source)(jnp.arange(SHARDS), jax.random.split(shuffle_key, SHARDS))
    return rows_all.reshape(TOKENS).astype(jnp.int32)


def draw_doc_lengths(key, part):
    key = jax.random.fold_in(key, 13)
    first_key, pick_key, side_key = jax.random.split(key, 3)
    first = jax.random.randint(first_key, (PACKS,), 1, PACK - 1)
    first = jnp.where(first >= PACK // 2, first + 1, first)
    chosen = jax.random.randint(pick_key, (), 0, PACKS)
    side = jax.random.randint(side_key, (), 0, 2)
    forced = jnp.where(side == 0, 1, PACK - 1)
    first = jnp.where(jnp.arange(PACKS) == chosen, forced, first)
    return jnp.stack([first, PACK - first], axis=1).astype(jnp.int32)


def levels(own_key, extent, shards, low, high):
    def one(axis_at, blocks):
        heights = jax.random.uniform(jax.random.fold_in(jax.random.fold_in(own_key, 6), axis_at), (blocks,), jnp.float32, low / len(shards), high / len(shards))
        return jnp.repeat(jnp.exp(heights), extent[axis_at] // blocks).reshape((-1,) + (1,) * (len(extent) - axis_at - 1))

    factor_of = one(*shards[0])
    for cut in shards[1:]:
        factor_of = factor_of * one(*cut)
    return factor_of


def picks_of(key, rows, number_of, top, lift):
    sequence = jax.random.permutation(jax.random.fold_in(key, 1), number_of)
    pull = sequence
    for power in range(3):
        pull = pull * pull // number_of
    pull = pull * lift // number_of
    tickets = jax.random.randint(jax.random.fold_in(key, 2), (rows, number_of), 0, 4096) + pull
    sure = jax.random.permutation(jax.random.fold_in(key, 3), rows)[jnp.arange(number_of) % rows]
    tickets = jnp.where(jnp.arange(rows)[:, None] == sure[None, :], 1 << 14, tickets)
    merit = tickets * number_of + jnp.arange(number_of)
    return lax.top_k(merit.astype(jnp.int32), top)[1].astype(jnp.int32)


def gaussian(own_key, shape, spread, most, cuts=(), held_as=jnp.bfloat16):
    drawn = jax.random.normal(own_key, shape, jnp.float32) * spread
    if len(cuts) > 0:
        drawn = levels(own_key, shape, cuts, -0.22, 0.18) * drawn
    return jnp.clip(drawn, min=-most, max=most).astype(held_as)


def setup_inputs(seed: int = 0) -> dict:
    key_of = jax.random.split(jax.random.key(seed), 13)
    inputs = gaussian(key_of[0], (TOKENS, D), 1.0, 6.0, ((0, 16),))
    cotangent = gaussian(key_of[1], (TOKENS, D), 1.0, 6.0, ((0, 16),))
    dealing = draw_dealing(jax.random.fold_in(key_of[12], 71), 0)
    routes = picks_of(key_of[3], TOKENS, EXPERTS, 1, 2048)
    slot_order = jax.random.permutation(key_of[4], TOKENS).astype(jnp.int32)
    doc_lengths = draw_doc_lengths(jax.random.fold_in(key_of[12], 71), 0)
    attn_weight = gaussian(key_of[6], (2, D, 3, HEADS * HEAD_DIM), D ** -0.5, 0.21875, ((0, 2), (1, 8), (3, 2)))
    attn_out_weight = gaussian(key_of[7], (2, HEADS * HEAD_DIM, D), (HEADS * HEAD_DIM // 16) ** -0.5, 0.875, ((0, 2), (1, 16)))
    expert_in_weight = gaussian(key_of[8], (2, EXPERTS, D, FF), D ** -0.5, 0.21875, ((0, 2), (2, 8), (3, 2)))
    expert_out_weight = gaussian(key_of[9], (2, EXPERTS, FF, D), (FF // 16) ** -0.5, 0.4375, ((0, 2), (2, 16)))
    norm_gains = jnp.clip(1.0 + 0.15 * jax.random.normal(key_of[10], (2, 2, D), jnp.float32), 0.25, 1.75)
    router_weight = gaussian(key_of[11], (2, D, EXPERTS), (2 * D) ** -0.5, 0.15625, ((0, 2), (1, 16)), jnp.float32)
    return {"inputs": inputs, "cotangent": cotangent, "dealing": dealing, "routes": routes, "slot_order": slot_order, "doc_lengths": doc_lengths, "attn_weight": attn_weight, "attn_out_weight": attn_out_weight, "expert_in_weight": expert_in_weight, "expert_out_weight": expert_out_weight, "norm_gains": norm_gains, "router_weight": router_weight}


@jax.custom_vjp
def low(v):
    return lax.optimization_barrier(v.astype(jnp.bfloat16)).astype(jnp.float32)

@jax.custom_vjp
def low_back(v):
    return v

def low_keep(v):
    return (low(v), None)

def low_pass(kept, grad):
    return (grad,)

def back_keep(v):
    return (v, None)

def back_low(kept, grad):
    return (low(grad),)
low.defvjp(low_keep, low_pass)
low_back.defvjp(back_keep, back_low)
EPSILON = 1e-06
NEGATIVE = -1e+30
HIGHEST_PREC = lax.Precision.HIGHEST

def round_both(values):
    return low_back(low(values))

def rms_norm(stream, gain_row):
    return stream * lax.rsqrt(lax.optimization_barrier(jnp.mean(stream * stream, axis=-1, keepdims=True)) + EPSILON) * gain_row

def doc_ids(lengths):
    doc_ends = jnp.cumsum(lengths)
    positions = jnp.arange(PACK)
    return lax.optimization_barrier(jnp.sum((positions[:, None] >= doc_ends[None, :]).astype(jnp.int32), axis=1))

def slot_plan(expert_ids, priority):
    same_expert = expert_ids[:, None] == expert_ids[None, :]
    earlier = priority[None, :] < priority[:, None]
    slot_rank = lax.optimization_barrier(jnp.sum((same_expert & earlier).astype(jnp.int32), axis=1))
    is_kept = slot_rank < CAP
    slot_ids = jnp.arange(EXPERTS * CAP)
    slot_hit = (expert_ids[None, :] == (slot_ids // CAP)[:, None]) & (slot_rank[None, :] == (slot_ids % CAP)[:, None])
    filled = jnp.any(slot_hit, axis=1)
    source = lax.optimization_barrier(jnp.sum(jnp.where(slot_hit, jnp.arange(PACK)[None, :], 0), axis=1))
    where_slot = jnp.clip(expert_ids * CAP + slot_rank, 0, EXPERTS * CAP - 1)
    return (is_kept, filled, source, where_slot)

def attention(normed, attn_weight, attn_out_weight, doc_row):
    pack_len = normed.shape[0]
    proj_qkv = round_both(jnp.dot(normed, attn_weight.reshape(D, 3 * HEADS * HEAD_DIM), precision=HIGHEST_PREC))
    proj_qkv = proj_qkv.reshape(pack_len, 3, HEADS, HEAD_DIM)
    query_rows = proj_qkv[:, 0]
    key_rows = proj_qkv[:, 1]
    value_rows = proj_qkv[:, 2]
    scores = low_back(jnp.einsum('qhd,khd->hqk', query_rows, key_rows, precision=HIGHEST_PREC) * HEAD_DIM ** (-0.5))
    positions = jnp.arange(pack_len)
    allowed = (doc_row[:, None] == doc_row[None, :]) & (positions[None, :] <= positions[:, None])
    scores = jnp.where(allowed[None], scores, NEGATIVE)
    row_max = lax.optimization_barrier(jnp.max(scores, axis=-1, keepdims=True))
    weights = jnp.exp(scores - row_max)
    attn_probs = low(weights / lax.optimization_barrier(jnp.sum(weights, axis=-1, keepdims=True)))
    mixed_heads = round_both(jnp.einsum('hqk,khd->qhd', attn_probs, value_rows, precision=HIGHEST_PREC))
    mixed_heads = mixed_heads.reshape(pack_len, HEADS * HEAD_DIM)
    return low_back(jnp.dot(mixed_heads, attn_out_weight, precision=HIGHEST_PREC))

def expert_branch(mlp_in, expert_in_weight, expert_out_weight, router_weight, expert_ids, priority):
    logits = jnp.dot(mlp_in, router_weight, precision=HIGHEST_PREC)
    row_max = lax.optimization_barrier(jnp.max(logits, axis=-1, keepdims=True))
    weights = jnp.exp(logits - row_max)
    router_probs = weights / lax.optimization_barrier(jnp.sum(weights, axis=-1, keepdims=True))
    onehot = expert_ids[:, None] == jnp.arange(EXPERTS)[None, :]
    gate_value = lax.optimization_barrier(jnp.sum(jnp.where(onehot, router_probs, 0.0), axis=1))
    is_kept, filled, source, where_slot = slot_plan(expert_ids, priority)
    dispatched = jnp.where(filled[:, None], mlp_in[source], 0.0).reshape(EXPERTS, CAP, D)
    pre_act = low_back(jnp.einsum('ecd,edf->ecf', dispatched, expert_in_weight, precision=HIGHEST_PREC))
    activated = low(jax.nn.gelu(pre_act))
    expert_out = low_back(jnp.einsum('ecf,efd->ecd', activated, expert_out_weight, precision=HIGHEST_PREC))
    expert_out = expert_out.reshape(EXPERTS * CAP, D)
    token_out = jnp.where(is_kept[:, None], expert_out[where_slot], 0.0)
    return low_back(gate_value[:, None] * token_out)

def layer(stream, params, expert_ids, priority, doc_row):
    attn_weight, attn_out_weight, expert_in_weight, expert_out_weight, norm_gains, router_weight = params
    attn_in = low(rms_norm(stream, norm_gains[0]))
    mid_stream = stream + attention(attn_in, attn_weight, attn_out_weight, doc_row)
    mlp_in = low(rms_norm(mid_stream, norm_gains[1]))
    out_stream = mid_stream + expert_branch(mlp_in, expert_in_weight, expert_out_weight, router_weight, expert_ids, priority)
    return round_both(out_stream)

def run_layer(stream_packs, params, route_packs, order_packs, doc_packs):

    def one_pack(members):
        return layer(members[0], params, members[1], members[2], members[3])
    return lax.map(jax.checkpoint(one_pack), (stream_packs, route_packs, order_packs, doc_packs))

def to_packs(values):
    rest = values.shape[1:]
    values = values.reshape((N_DP, N_TENSOR, MB, TOK_MB) + rest)
    values = jnp.swapaxes(values, 1, 2)
    return values.reshape((N_DP * MB, PACK) + rest)

def from_packs(values):
    rest = values.shape[2:]
    values = values.reshape((N_DP, MB, N_TENSOR, TOK_MB) + rest)
    values = jnp.swapaxes(values, 1, 2)
    return values.reshape((TOKENS,) + rest)

def reference(inputs, cotangent, dealing, routes, slot_order, doc_lengths, attn_weight, attn_out_weight, expert_in_weight, expert_out_weight, norm_gains, router_weight):

    def to_dealt(values):
        return jnp.zeros_like(values).at[dealing].set(values)
    route_packs = to_packs(to_dealt(routes[:, 0]))
    order_packs = to_packs(to_dealt(slot_order))
    doc_packs = jax.vmap(doc_ids)(doc_lengths)
    params = (attn_weight.astype(jnp.float32), attn_out_weight.astype(jnp.float32), expert_in_weight.astype(jnp.float32), expert_out_weight.astype(jnp.float32), norm_gains.astype(jnp.float32), router_weight.astype(jnp.float32))

    def forward(first_input, second_shift, all_params):
        first_params = tuple((member[0] for member in all_params))
        second_params = tuple((member[1] for member in all_params))
        first_out = run_layer(to_packs(to_dealt(first_input)), first_params, route_packs, order_packs, doc_packs)
        second_in = first_out + to_packs(to_dealt(second_shift))
        second_out = run_layer(second_in, second_params, route_packs, order_packs, doc_packs)
        return (from_packs(first_out)[dealing], from_packs(second_out)[dealing])
    start_input = inputs.astype(jnp.float32)
    (first_out, second_out), pull_back = jax.vjp(forward, start_input, jnp.zeros_like(start_input), params)
    grad_input, grad_shift, grad_params = pull_back((jnp.zeros_like(first_out), cotangent.astype(jnp.float32)))
    activations = jnp.stack([first_out, second_out]).astype(jnp.bfloat16)
    input_grads = jnp.stack([grad_input, grad_shift]).astype(jnp.bfloat16)
    return (activations, input_grads, grad_params[0], grad_params[1], grad_params[2], grad_params[3], grad_params[4], grad_params[5])
```

```python
import jax
import jax.numpy as jnp
from jax import lax
from jax.sharding import PartitionSpec as P

HEAD_DIM = 64
EPSILON = 1e-06
NEGATIVE = -1e30
EXACT = lax.Precision.HIGHEST
EXTRA = 128
BF = jnp.bfloat16
F32 = jnp.float32


def dot32(a, b):
    return jnp.dot(a, b, preferred_element_type=F32)


def dot_nt(a, b):
    return lax.dot_general(a, b, (((1,), (1,)), ((), ())), preferred_element_type=F32)


def dot_tn(a, b):
    return lax.dot_general(a, b, (((0,), (0,)), ((), ())), preferred_element_type=F32)


def round_bf(v):
    return lax.reduce_precision(v, 8, 7)


def norm_scale(x):
    return lax.rsqrt(jnp.mean(x * x, axis=-1, keepdims=True) + EPSILON)


def norm_back(x, scale, gain, grad):
    weighted = grad * gain
    grad_x = scale * weighted - x * (scale * scale * scale) * jnp.mean(
        x * weighted, axis=-1, keepdims=True
    )
    return grad_x, jnp.sum(grad * x * scale, axis=0)


def heads_of(flat, heads):
    return flat.reshape(flat.shape[0], heads, HEAD_DIM)


def probs_of(query, key, allowed):
    scores = jnp.einsum("qhd,khd->hqk", query, key, preferred_element_type=F32)
    scores = jnp.where(allowed[None], scores * HEAD_DIM ** (-0.5), NEGATIVE)
    weights = jnp.exp(scores - jnp.max(scores, axis=-1, keepdims=True))
    return weights / jnp.sum(weights, axis=-1, keepdims=True)


def attn_forward(stream, weights, plan):
    qkv_weight, out_weight, gains, router = weights
    slots, onehot, allowed = plan
    width = stream.shape[1]
    heads = width // HEAD_DIM
    x = stream.astype(F32)
    attn_in = (x * norm_scale(x) * gains[0]).astype(BF)
    proj = dot32(attn_in, qkv_weight).astype(BF)
    query, key, value = (heads_of(proj[:, i * width : (i + 1) * width], heads) for i in range(3))
    probs = probs_of(query, key, allowed).astype(BF)
    mixed = jnp.einsum("hqk,khd->qhd", probs, value, preferred_element_type=F32)
    mixed = mixed.reshape(x.shape).astype(BF)
    mid = x + dot32(mixed, out_weight)
    mlp_in = (mid * norm_scale(mid) * gains[1]).astype(BF)
    logits = jnp.dot(mlp_in.astype(F32), router, precision=EXACT)
    rel = jnp.exp(logits - jnp.max(logits, axis=-1, keepdims=True))
    router_probs = rel / jnp.sum(rel, axis=-1, keepdims=True)
    gate = jnp.sum(jnp.where(onehot, router_probs, 0.0), axis=1, keepdims=True)
    dispatched = dot32(slots, mlp_in).astype(BF)
    return mid, attn_in, proj, mixed, mlp_in, router_probs, gate, dispatched


def attn_backward(grad_out, grad_slots, expert_slots, stream, saved, weights, plan):
    mid, attn_in, proj, mixed, mlp_in, router_probs, gate, _ = saved
    qkv_weight, out_weight, gains, router = weights
    slots, onehot, allowed = plan
    width = stream.shape[1]
    heads = width // HEAD_DIM
    x = stream.astype(F32)
    g = grad_out.astype(F32)
    grad_gate = jnp.sum(g * dot_tn(slots, expert_slots), axis=1, keepdims=True)
    grad_logits = grad_gate * gate * (onehot.astype(F32) - router_probs)
    grad_mlp = dot_tn(slots, grad_slots) + jnp.dot(grad_logits, router.T, precision=EXACT)
    grad_norm, gain_two = norm_back(mid, norm_scale(mid), gains[1], grad_mlp)
    grad_mid = g + grad_norm
    grad_low = grad_mid.astype(BF)
    grad_mixed = heads_of(dot_nt(grad_low, out_weight).astype(BF), heads)
    query, key, value = (heads_of(proj[:, i * width : (i + 1) * width], heads) for i in range(3))
    probs = probs_of(query, key, allowed)
    grad_probs = jnp.einsum("qhd,khd->hqk", grad_mixed, value, preferred_element_type=F32)
    inner = jnp.sum(probs * grad_probs, axis=-1, keepdims=True)
    grad_scores = (probs * (grad_probs - inner) * HEAD_DIM ** (-0.5)).astype(BF)
    grad_query = jnp.einsum("hqk,khd->qhd", grad_scores, key, preferred_element_type=F32)
    grad_key = jnp.einsum("hqk,qhd->khd", grad_scores, query, preferred_element_type=F32)
    grad_value = jnp.einsum(
        "hqk,qhd->khd", probs.astype(BF), grad_mixed, preferred_element_type=F32
    )
    grad_proj = jnp.concatenate(
        [m.reshape(x.shape).astype(BF) for m in (grad_query, grad_key, grad_value)], axis=1
    )
    grad_norm, gain_one = norm_back(x, norm_scale(x), gains[0], dot_nt(grad_proj, qkv_weight))
    grad_stream = (grad_mid + grad_norm).astype(BF)
    grad_router = jnp.dot(mlp_in.astype(F32).T, grad_logits, precision=EXACT)
    return grad_stream, (attn_in, grad_proj, mixed, grad_low, gain_one, gain_two, grad_router)


def solution(mesh):
    shape = mesh.shape
    n_pipe, n_dp, n_t = shape["pipe"], shape["dp"], shape["tensor"]
    axes = ("pipe", "dp", "tensor")
    plane = ("dp", "tensor")
    n_dev = n_dp * n_t

    def local(
        inputs,
        cotangent,
        dealing,
        routes,
        slot_order,
        doc_lengths,
        attn_weight,
        attn_out_weight,
        expert_in_weight,
        expert_out_weight,
        norm_gains,
        router_weight,
    ):
        dev_rows, width = inputs.shape
        experts = expert_in_weight.shape[1]
        reps = n_dp // experts
        half = dev_rows // n_t
        pack = dev_rows
        cap = pack // experts
        per = dev_rows // n_dev
        pipe = lax.axis_index("pipe")
        dp = lax.axis_index("dp")
        core = lax.axis_index("tensor")
        mine = dp // reps
        rep = dp % reps

        def moved(value, rule):
            pairs = []
            for a in range(n_pipe):
                for b in range(experts):
                    for c in range(reps):
                        for d in range(n_t):
                            to = rule(a, b, c, d)
                            if to is not None:
                                flat = [
                                    ((w * experts + x) * reps + y) * n_t + z
                                    for w, x, y, z in ((a, b, c, d), to)
                                ]
                                pairs.append(tuple(flat))
            return lax.ppermute(value, axes, pairs)

        def swap_core(value):
            return moved(value, lambda a, b, c, d: (a, b, c, 1 - d))

        def pick(blocks, step):
            return lax.dynamic_index_in_dim(blocks, mine ^ step, 0, keepdims=False)

        def exchange(blocks, rule_of=None):
            parts = []
            for step in range(experts):
                block = pick(blocks, step)
                if rule_of is not None:
                    block = moved(block, rule_of(step))
                elif step:
                    block = moved(block, lambda a, b, c, d: (a, b ^ step, c, d))
                parts.append(block)
            return jnp.stack(parts)

        def unswizzle(blocks):
            return jnp.stack([pick(blocks, owner) for owner in range(experts)])

        def rep_groups():
            return [[b * reps + c for c in range(reps)] for b in range(experts)]

        def rep_gather(value):
            if reps == 2:
                other = moved(value, lambda a, b, c, d: (a, b, 1 - c, d))
                both = jnp.stack([value, other])
                return jnp.where(rep == 0, both, both[::-1])
            return lax.all_gather(value, "dp", axis_index_groups=rep_groups())

        def rep_scatter(blocks):
            if reps == 2:
                other = lax.dynamic_index_in_dim(blocks, 1 - rep, 0, keepdims=False).astype(BF)
                kept = lax.dynamic_index_in_dim(blocks, rep, 0, keepdims=False)
                return kept + moved(other, lambda a, b, c, d: (a, b, 1 - c, d)).astype(F32)
            return lax.psum_scatter(
                blocks.astype(BF), "dp", axis_index_groups=rep_groups(), scatter_dimension=0
            ).astype(F32)

        target = dealing // dev_rows
        rows_at = jnp.arange(dev_rows)
        earlier = (target[:, None] == target[None, :]) & (rows_at[None, :] < rows_at[:, None])
        send_slot = target * per + jnp.sum(earlier.astype(jnp.int32), axis=1)
        send_hot = (rows_at[:, None] == send_slot[None, :]).astype(BF)
        small = jnp.concatenate([norm_gains[0].reshape(-1), router_weight[0].reshape(-1)])
        small_high = round_bf(small)
        small_mid = round_bf(small - small_high)
        small_low = round_bf(small - small_high - small_mid)
        small_cols = 3 * small.shape[0] // per
        params = jnp.concatenate([small_high, small_mid, small_low]).astype(BF)
        params = jnp.tile(params.reshape(per, small_cols), (n_dev, 1))
        numbers = jnp.stack(
            [dealing % dev_rows, routes[:, 0], slot_order // 256, slot_order % 256], axis=1
        ).astype(BF)
        payload = jnp.concatenate([jnp.where(pipe == 0, inputs, cotangent), numbers], axis=1)
        payload = dot32(send_hot, payload).astype(BF)
        blank = jnp.zeros((dev_rows, EXTRA - 4 - small_cols), BF)
        payload = jnp.concatenate([payload, params, blank], axis=1)
        dealt = lax.all_to_all(payload, plane, split_axis=0, concat_axis=0, tiled=True)
        small_all = dealt[:, width + 4 : width + 4 + small_cols].astype(F32)
        small_all = small_all.reshape(n_dev, 3, -1)
        small_all = small_all[:, 0] + small_all[:, 1] + small_all[:, 2]
        gain_count = norm_gains.shape[1] * norm_gains.shape[2]
        gains = jnp.swapaxes(small_all[:, :gain_count].reshape(n_dev, 2, -1), 0, 1)
        gains = gains.reshape(2, width)
        router = small_all[:, gain_count:].reshape(width, experts)
        both = lax.all_gather(dealt[:, : width + 4], "tensor", axis=0, tiled=False)
        place = both[:, :, width].astype(jnp.int32)
        row_pos = jnp.arange(n_t)[:, None] * half + place % half
        row_pos = jnp.where(place // half == core, row_pos, -1).reshape(-1)
        place_hot = (jnp.arange(pack)[:, None] == row_pos[None, :]).astype(BF)
        rows = dot32(place_hot, both.reshape(n_t * dev_rows, -1)).astype(BF)
        own_rows = rows[:, :width]
        numbers = rows[:, width:].astype(jnp.int32)
        expert_ids = numbers[:, 1]
        priority = numbers[:, 2] * 256 + numbers[:, 3]

        ends = jnp.cumsum(lax.dynamic_index_in_dim(doc_lengths, core, 0, keepdims=False))
        spots = jnp.arange(pack)
        doc = jnp.sum((spots[:, None] >= ends[None, :]).astype(jnp.int32), axis=1)
        allowed = (doc[:, None] == doc[None, :]) & (spots[None, :] <= spots[:, None])
        same = expert_ids[:, None] == expert_ids[None, :]
        before = priority[None, :] < priority[:, None]
        rank = jnp.sum((same & before).astype(jnp.int32), axis=1)
        slot_of = jnp.where(rank < cap, expert_ids * cap + rank, -1)
        slots = (jnp.arange(experts * cap)[:, None] == slot_of[None, :]).astype(BF)
        onehot = expert_ids[:, None] == jnp.arange(experts)[None, :]
        plan = (slots, onehot, allowed)

        shard, qkv_half = attn_weight.shape[1], attn_weight.shape[3]
        attn_bundle = jnp.concatenate(
            [attn_weight[0].reshape(shard, 3 * qkv_half), attn_out_weight[0].reshape(shard, -1)],
            axis=1,
        )
        attn_mine = lax.all_gather(attn_bundle, "dp", axis=0, tiled=True)
        attn_other = swap_core(attn_mine)
        attn_both = jnp.stack([attn_mine, attn_other])
        attn_both = jnp.where(core == 0, attn_both, attn_both[::-1])
        qkv_weight = attn_both[:, :, : 3 * qkv_half].reshape(n_t, width, 3, qkv_half)
        qkv_weight = qkv_weight.transpose(1, 2, 0, 3).reshape(width, -1)
        out_weight = attn_both[:, :, 3 * qkv_half :].reshape(width, width)
        weights = (qkv_weight, out_weight, gains, router)

        ff_half = expert_in_weight.shape[3]
        in_rows, out_rows = expert_in_weight.shape[2], expert_out_weight.shape[2]
        blocks_in = rep_gather(unswizzle(exchange(expert_in_weight[0])))
        blocks_out = rep_gather(unswizzle(exchange(expert_out_weight[0])))
        w_in = jnp.swapaxes(blocks_in, 0, 1).reshape(width, ff_half)
        w_out = jnp.swapaxes(blocks_out, 0, 1).reshape(ff_half, width)

        def spread(blocks, rule_of=None):
            got = exchange(blocks.reshape(experts, cap, width), rule_of).reshape(-1, width)
            return got

        def with_other(got):
            return jnp.concatenate([got, swap_core(got)], axis=0)

        def folded(partial):
            count = partial.shape[0] // 2
            return (partial[:count] + swap_core(partial[count:].astype(BF)).astype(F32)).astype(BF)

        def returned(values, rule_of=None):
            parts = []
            for step in range(experts):
                block = values[step * cap : (step + 1) * cap]
                if rule_of is not None:
                    block = moved(block, rule_of(step))
                elif step:
                    block = moved(block, lambda a, b, c, d: (a, b ^ step, c, d))
                parts.append(block)
            return unswizzle(jnp.stack(parts)).reshape(-1, width)

        def up(step):
            return lambda a, b, c, d: (1, b ^ step, c, d) if a == 0 else None

        def down(step):
            return lambda a, b, c, d: (0, b ^ step, c, d) if a == 1 else None

        def expert_forward(dispatched):
            pre = dot32(dispatched, w_in)
            act = jax.nn.gelu(pre).astype(BF)
            return pre, act, folded(dot32(act, w_out))

        def expert_backward(grad_slot, pre):
            grad_act = dot_nt(grad_slot, w_out)
            grad_pre = jax.vjp(jax.nn.gelu, pre)[1](grad_act)[0].astype(BF)
            return grad_pre, folded(dot_nt(grad_pre, w_in))

        def merged(mid, gate, expert_slots):
            return (mid + gate * dot_tn(slots, expert_slots)).astype(BF)

        saved = attn_forward(own_rows, weights, plan)
        mid_low, gate_low = saved[0], saved[6]
        got = with_other(spread(saved[7]))
        _, _, expert_slots = expert_forward(got)
        from_first = returned(expert_slots, up)
        mid_up = moved(mid_low, lambda a, b, c, d: (1, b, c, d) if a == 0 else None)
        gate_up = moved(gate_low, lambda a, b, c, d: (1, b, c, d) if a == 0 else None)
        stream = jnp.where(pipe == 0, own_rows, merged(mid_up, gate_up, from_first))

        saved = attn_forward(stream, weights, plan)
        mid, gate = saved[0], saved[6]
        dispatched = with_other(spread(saved[7]))
        pre, act, expert_slots = expert_forward(dispatched)
        expert_slots = returned(expert_slots)
        layer_out = merged(mid, gate, expert_slots)

        def slotted(gate_now, grad):
            return dot32(slots, (gate_now * grad.astype(F32)).astype(BF)).astype(BF)

        grad_got = spread(slotted(gate, own_rows))
        _, grad_disp = expert_backward(with_other(grad_got), pre)
        grad_stream, _ = attn_backward(
            own_rows, returned(grad_disp), expert_slots, stream, saved, weights, plan
        )
        grad_down = moved(grad_stream, lambda a, b, c, d: (0, b, c, d) if a == 1 else None)
        got_down = spread(slotted(gate_up, grad_stream), down)

        grad_out = jnp.where(pipe == 0, grad_down, own_rows)
        grad_got = with_other(jnp.where(pipe == 0, got_down, grad_got))
        grad_pre, grad_disp = expert_backward(grad_got, pre)
        grad_w_in = dot_tn(dispatched, grad_pre)
        grad_w_out = dot_tn(act, grad_got)
        layer_grad, record = attn_backward(
            grad_out, returned(grad_disp), expert_slots, stream, saved, weights, plan
        )

        def to_owner(grad, rows_each):
            blocks = grad.reshape(experts, reps, rows_each, -1)
            summed = rep_scatter(jnp.swapaxes(blocks, 0, 1))
            own = pick(summed, 0)
            parts = [own]
            for step in range(1, experts):
                block = pick(summed, step).astype(BF)
                parts.append(moved(block, lambda a, b, c, d: (a, b ^ step, c, d)).astype(F32))
            return unswizzle(jnp.stack(parts))[None]

        grad_expert_in = to_owner(grad_w_in, in_rows)
        grad_expert_out = to_owner(grad_w_out, out_rows)

        attn_in, grad_proj, mixed, grad_low, gain_one, gain_two, grad_router = record
        grad_qkv = dot_tn(attn_in, grad_proj).reshape(n_dp, shard, 3, n_t, qkv_half)
        grad_qkv = grad_qkv.transpose(3, 0, 1, 2, 4).reshape(n_t, n_dp, shard * 3, qkv_half)
        grad_o = dot_tn(mixed, grad_low).reshape(n_t, n_dp, -1, qkv_half)
        tiny = jnp.concatenate(
            [
                jnp.stack([gain_one, gain_two]).reshape(2, n_dp, n_t, -1).transpose(2, 1, 0, 3).reshape(n_t, n_dp, -1),
                grad_router.reshape(n_dp, n_t, -1).transpose(1, 0, 2),
            ],
            axis=2,
        )
        tiny_count = tiny.shape[2]
        tiny = jnp.pad(tiny, ((0, 0), (0, 0), (0, 16 * qkv_half - tiny_count)))
        tiny = tiny.reshape(n_t, n_dp, 16, qkv_half)
        bundle = jnp.concatenate([grad_qkv, grad_o, tiny], axis=2)
        kept = lax.dynamic_index_in_dim(bundle, core, 0, keepdims=False)
        other = lax.dynamic_index_in_dim(bundle, 1 - core, 0, keepdims=False).astype(BF)
        bundle = kept + swap_core(other).astype(F32)
        bundle = bundle.reshape((experts, reps) + bundle.shape[1:])
        bundle = rep_scatter(jnp.swapaxes(bundle, 0, 1))
        total = pick(bundle, 0)
        for step in range(1, experts):
            block = pick(bundle, step).astype(BF)
            total = total + moved(block, lambda a, b, c, d: (a, b ^ step, c, d)).astype(F32)
        qkv_rows = shard * 3
        grad_attn = total[:qkv_rows].reshape(1, shard, 3, qkv_half)
        grad_attn_out = total[qkv_rows:-16].reshape(1, -1, width)
        tiny = total[-16:].reshape(-1)[:tiny_count]
        grad_gains = tiny[:gain_count].reshape(1, 2, -1)
        grad_router = tiny[gain_count:].reshape(1, -1, experts)

        def sent_back(values):
            spread_out = dot_tn(place_hot, values).astype(BF).reshape(n_t, dev_rows, width)
            own = lax.dynamic_index_in_dim(spread_out, core, 0, keepdims=False)
            other = lax.dynamic_index_in_dim(spread_out, 1 - core, 0, keepdims=False)
            full = own + swap_core(other)
            back = lax.all_to_all(full, plane, split_axis=0, concat_axis=0, tiled=True)
            return dot_tn(send_hot, back).astype(BF)[None]

        return (
            sent_back(layer_out),
            sent_back(layer_grad),
            grad_attn,
            grad_attn_out,
            grad_expert_in,
            grad_expert_out,
            grad_gains,
            grad_router,
        )

    in_specs = (
        P(("dp", "tensor"), None),
        P(("dp", "tensor"), None),
        P(("dp", "tensor")),
        P(("dp", "tensor"), None),
        P(("dp", "tensor")),
        P("dp", None),
        P("pipe", "dp", None, "tensor"),
        P("pipe", ("tensor", "dp"), None),
        P("pipe", None, "dp", "tensor"),
        P("pipe", None, ("tensor", "dp"), None),
        P("pipe", None, ("dp", "tensor")),
        P("pipe", ("dp", "tensor"), None),
    )
    out_specs = (
        P("pipe", ("dp", "tensor"), None),
        P("pipe", ("dp", "tensor"), None),
        P("pipe", "dp", None, "tensor"),
        P("pipe", ("tensor", "dp"), None),
        P("pipe", None, "dp", "tensor"),
        P("pipe", None, ("tensor", "dp"), None),
        P("pipe", None, ("dp", "tensor")),
        P("pipe", ("dp", "tensor"), None),
    )
    return jax.shard_map(local, mesh=mesh, in_specs=in_specs, out_specs=out_specs, check_vma=False)
```

```python
import functools

import jax
import jax.numpy as jnp
from jax import lax
from jax.experimental import pallas as pl
from jax.experimental.pallas import tpu as pltpu
from jax.sharding import PartitionSpec as P

HEAD_DIM = 64
EPSILON = 1e-06
NEGATIVE = -1e30
EXACT = lax.Precision.HIGHEST
EXTRA = 128
BF = jnp.bfloat16
F32 = jnp.float32
VM = pl.BlockSpec(memory_space=pltpu.VMEM)
SM = pl.BlockSpec(memory_space=pltpu.SMEM)
HB = pl.BlockSpec(memory_space=pl.ANY)
PIPE, MINE, REP, CORE, SPLIT = range(5)


def dot32(a, b):
    return jnp.dot(a, b, preferred_element_type=F32)


def dot_nt(a, b):
    return lax.dot_general(a, b, (((1,), (1,)), ((), ())), preferred_element_type=F32)


def dot_tn(a, b):
    return lax.dot_general(a, b, (((0,), (0,)), ((), ())), preferred_element_type=F32)


def norm_scale(x):
    return lax.rsqrt(jnp.mean(x * x, axis=-1, keepdims=True) + EPSILON)


def norm_back(x, scale, gain, grad):
    weighted = grad * gain
    grad_x = scale * weighted - x * (scale * scale * scale) * jnp.mean(
        x * weighted, axis=-1, keepdims=True
    )
    return grad_x, jnp.sum(grad * (x * scale), axis=0, keepdims=True)


def kernel_call(body, name, outs, ins, specs, scratch=(), flops=0, size=0, exps=0):
    return pl.pallas_call(
        body,
        name=name,
        out_shape=[jax.ShapeDtypeStruct(shape, kind) for shape, kind in outs],
        in_specs=specs,
        out_specs=[VM] * len(outs),
        scratch_shapes=list(scratch),
        compiler_params=pltpu.CompilerParams(vmem_limit_bytes=50 << 20),
        cost_estimate=pl.CostEstimate(flops=flops, bytes_accessed=size, transcendentals=exps),
    )(*ins)


def deal_kernel(facts, both, own_rows, slots, onehot, place):
    width = own_rows.shape[1]
    pack = own_rows.shape[0]
    total = both.shape[0]
    half = pack // 2
    core = facts[CORE].astype(F32)
    numbers = both[:, width:]
    spot = numbers[:, 0:1].astype(F32)
    source = (lax.broadcasted_iota(jnp.int32, (total, 1), 0) >= pack).astype(F32)
    upper = (spot >= half).astype(F32)
    where = jnp.where(upper == core, source * half + spot - upper * half, -1.0)
    spots = lax.broadcasted_iota(jnp.int32, (total, pack), 1).astype(F32)
    hot = (spots == where).astype(F32).astype(BF)
    place[...] = hot
    own_rows[...] = dot_tn(hot, both[:, :width]).astype(BF)
    mine = dot_tn(hot, numbers)
    lanes = lax.broadcasted_iota(jnp.int32, (EXTRA, EXTRA), 0)
    eye = (lanes == lax.broadcasted_iota(jnp.int32, (EXTRA, EXTRA), 1)).astype(F32).astype(BF)
    across = dot_nt(eye, mine.astype(BF))
    expert_col, expert_row = mine[:, 1:2], across[1:2, :]
    order_col = mine[:, 2:3] * 256.0 + mine[:, 3:4]
    order_row = across[2:3, :] * 256.0 + across[3:4, :]
    ahead = (expert_col == expert_row) & (order_col < order_row)
    rank = jnp.sum(ahead.astype(F32), axis=0, keepdims=True).astype(jnp.int32)
    experts = 4
    cap = pack // experts
    block = jnp.bitwise_xor(expert_row.astype(jnp.int32), facts[MINE])
    slot = jnp.where(rank < cap, block * cap + rank, -1)
    slots[...] = (lax.broadcasted_iota(jnp.int32, (pack, pack), 0) == slot).astype(F32).astype(BF)
    onehot[...] = (
        lax.broadcasted_iota(jnp.int32, (pack, EXTRA), 1) == expert_col.astype(jnp.int32)
    ).astype(F32)


def mask_of(facts, pack):
    query = lax.broadcasted_iota(jnp.int32, (pack, pack), 0)
    key = lax.broadcasted_iota(jnp.int32, (pack, pack), 1)
    split = facts[SPLIT]
    return ((query < split) == (key < split)) & (key <= query)


def stacked(refs):
    return jnp.concatenate([ref[...] for ref in refs], axis=0)


def attn_kernel(second, facts, *refs):
    refs = list(refs)
    own_rows = refs.pop(0)
    if second:
        up = refs.pop(0)
        slots_in = [refs.pop(0) for _ in range(4)]
    attn_own, attn_other, gains, router, slots, onehot = (refs.pop(0) for _ in range(6))
    mid, attn_in, proj, mixed, mlp_in, probs = (refs.pop(0) for _ in range(6))
    blocks = [refs.pop(0) for _ in range(4)]
    pack, width = own_rows.shape
    cols = attn_own.shape[1]
    cap = pack // 4
    hot = slots[...]
    if second:
        stream = refs.pop(0)
        grads = [refs.pop(0) for _ in range(4)]
        came = up[:, :width] + up[:, width : width + 1] * dot_tn(hot, stacked(slots_in))
        rows = jnp.where(facts[PIPE] == 0, own_rows[...], came.astype(BF))
        stream[...] = rows
    else:
        rows = own_rows[...]
    x = rows.astype(F32)
    normed = (x * norm_scale(x) * gains[0:1, :]).astype(BF)
    attn_in[...] = normed
    allowed = mask_of(facts, pack)
    for at, weight in ((0, attn_own), (1, attn_other)):
        for part in range(3):
            proj[at, part] = dot32(normed, weight[part * width : (part + 1) * width, :]).astype(BF)
        for head in range(cols // HEAD_DIM):
            lanes = slice(head * HEAD_DIM, (head + 1) * HEAD_DIM)
            scores = dot_nt(proj[at, 0, :, lanes], proj[at, 1, :, lanes]) * HEAD_DIM ** (-0.5)
            scores = jnp.where(allowed, scores, NEGATIVE)
            weights = jnp.exp(scores - jnp.max(scores, axis=-1, keepdims=True))
            share = (weights * (1.0 / jnp.sum(weights, axis=-1, keepdims=True))).astype(BF)
            spot = at * cols + head * HEAD_DIM
            mixed[:, spot : spot + HEAD_DIM] = dot32(share, proj[at, 2, :, lanes]).astype(BF)
    base = 3 * width
    for side in range(2):
        rows_at = slice(base + side * cols, base + (side + 1) * cols)
        lanes = slice(side * cols, (side + 1) * cols)
        mid[:, lanes] = (
            x[:, lanes]
            + dot32(mixed[:, :cols], attn_own[rows_at, :])
            + dot32(mixed[:, cols:], attn_other[rows_at, :])
        )
    m = mid[:, :width]
    low = (m * norm_scale(m) * gains[1:2, :]).astype(BF)
    mlp_in[...] = low
    logits = dot32(low, router[...])
    lane = lax.broadcasted_iota(jnp.int32, logits.shape, 1)
    logits = logits + pltpu.roll(logits, EXTRA - 4, 1) + pltpu.roll(logits, EXTRA - 8, 1)
    logits = jnp.where(lane < 4, logits, NEGATIVE)
    rel = jnp.exp(logits - jnp.max(logits, axis=-1, keepdims=True))
    share = rel / jnp.sum(rel, axis=-1, keepdims=True)
    probs[...] = share
    gate = jnp.sum(share * onehot[...], axis=-1, keepdims=True)
    mid[:, width:] = jnp.broadcast_to(gate, (pack, EXTRA))
    for step in range(4):
        blocks[step][...] = dot32(hot[step * cap : (step + 1) * cap, :], low).astype(BF)
    if second:
        weighted = (gate * own_rows[...].astype(F32)).astype(BF)
        for step in range(4):
            grads[step][...] = dot32(hot[step * cap : (step + 1) * cap, :], weighted).astype(BF)


def attn_forward(facts, own_rows, weights, plan, came=None):
    attn_own, attn_other, gains, router3, _ = weights
    slots, onehot = plan
    pack, width = own_rows.shape
    cols = attn_own.shape[1]
    cap = pack // 4
    second = came is not None
    ins = [facts, own_rows] + (list(came) if second else [])
    ins += [attn_own, attn_other, gains, router3, slots, onehot]
    outs = [
        ((pack, width + EXTRA), F32),
        ((pack, width), BF),
        ((2, 3, pack, cols), BF),
        ((pack, width), BF),
        ((pack, width), BF),
        ((pack, EXTRA), F32),
    ]
    outs += [((cap, width), BF)] * 4
    if second:
        outs += [((pack, width), BF)] + [((cap, width), BF)] * 4
    return kernel_call(
        functools.partial(attn_kernel, second),
        "attn_second" if second else "attn_first",
        outs,
        ins,
        [SM] + [VM] * (len(ins) - 1),
        flops=2 * pack * width * width * 5,
        size=8 * width * width,
        exps=pack * pack * 12,
    )


def attn_back_kernel(first, facts, *refs):
    refs = list(refs)
    grad_out = refs.pop(0)
    if first:
        up = refs.pop(0)
    else:
        own_rows = refs.pop(0)
    grad_slots = [refs.pop(0) for _ in range(4)]
    expert_slots = [refs.pop(0) for _ in range(4)]
    stream, mid, proj, mlp_in, probs = (refs.pop(0) for _ in range(5))
    attn_own, attn_other, gains, router, slots, onehot = (refs.pop(0) for _ in range(6))
    grad_stream = refs.pop(0)
    if first:
        blocks = [refs.pop(0) for _ in range(4)]
        grad_proj = refs.pop(0)
    else:
        grad_proj, grad_low, grad_gains, grad_router = (refs.pop(0) for _ in range(4))
    pack, width = stream.shape
    cols = attn_own.shape[1]
    cap = pack // 4
    hot = slots[...]
    rows = grad_out[...]
    if not first:
        rows = jnp.where(facts[PIPE] == 0, rows, own_rows[...])
    g = rows.astype(F32)
    grad_gate = jnp.sum(g * dot_tn(hot, stacked(expert_slots)), axis=-1, keepdims=True)
    gate = mid[:, width : width + 1]
    grad_logits = grad_gate * gate * (onehot[...] - probs[...])
    m = mid[:, :width]
    grad_mlp = dot_tn(hot, stacked(grad_slots)) + jnp.dot(
        grad_logits, router[...], preferred_element_type=F32, precision=EXACT
    )
    grad_norm, gain_two = norm_back(m, norm_scale(m), gains[1:2, :], grad_mlp)
    grad_mid = g + grad_norm
    low = grad_mid.astype(BF)
    allowed = mask_of(facts, pack)
    grad_in = jnp.zeros((pack, width), F32)
    base = 3 * width
    for at, weight in ((0, attn_own), (1, attn_other)):
        grad_mixed = (
            dot_nt(low[:, :cols], weight[base : base + cols, :])
            + dot_nt(low[:, cols:], weight[base + cols : base + 2 * cols, :])
        ).astype(BF)
        for head in range(cols // HEAD_DIM):
            lanes = slice(head * HEAD_DIM, (head + 1) * HEAD_DIM)
            query, key, value = (proj[at, part, :, lanes] for part in range(3))
            grad_head = grad_mixed[:, lanes]
            scores = dot_nt(query, key) * HEAD_DIM ** (-0.5)
            scores = jnp.where(allowed, scores, NEGATIVE)
            share = jnp.exp(scores - jnp.max(scores, axis=-1, keepdims=True))
            share = share * (1.0 / jnp.sum(share, axis=-1, keepdims=True))
            grad_share = dot_nt(grad_head, value)
            pulled = share * grad_share
            inner = jnp.sum(pulled, axis=-1, keepdims=True)
            grad_scores = ((pulled - share * inner) * HEAD_DIM ** (-0.5)).astype(BF)
            grad_proj[at, 0, :, lanes] = dot32(grad_scores, key).astype(BF)
            grad_proj[at, 1, :, lanes] = dot_tn(grad_scores, query).astype(BF)
            grad_proj[at, 2, :, lanes] = dot_tn(share.astype(BF), grad_head).astype(BF)
        for part in range(3):
            grad_in += dot_nt(grad_proj[at, part], weight[part * width : (part + 1) * width, :])
    x = stream[...].astype(F32)
    grad_norm, gain_one = norm_back(x, norm_scale(x), gains[0:1, :], grad_in)
    result = (grad_mid + grad_norm).astype(BF)
    grad_stream[...] = result
    if first:
        weighted = (up[:, width : width + 1] * result.astype(F32)).astype(BF)
        for step in range(4):
            blocks[step][...] = dot32(hot[step * cap : (step + 1) * cap, :], weighted).astype(BF)
    else:
        grad_low[...] = low
        grad_gains[0:1, :] = gain_one
        grad_gains[1:2, :] = gain_two
        high = grad_logits.astype(BF)
        rest = (grad_logits - high.astype(F32)).astype(BF)
        grad_router[...] = dot_tn(mlp_in[...], high) + dot_tn(mlp_in[...], rest)


def attn_backward(facts, grad_out, extra, grad_slots, expert_slots, saved, weights, plan, first):
    attn_own, attn_other, gains, _, router = weights
    slots, onehot = plan
    stream, mid, proj, mlp_in, probs = saved
    pack, width = stream.shape
    cols = attn_own.shape[1]
    cap = pack // 4
    ins = [facts, grad_out, extra, *grad_slots, *expert_slots, stream, mid, proj, mlp_in, probs]
    ins += [attn_own, attn_other, gains, router, slots, onehot]
    outs = [((pack, width), BF)]
    if first:
        outs += [((cap, width), BF)] * 4
    outs += [((2, 3, pack, cols), BF)]
    if not first:
        outs += [((pack, width), BF), ((2, width), F32), ((width, EXTRA), F32)]
    return kernel_call(
        functools.partial(attn_back_kernel, first),
        "attn_back_first" if first else "attn_back_second",
        outs,
        ins,
        [SM] + [VM] * (len(ins) - 1),
        flops=2 * pack * width * width * 8,
        size=8 * width * width,
        exps=pack * pack * 12,
    )


def gelu_parts(u):
    inner = 0.7978845608028654 * (u + 0.044715 * (u * u * u))
    t = jnp.tanh(inner)
    return t, 0.5 * u * (1.0 + t)


def gelu_slope(u):
    t, _ = gelu_parts(u)
    slope = 0.7978845608028654 * (1.0 + 3.0 * 0.044715 * (u * u))
    return 0.5 * (1.0 + t) + 0.5 * u * (1.0 - t * t) * slope


def bring(facts, pieces, places, scratch, sems):
    copies = []
    for piece, spots in zip(pieces, places, strict=True):
        for source, target, rows, column, columns in spots(facts):
            copies.append(
                pltpu.make_async_copy(
                    piece.at[pl.ds(source, rows), pl.ds(0, columns)],
                    scratch.at[pl.ds(target, rows), pl.ds(column, columns)],
                    sems.at[len(copies)],
                )
            )
    for copy in copies:
        copy.start()
    return copies


TILE = 256


def expert_kernel(places_in, places_out, facts, *refs):
    refs = list(refs)
    blocks = [refs.pop(0) for _ in range(8)]
    pieces = [refs.pop(0) for _ in range(len(places_in))]
    pre, act, own, other = (refs.pop(0) for _ in range(4))
    w_in, w_out, rows, sems_in, sems_out = refs
    arriving = bring(facts, pieces, places_in, w_in, sems_in)
    later = bring(facts, pieces, places_out, w_out, sems_out)
    cap = blocks[0].shape[0]
    for at, block in enumerate(blocks):
        rows[at * cap : (at + 1) * cap, :] = block[...]
    for copy in arriving:
        copy.wait()
    ff = w_in.shape[1]
    width = w_in.shape[0]

    @pl.loop(0, ff // TILE)
    def _(tile):
        lanes = pl.ds(pl.multiple_of(tile * TILE, TILE), TILE)
        value = dot32(rows[...], w_in[:, lanes])
        pre[:, lanes] = value
        act[:, lanes] = gelu_parts(value)[1].astype(BF)

    for copy in later:
        copy.wait()
    count = 4 * cap

    @pl.loop(0, width // TILE)
    def _(tile):
        lanes = pl.ds(pl.multiple_of(tile * TILE, TILE), TILE)
        value = dot32(act[...], w_out[:, lanes])
        own[:, lanes] = value[:count]
        other[:, lanes] = value[count:].astype(BF)


def expert_back_kernel(places_in, places_out, facts, *refs):
    refs = list(refs)
    blocks = [refs.pop(0) for _ in range(8)]
    pre = refs.pop(0)
    pieces = [refs.pop(0) for _ in range(len(places_in))]
    grad_pre, own, other = (refs.pop(0) for _ in range(3))
    w_in, w_out, rows, sems_in, sems_out = refs
    arriving = bring(facts, pieces, places_out, w_out, sems_out)
    later = bring(facts, pieces, places_in, w_in, sems_in)
    cap = blocks[0].shape[0]
    for at, block in enumerate(blocks):
        rows[at * cap : (at + 1) * cap, :] = block[...]
    for copy in arriving:
        copy.wait()
    ff = w_in.shape[1]
    width = w_in.shape[0]

    @pl.loop(0, ff // TILE)
    def _(tile):
        lanes = pl.ds(pl.multiple_of(tile * TILE, TILE), TILE)
        value = dot_nt(rows[...], w_out[lanes, :])
        grad_pre[:, lanes] = (value * gelu_slope(pre[:, lanes])).astype(BF)

    for copy in later:
        copy.wait()
    count = 4 * cap

    @pl.loop(0, width // TILE)
    def _(tile):
        lanes = pl.ds(pl.multiple_of(tile * TILE, TILE), TILE)
        value = dot_nt(grad_pre[...], w_in[lanes, :])
        own[:, lanes] = value[:count]
        other[:, lanes] = value[count:].astype(BF)


def expert_call(body, name, facts, blocks, pre, pieces, places, width, ff):
    places_in, places_out = places
    cap = blocks[0].shape[0]
    count = 4 * cap
    back = pre is not None
    ins = [facts, *blocks] + ([pre] if back else []) + list(pieces)
    outs = [((2 * count, ff), BF)] if back else [((2 * count, ff), F32), ((2 * count, ff), BF)]
    outs += [((count, width), F32), ((count, width), BF)]
    numbers = jnp.zeros((8,), jnp.int32)
    sizes = [sum(len(spots(numbers)) for spots in each) for each in places]
    scratch = [
        pltpu.VMEM((width, ff), BF),
        pltpu.VMEM((ff, width), BF),
        pltpu.VMEM((2 * count, width), BF),
        pltpu.SemaphoreType.DMA((sizes[0],)),
        pltpu.SemaphoreType.DMA((sizes[1],)),
    ]
    specs = [SM] + [VM] * (len(ins) - 1 - len(pieces)) + [HB] * len(pieces)
    return kernel_call(
        functools.partial(body, places_in, places_out),
        name,
        outs,
        ins,
        specs,
        scratch,
        flops=8 * count * width * ff,
        size=6 * width * ff,
        exps=2 * count * ff,
    )


def fold_kernel(own, other, *blocks):
    cap = blocks[0].shape[0]
    for step, block in enumerate(blocks):
        rows = slice(step * cap, (step + 1) * cap)
        block[...] = (own[rows, :] + other[rows, :].astype(F32)).astype(BF)


def fold(own, other, name):
    count, width = own.shape
    cap = count // 4
    return kernel_call(
        fold_kernel, name, [((cap, width), BF)] * 4, [own, other], [VM, VM], size=8 * count * width
    )


def return_kernel(merge, *refs):
    refs = list(refs)
    rows = refs.pop(0)
    if merge:
        hot = refs.pop(0)
        slots_in = [refs.pop(0) for _ in range(4)]
        width = slots_in[0].shape[1]
        values = rows[:, :width] + rows[:, width : width + 1] * dot_tn(hot[...], stacked(slots_in))
        values = values.astype(BF)
    else:
        values = rows[...]
    place, own, other, facts = refs[0], refs[2], refs[3], refs[1]
    pack = own.shape[0]
    core = facts[CORE]
    own[...] = dot32(place[pl.ds(pl.multiple_of(core * pack, pack), pack), :], values).astype(BF)
    other[...] = dot32(
        place[pl.ds(pl.multiple_of((1 - core) * pack, pack), pack), :], values
    ).astype(BF)


def sent_rows(facts, merge, rows, extra, place, width):
    pack = place.shape[1]
    ins = [rows, *extra, place, facts]
    outs = [((pack, width), BF)] * 2
    return kernel_call(
        functools.partial(return_kernel, merge),
        "return_merged" if merge else "return_rows",
        outs,
        ins,
        [VM] * (len(ins) - 1) + [SM],
        flops=4 * pack * pack * width,
        size=8 * pack * width,
    )


def gather_kernel(places, facts, *refs):
    pieces, out, sems = refs[:-2], refs[-2], refs[-1]
    for copy in bring(facts, pieces, places, out, sems):
        copy.wait()


def gather_pieces(facts, pieces, places, shape):
    numbers = jnp.zeros((8,), jnp.int32)
    count = sum(len(spots(numbers)) for spots in places)
    return pl.pallas_call(
        functools.partial(gather_kernel, places),
        name="gather_pieces",
        out_shape=jax.ShapeDtypeStruct(shape, BF),
        in_specs=[SM] + [HB] * len(pieces),
        out_specs=HB,
        scratch_shapes=[pltpu.SemaphoreType.DMA((count,))],
        compiler_params=pltpu.CompilerParams(vmem_limit_bytes=16 << 20),
        cost_estimate=pl.CostEstimate(
            flops=0, bytes_accessed=4 * shape[0] * shape[1], transcendentals=0
        ),
    )(facts, *pieces)


def expert_grad_kernel(split, facts, *refs):
    refs = list(refs)
    blocks = [refs.pop(0) for _ in range(8)]
    grads = [refs.pop(0) for _ in range(8)]
    act, grad_pre = refs.pop(0), refs.pop(0)
    if split:
        sends = [refs.pop(0) for _ in range(4)]
        keeps = [refs.pop(0) for _ in range(4)]
        grad_in, grad_out, rows, grad_rows = refs
    else:
        grad_in, grad_out, rows, grad_rows = refs
    cap = blocks[0].shape[0]
    for at in range(8):
        rows[at * cap : (at + 1) * cap, :] = blocks[at][...]
        grad_rows[at * cap : (at + 1) * cap, :] = grads[at][...]
    ff = act.shape[1]
    width = rows.shape[1]

    @pl.loop(0, ff // TILE)
    def _(tile):
        lanes = pl.ds(pl.multiple_of(tile * TILE, TILE), TILE)
        grad_in[:, lanes] = dot_tn(rows[...], grad_pre[:, lanes])
        grad_out[lanes, :] = dot_tn(act[:, lanes], grad_rows[...])

    if split:
        shard, out_shard = width // 8, ff // 8
        for step in range(4):
            owner = jnp.bitwise_xor(facts[MINE], step) * 2
            for rep, target in ((1 - facts[REP], sends[step]), (facts[REP], keeps[step])):
                spot = pl.ds(pl.multiple_of((owner + rep) * shard, shard), shard)
                target[0:shard, :] = grad_in[spot, :width].astype(BF)
                target[shard : 2 * shard, :] = grad_in[spot, width:].astype(BF)
                spot = pl.ds(pl.multiple_of((owner + rep) * out_shard, out_shard), out_shard)
                target[2 * shard :, :] = grad_out[spot, :].astype(BF)


def expert_grads(facts, blocks, grads, act, grad_pre, split):
    cap, width = blocks[0].shape
    ff = act.shape[1]
    ins = [facts, *blocks, *grads, act, grad_pre]
    full = [((width, ff), F32), ((ff, width), F32)]
    rows = [pltpu.VMEM((8 * cap, width), BF)] * 2
    if split:
        outs = [((width // 2, width), BF)] * 8
        scratch = [pltpu.VMEM(*each) for each in full] + rows
    else:
        outs, scratch = full, rows
    return kernel_call(
        functools.partial(expert_grad_kernel, split),
        "expert_grads",
        outs,
        ins,
        [SM] + [VM] * (len(ins) - 1),
        scratch,
        flops=32 * cap * width * ff,
        size=8 * width * ff,
    )


def owner_kernel(facts, *refs):
    pieces, grad_in, grad_out = refs[:-2], refs[-2], refs[-1]
    shard = grad_in.shape[1]
    width = grad_out.shape[2]
    for step, piece in enumerate(pieces):
        at = jnp.bitwise_xor(facts[MINE], step)
        grad_in[at, :, :width] = piece[:shard, :].astype(F32)
        grad_in[at, :, width:] = piece[shard : 2 * shard, :].astype(F32)
        grad_out[at] = piece[2 * shard :, :].astype(F32)


def owner_grads(facts, pieces, in_shape, out_shape):
    return kernel_call(
        owner_kernel,
        "owner_grads",
        [(in_shape, F32), (out_shape, F32)],
        [facts, *pieces],
        [SM] + [VM] * len(pieces),
        size=24 * pieces[0].size,
    )


def attn_grad_kernel(attn_in, grad_proj, mixed, low, own, other):
    width = attn_in.shape[1]
    cols = own.shape[1]
    for at, target in ((0, own), (1, other)):
        for part in range(3):
            target[part * width : (part + 1) * width, :] = dot_tn(
                attn_in[...], grad_proj[at, part]
            ).astype(BF)
        for side in range(2):
            spot = 3 * width + side * cols
            target[spot : spot + cols, :] = dot_tn(
                mixed[:, at * cols : (at + 1) * cols], low[:, side * cols : (side + 1) * cols]
            ).astype(BF)


def attn_grads(attn_in, grad_proj, mixed, low):
    pack, width = attn_in.shape
    cols = grad_proj.shape[3]
    return kernel_call(
        attn_grad_kernel,
        "attn_grads",
        [((3 * width + 2 * cols, cols), BF)] * 2,
        [attn_in, grad_proj, mixed, low],
        [VM] * 4,
        flops=8 * pack * width * width,
        size=8 * width * width,
    )


def attn_split_kernel(facts, own, came, *refs):
    sends, keeps = refs[:4], refs[4:]
    cols = own.shape[1]
    width = 2 * cols
    shard = width // 8
    for step in range(4):
        owner = jnp.bitwise_xor(facts[MINE], step) * 2
        for rep, target in ((1 - facts[REP], sends[step]), (facts[REP], keeps[step])):
            at = owner + rep
            for source, rows, spot in attn_rows(width, shard):
                where = pl.ds(pl.multiple_of(source + at * rows, rows), rows)
                target[spot : spot + rows, :] = (
                    own[where, :].astype(F32) + came[where, :].astype(F32)
                ).astype(BF)


def attn_rows(width, shard):
    out = shard // 2
    return (
        (0, shard, 0),
        (width, shard, shard),
        (2 * width, shard, 2 * shard),
        (3 * width, out, 3 * shard),
        (3 * width + width // 2, out, 3 * shard + out),
    )


def attn_split(facts, own, came):
    rows, cols = own.shape
    return kernel_call(
        attn_split_kernel,
        "attn_split",
        [((rows // 8, cols), BF)] * 8,
        [facts, own, came],
        [SM, VM, VM],
        size=6 * rows * cols,
    )


def solution(mesh):
    shape = mesh.shape
    n_pipe, n_dp, n_t = shape["pipe"], shape["dp"], shape["tensor"]
    axes = ("pipe", "dp", "tensor")
    plane = ("dp", "tensor")
    n_dev = n_dp * n_t

    def local(
        inputs,
        cotangent,
        dealing,
        routes,
        slot_order,
        doc_lengths,
        attn_weight,
        attn_out_weight,
        expert_in_weight,
        expert_out_weight,
        norm_gains,
        router_weight,
    ):
        dev_rows, width = inputs.shape
        experts = expert_in_weight.shape[1]
        reps = n_dp // experts
        paired = reps == 2
        pack = dev_rows
        cap = pack // experts
        per = dev_rows // n_dev
        shard, cols = attn_weight.shape[1], attn_weight.shape[3]
        ff = expert_in_weight.shape[3]
        in_rows, out_rows = expert_in_weight.shape[2], expert_out_weight.shape[2]
        pipe = lax.axis_index("pipe")
        dp = lax.axis_index("dp")
        core = lax.axis_index("tensor")
        mine = dp // reps
        rep = dp % reps
        lengths = lax.dynamic_index_in_dim(doc_lengths, core, 0, keepdims=False)
        zero = jnp.int32(0)
        facts = jnp.stack([pipe, mine, rep, core, lengths[0], zero, zero, zero]).astype(jnp.int32)

        def moved(value, rule):
            pairs = []
            for a in range(n_pipe):
                for b in range(experts):
                    for c in range(reps):
                        for d in range(n_t):
                            to = rule(a, b, c, d)
                            if to is not None:
                                flat = [
                                    ((w * experts + x) * reps + y) * n_t + z
                                    for w, x, y, z in ((a, b, c, d), to)
                                ]
                                pairs.append(tuple(flat))
            return lax.ppermute(value, axes, pairs)

        def swap_core(value):
            return moved(value, lambda a, b, c, d: (a, b, c, 1 - d))

        def swap_rep(value):
            return moved(value, lambda a, b, c, d: (a, b, 1 - c, d))

        def across(step):
            return lambda a, b, c, d: (a, b ^ step, c, d)

        def up(step):
            return lambda a, b, c, d: (1, b ^ step, c, d) if a == 0 else None

        def down(step):
            return lambda a, b, c, d: (0, b ^ step, c, d) if a == 1 else None

        order = (2, 3, 1)

        def exchange(blocks):
            out = {0: blocks[0]}
            for step in order:
                out[step] = moved(blocks[step], across(step))
            return [out[step] for step in range(experts)]

        def crossed(blocks, way):
            out = {}
            for step in (*order, 0):
                out[step] = moved(blocks[step], way(step))
            return [out[step] for step in range(experts)]

        def with_other(blocks):
            out = {}
            for step in (0, 1, 2, 3):
                out[step] = swap_core(blocks[step])
            return list(blocks) + [out[step] for step in range(experts)]

        def pick(blocks, step):
            return lax.dynamic_index_in_dim(blocks, mine ^ step, 0, keepdims=False)

        rep_groups = [[b * reps + c for c in range(reps)] for b in range(experts)]

        target = dealing // dev_rows
        rows_at = jnp.arange(dev_rows)
        earlier = (target[:, None] == target[None, :]) & (rows_at[None, :] < rows_at[:, None])
        send_slot = target * per + jnp.sum(earlier.astype(jnp.int32), axis=1)
        send_hot = (rows_at[:, None] == send_slot[None, :]).astype(BF)
        small = jnp.concatenate([norm_gains[0].reshape(-1), router_weight[0].reshape(-1)])
        small_high = lax.reduce_precision(small, 8, 7)
        small_mid = lax.reduce_precision(small - small_high, 8, 7)
        small_low = lax.reduce_precision(small - small_high - small_mid, 8, 7)
        small_cols = 3 * small.shape[0] // per
        params = jnp.concatenate([small_high, small_mid, small_low]).astype(BF)
        params = jnp.tile(params.reshape(per, small_cols), (n_dev, 1))
        numbers = jnp.stack(
            [dealing % dev_rows, routes[:, 0], slot_order // 256, slot_order % 256], axis=1
        ).astype(BF)
        payload = jnp.concatenate([jnp.where(pipe == 0, inputs, cotangent), numbers], axis=1)
        payload = dot32(send_hot, payload).astype(BF)
        blank = jnp.zeros((dev_rows, EXTRA - 4 - small_cols), BF)
        payload = jnp.concatenate([payload, params, blank], axis=1)
        dealt = lax.all_to_all(payload, plane, split_axis=0, concat_axis=0, tiled=True)
        parts = dealt[:, width + 4 : width + 4 + small_cols].reshape(n_dev, 3, -1)
        gain_count = norm_gains.shape[1] * norm_gains.shape[2]
        gains = jnp.sum(parts[:, :, :gain_count].astype(F32), axis=1)
        gains = jnp.swapaxes(gains.reshape(n_dev, 2, -1), 0, 1).reshape(2, width)
        router = parts[:, :, gain_count:].reshape(n_dev, 3, -1, experts)
        router3 = jnp.swapaxes(router, 1, 2).reshape(width, 3 * experts)
        router3 = jnp.pad(router3, ((0, 0), (0, EXTRA - 3 * experts)))
        router = jnp.sum(router.astype(F32), axis=1).reshape(width, experts)
        router = jnp.pad(router.T, ((0, EXTRA - experts), (0, 0)))
        both = lax.all_gather(dealt, "tensor", axis=0, tiled=True)
        own_rows, slots, onehot, place = kernel_call(
            deal_kernel,
            "deal",
            [((pack, width), BF), ((pack, pack), BF), ((pack, EXTRA), F32), ((2 * pack, pack), BF)],
            [facts, both],
            [SM, VM],
            flops=4 * pack * pack * width,
            size=4 * pack * width,
        )
        plan = (slots, onehot)

        out_shard = attn_out_weight[0]
        attn_bundle = jnp.concatenate(
            [attn_weight[0, :, part] for part in range(3)] + [out_shard[:, :cols], out_shard[:, cols:]],
            axis=0,
        )
        attn_shape = (4 * width, cols)

        def attn_places(way, step):
            def spots(numbers):
                owner = jnp.bitwise_xor(numbers[MINE], step) * 2
                owner = owner + (numbers[REP] if way == 0 else 1 - numbers[REP])
                return [
                    (spot, pl.multiple_of(source + owner * rows, rows), rows, 0, cols)
                    for source, rows, spot in attn_rows(width, shard)
                ]

            return spots

        def expert_places(way, step):
            def owner_of(numbers):
                owner = jnp.bitwise_xor(numbers[MINE], step) * 2
                return owner + (numbers[REP] if way == 0 else 1 - numbers[REP])

            def spots_in(numbers):
                at = pl.multiple_of(owner_of(numbers) * in_rows, in_rows)
                return [(0, at, in_rows, 0, width), (in_rows, at, in_rows, width, width)]

            def spots_out(numbers):
                at = pl.multiple_of(owner_of(numbers) * out_rows, out_rows)
                return [(2 * in_rows, at, out_rows, 0, width)]

            return spots_in, spots_out

        if paired:
            attn_near = exchange([attn_bundle] * experts)
            w_in_raw = expert_in_weight[0]
            w_out_raw = expert_out_weight[0]
            bundles = []
            for step in range(experts):
                piece = pick(w_in_raw, step)
                bundles.append(
                    jnp.concatenate(
                        [piece[:, :width], piece[:, width:], pick(w_out_raw, step)], axis=0
                    )
                )
            attn_far = [swap_rep(piece) for piece in attn_near]
            attn_own = gather_pieces(
                facts,
                attn_near + attn_far,
                [attn_places(way, step) for way in range(2) for step in range(experts)],
                attn_shape,
            )
            near = exchange(bundles)
            far = {}
            for step in (0, 1, 2, 3):
                far[step] = swap_rep(near[step])
            pieces = near + [far[step] for step in range(experts)]
            both_places = [
                expert_places(way, step) for way in range(2) for step in range(experts)
            ]
            places = ([each[0] for each in both_places], [each[1] for each in both_places])
        else:
            every = lax.all_gather(attn_bundle, "dp", axis=0)
            attn_own = jnp.concatenate(
                [
                    every[:, spot : spot + rows].reshape(-1, cols)
                    for _, rows, spot in attn_rows(width, shard)
                ],
                axis=0,
            )

            def assembled(blocks):
                got = exchange([pick(blocks, step) for step in range(experts)])
                got = jnp.stack(got)
                got = jnp.stack([pick(got, owner) for owner in range(experts)])
                got = lax.all_gather(got, "dp", axis_index_groups=rep_groups)
                return jnp.swapaxes(got, 0, 1)

            pieces = [
                assembled(expert_in_weight[0]).reshape(width, ff),
                assembled(expert_out_weight[0]).reshape(ff, width),
            ]
            places = (
                [lambda numbers: [(0, 0, width, 0, ff)], lambda numbers: []],
                [lambda numbers: [], lambda numbers: [(0, 0, ff, 0, width)]],
            )
        attn_other = swap_core(attn_own)
        weights = (attn_own, attn_other, gains, router3, router)

        def expert_forward(blocks, name):
            pre, act, own, other = expert_call(
                expert_kernel, name, facts, blocks, None, pieces, places, width, ff
            )
            return pre, act, fold(own, swap_core(other), "fold_" + name)

        def expert_backward(blocks, pre, name):
            grad_pre, own, other = expert_call(
                expert_back_kernel, name, facts, blocks, pre, pieces, places, width, ff
            )
            return grad_pre, fold(own, swap_core(other), "fold_" + name)

        out = attn_forward(facts, own_rows, weights, plan)
        mid_up = moved(out[0], lambda a, b, c, d: (1, b, c, d) if a == 0 else None)
        blocks = with_other(exchange(out[6:10]))
        _, _, expert_slots = expert_forward(blocks, "expert_first")
        from_first = crossed(expert_slots, up)

        out = attn_forward(facts, own_rows, weights, plan, (mid_up, *from_first))
        mid, attn_in, proj, mixed, mlp_in, probs = out[:6]
        stream = out[10]
        blocks = with_other(exchange(out[6:10]))
        grads = exchange(out[11:15])
        pre, act, expert_slots = expert_forward(blocks, "expert_second")
        expert_slots = exchange(expert_slots)

        saved = (stream, mid, proj, mlp_in, probs)
        _, grad_slots = expert_backward(with_other(grads), pre, "expert_back_first")
        back = attn_backward(
            facts, own_rows, mid_up, exchange(grad_slots), expert_slots, saved, weights, plan, True
        )
        grad_down = moved(back[0], lambda a, b, c, d: (0, b, c, d) if a == 1 else None)
        got_down = crossed(back[1:5], down)

        grads = with_other(
            [jnp.where(pipe == 0, came, kept) for came, kept in zip(got_down, grads)]
        )
        grad_pre, grad_slots = expert_backward(grads, pre, "expert_back_second")
        layer_grad, grad_proj, low, grad_gains, grad_router = attn_backward(
            facts,
            grad_down,
            own_rows,
            exchange(grad_slots),
            expert_slots,
            saved,
            weights,
            plan,
            False,
        )

        if paired:
            out = expert_grads(facts, blocks, grads, act, grad_pre, True)
            sums = {}
            for step in (*order, 0):
                came = swap_rep(out[step])
                total = (out[4 + step].astype(F32) + came.astype(F32)).astype(BF)
                sums[step] = moved(total, across(step)) if step else total
            grad_expert_in, grad_expert_out = owner_grads(
                facts,
                [sums[step] for step in range(experts)],
                expert_in_weight.shape[1:],
                expert_out_weight.shape[1:],
            )
        else:

            def rep_scatter(each):
                return lax.psum_scatter(
                    each, "dp", axis_index_groups=rep_groups, scatter_dimension=0
                )

            def to_owner(grad, rows_each):
                each = grad.reshape(experts, reps, rows_each, -1).astype(BF)
                summed = rep_scatter(jnp.swapaxes(each, 0, 1))
                got = exchange([pick(summed, step) for step in range(experts)])
                got = jnp.stack(got)
                return jnp.stack([pick(got, owner) for owner in range(experts)]).astype(F32)

            grad_w_in, grad_w_out = expert_grads(facts, blocks, grads, act, grad_pre, False)
            grad_expert_in = to_owner(grad_w_in, in_rows)
            grad_expert_out = to_owner(grad_w_out, out_rows)

        grad_own, grad_other = attn_grads(attn_in, grad_proj, mixed, low)
        came = swap_core(grad_other)
        if paired:
            out = attn_split(facts, grad_own, came)
            total = None
            sums = {}
            for step in (*order, 0):
                came = swap_rep(out[step])
                both = out[4 + step].astype(F32) + came.astype(F32)
                sums[step] = moved(both.astype(BF), across(step)).astype(F32) if step else both
            total = sums[0] + sums[1] + sums[2] + sums[3]
        else:
            full = grad_own.astype(F32) + came.astype(F32)
            pieces_of = [
                full[source : source + rows * n_dp].reshape(n_dp, rows, cols)
                for source, rows, _ in attn_rows(width, shard)
            ]
            full = jnp.concatenate(pieces_of, axis=1).astype(BF)
            full = full.reshape((experts, reps) + full.shape[1:])
            full = rep_scatter(jnp.swapaxes(full, 0, 1))
            got = exchange([pick(full, step) for step in range(experts)])
            total = sum(each.astype(F32) for each in got)
        grad_attn = total[: 3 * shard].reshape(3, shard, cols)
        grad_attn = jnp.swapaxes(grad_attn, 0, 1)[None]
        rows = shard // 2
        grad_attn_out = jnp.concatenate(
            [total[3 * shard : 3 * shard + rows], total[3 * shard + rows :]], axis=1
        )[None]

        tiny = jnp.concatenate(
            [
                jnp.swapaxes(grad_gains.reshape(2, n_dev, -1), 0, 1).reshape(n_dev, -1),
                grad_router[:, :experts].reshape(n_dev, -1),
            ],
            axis=1,
        )
        tiny_count = tiny.shape[1]
        tiny = jnp.pad(tiny, ((0, 0), (0, -tiny_count % EXTRA))).reshape(n_dev, -1, EXTRA)
        tiny = lax.all_to_all(tiny, plane, split_axis=0, concat_axis=0, tiled=True)
        tiny = jnp.sum(tiny, axis=0).reshape(-1)[:tiny_count]
        tiny_gains = tiny[:gain_count].reshape(1, 2, -1)
        tiny_router = tiny[gain_count:].reshape(1, -1, experts)

        def sent_back(merge, rows, extra):
            own, other = sent_rows(facts, merge, rows, extra, place, width)
            full = own + swap_core(other)
            back = lax.all_to_all(full, plane, split_axis=0, concat_axis=0, tiled=True)
            return dot_tn(send_hot, back).astype(BF)[None]

        return (
            sent_back(True, mid, (slots, *expert_slots)),
            sent_back(False, layer_grad, ()),
            grad_attn,
            grad_attn_out,
            grad_expert_in[None],
            grad_expert_out[None],
            tiny_gains,
            tiny_router,
        )

    in_specs = (
        P(("dp", "tensor"), None),
        P(("dp", "tensor"), None),
        P(("dp", "tensor")),
        P(("dp", "tensor"), None),
        P(("dp", "tensor")),
        P("dp", None),
        P("pipe", "dp", None, "tensor"),
        P("pipe", ("tensor", "dp"), None),
        P("pipe", None, "dp", "tensor"),
        P("pipe", None, ("tensor", "dp"), None),
        P("pipe", None, ("dp", "tensor")),
        P("pipe", ("dp", "tensor"), None),
    )
    out_specs = (
        P("pipe", ("dp", "tensor"), None),
        P("pipe", ("dp", "tensor"), None),
        P("pipe", "dp", None, "tensor"),
        P("pipe", ("tensor", "dp"), None),
        P("pipe", None, "dp", "tensor"),
        P("pipe", None, ("tensor", "dp"), None),
        P("pipe", None, ("dp", "tensor")),
        P("pipe", ("dp", "tensor"), None),
    )
    return jax.shard_map(local, mesh=mesh, in_specs=in_specs, out_specs=out_specs, check_vma=False)
```

```python
import functools

import jax
import jax.numpy as jnp
from jax import lax
from jax.experimental import pallas as pl
from jax.experimental.pallas import tpu as pltpu
from jax.sharding import PartitionSpec as P

HEAD_DIM = 64
EPSILON = 1e-06
NEGATIVE = -1e30
EXACT = lax.Precision.HIGHEST
EXTRA = 128
BF = jnp.bfloat16
F32 = jnp.float32
VM = pl.BlockSpec(memory_space=pltpu.VMEM)
SM = pl.BlockSpec(memory_space=pltpu.SMEM)
HB = pl.BlockSpec(memory_space=pltpu.HBM)
AFTER = pl.BlockSpec(memory_space=pl.ANY)
VH = pl.BlockSpec(memory_space=pltpu.VMEM)
FAR = True
PIPE, MINE, REP, CORE, SPLIT = range(5)


def dot32(a, b):
    return jnp.dot(a, b, preferred_element_type=F32)


def dot_nt(a, b):
    return lax.dot_general(a, b, (((1,), (1,)), ((), ())), preferred_element_type=F32)


def dot_tn(a, b):
    return lax.dot_general(a, b, (((0,), (0,)), ((), ())), preferred_element_type=F32)


def norm_scale(x):
    return lax.rsqrt(jnp.mean(x * x, axis=-1, keepdims=True) + EPSILON)


def norm_back(x, scale, gain, grad):
    weighted = grad * gain
    grad_x = scale * weighted - x * (scale * scale * scale) * jnp.mean(
        x * weighted, axis=-1, keepdims=True
    )
    return grad_x, jnp.sum(grad * (x * scale), axis=0, keepdims=True)


def pinned(value):
    return pltpu.with_memory_space_constraint(value, pltpu.HBM)


def kernel_call(body, name, outs, ins, specs, scratch=(), cost=1, room=24, hbm_outs=False):
    ins = [
        pinned(each) if spec is HB or spec is VH else each
        for each, spec in zip(ins, specs, strict=True)
    ]
    far = [hbm_outs or len(each) > 2 for each in outs]
    return pl.pallas_call(
        body,
        name=name,
        out_shape=[
            (pltpu.HBM if away else jax.ShapeDtypeStruct)(each[0], each[1])
            for each, away in zip(outs, far, strict=True)
        ],
        in_specs=specs,
        out_specs=[VM] * len(outs),
        scratch_shapes=list(scratch),
        compiler_params=pltpu.CompilerParams(vmem_limit_bytes=room << 20),
        cost_estimate=pl.CostEstimate(
            flops=int(cost * 1.1e9), bytes_accessed=0, transcendentals=0
        ),
    )(*ins)


def eye(count):
    rows = lax.broadcasted_iota(jnp.int32, (count, count), 0)
    return (rows == lax.broadcasted_iota(jnp.int32, (count, count), 1)).astype(F32).astype(BF)


def send_kernel(per, facts, inputs, cotangent, dealing, routes, order, router, gains, out, hot_out):
    rows, width = inputs.shape
    place = dealing[...]
    target = place >> 8
    numbers = [place & 255, routes[...], order[...] >> 8, order[...] & 255, target]
    numbers = [each.astype(F32) for each in numbers]
    numbers = jnp.concatenate(numbers + [jnp.zeros((EXTRA - 5, rows), F32)], axis=0)
    columns = dot_nt(eye(rows), numbers.astype(BF))
    targets = target.astype(F32)
    before = lax.broadcasted_iota(jnp.int32, (rows, rows), 0)
    after = lax.broadcasted_iota(jnp.int32, (rows, rows), 1)
    ahead = (columns[:, 4:5] == targets) & (before < after)
    slot = targets * per + jnp.sum(ahead.astype(F32), axis=0, keepdims=True)
    hot = (before.astype(F32) == slot).astype(F32).astype(BF)
    hot_out[...] = hot
    chosen = jnp.where(facts[PIPE] == 0, inputs[...], cotangent[...])
    out[:, :width] = dot32(hot, chosen).astype(BF)
    lane = lax.broadcasted_iota(jnp.int32, (rows, EXTRA), 1)
    tail = dot32(hot, jnp.where(lane < 4, columns, 0.0).astype(BF))
    parts = []
    for values in (router[...], gains[...]):
        high = values.astype(BF).astype(F32)
        mid = (values - high).astype(BF).astype(F32)
        parts += [high, mid, values - high - mid]
    count = gains.shape[1]
    blank = jnp.zeros((4, count), F32)
    block = jnp.concatenate([blank] + parts + [jnp.zeros((10, count), F32)], axis=0)
    block = dot_nt(eye(count), block.astype(BF))
    groups = [block[at * per : (at + 1) * per, :] for at in range(3)]
    block = jnp.concatenate(groups + [jnp.zeros((per, 32), F32)], axis=1)
    block = jnp.concatenate([block] * (rows // per), axis=0)
    out[:, width:] = (tail + block).astype(BF)


def deal_kernel(facts, both, own_rows, slots, onehot, place):
    width = own_rows.shape[1]
    pack = own_rows.shape[0]
    total = both.shape[0]
    half = pack // 2
    core = facts[CORE].astype(F32)
    numbers = both[:, width:]
    spot = numbers[:, 0:1].astype(F32)
    source = (lax.broadcasted_iota(jnp.int32, (total, 1), 0) >= pack).astype(F32)
    upper = (spot >= half).astype(F32)
    where = jnp.where(upper == core, source * half + spot - upper * half, -1.0)
    spots = lax.broadcasted_iota(jnp.int32, (total, pack), 1).astype(F32)
    hot = (spots == where).astype(F32).astype(BF)
    place[...] = hot
    own_rows[...] = dot_tn(hot, both[:, :width]).astype(BF)
    mine = dot_tn(hot, numbers)
    across = dot_nt(eye(EXTRA), mine.astype(BF))
    expert_col, expert_row = mine[:, 1:2], across[1:2, :]
    order_col = mine[:, 2:3] * 256.0 + mine[:, 3:4]
    order_row = across[2:3, :] * 256.0 + across[3:4, :]
    ahead = (expert_col == expert_row) & (order_col < order_row)
    rank = jnp.sum(ahead.astype(F32), axis=0, keepdims=True).astype(jnp.int32)
    experts = 4
    cap = pack // experts
    block = jnp.bitwise_xor(expert_row.astype(jnp.int32), facts[MINE])
    slot = jnp.where(rank < cap, block * cap + rank, -1)
    slots[...] = (lax.broadcasted_iota(jnp.int32, (pack, pack), 0) == slot).astype(F32).astype(BF)
    onehot[...] = (
        lax.broadcasted_iota(jnp.int32, (pack, EXTRA), 1) == expert_col.astype(jnp.int32)
    ).astype(F32)


def mask_of(facts, pack):
    query = lax.broadcasted_iota(jnp.int32, (pack, pack), 0)
    key = lax.broadcasted_iota(jnp.int32, (pack, pack), 1)
    split = facts[SPLIT]
    return ((query < split) == (key < split)) & (key <= query)


def stacked(refs):
    return jnp.concatenate([ref[...] for ref in refs], axis=0)


def flipped(params):
    flat = dot_nt(eye(EXTRA), params[...])
    router = flat[4:8] + flat[8:12] + flat[12:16]
    return router, flat[16:18] + flat[18:20] + flat[20:22]


def weight_copies(sources, scratch, sems, width, cols):
    copies = []
    for at in range(2):
        each = []
        for start, rows in (*((part * width, width) for part in range(3)), (3 * width, 2 * cols)):
            spot = pl.ds(start, rows)
            each.append(
                pltpu.make_async_copy(
                    sources[at].at[spot], scratch.at[at, spot], sems.at[4 * at + len(each)]
                )
            )
        copies.append(each)
    return copies


def attn_kernel(second, dropped, facts, *refs):
    refs = list(refs)
    weights, sems = refs[-2:] if second else refs[-4:-2]
    refs = refs[:-2] if second else refs[:-4] + refs[-2:]
    own_rows = refs.pop(0)
    if second:
        up = refs.pop(0)
        slots_in = [refs.pop(0) for _ in range(4)]
    attn_own, attn_other, params, slots, onehot = (refs.pop(0) for _ in range(5))
    refs = refs[dropped:]
    if second:
        mid, attn_in, proj, mixed, mlp_in, probs = (refs.pop(0) for _ in range(6))
    else:
        mid = refs.pop(0)
        proj, mixed = refs[4:]
    blocks = [refs.pop(0) for _ in range(4)]
    pack, width = own_rows.shape
    cols = attn_own.shape[1]
    cap = pack // 4
    copies = weight_copies((attn_own, attn_other), weights, sems, width, cols)
    for each in copies:
        for copy in each:
            copy.start()
    _, gains = flipped(params)
    hot = slots[...]
    if second:
        stream = refs.pop(0)
        grads = [refs.pop(0) for _ in range(4)]
        came = up[:, :width] + up[:, width : width + 1] * dot_tn(hot, stacked(slots_in))
        rows = jnp.where(facts[PIPE] == 0, own_rows[...], came.astype(BF))
        stream[...] = rows
    else:
        rows = own_rows[...]
    x = rows.astype(F32)
    normed = (x * norm_scale(x) * gains[0:1, :]).astype(BF)
    if second:
        attn_in[...] = normed
    allowed = mask_of(facts, pack)
    for at in range(2):
        for part in range(3):
            copies[at][part].wait()
            proj[at, part] = dot32(
                normed, weights[at, part * width : (part + 1) * width, :]
            ).astype(BF)
        for head in range(cols // HEAD_DIM):
            lanes = slice(head * HEAD_DIM, (head + 1) * HEAD_DIM)
            scores = dot_nt(proj[at, 0, :, lanes], proj[at, 1, :, lanes]) * HEAD_DIM ** (-0.5)
            scores = jnp.where(allowed, scores, NEGATIVE)
            share = jnp.exp(scores - jnp.max(scores, axis=-1, keepdims=True))
            share = (share * (1.0 / jnp.sum(share, axis=-1, keepdims=True))).astype(BF)
            spot = at * cols + head * HEAD_DIM
            mixed[:, spot : spot + HEAD_DIM] = dot32(share, proj[at, 2, :, lanes]).astype(BF)
    base = 3 * width
    copies[0][3].wait()
    copies[1][3].wait()
    for side in range(2):
        rows_at = slice(base + side * cols, base + (side + 1) * cols)
        lanes = slice(side * cols, (side + 1) * cols)
        mid[:, lanes] = (
            x[:, lanes]
            + dot32(mixed[:, :cols], weights[0, rows_at, :])
            + dot32(mixed[:, cols:], weights[1, rows_at, :])
        )
    m = mid[:, :width]
    low = (m * norm_scale(m) * gains[1:2, :]).astype(BF)
    if second:
        mlp_in[...] = low
    logits = dot32(low, params[...])
    lane = lax.broadcasted_iota(jnp.int32, logits.shape, 1)
    logits = sum(pltpu.roll(logits, EXTRA - 4 * at, 1) for at in (1, 2, 3))
    logits = jnp.where(lane < 4, logits, NEGATIVE)
    rel = jnp.exp(logits - jnp.max(logits, axis=-1, keepdims=True))
    share = rel / jnp.sum(rel, axis=-1, keepdims=True)
    if second:
        probs[...] = share
    gate = jnp.sum(share * onehot[...], axis=-1, keepdims=True)
    mid[:, width:] = jnp.broadcast_to(gate, (pack, EXTRA))
    for step in range(4):
        blocks[step][...] = dot32(hot[step * cap : (step + 1) * cap, :], low).astype(BF)
    if second:
        weighted = (gate * own_rows[...].astype(F32)).astype(BF)
        for step in range(4):
            grads[step][...] = dot32(hot[step * cap : (step + 1) * cap, :], weighted).astype(BF)


def attn_forward(facts, own_rows, weights, plan, came=None, after=()):
    attn_own, attn_other, params = weights
    slots, onehot = plan
    pack, width = own_rows.shape
    cols = attn_own.shape[1]
    cap = pack // 4
    second = came is not None
    ins = [facts, own_rows] + (list(came) if second else [])
    specs = [SM, VH] + ([VH] if second else []) + [VM] * (len(ins) - (3 if second else 2))
    specs += [HB] * 2 + [VH] * 3 + [AFTER] * len(after)
    ins += [attn_own, attn_other, params, slots, onehot, *after]
    if second:
        outs = [
            ((pack, width + EXTRA), F32, FAR),
            ((pack, width), BF, FAR),
            ((2, 3, pack, cols), BF, FAR),
            ((pack, width), BF, FAR),
            ((pack, width), BF, FAR),
            ((pack, EXTRA), F32, FAR),
        ]
    else:
        outs = [((pack, width + EXTRA), F32, FAR)]
    outs += [((cap, width), BF)] * 4
    if second:
        outs += [((pack, width), BF, FAR)] + [((cap, width), BF)] * 4
    return kernel_call(
        functools.partial(attn_kernel, second, len(after)),
        "attn_second" if second else "attn_first",
        outs,
        ins,
        specs,
        [pltpu.VMEM((2, 3 * width + 2 * cols, cols), BF), pltpu.SemaphoreType.DMA((8,))]
        + ([] if second else [pltpu.VMEM((2, 3, pack, cols), BF), pltpu.VMEM((pack, width), BF)]),
        cost=8,
    )


def attn_back_kernel(first, facts, *refs):
    refs = list(refs)
    weights, sems = refs[-2:]
    refs = refs[:-2]
    grad_out = refs.pop(0)
    if first:
        up = refs.pop(0)
    else:
        own_rows = refs.pop(0)
        refs.pop(0)
        refs.pop(0)
    grad_slots = [refs.pop(0) for _ in range(4)]
    stream, mid, proj, mlp_in, probs = (refs.pop(0) for _ in range(5))
    attn_own, attn_other, params, slots, onehot = (refs.pop(0) for _ in range(5))
    grad_stream = refs.pop(0)
    if first:
        blocks = [refs.pop(0) for _ in range(4)]
        grad_proj = refs.pop(0)
    else:
        grad_proj, grad_low, tiny = (refs.pop(0) for _ in range(3))
    pack, width = stream.shape
    cols = attn_own.shape[1]
    cap = pack // 4
    copies = weight_copies((attn_own, attn_other), weights, sems, width, cols)
    for part in (3, 0, 1, 2):
        for each in copies:
            each[part].start()
    router, gains = flipped(params)
    hot = slots[...]
    rows = grad_out[...]
    if not first:
        rows = jnp.where(facts[PIPE] == 0, rows, own_rows[...])
    g = rows.astype(F32)
    slot_rows = stacked(grad_slots)
    at_tokens = dot_tn(hot, slot_rows[:, width:])
    grad_logits = (at_tokens[:, 0:1] + at_tokens[:, 1:2]) * (onehot[...] - probs[...])
    m = mid[:, :width]
    wide = jnp.concatenate([router, jnp.zeros((EXTRA - 4, width), F32)], axis=0)
    grad_mlp = dot_tn(hot, slot_rows[:, :width]) + jnp.dot(
        grad_logits, wide, preferred_element_type=F32, precision=EXACT
    )
    grad_norm, gain_two = norm_back(m, norm_scale(m), gains[1:2, :], grad_mlp)
    grad_mid = g + grad_norm
    low = grad_mid.astype(BF)
    allowed = mask_of(facts, pack)
    grad_in = jnp.zeros((pack, width), F32)
    base = 3 * width
    copies[0][3].wait()
    copies[1][3].wait()
    for at in range(2):
        grad_mixed = (
            dot_nt(low[:, :cols], weights[at, base : base + cols, :])
            + dot_nt(low[:, cols:], weights[at, base + cols : base + 2 * cols, :])
        ).astype(BF)
        for head in range(cols // HEAD_DIM):
            lanes = slice(head * HEAD_DIM, (head + 1) * HEAD_DIM)
            query, key, value = (proj[at, part, :, lanes] for part in range(3))
            grad_head = grad_mixed[:, lanes]
            scores = dot_nt(query, key) * HEAD_DIM ** (-0.5)
            scores = jnp.where(allowed, scores, NEGATIVE)
            share = jnp.exp(scores - jnp.max(scores, axis=-1, keepdims=True))
            share = share * (1.0 / jnp.sum(share, axis=-1, keepdims=True))
            grad_share = dot_nt(grad_head, value)
            pulled = share * grad_share
            inner = jnp.sum(pulled, axis=-1, keepdims=True)
            grad_scores = ((pulled - share * inner) * HEAD_DIM ** (-0.5)).astype(BF)
            grad_proj[at, 0, :, lanes] = dot32(grad_scores, key).astype(BF)
            grad_proj[at, 1, :, lanes] = dot_tn(grad_scores, query).astype(BF)
            grad_proj[at, 2, :, lanes] = dot_tn(share.astype(BF), grad_head).astype(BF)
        for part in range(3):
            copies[at][part].wait()
            grad_in += dot_nt(
                grad_proj[at, part], weights[at, part * width : (part + 1) * width, :]
            )
    x = stream[...].astype(F32)
    grad_norm, gain_one = norm_back(x, norm_scale(x), gains[0:1, :], grad_in)
    result = (grad_mid + grad_norm).astype(BF)
    grad_stream[...] = result
    if first:
        weighted = (up[:, width : width + 1] * result.astype(F32)).astype(BF)
        for step in range(4):
            blocks[step][...] = dot32(hot[step * cap : (step + 1) * cap, :], weighted).astype(BF)
    else:
        grad_low[...] = low
        high = grad_logits.astype(BF)
        rest = (grad_logits - high.astype(F32)).astype(BF)
        lane = lax.broadcasted_iota(jnp.int32, (width, EXTRA), 1)
        both = dot_tn(mlp_in[...], high) + dot_tn(mlp_in[...], rest)
        both = jnp.where(lane < 4, both, 0.0)
        high = both.astype(BF).astype(F32)
        flat = [gain_one.astype(BF).astype(F32), gain_two.astype(BF).astype(F32)]
        flat += [gain_one - flat[0], gain_two - flat[1]]
        flat = jnp.concatenate(flat + [jnp.zeros((12, width), F32)], axis=0).astype(BF)
        spot = lax.broadcasted_iota(jnp.int32, (16, EXTRA), 0) + 8
        spot = spot == lax.broadcasted_iota(jnp.int32, (16, EXTRA), 1)
        turned = dot_tn(flat, spot.astype(F32).astype(BF))
        tiny[...] = (high + pltpu.roll(both - high, 4, 1) + turned).astype(BF)


def attn_backward(facts, grad_out, extra, grad_slots, saved, weights, plan, first):
    attn_own, attn_other, params = weights
    slots, onehot = plan
    stream, mid, proj, mlp_in, probs = saved
    pack, width = stream.shape
    cols = attn_own.shape[1]
    cap = pack // 4
    ins = [facts, grad_out, *extra, *grad_slots, stream, mid, proj, mlp_in, probs]
    specs = [SM, VH if first else VM, VH] + [AFTER] * (len(extra) - 1)
    specs += [VM] * 4 + [VH] * 5 + [HB] * 2 + [VH] * 3
    ins += [attn_own, attn_other, params, slots, onehot]
    outs = [((pack, width), BF)]
    if first:
        outs += [((cap, width), BF)] * 4
    outs += [((2, 3, pack, cols), BF)]
    if not first:
        outs += [((pack, width), BF), ((width, EXTRA), BF)]
    return kernel_call(
        functools.partial(attn_back_kernel, first),
        "attn_back_first" if first else "attn_back_second",
        outs,
        ins,
        specs,
        [pltpu.VMEM((2, 3 * width + 2 * cols, cols), BF), pltpu.SemaphoreType.DMA((8,))],
        cost=13,
    )


def gelu_both(u):
    square = u * u
    t = jnp.tanh(0.7978845608028654 * u * (1.0 + 0.044715 * square))
    half = 0.5 * (1.0 + t)
    inner = 0.7978845608028654 * (1.0 + 3.0 * 0.044715 * square)
    return half + 0.5 * u * (1.0 - t * t) * inner, half * u


def bring(facts, pieces, places, scratch, sems):
    copies = []
    for piece, spots in zip(pieces, places, strict=True):
        for source, target, rows, column, columns in spots(facts):
            copies.append(
                pltpu.make_async_copy(
                    piece.at[pl.ds(source, rows), pl.ds(0, columns)],
                    scratch.at[pl.ds(target, rows), pl.ds(column, columns)],
                    sems.at[len(copies)],
                )
            )
    for copy in copies:
        copy.start()
    return copies


TILE = 256


def expert_kernel(keep, places_in, places_out, facts, *refs):
    refs = list(refs)
    blocks = [refs.pop(0) for _ in range(8)]
    pieces = [refs.pop(0) for _ in range(len(places_in))]
    if keep:
        pre = refs.pop(0)
    if keep:
        act = refs.pop(0)
        rows = refs.pop(0)
        own, other, w_in, w_out, sems_in, sems_out = refs
    else:
        own, other, w_in, w_out, sems_in, sems_out, act, rows = refs
    arriving = bring(facts, pieces, places_in, w_in, sems_in)
    later = bring(facts, pieces, places_out, w_out, sems_out)
    cap = blocks[0].shape[0]
    for at, block in enumerate(blocks):
        rows[at * cap : (at + 1) * cap, :] = block[...]
    for copy in arriving:
        copy.wait()
    ff = w_in.shape[1]
    width = w_in.shape[0]

    @pl.loop(0, ff // TILE)
    def _(tile):
        lanes = pl.ds(pl.multiple_of(tile * TILE, TILE), TILE)
        value = dot32(rows[...], w_in[:, lanes])
        slope, result = gelu_both(value)
        act[:, lanes] = result.astype(BF)
        if keep:
            pre[:, lanes] = slope.astype(BF)

    for copy in later:
        copy.wait()
    count = 4 * cap

    @pl.loop(0, width // TILE)
    def _(tile):
        lanes = pl.ds(pl.multiple_of(tile * TILE, TILE), TILE)
        value = dot32(act[...], w_out[:, lanes])
        own[:, lanes] = value[:count]
        other[:, lanes] = value[count:].astype(BF)


def halves(value, shape):
    high = value.astype(BF).astype(F32)
    lane = lax.broadcasted_iota(jnp.int32, shape, 1)
    return jnp.where(lane == 0, high, jnp.where(lane == 1, value - high, 0.0))


def expert_back_kernel(chosen, places_in, places_out, facts, *refs):
    refs = list(refs)
    blocks = [refs.pop(0) for _ in range(8)]
    if chosen:
        others = refs.pop(0)
        refs.pop(0)
    pre, own_out, other_out = (refs.pop(0) for _ in range(3))
    pieces = [refs.pop(0) for _ in range(len(places_in))]
    grad_pre, own, other, rows = (refs.pop(0) for _ in range(4))
    w_in, w_out, sems_in, sems_out = refs
    arriving = bring(facts, pieces, places_out, w_out, sems_out)
    later = bring(facts, pieces, places_in, w_in, sems_in)
    cap = blocks[0].shape[0]
    for at, block in enumerate(blocks):
        value = block[...]
        if chosen:
            value = jnp.where(facts[PIPE] == 0, value, others[at * cap : (at + 1) * cap, :])
        rows[at * cap : (at + 1) * cap, :] = value
    for copy in arriving:
        copy.wait()
    ff = w_in.shape[1]
    width = w_in.shape[0]
    count = 4 * cap

    @pl.loop(0, ff // TILE)
    def _(tile):
        lanes = pl.ds(pl.multiple_of(tile * TILE, TILE), TILE)
        value = dot_nt(rows[...], w_out[lanes, :])
        grad_pre[:, lanes] = (value * pre[:, lanes].astype(F32)).astype(BF)

    for copy in later:
        copy.wait()

    @pl.loop(0, width // TILE)
    def _(tile):
        lanes = pl.ds(pl.multiple_of(tile * TILE, TILE), TILE)
        value = dot_nt(grad_pre[...], w_in[lanes, :])
        own[:, lanes] = value[:count]
        other[:, lanes] = value[count:].astype(BF)

    pull = jnp.sum(rows[:count, :].astype(F32) * own_out[...], axis=-1, keepdims=True)
    own[:, width:] = halves(pull, (count, EXTRA))
    pull = jnp.sum(
        rows[count:, :].astype(F32) * other_out[...].astype(F32), axis=-1, keepdims=True
    )
    other[:, width:] = halves(pull, (count, EXTRA)).astype(BF)


def expert_scratch(width, ff, places):
    numbers = jnp.zeros((8,), jnp.int32)
    sizes = [sum(len(spots(numbers)) for spots in each) for each in places]
    return (
        [pltpu.VMEM((width, ff), BF), pltpu.VMEM((ff, width), BF)],
        [pltpu.SemaphoreType.DMA((size,)) for size in sizes],
    )


def expert_call(name, keep, facts, blocks, pieces, places, width, ff):
    count = 4 * blocks[0].shape[0]
    ins = [facts, *blocks, *pieces]
    kept = [((2 * count, ff), BF, FAR)] * 2 + [((2 * count, width), BF, FAR)] if keep else []
    buffers, sems = expert_scratch(width, ff, places)
    scratch = [*buffers, *sems]
    if not keep:
        scratch += [pltpu.VMEM((2 * count, ff), BF), pltpu.VMEM((2 * count, width), BF)]
    return kernel_call(
        functools.partial(expert_kernel, keep, *places),
        name,
        kept + [((count, width), F32), ((count, width), BF)],
        ins,
        [SM] + [VM] * 8 + [HB] * len(pieces),
        scratch,
        cost=7,
    )


def expert_back_call(name, facts, blocks, others, after, saved, pieces, places, width, ff):
    count = 4 * blocks[0].shape[0]
    wide = width + EXTRA
    ins = [facts, *blocks, *others, *after, *saved, *pieces]
    buffers, sems = expert_scratch(width, ff, places)
    return kernel_call(
        functools.partial(expert_back_kernel, len(after) > 0, *places),
        name,
        [
            ((2 * count, ff), BF),
            ((count, wide), F32),
            ((count, wide), BF),
            ((2 * count, width), BF, FAR),
        ],
        ins,
        [SM]
        + [VM] * 8
        + [VH] * len(others)
        + [AFTER] * len(after)
        + [VH, VM, VM]
        + [HB] * len(pieces),
        [*buffers, *sems],
        cost=7,
    )


def fold_kernel(own, other, *blocks):
    cap = blocks[0].shape[0]
    width = own.shape[1] // TILE * TILE
    for step, block in enumerate(blocks):
        rows = slice(step * cap, (step + 1) * cap)
        block[:, :width] = (own[rows, :width] + other[rows, :width].astype(F32)).astype(BF)
        if own.shape[1] > width:
            both = own[rows, width:] + other[rows, width:].astype(F32)
            block[:, width:] = halves(both[:, 0:1] + both[:, 1:2], (cap, EXTRA)).astype(BF)


def fold(own, other, name):
    count, width = own.shape
    cap = count // 4
    return kernel_call(
        fold_kernel, name, [((cap, width), BF)] * 4, [own, other], [VM, VM], cost=1
    )


def return_kernel(merge, *refs):
    refs = list(refs)
    rows = refs.pop(0)
    if merge:
        hot = refs.pop(0)
        slots_in = [refs.pop(0) for _ in range(4)]
        width = slots_in[0].shape[1]
        values = rows[:, :width] + rows[:, width : width + 1] * dot_tn(hot[...], stacked(slots_in))
        values = values.astype(BF)
    else:
        values = rows[...]
    place, own, other, facts = refs[0], refs[2], refs[3], refs[1]
    pack = own.shape[0]
    core = facts[CORE]
    own[...] = dot32(place[pl.ds(pl.multiple_of(core * pack, pack), pack), :], values).astype(BF)
    other[...] = dot32(
        place[pl.ds(pl.multiple_of((1 - core) * pack, pack), pack), :], values
    ).astype(BF)


def sent_rows(facts, merge, rows, extra, place, width):
    pack = place.shape[1]
    ins = [rows, *extra, place, facts]
    outs = [((pack, width), BF)] * 2
    return kernel_call(
        functools.partial(return_kernel, merge),
        "return_merged" if merge else "return_rows",
        outs,
        ins,
        ([VH, VH] + [VM] * 4 if merge else [VM]) + [VH, SM],
        cost=1,
    )


def run_copies(moves, sems):
    copies = [
        pltpu.make_async_copy(source, target, sems.at[at])
        for at, (source, target) in enumerate(moves)
    ]
    for copy in copies:
        copy.start()
    for copy in copies:
        copy.wait()


def stack_kernel(count, facts, *refs):
    pieces, out, sems = refs[:count], refs[-2], refs[-1]
    run_copies(
        [
            (piece, out.at[jnp.bitwise_xor(facts[MINE], step)])
            for step, piece in enumerate(pieces)
        ],
        sems,
    )


def stack_pieces(facts, pieces, after):
    count = len(pieces)
    return kernel_call(
        functools.partial(stack_kernel, count),
        "stack_pieces",
        [((count, *pieces[0].shape), BF)],
        [facts, *pieces, *after],
        [SM] + [HB] * count + [AFTER] * len(after),
        [pltpu.SemaphoreType.DMA((count,))],
        room=12,
        hbm_outs=True,
    )[0]


def gather_kernel(facts, near, far, *refs):
    out, sems = refs[-2:]
    groups = near.shape[0]
    moves = []
    for rep, source in ((facts[REP], near), (1 - facts[REP], far)):
        for part in range(3):
            moves.append(
                (
                    source.at[:, pl.ds(2 * part, 2)],
                    out.at[pl.ds(part * groups, groups), pl.ds(2 * rep, 2)],
                )
            )
        for side in range(2):
            for group in range(groups):
                moves.append(
                    (
                        source.at[group, 6 + side],
                        out.at[3 * groups + 2 * side + group // 2, group % 2 * 2 + rep],
                    )
                )
    run_copies(moves, sems)


def pack_attn_kernel(attn, attn_out, bundle, sems):
    parts, shard, cols = attn.shape
    rows = attn_out.shape[0]
    moves = [(attn.at[part], bundle.at[pl.ds(part * shard, shard)]) for part in range(parts)]
    for side in range(2):
        moves.append(
            (
                attn_out.at[:, pl.ds(side * cols, cols)],
                bundle.at[pl.ds(parts * shard + side * rows, rows)],
            )
        )
    run_copies(moves, sems)


def pack_attn(attn, attn_out):
    parts, shard, cols = attn.shape
    rows = attn_out.shape[0]
    return kernel_call(
        pack_attn_kernel,
        "pack_attn",
        [((parts * shard + 2 * rows, cols), BF)],
        [attn, attn_out],
        [HB] * 2,
        [pltpu.SemaphoreType.DMA((parts + 2,))],
        room=12,
        hbm_outs=True,
    )[0]


def pack_expert_kernel(steps, facts, w_in, w_out, *refs):
    blocks, sems = refs[-1 - len(steps) : -1], refs[-1]
    in_rows, out_rows, width = w_in.shape[1], w_out.shape[1], w_out.shape[2]
    moves = []
    for step, block in zip(steps, blocks, strict=True):
        at = jnp.bitwise_xor(facts[MINE], step)
        for side in range(2):
            moves.append(
                (
                    w_in.at[at, :, pl.ds(side * width, width)],
                    block.at[pl.ds(side * in_rows, in_rows)],
                )
            )
        moves.append((w_out.at[at], block.at[pl.ds(2 * in_rows, out_rows)]))
    run_copies(moves, sems)


def pack_expert(facts, w_in, w_out, steps, after=()):
    block = (2 * w_in.shape[1] + w_out.shape[1], w_out.shape[2])
    return kernel_call(
        functools.partial(pack_expert_kernel, steps),
        "pack_expert",
        [(block, BF)] * len(steps),
        [facts, w_in, w_out, *after],
        [SM, HB, HB] + [AFTER] * len(after),
        [pltpu.SemaphoreType.DMA((3 * len(steps),))],
        room=12,
        hbm_outs=True,
    )


def expert_grad_kernel(split, facts, *refs):
    refs = list(refs)
    rows, grad_rows, act, grad_pre = (refs.pop(0) for _ in range(4))
    if split:
        sends = [refs.pop(0) for _ in range(4)]
        keeps = [refs.pop(0) for _ in range(4)]
        grad_in, grad_out = refs
    else:
        grad_in, grad_out = refs
    ff = act.shape[1]
    width = rows.shape[1]

    @pl.loop(0, ff // TILE)
    def _(tile):
        lanes = pl.ds(pl.multiple_of(tile * TILE, TILE), TILE)
        grad_in[:, lanes] = dot_tn(rows[...], grad_pre[:, lanes])
        grad_out[lanes, :] = dot_tn(act[:, lanes], grad_rows[...])

    if split:
        shard, out_shard = width // 8, ff // 8
        for step in range(4):
            owner = jnp.bitwise_xor(facts[MINE], step) * 2
            for rep, target in ((1 - facts[REP], sends[step]), (facts[REP], keeps[step])):
                spot = pl.ds(pl.multiple_of((owner + rep) * shard, shard), shard)
                target[0:shard, :] = grad_in[spot, :width].astype(BF)
                target[shard : 2 * shard, :] = grad_in[spot, width:].astype(BF)
                spot = pl.ds(pl.multiple_of((owner + rep) * out_shard, out_shard), out_shard)
                target[2 * shard :, :] = grad_out[spot, :].astype(BF)


def expert_grads(facts, rows, grad_rows, act, grad_pre, split):
    width = rows.shape[1]
    ff = act.shape[1]
    full = [((width, ff), F32), ((ff, width), F32)]
    if split:
        outs = [((width // 2, width), BF, FAR)] * 8
        scratch = [pltpu.VMEM(*each) for each in full]
    else:
        outs, scratch = full, []
    return kernel_call(
        functools.partial(expert_grad_kernel, split),
        "expert_grads",
        outs,
        [facts, rows, grad_rows, act, grad_pre],
        [SM, VH, VH, VH, VM],
        scratch,
        cost=6,
        room=32,
    )


def owner_kernel(facts, *refs):
    pieces, grad_in, grad_out = refs[:-2], refs[-2], refs[-1]
    shard = grad_in.shape[1]
    width = grad_out.shape[2]
    for step, piece in enumerate(pieces):
        at = jnp.bitwise_xor(facts[MINE], step)
        grad_in[at, :, :width] = piece[:shard, :].astype(F32)
        grad_in[at, :, width:] = piece[shard : 2 * shard, :].astype(F32)
        grad_out[at] = piece[2 * shard :, :].astype(F32)


def owner_grads(facts, pieces, in_shape, out_shape):
    return kernel_call(
        owner_kernel,
        "owner_grads",
        [(in_shape, F32), (out_shape, F32)],
        [facts, *pieces],
        [SM] + [VM] * len(pieces),
        cost=3,
    )


def attn_grad_kernel(attn_in, grad_proj, mixed, low, *refs):
    own, other = refs[-2:]
    width = attn_in.shape[1]
    cols = own.shape[1]
    for at, target in ((0, own), (1, other)):
        for part in range(3):
            target[part * width : (part + 1) * width, :] = dot_tn(
                attn_in[...], grad_proj[at, part]
            ).astype(BF)
        for side in range(2):
            spot = 3 * width + side * cols
            target[spot : spot + cols, :] = dot_tn(
                mixed[:, at * cols : (at + 1) * cols], low[:, side * cols : (side + 1) * cols]
            ).astype(BF)


def attn_grads(attn_in, grad_proj, mixed, low, after):
    pack, width = attn_in.shape
    cols = grad_proj.shape[3]
    return kernel_call(
        attn_grad_kernel,
        "attn_grads",
        [((3 * width + 2 * cols, cols), BF)] * 2,
        [attn_in, grad_proj, mixed, low, *after],
        [VH, VM, VH, VM] + [AFTER] * len(after),
        cost=3,
    )


SPLIT_ORDER = (2, 3, 1, 0)


def attn_split_kernel(facts, own, came, *refs):
    sends, keeps = refs[:2], refs[2:]
    cols = own.shape[1]
    width = 2 * cols
    shard = width // 8
    count = 4 * shard
    for at, step in enumerate(SPLIT_ORDER):
        owner = jnp.bitwise_xor(facts[MINE], step) * 2
        for rep, target, first in (
            (1 - facts[REP], sends[at // 2], at % 2 * count),
            (facts[REP], keeps[at // 2], at % 2 * count),
        ):
            for source, rows, spot in attn_rows(width, shard):
                where = pl.ds(pl.multiple_of(source + (owner + rep) * rows, rows), rows)
                target[first + spot : first + spot + rows, :] = (
                    own[where, :].astype(F32) + came[where, :].astype(F32)
                ).astype(BF)


def sum_kernel(steps, keep, came, *outs):
    count = outs[0].shape[0]
    for at, (step, out) in enumerate(zip(steps, outs, strict=True)):
        rows = slice(at * count, (at + 1) * count)
        both = keep[rows, :].astype(F32) + came[rows, :].astype(F32)
        out[...] = both.astype(out.dtype)


def sum_pieces(steps, keep, came):
    count = keep.shape[0] // len(steps)
    kinds = [F32 if step == 0 else BF for step in steps]
    return kernel_call(
        functools.partial(sum_kernel, steps),
        "sum_pieces",
        [((count, keep.shape[1]), kind) for kind in kinds],
        [keep, came],
        [VH] * 2,
    )


def attn_rows(width, shard):
    out = shard // 2
    return (
        (0, shard, 0),
        (width, shard, shard),
        (2 * width, shard, 2 * shard),
        (3 * width, out, 3 * shard),
        (3 * width + width // 2, out, 3 * shard + out),
    )


def attn_split(facts, own, came):
    rows, cols = own.shape
    return kernel_call(
        attn_split_kernel,
        "attn_split",
        [((rows // 4, cols), BF, FAR)] * 4,
        [facts, own, came],
        [SM, VM, VM],
        cost=3,
    )


def solution(mesh):
    shape = mesh.shape
    n_pipe, n_dp, n_t = shape["pipe"], shape["dp"], shape["tensor"]
    axes = ("pipe", "dp", "tensor")
    plane = ("dp", "tensor")
    n_dev = n_dp * n_t

    def local(
        inputs,
        cotangent,
        dealing,
        routes,
        slot_order,
        doc_lengths,
        attn_weight,
        attn_out_weight,
        expert_in_weight,
        expert_out_weight,
        norm_gains,
        router_weight,
    ):
        dev_rows, width = inputs.shape
        experts = expert_in_weight.shape[1]
        reps = n_dp // experts
        paired = reps == 2
        pack = dev_rows
        cap = pack // experts
        per = dev_rows // n_dev
        shard, cols = attn_weight.shape[1], attn_weight.shape[3]
        ff = expert_in_weight.shape[3]
        in_rows, out_rows = expert_in_weight.shape[2], expert_out_weight.shape[2]
        pipe = lax.axis_index("pipe")
        dp = lax.axis_index("dp")
        core = lax.axis_index("tensor")
        mine = dp // reps
        rep = dp % reps
        lengths = lax.dynamic_index_in_dim(doc_lengths, core, 0, keepdims=False)
        zero = jnp.int32(0)
        facts = jnp.stack([pipe, mine, rep, core, lengths[0], zero, zero, zero]).astype(jnp.int32)

        def moved(value, rule):
            pairs = []
            for a in range(n_pipe):
                for b in range(experts):
                    for c in range(reps):
                        for d in range(n_t):
                            to = rule(a, b, c, d)
                            if to is not None:
                                flat = [
                                    ((w * experts + x) * reps + y) * n_t + z
                                    for w, x, y, z in ((a, b, c, d), to)
                                ]
                                pairs.append(tuple(flat))
            return lax.ppermute(value, axes, pairs)

        def swap_core(value):
            return moved(value, lambda a, b, c, d: (a, b, c, 1 - d))

        def swap_rep(value):
            return moved(value, lambda a, b, c, d: (a, b, 1 - c, d))

        def across(step):
            return lambda a, b, c, d: (a, b ^ step, c, d)

        def up(step):
            return lambda a, b, c, d: (1, b ^ step, c, d) if a == 0 else None

        def down(step):
            return lambda a, b, c, d: (0, b ^ step, c, d) if a == 1 else None

        order = (2, 3, 1)

        def exchange(blocks):
            out = {0: blocks[0]}
            for step in order:
                out[step] = moved(blocks[step], across(step))
            return [out[step] for step in range(experts)]

        def crossed(blocks, way):
            out = {}
            for step in (*order, 0):
                out[step] = moved(blocks[step], way(step))
            return [out[step] for step in range(experts)]

        def with_other(blocks):
            out = {}
            for step in (0, 1, 2, 3):
                out[step] = swap_core(blocks[step])
            return list(blocks) + [out[step] for step in range(experts)]

        def pick(blocks, step):
            return lax.dynamic_index_in_dim(blocks, mine ^ step, 0, keepdims=False)

        rep_groups = [[b * reps + c for c in range(reps)] for b in range(experts)]

        payload, send_hot = kernel_call(
            functools.partial(send_kernel, per),
            "send",
            [((dev_rows, width + EXTRA), BF), ((dev_rows, dev_rows), BF)],
            [
                facts,
                inputs,
                cotangent,
                dealing.reshape(1, dev_rows),
                routes.reshape(1, dev_rows),
                slot_order.reshape(1, dev_rows),
                router_weight[0].T,
                norm_gains[0],
            ],
            [SM] + [VM] * 7,
            cost=2,
        )
        dealt = lax.all_to_all(payload, plane, split_axis=0, concat_axis=0, tiled=True)
        params = dealt[:, width:].reshape(n_dev, per, 4, 32)[:, :, :3]
        params = jnp.swapaxes(params, 1, 2).reshape(width, 32)
        params = jnp.pad(params, ((0, 0), (0, EXTRA - 32)))
        both = lax.all_gather(dealt, "tensor", axis=0, tiled=True)
        own_rows, slots, onehot, place = kernel_call(
            deal_kernel,
            "deal",
            [
                ((pack, width), BF, FAR),
                ((pack, pack), BF, FAR),
                ((pack, EXTRA), F32, FAR),
                ((2 * pack, pack), BF, FAR),
            ],
            [facts, both],
            [SM, VM],
            cost=1.5,
        )
        plan = (slots, onehot)

        out_shard = attn_out_weight[0]
        attn_shape = (4 * width, cols)

        def expert_places(way, step):
            def owner_of(numbers):
                owner = jnp.bitwise_xor(numbers[MINE], step) * 2
                return owner + (numbers[REP] if way == 0 else 1 - numbers[REP])

            def spots_in(numbers):
                at = pl.multiple_of(owner_of(numbers) * in_rows, in_rows)
                return [(0, at, in_rows, 0, width), (in_rows, at, in_rows, width, width)]

            def spots_out(numbers):
                at = pl.multiple_of(owner_of(numbers) * out_rows, out_rows)
                return [(2 * in_rows, at, out_rows, 0, width)]

            return spots_in, spots_out

        if paired:
            w_in_raw, w_out_raw = expert_in_weight[0], expert_out_weight[0]
            attn_bundle = pack_attn(jnp.swapaxes(attn_weight[0], 0, 1), out_shard)
            near, far = {}, {}
            near[0], first, bundle = pack_expert(facts, w_in_raw, w_out_raw, (0, 1, 2))
            near[1] = moved(first, across(1))
            far[0] = swap_rep(near[0])
            attn_near = exchange([attn_bundle] * experts)
            attn_near = stack_pieces(
                facts, [each.reshape(8, shard // 2, cols) for each in attn_near],
                [payload, near[1], far[0]],
            )
            attn_far = swap_rep(attn_near)
            near[2] = moved(bundle, across(2))
            attn_own = kernel_call(
                gather_kernel,
                "gather_attn",
                [((4 * experts, 4, shard // 2, cols), BF)],
                [facts, attn_near, attn_far, near[2], dealt],
                [SM, HB, HB] + [AFTER] * 2,
                [pltpu.SemaphoreType.DMA((22,))],
                room=12,
                hbm_outs=True,
            )[0].reshape(attn_shape)
            (bundle,) = pack_expert(facts, w_in_raw, w_out_raw, (3,), (near[2],))
            near[3] = moved(bundle, across(3))
            for step in (1, 2, 3):
                far[step] = swap_rep(near[step])
            pieces = [each[step] for each in (near, far) for step in range(experts)]
            ready = (far[2],)
            both_places = [
                expert_places(way, step) for way in range(2) for step in range(experts)
            ]
            places = ([each[0] for each in both_places], [each[1] for each in both_places])
        else:
            attn_bundle = jnp.concatenate(
                [attn_weight[0, :, part] for part in range(3)]
                + [out_shard[:, :cols], out_shard[:, cols:]],
                axis=0,
            )
            every = lax.all_gather(attn_bundle, "dp", axis=0)
            attn_own = jnp.concatenate(
                [
                    every[:, spot : spot + rows].reshape(-1, cols)
                    for _, rows, spot in attn_rows(width, shard)
                ],
                axis=0,
            )

            def assembled(blocks):
                got = exchange([pick(blocks, step) for step in range(experts)])
                got = jnp.stack(got)
                got = jnp.stack([pick(got, owner) for owner in range(experts)])
                got = lax.all_gather(got, "dp", axis_index_groups=rep_groups)
                return jnp.swapaxes(got, 0, 1)

            ready = ()
            pieces = [
                assembled(expert_in_weight[0]).reshape(width, ff),
                assembled(expert_out_weight[0]).reshape(ff, width),
            ]
            places = (
                [lambda numbers: [(0, 0, width, 0, ff)], lambda numbers: []],
                [lambda numbers: [], lambda numbers: [(0, 0, ff, 0, width)]],
            )
        attn_other = swap_core(attn_own)
        weights = (attn_own, attn_other, params)

        def expert_forward(blocks, name, keep):
            *kept, own, other = expert_call(name, keep, facts, blocks, pieces, places, width, ff)
            folded = fold(own, swap_core(other), "fold_" + name)
            return kept, own, other, folded

        def expert_backward(blocks, others, after, saved, name):
            grad_pre, own, other, rows = expert_back_call(
                name, facts, blocks, others, after, saved, pieces, places, width, ff
            )
            return grad_pre, rows, fold(own, swap_core(other), "fold_" + name)

        def sent_back(merge, rows, extra, tail):
            own, other = sent_rows(facts, merge, rows, extra, place, width)
            full = own + swap_core(other)
            if tail is not None:
                full = jnp.concatenate([full, tail], axis=1)
            return own, lax.all_to_all(full, plane, split_axis=0, concat_axis=0, tiled=True)

        def restored(back):
            return dot_tn(send_hot, back[:, :width]).astype(BF)[None]

        out = attn_forward(facts, own_rows, weights, plan, None, ready)
        mid_up = moved(out[0], lambda a, b, c, d: (1, b, c, d) if a == 0 else None)
        blocks = with_other(exchange(out[1:5]))
        _, _, _, expert_slots = expert_forward(blocks, "expert_first", False)
        from_first = crossed(expert_slots, up)

        out = attn_forward(facts, own_rows, weights, plan, (mid_up, *from_first))
        mid, attn_in, proj, mixed, mlp_in, probs = out[:6]
        stream = out[10]
        blocks = with_other(exchange(out[6:10]))
        kept_grads = with_other(exchange(out[11:15]))
        (slope, act, rows), own_out, other_out, expert_slots = expert_forward(blocks, "expert_second", True)
        expert_saved = (slope, own_out, other_out)

        saved = (stream, mid, proj, mlp_in, probs)
        _, kept_rows, grad_slots = expert_backward(kept_grads, [], [], expert_saved, "expert_back_first")
        back = attn_backward(
            facts, own_rows, [mid_up], exchange(grad_slots), saved, weights, plan, True
        )
        grad_down = moved(back[0], lambda a, b, c, d: (0, b, c, d) if a == 1 else None)
        expert_slots = exchange(expert_slots)
        marker, out_back = sent_back(True, mid, (slots, *expert_slots), None)

        grads = with_other(crossed(back[1:5], down))
        grad_pre, grad_rows, grad_slots = expert_backward(
            grads, [kept_rows], [marker], expert_saved, "expert_back_second"
        )
        grads_out = expert_grads(facts, rows, grad_rows, act, grad_pre, paired)
        layer_grad, grad_proj, low, tiny = attn_backward(
            facts,
            grad_down,
            [own_rows, grads_out[0], out_back],
            exchange(grad_slots),
            saved,
            weights,
            plan,
            False,
        )

        if paired:
            sums = {}
            for step in (*order, 0):
                (sums[step],) = sum_pieces(
                    (step,), grads_out[4 + step], swap_rep(grads_out[step])
                )
            marker = [sums[2]]
            for step in order:
                sums[step] = moved(sums[step], across(step))
            grad_expert_in, grad_expert_out = owner_grads(
                facts,
                [sums[step] for step in range(experts)],
                expert_in_weight.shape[1:],
                expert_out_weight.shape[1:],
            )
        else:

            def rep_scatter(each):
                return lax.psum_scatter(
                    each, "dp", axis_index_groups=rep_groups, scatter_dimension=0
                )

            def to_owner(grad, rows_each):
                each = grad.reshape(experts, reps, rows_each, -1).astype(BF)
                summed = rep_scatter(jnp.swapaxes(each, 0, 1))
                got = exchange([pick(summed, step) for step in range(experts)])
                got = jnp.stack(got)
                return jnp.stack([pick(got, owner) for owner in range(experts)]).astype(F32)

            marker = []
            grad_w_in, grad_w_out = grads_out
            grad_expert_in = to_owner(grad_w_in, in_rows)
            grad_expert_out = to_owner(grad_w_out, out_rows)

        grad_own, grad_other = attn_grads(attn_in, grad_proj, mixed, low, marker)
        came = swap_core(grad_other)
        if paired:
            out = attn_split(facts, grad_own, came)
            total = {}
            for at in range(2):
                steps = SPLIT_ORDER[2 * at : 2 * at + 2]
                for step, each in zip(
                    steps, sum_pieces(steps, out[2 + at], swap_rep(out[at])), strict=True
                ):
                    total[step] = moved(each, across(step)).astype(F32) if step else each
            total = total[0] + total[1] + total[2] + total[3]
        else:
            full = grad_own.astype(F32) + came.astype(F32)
            pieces_of = [
                full[source : source + rows * n_dp].reshape(n_dp, rows, cols)
                for source, rows, _ in attn_rows(width, shard)
            ]
            full = jnp.concatenate(pieces_of, axis=1).astype(BF)
            full = full.reshape((experts, reps) + full.shape[1:])
            full = rep_scatter(jnp.swapaxes(full, 0, 1))
            got = exchange([pick(full, step) for step in range(experts)])
            total = sum(each.astype(F32) for each in got)
        grad_attn = total[: 3 * shard].reshape(3, shard, cols)
        grad_attn = jnp.swapaxes(grad_attn, 0, 1)[None]
        rows = shard // 2
        grad_attn_out = jnp.concatenate(
            [total[3 * shard : 3 * shard + rows], total[3 * shard + rows :]], axis=1
        )[None]

        tiny = jnp.swapaxes(tiny[:, :32].reshape(n_dev, 3, per, 32), 1, 2)
        tiny = jnp.pad(tiny.reshape(dev_rows, 96), ((0, 0), (0, EXTRA - 96)))
        _, grad_back = sent_back(False, layer_grad, (), tiny)
        tiny = grad_back[:, width:].reshape(n_dev, per, EXTRA).astype(F32)
        tiny = jnp.sum(tiny, axis=0).reshape(per, 4, 32)[:, :3]
        tiny = jnp.swapaxes(tiny, 0, 1).reshape(3 * per, 32)
        grad_router = (tiny[:, :experts] + tiny[:, experts : 2 * experts])[None]
        grad_gains = (tiny[:, 8:10] + tiny[:, 10:12]).T[None]

        return (
            restored(out_back),
            restored(grad_back),
            grad_attn,
            grad_attn_out,
            grad_expert_in[None],
            grad_expert_out[None],
            grad_gains,
            grad_router,
        )

    in_specs = (
        P(("dp", "tensor"), None),
        P(("dp", "tensor"), None),
        P(("dp", "tensor")),
        P(("dp", "tensor"), None),
        P(("dp", "tensor")),
        P("dp", None),
        P("pipe", "dp", None, "tensor"),
        P("pipe", ("tensor", "dp"), None),
        P("pipe", None, "dp", "tensor"),
        P("pipe", None, ("tensor", "dp"), None),
        P("pipe", None, ("dp", "tensor")),
        P("pipe", ("dp", "tensor"), None),
    )
    out_specs = (
        P("pipe", ("dp", "tensor"), None),
        P("pipe", ("dp", "tensor"), None),
        P("pipe", "dp", None, "tensor"),
        P("pipe", ("tensor", "dp"), None),
        P("pipe", None, "dp", "tensor"),
        P("pipe", None, ("tensor", "dp"), None),
        P("pipe", None, ("dp", "tensor")),
        P("pipe", ("dp", "tensor"), None),
    )
    return jax.shard_map(local, mesh=mesh, in_specs=in_specs, out_specs=out_specs, check_vma=False)
```

```python
import functools

import jax
import jax.numpy as jnp
from jax import lax
from jax.experimental import pallas as pl
from jax.experimental.pallas import tpu as pltpu
from jax.sharding import PartitionSpec as P

HEAD_DIM = 64
EPSILON = 1e-06
NEGATIVE = -1e30
EXACT = lax.Precision.HIGHEST
EXTRA = 128
BF = jnp.bfloat16
F32 = jnp.float32
VM = pl.BlockSpec(memory_space=pltpu.VMEM)
SM = pl.BlockSpec(memory_space=pltpu.SMEM)
HB = pl.BlockSpec(memory_space=pltpu.HBM)
AFTER = pl.BlockSpec(memory_space=pl.ANY)
VH = pl.BlockSpec(memory_space=pltpu.VMEM)
FAR = True
PIPE, MINE, REP, CORE, SPLIT = range(5)


def dot32(a, b):
    return jnp.dot(a, b, preferred_element_type=F32)


def dot_nt(a, b):
    return lax.dot_general(a, b, (((1,), (1,)), ((), ())), preferred_element_type=F32)


def dot_tn(a, b):
    return lax.dot_general(a, b, (((0,), (0,)), ((), ())), preferred_element_type=F32)


def norm_scale(x):
    return lax.rsqrt(jnp.mean(x * x, axis=-1, keepdims=True) + EPSILON)


def norm_back(x, scale, gain, grad):
    weighted = grad * gain
    grad_x = scale * weighted - x * (scale * scale * scale) * jnp.mean(
        x * weighted, axis=-1, keepdims=True
    )
    return grad_x, jnp.sum(grad * (x * scale), axis=0, keepdims=True)


def pinned(value):
    return pltpu.with_memory_space_constraint(value, pltpu.HBM)


def kernel_call(body, name, outs, ins, specs, scratch=(), cost=1, room=24, hbm_outs=False):
    ins = [
        pinned(each) if spec is HB or spec is VH else each
        for each, spec in zip(ins, specs, strict=True)
    ]
    far = [hbm_outs or len(each) > 2 for each in outs]
    return pl.pallas_call(
        body,
        name=name,
        out_shape=[
            (pltpu.HBM if away else jax.ShapeDtypeStruct)(each[0], each[1])
            for each, away in zip(outs, far, strict=True)
        ],
        in_specs=specs,
        out_specs=[VM] * len(outs),
        scratch_shapes=list(scratch),
        compiler_params=pltpu.CompilerParams(vmem_limit_bytes=room << 20),
        cost_estimate=pl.CostEstimate(
            flops=int(cost * 1.1e9), bytes_accessed=0, transcendentals=0
        ),
    )(*ins)


def eye(count):
    rows = lax.broadcasted_iota(jnp.int32, (count, count), 0)
    return (rows == lax.broadcasted_iota(jnp.int32, (count, count), 1)).astype(F32).astype(BF)


def send_kernel(per, facts, inputs, cotangent, dealing, routes, order, router, gains, out, hot_out):
    rows, width = inputs.shape
    place = dealing[...]
    target = place >> 8
    numbers = [place & 255, routes[...], order[...] >> 8, order[...] & 255, target]
    numbers = [each.astype(F32) for each in numbers]
    numbers = jnp.concatenate(numbers + [jnp.zeros((EXTRA - 5, rows), F32)], axis=0)
    columns = dot_nt(eye(rows), numbers.astype(BF))
    targets = target.astype(F32)
    before = lax.broadcasted_iota(jnp.int32, (rows, rows), 0)
    after = lax.broadcasted_iota(jnp.int32, (rows, rows), 1)
    ahead = (columns[:, 4:5] == targets) & (before < after)
    slot = targets * per + jnp.sum(ahead.astype(F32), axis=0, keepdims=True)
    hot = (before.astype(F32) == slot).astype(F32).astype(BF)
    hot_out[...] = hot
    chosen = jnp.where(facts[PIPE] == 0, inputs[...], cotangent[...])
    out[:, :width] = dot32(hot, chosen).astype(BF)
    lane = lax.broadcasted_iota(jnp.int32, (rows, EXTRA), 1)
    tail = dot32(hot, jnp.where(lane < 4, columns, 0.0).astype(BF))
    parts = []
    for values in (router[...], gains[...]):
        high = values.astype(BF).astype(F32)
        mid = (values - high).astype(BF).astype(F32)
        parts += [high, mid, values - high - mid]
    count = gains.shape[1]
    blank = jnp.zeros((4, count), F32)
    block = jnp.concatenate([blank] + parts + [jnp.zeros((10, count), F32)], axis=0)
    block = dot_nt(eye(count), block.astype(BF))
    groups = [block[at * per : (at + 1) * per, :] for at in range(3)]
    block = jnp.concatenate(groups + [jnp.zeros((per, 32), F32)], axis=1)
    block = jnp.concatenate([block] * (rows // per), axis=0)
    out[:, width:] = (tail + block).astype(BF)


def deal_kernel(facts, both, own_rows, slots, onehot, place):
    width = own_rows.shape[1]
    pack = own_rows.shape[0]
    total = both.shape[0]
    half = pack // 2
    core = facts[CORE].astype(F32)
    numbers = both[:, width:]
    spot = numbers[:, 0:1].astype(F32)
    source = (lax.broadcasted_iota(jnp.int32, (total, 1), 0) >= pack).astype(F32)
    upper = (spot >= half).astype(F32)
    where = jnp.where(upper == core, source * half + spot - upper * half, -1.0)
    spots = lax.broadcasted_iota(jnp.int32, (total, pack), 1).astype(F32)
    hot = (spots == where).astype(F32).astype(BF)
    place[...] = hot
    own_rows[...] = dot_tn(hot, both[:, :width]).astype(BF)
    mine = dot_tn(hot, numbers)
    across = dot_nt(eye(EXTRA), mine.astype(BF))
    expert_col, expert_row = mine[:, 1:2], across[1:2, :]
    order_col = mine[:, 2:3] * 256.0 + mine[:, 3:4]
    order_row = across[2:3, :] * 256.0 + across[3:4, :]
    ahead = (expert_col == expert_row) & (order_col < order_row)
    rank = jnp.sum(ahead.astype(F32), axis=0, keepdims=True).astype(jnp.int32)
    experts = 4
    cap = pack // experts
    block = jnp.bitwise_xor(expert_row.astype(jnp.int32), facts[MINE])
    slot = jnp.where(rank < cap, block * cap + rank, -1)
    slots[...] = (lax.broadcasted_iota(jnp.int32, (pack, pack), 0) == slot).astype(F32).astype(BF)
    onehot[...] = (
        lax.broadcasted_iota(jnp.int32, (pack, EXTRA), 1) == expert_col.astype(jnp.int32)
    ).astype(F32)


def mask_of(facts, pack):
    query = lax.broadcasted_iota(jnp.int32, (pack, pack), 0)
    key = lax.broadcasted_iota(jnp.int32, (pack, pack), 1)
    split = facts[SPLIT]
    return ((query < split) == (key < split)) & (key <= query)


def stacked(refs):
    return jnp.concatenate([ref[...] for ref in refs], axis=0)


def flipped(params):
    flat = dot_nt(eye(EXTRA), params[...])
    router = flat[4:8] + flat[8:12] + flat[12:16]
    return router, flat[16:18] + flat[18:20] + flat[20:22]


def weight_copies(sources, scratch, sems, width, cols):
    copies = []
    for at in range(2):
        each = []
        for start, rows in (*((part * width, width) for part in range(3)), (3 * width, 2 * cols)):
            spot = pl.ds(start, rows)
            each.append(
                pltpu.make_async_copy(
                    sources[at].at[spot], scratch.at[at, spot], sems.at[4 * at + len(each)]
                )
            )
        copies.append(each)
    return copies


def gate_of(up):
    return jnp.sum(up[:, up.shape[1] - EXTRA :].astype(F32), axis=-1, keepdims=True)


def attn_kernel(second, dropped, facts, *refs):
    refs = list(refs)
    weights, sems = refs[-2:] if second else refs[-5:-3]
    refs = refs[:-2] if second else refs[:-5] + refs[-3:]
    own_rows = refs.pop(0)
    if second:
        up = refs.pop(0)
        slots_in = [refs.pop(0) for _ in range(4)]
    attn_own, attn_other, params, slots, onehot = (refs.pop(0) for _ in range(5))
    refs = refs[dropped:]
    if second:
        mid, attn_in, proj, mixed, mlp_in, probs = (refs.pop(0) for _ in range(6))
    else:
        send_up = refs.pop(0)
        proj, mixed, mid = refs[4:]
    blocks = [refs.pop(0) for _ in range(4)]
    pack, width = own_rows.shape
    cols = attn_own.shape[1]
    cap = pack // 4
    copies = weight_copies((attn_own, attn_other), weights, sems, width, cols)
    for each in copies:
        for copy in each:
            copy.start()
    _, gains = flipped(params)
    hot = slots[...]
    if second:
        stream = refs.pop(0)
        grads = [refs.pop(0) for _ in range(4)]
        came = up[:, :width].astype(F32) + gate_of(up) * dot_tn(hot, stacked(slots_in))
        rows = jnp.where(facts[PIPE] == 0, own_rows[...], came.astype(BF))
        stream[...] = rows
    else:
        rows = own_rows[...]
    x = rows.astype(F32)
    normed = (x * norm_scale(x) * gains[0:1, :]).astype(BF)
    if second:
        attn_in[...] = normed
    allowed = mask_of(facts, pack)
    for at in range(2):
        for part in range(3):
            copies[at][part].wait()
            proj[at, part] = dot32(
                normed, weights[at, part * width : (part + 1) * width, :]
            ).astype(BF)
        for head in range(cols // HEAD_DIM):
            lanes = slice(head * HEAD_DIM, (head + 1) * HEAD_DIM)
            scores = dot_nt(proj[at, 0, :, lanes], proj[at, 1, :, lanes]) * HEAD_DIM ** (-0.5)
            scores = jnp.where(allowed, scores, NEGATIVE)
            share = jnp.exp(scores - jnp.max(scores, axis=-1, keepdims=True))
            share = (share * (1.0 / jnp.sum(share, axis=-1, keepdims=True))).astype(BF)
            spot = at * cols + head * HEAD_DIM
            mixed[:, spot : spot + HEAD_DIM] = dot32(share, proj[at, 2, :, lanes]).astype(BF)
    base = 3 * width
    copies[0][3].wait()
    copies[1][3].wait()
    for side in range(2):
        rows_at = slice(base + side * cols, base + (side + 1) * cols)
        lanes = slice(side * cols, (side + 1) * cols)
        mid[:, lanes] = (
            x[:, lanes]
            + dot32(mixed[:, :cols], weights[0, rows_at, :])
            + dot32(mixed[:, cols:], weights[1, rows_at, :])
        )
    m = mid[:, :width]
    low = (m * norm_scale(m) * gains[1:2, :]).astype(BF)
    if second:
        mlp_in[...] = low
    logits = dot32(low, params[...])
    lane = lax.broadcasted_iota(jnp.int32, logits.shape, 1)
    logits = sum(pltpu.roll(logits, EXTRA - 4 * at, 1) for at in (1, 2, 3))
    logits = jnp.where(lane < 4, logits, NEGATIVE)
    rel = jnp.exp(logits - jnp.max(logits, axis=-1, keepdims=True))
    share = rel / jnp.sum(rel, axis=-1, keepdims=True)
    if second:
        probs[...] = share
    gate = jnp.sum(share * onehot[...], axis=-1, keepdims=True)
    if second:
        mid[:, width:] = jnp.broadcast_to(gate, (pack, EXTRA))
    else:
        send_up[:, :width] = m.astype(BF)
        high = gate.astype(BF).astype(F32)
        middle = (gate - high).astype(BF).astype(F32)
        parts = jnp.where(lane == 1, middle, jnp.where(lane == 2, gate - high - middle, 0.0))
        send_up[:, width:] = jnp.where(lane == 0, high, parts).astype(BF)
    for step in range(4):
        blocks[step][...] = dot32(hot[step * cap : (step + 1) * cap, :], low).astype(BF)
    if second:
        weighted = (gate * own_rows[...].astype(F32)).astype(BF)
        for step in range(4):
            grads[step][...] = dot32(hot[step * cap : (step + 1) * cap, :], weighted).astype(BF)


def attn_forward(facts, own_rows, weights, plan, came=None, after=()):
    attn_own, attn_other, params = weights
    slots, onehot = plan
    pack, width = own_rows.shape
    cols = attn_own.shape[1]
    cap = pack // 4
    second = came is not None
    ins = [facts, own_rows] + (list(came) if second else [])
    specs = [SM, VH] + ([VH] if second else []) + [VM] * (len(ins) - (3 if second else 2))
    specs += [HB] * 2 + [VH] * 3 + [AFTER] * len(after)
    ins += [attn_own, attn_other, params, slots, onehot, *after]
    if second:
        outs = [
            ((pack, width + EXTRA), F32, FAR),
            ((pack, width), BF, FAR),
            ((2, 3, pack, cols), BF, FAR),
            ((pack, width), BF, FAR),
            ((pack, width), BF, FAR),
            ((pack, EXTRA), F32, FAR),
        ]
    else:
        outs = [((pack, width + EXTRA), BF, FAR)]
    outs += [((cap, width), BF)] * 4
    if second:
        outs += [((pack, width), BF, FAR)] + [((cap, width), BF)] * 4
    return kernel_call(
        functools.partial(attn_kernel, second, len(after)),
        "attn_second" if second else "attn_first",
        outs,
        ins,
        specs,
        [pltpu.VMEM((2, 3 * width + 2 * cols, cols), BF), pltpu.SemaphoreType.DMA((8,))]
        + ([] if second else [
            pltpu.VMEM((2, 3, pack, cols), BF),
            pltpu.VMEM((pack, width), BF),
            pltpu.VMEM((pack, width), F32),
        ]),
        cost=8,
    )


def attn_back_kernel(first, dropped, facts, *refs):
    refs = list(refs)
    weights, sems = refs[-2:]
    refs = refs[:-2]
    grad_out = refs.pop(0)
    if first:
        up = refs.pop(0)
    else:
        own_rows = refs.pop(0)
        refs = refs[dropped:]
    grad_slots = [refs.pop(0) for _ in range(4)]
    stream, mid, proj, mlp_in, probs = (refs.pop(0) for _ in range(5))
    attn_own, attn_other, params, slots, onehot = (refs.pop(0) for _ in range(5))
    grad_stream = refs.pop(0)
    if first:
        blocks = [refs.pop(0) for _ in range(4)]
        grad_proj = refs.pop(0)
    else:
        grad_proj, grad_low, tiny = (refs.pop(0) for _ in range(3))
    pack, width = stream.shape
    cols = attn_own.shape[1]
    cap = pack // 4
    copies = weight_copies((attn_own, attn_other), weights, sems, width, cols)
    for part in (3, 0, 1, 2):
        for each in copies:
            each[part].start()
    router, gains = flipped(params)
    hot = slots[...]
    rows = grad_out[...]
    if not first:
        rows = jnp.where(facts[PIPE] == 0, rows, own_rows[...])
    g = rows.astype(F32)
    slot_rows = stacked(grad_slots)
    at_tokens = dot_tn(hot, slot_rows[:, width:])
    grad_logits = (at_tokens[:, 0:1] + at_tokens[:, 1:2]) * (onehot[...] - probs[...])
    m = mid[:, :width]
    wide = jnp.concatenate([router, jnp.zeros((EXTRA - 4, width), F32)], axis=0)
    grad_mlp = dot_tn(hot, slot_rows[:, :width]) + jnp.dot(
        grad_logits, wide, preferred_element_type=F32, precision=EXACT
    )
    grad_norm, gain_two = norm_back(m, norm_scale(m), gains[1:2, :], grad_mlp)
    grad_mid = g + grad_norm
    low = grad_mid.astype(BF)
    allowed = mask_of(facts, pack)
    grad_in = jnp.zeros((pack, width), F32)
    base = 3 * width
    copies[0][3].wait()
    copies[1][3].wait()
    for at in range(2):
        grad_mixed = (
            dot_nt(low[:, :cols], weights[at, base : base + cols, :])
            + dot_nt(low[:, cols:], weights[at, base + cols : base + 2 * cols, :])
        ).astype(BF)
        for head in range(cols // HEAD_DIM):
            lanes = slice(head * HEAD_DIM, (head + 1) * HEAD_DIM)
            query, key, value = (proj[at, part, :, lanes] for part in range(3))
            grad_head = grad_mixed[:, lanes]
            scores = dot_nt(query, key) * HEAD_DIM ** (-0.5)
            scores = jnp.where(allowed, scores, NEGATIVE)
            share = jnp.exp(scores - jnp.max(scores, axis=-1, keepdims=True))
            share = share * (1.0 / jnp.sum(share, axis=-1, keepdims=True))
            grad_share = dot_nt(grad_head, value)
            pulled = share * grad_share
            inner = jnp.sum(pulled, axis=-1, keepdims=True)
            grad_scores = ((pulled - share * inner) * HEAD_DIM ** (-0.5)).astype(BF)
            grad_proj[at, 0, :, lanes] = dot32(grad_scores, key).astype(BF)
            grad_proj[at, 1, :, lanes] = dot_tn(grad_scores, query).astype(BF)
            grad_proj[at, 2, :, lanes] = dot_tn(share.astype(BF), grad_head).astype(BF)
        for part in range(3):
            copies[at][part].wait()
            grad_in += dot_nt(
                grad_proj[at, part], weights[at, part * width : (part + 1) * width, :]
            )
    x = stream[...].astype(F32)
    grad_norm, gain_one = norm_back(x, norm_scale(x), gains[0:1, :], grad_in)
    result = (grad_mid + grad_norm).astype(BF)
    grad_stream[...] = result
    if first:
        weighted = (gate_of(up) * result.astype(F32)).astype(BF)
        for step in range(4):
            blocks[step][...] = dot32(hot[step * cap : (step + 1) * cap, :], weighted).astype(BF)
    else:
        grad_low[...] = low
        high = grad_logits.astype(BF)
        rest = (grad_logits - high.astype(F32)).astype(BF)
        lane = lax.broadcasted_iota(jnp.int32, (width, EXTRA), 1)
        both = dot_tn(mlp_in[...], high) + dot_tn(mlp_in[...], rest)
        both = jnp.where(lane < 4, both, 0.0)
        high = both.astype(BF).astype(F32)
        flat = [gain_one.astype(BF).astype(F32), gain_two.astype(BF).astype(F32)]
        flat += [gain_one - flat[0], gain_two - flat[1]]
        flat = jnp.concatenate(flat + [jnp.zeros((12, width), F32)], axis=0).astype(BF)
        spot = lax.broadcasted_iota(jnp.int32, (16, EXTRA), 0) + 8
        spot = spot == lax.broadcasted_iota(jnp.int32, (16, EXTRA), 1)
        turned = dot_tn(flat, spot.astype(F32).astype(BF))
        tiny[...] = (high + pltpu.roll(both - high, 4, 1) + turned).astype(BF)


def attn_backward(facts, grad_out, extra, grad_slots, saved, weights, plan, first):
    attn_own, attn_other, params = weights
    slots, onehot = plan
    stream, mid, proj, mlp_in, probs = saved
    pack, width = stream.shape
    cols = attn_own.shape[1]
    cap = pack // 4
    ins = [facts, grad_out, *extra, *grad_slots, stream, mid, proj, mlp_in, probs]
    specs = [SM, VH if first else VM, VH] + [AFTER] * (len(extra) - 1)
    specs += [VM] * 4 + [VH] * 5 + [HB] * 2 + [VH] * 3
    ins += [attn_own, attn_other, params, slots, onehot]
    outs = [((pack, width), BF)]
    if first:
        outs += [((cap, width), BF)] * 4
    outs += [((2, 3, pack, cols), BF)]
    if not first:
        outs += [((pack, width), BF), ((width, EXTRA), BF)]
    return kernel_call(
        functools.partial(attn_back_kernel, first, len(extra) - 1),
        "attn_back_first" if first else "attn_back_second",
        outs,
        ins,
        specs,
        [pltpu.VMEM((2, 3 * width + 2 * cols, cols), BF), pltpu.SemaphoreType.DMA((8,))],
        cost=13,
    )


def gelu_both(u):
    square = u * u
    t = jnp.tanh(0.7978845608028654 * u * (1.0 + 0.044715 * square))
    half = 0.5 * (1.0 + t)
    inner = 0.7978845608028654 * (1.0 + 3.0 * 0.044715 * square)
    return half + 0.5 * u * (1.0 - t * t) * inner, half * u


def bring(facts, pieces, places, scratch, sems):
    copies = []
    for piece, spots in zip(pieces, places, strict=True):
        for source, target, rows, column, columns in spots(facts):
            copies.append(
                pltpu.make_async_copy(
                    piece.at[pl.ds(source, rows), pl.ds(0, columns)],
                    scratch.at[pl.ds(target, rows), pl.ds(column, columns)],
                    sems.at[len(copies)],
                )
            )
    for copy in copies:
        copy.start()
    return copies


TILE = 256


def expert_kernel(keep, places_in, places_out, facts, *refs):
    refs = list(refs)
    blocks = [refs.pop(0) for _ in range(8)]
    pieces = [refs.pop(0) for _ in range(len(places_in))]
    if keep:
        pre = refs.pop(0)
    if keep:
        act = refs.pop(0)
        rows = refs.pop(0)
        own, other, w_in, w_out, sems_in, sems_out = refs
    else:
        own, other, w_in, w_out, sems_in, sems_out, act, rows = refs
    arriving = bring(facts, pieces, places_in, w_in, sems_in)
    later = bring(facts, pieces, places_out, w_out, sems_out)
    cap = blocks[0].shape[0]
    for at, block in enumerate(blocks):
        rows[at * cap : (at + 1) * cap, :] = block[...]
    for copy in arriving:
        copy.wait()
    ff = w_in.shape[1]
    width = w_in.shape[0]

    @pl.loop(0, ff // TILE)
    def _(tile):
        lanes = pl.ds(pl.multiple_of(tile * TILE, TILE), TILE)
        value = dot32(rows[...], w_in[:, lanes])
        slope, result = gelu_both(value)
        act[:, lanes] = result.astype(BF)
        if keep:
            pre[:, lanes] = slope.astype(BF)

    for copy in later:
        copy.wait()
    count = 4 * cap

    @pl.loop(0, width // TILE)
    def _(tile):
        lanes = pl.ds(pl.multiple_of(tile * TILE, TILE), TILE)
        value = dot32(act[...], w_out[:, lanes])
        own[:, lanes] = value[:count]
        other[:, lanes] = value[count:].astype(BF)


def halves(value, shape):
    high = value.astype(BF).astype(F32)
    lane = lax.broadcasted_iota(jnp.int32, shape, 1)
    return jnp.where(lane == 0, high, jnp.where(lane == 1, value - high, 0.0))


def expert_back_kernel(chosen, places_in, places_out, facts, *refs):
    refs = list(refs)
    blocks = [refs.pop(0) for _ in range(1 if chosen else 2)]
    pre, own_out, other_out = (refs.pop(0) for _ in range(3))
    pieces = [refs.pop(0) for _ in range(len(places_in))]
    grad_pre, own, other = (refs.pop(0) for _ in range(3))
    rows = blocks[0] if chosen else refs.pop(0)
    w_in, w_out, sems_in, sems_out = refs
    arriving = bring(facts, pieces, places_out, w_out, sems_out)
    later = bring(facts, pieces, places_in, w_in, sems_in)
    if not chosen:
        half = rows.shape[0] // 2
        for at, block in enumerate(blocks):
            rows[at * half : (at + 1) * half, :] = block[...]
    for copy in arriving:
        copy.wait()
    ff = w_in.shape[1]
    width = w_in.shape[0]
    count = rows.shape[0] // 2

    @pl.loop(0, ff // TILE)
    def _(tile):
        lanes = pl.ds(pl.multiple_of(tile * TILE, TILE), TILE)
        value = dot_nt(rows[...], w_out[lanes, :])
        grad_pre[:, lanes] = (value * pre[:, lanes].astype(F32)).astype(BF)

    for copy in later:
        copy.wait()

    @pl.loop(0, width // TILE)
    def _(tile):
        lanes = pl.ds(pl.multiple_of(tile * TILE, TILE), TILE)
        value = dot_nt(grad_pre[...], w_in[lanes, :])
        own[:, lanes] = value[:count]
        other[:, lanes] = value[count:].astype(BF)

    pull = jnp.sum(rows[:count, :].astype(F32) * own_out[...], axis=-1, keepdims=True)
    own[:, width:] = halves(pull, (count, EXTRA))
    pull = jnp.sum(
        rows[count:, :].astype(F32) * other_out[...].astype(F32), axis=-1, keepdims=True
    )
    other[:, width:] = halves(pull, (count, EXTRA)).astype(BF)


def expert_scratch(width, ff, places):
    numbers = jnp.zeros((8,), jnp.int32)
    sizes = [sum(len(spots(numbers)) for spots in each) for each in places]
    return (
        [pltpu.VMEM((width, ff), BF), pltpu.VMEM((ff, width), BF)],
        [pltpu.SemaphoreType.DMA((size,)) for size in sizes],
    )


def expert_call(name, keep, facts, blocks, pieces, places, width, ff):
    count = 4 * blocks[0].shape[0]
    ins = [facts, *blocks, *pieces]
    kept = [((2 * count, ff), BF, FAR)] * 2 + [((2 * count, width), BF, FAR)] if keep else []
    buffers, sems = expert_scratch(width, ff, places)
    scratch = [*buffers, *sems]
    if not keep:
        scratch += [pltpu.VMEM((2 * count, ff), BF), pltpu.VMEM((2 * count, width), BF)]
    return kernel_call(
        functools.partial(expert_kernel, keep, *places),
        name,
        kept + [((count, width), F32), ((count, width), BF)],
        ins,
        [SM] + [VM] * 8 + [HB] * len(pieces),
        scratch,
        cost=7,
    )


def expert_back_call(name, facts, blocks, saved, pieces, places, width, ff):
    chosen = len(blocks) == 1
    count = blocks[0].shape[0] * len(blocks) // 2
    wide = width + EXTRA
    ins = [facts, *blocks, *saved, *pieces]
    buffers, sems = expert_scratch(width, ff, places)
    outs = [((2 * count, ff), BF), ((count, wide), F32), ((count, wide), BF)]
    if not chosen:
        outs.append(((2 * count, width), BF, FAR))
    return kernel_call(
        functools.partial(expert_back_kernel, chosen, *places),
        name,
        outs,
        ins,
        [SM] + ([VH] if chosen else [VM] * 2) + [VH, VM, VM] + [HB] * len(pieces),
        [*buffers, *sems],
        cost=8,
    )


def fold_kernel(own, other, *blocks):
    blocks = blocks[-4:]
    cap = blocks[0].shape[0]
    width = own.shape[1] // TILE * TILE
    for step, block in enumerate(blocks):
        rows = slice(step * cap, (step + 1) * cap)
        block[:, :width] = (own[rows, :width] + other[rows, :width].astype(F32)).astype(BF)
        if own.shape[1] > width:
            both = own[rows, width:] + other[rows, width:].astype(F32)
            block[:, width:] = halves(both[:, 0:1] + both[:, 1:2], (cap, EXTRA)).astype(BF)


def fold(own, other, name, after=()):
    count, width = own.shape
    cap = count // 4
    return kernel_call(
        fold_kernel, name, [((cap, width), BF)] * 4, [own, other, *after], [VM, VM] + [AFTER] * len(after)
    )


def return_kernel(merge, *refs):
    refs = list(refs)
    rows = refs.pop(0)
    if merge:
        hot = refs.pop(0)
        slots_in = [refs.pop(0) for _ in range(4)]
        width = slots_in[0].shape[1]
        values = rows[:, :width] + rows[:, width : width + 1] * dot_tn(hot[...], stacked(slots_in))
        values = values.astype(BF)
    else:
        values = rows[...]
    place, facts = refs[:2]
    own, other = refs[-2:]
    pack = own.shape[0]
    core = facts[CORE]
    own[...] = dot32(place[pl.ds(pl.multiple_of(core * pack, pack), pack), :], values).astype(BF)
    other[...] = dot32(
        place[pl.ds(pl.multiple_of((1 - core) * pack, pack), pack), :], values
    ).astype(BF)


def sent_rows(facts, merge, rows, extra, place, width, after):
    pack = place.shape[1]
    ins = [rows, *extra, place, facts, *after]
    outs = [((pack, width), BF)] * 2
    return kernel_call(
        functools.partial(return_kernel, merge),
        "return_merged" if merge else "return_rows",
        outs,
        ins,
        ([VH, VH] + [VM] * 4 if merge else [VM]) + [VH, SM] + [AFTER] * len(after),
        cost=1,
    )


def run_copies(moves, sems):
    copies = [
        pltpu.make_async_copy(source, target, sems.at[at])
        for at, (source, target) in enumerate(moves)
    ]
    for copy in copies:
        copy.start()
    for copy in copies:
        copy.wait()


def rows_kernel(*refs):
    cap = refs[0].shape[0]
    out = refs[-1]
    for at, ref in enumerate(refs[:4]):
        out[at * cap : (at + 1) * cap, :] = ref[...]


def joined_rows(blocks, after):
    cap, width = blocks[0].shape
    return kernel_call(
        rows_kernel,
        "join_rows",
        [((4 * cap, width), BF)],
        [*blocks, *after],
        [VM] * 4 + [AFTER] * len(after),
    )[0]


def ordered_kernel(*refs):
    del refs


def ordered(value, after):
    return pl.pallas_call(
        ordered_kernel,
        name="ordered",
        out_shape=pltpu.HBM(value.shape, value.dtype),
        in_specs=[HB] + [AFTER] * len(after),
        out_specs=HB,
        input_output_aliases={0: 0},
        compiler_params=pltpu.CompilerParams(vmem_limit_bytes=1 << 20),
        cost_estimate=pl.CostEstimate(flops=0, bytes_accessed=0, transcendentals=0),
    )(pinned(value), *after)


def restore_kernel(hot, back, activations, grads, tiny):
    width = activations.shape[1]
    activations[...] = dot_tn(hot[...], back[:, :width]).astype(BF)
    grads[...] = dot_tn(hot[...], back[:, width : 2 * width]).astype(BF)
    rows = tiny.shape[0]
    total = jnp.zeros(tiny.shape, F32)
    for at in range(back.shape[0] // rows):
        total += back[at * rows : (at + 1) * rows, 2 * width :].astype(F32)
    tiny[...] = total


def finish_kernel(*refs):
    pieces, attn, attn_out = refs[:4], refs[4], refs[5]
    _, shard, cols = attn.shape
    total = sum(piece[...].astype(F32) for piece in pieces)
    for part in range(3):
        attn[part] = total[part * shard : (part + 1) * shard, :]
    rows = attn_out.shape[0]
    for side in range(2):
        spot = 3 * shard + side * rows
        attn_out[:, side * cols : (side + 1) * cols] = total[spot : spot + rows, :]


def stack_kernel(count, facts, *refs):
    pieces, out, sems = refs[:count], refs[-2], refs[-1]
    run_copies(
        [
            (piece, out.at[jnp.bitwise_xor(facts[MINE], step)])
            for step, piece in enumerate(pieces)
        ],
        sems,
    )


def stack_pieces(facts, pieces, after):
    count = len(pieces)
    return kernel_call(
        functools.partial(stack_kernel, count),
        "stack_pieces",
        [((count, *pieces[0].shape), BF)],
        [facts, *pieces, *after],
        [SM] + [HB] * count + [AFTER] * len(after),
        [pltpu.SemaphoreType.DMA((count,))],
        room=12,
        hbm_outs=True,
    )[0]


def gather_kernel(facts, near, far, *refs):
    out, sems = refs[-2:]
    groups = near.shape[0]
    moves = []
    for rep, source in ((facts[REP], near), (1 - facts[REP], far)):
        for part in range(3):
            moves.append(
                (
                    source.at[:, pl.ds(2 * part, 2)],
                    out.at[pl.ds(part * groups, groups), pl.ds(2 * rep, 2)],
                )
            )
        for side in range(2):
            for group in range(groups):
                moves.append(
                    (
                        source.at[group, 6 + side],
                        out.at[3 * groups + 2 * side + group // 2, group % 2 * 2 + rep],
                    )
                )
    run_copies(moves, sems)


def pack_attn_kernel(attn, attn_out, bundle, sems):
    parts, shard, cols = attn.shape
    rows = attn_out.shape[0]
    moves = [(attn.at[part], bundle.at[pl.ds(part * shard, shard)]) for part in range(parts)]
    for side in range(2):
        moves.append(
            (
                attn_out.at[:, pl.ds(side * cols, cols)],
                bundle.at[pl.ds(parts * shard + side * rows, rows)],
            )
        )
    run_copies(moves, sems)


def pack_attn(attn, attn_out):
    parts, shard, cols = attn.shape
    rows = attn_out.shape[0]
    return kernel_call(
        pack_attn_kernel,
        "pack_attn",
        [((parts * shard + 2 * rows, cols), BF)],
        [attn, attn_out],
        [HB] * 2,
        [pltpu.SemaphoreType.DMA((parts + 2,))],
        room=12,
        hbm_outs=True,
    )[0]


def pack_expert_kernel(steps, facts, w_in, w_out, *refs):
    blocks, sems = refs[-1 - len(steps) : -1], refs[-1]
    in_rows, out_rows, width = w_in.shape[1], w_out.shape[1], w_out.shape[2]
    moves = []
    for step, block in zip(steps, blocks, strict=True):
        at = jnp.bitwise_xor(facts[MINE], step)
        for side in range(2):
            moves.append(
                (
                    w_in.at[at, :, pl.ds(side * width, width)],
                    block.at[pl.ds(side * in_rows, in_rows)],
                )
            )
        moves.append((w_out.at[at], block.at[pl.ds(2 * in_rows, out_rows)]))
    run_copies(moves, sems)


def pack_expert(facts, w_in, w_out, steps, after=()):
    block = (2 * w_in.shape[1] + w_out.shape[1], w_out.shape[2])
    return kernel_call(
        functools.partial(pack_expert_kernel, steps),
        "pack_expert",
        [(block, BF)] * len(steps),
        [facts, w_in, w_out, *after],
        [SM, HB, HB] + [AFTER] * len(after),
        [pltpu.SemaphoreType.DMA((3 * len(steps),))],
        room=12,
        hbm_outs=True,
    )


SPLIT_ORDER = (2, 3, 1, 0)


def expert_out_grad_kernel(split, dropped, facts, *refs):
    blocks, refs = refs[:8], refs[8:]
    kept, act = refs[:2]
    refs = refs[2 + dropped :]
    rows, refs = refs[0], refs[1:]
    cap = blocks[0].shape[0]
    for at, block in enumerate(blocks):
        spot = slice(at * cap, (at + 1) * cap)
        rows[spot, :] = jnp.where(facts[PIPE] == 0, block[...], kept[spot, :])
    ff = act.shape[1]
    grad = refs[-1]

    @pl.loop(0, ff // TILE)
    def _(tile):
        lanes = pl.ds(pl.multiple_of(tile * TILE, TILE), TILE)
        grad[lanes, :] = dot_tn(act[:, lanes], rows[...])

    if split:
        count = ff // 8
        for at, step in enumerate(SPLIT_ORDER):
            owner = jnp.bitwise_xor(facts[MINE], step) * 2
            to = slice(at * count, (at + 1) * count)
            for rep, target in ((1 - facts[REP], refs[0]), (facts[REP], refs[1])):
                spot = pl.ds(pl.multiple_of((owner + rep) * count, count), count)
                target[to, :] = grad[spot, :].astype(BF)


def expert_in_grad_kernel(split, dropped, facts, rows, grad_pre, *refs):
    refs = refs[dropped:]
    ff = grad_pre.shape[1]
    width = rows.shape[1]
    grad = refs[-1]

    @pl.loop(0, ff // TILE)
    def _(tile):
        lanes = pl.ds(pl.multiple_of(tile * TILE, TILE), TILE)
        grad[:, lanes] = dot_tn(rows[...], grad_pre[:, lanes])

    if split:
        count = width // 8
        for at, step in enumerate(SPLIT_ORDER):
            owner = jnp.bitwise_xor(facts[MINE], step) * 2
            first = at * 2 * count
            for rep, target in ((1 - facts[REP], refs[0]), (facts[REP], refs[1])):
                spot = pl.ds(pl.multiple_of((owner + rep) * count, count), count)
                target[first : first + count, :] = grad[spot, :width].astype(BF)
                target[first + count : first + 2 * count, :] = grad[spot, width:].astype(BF)


def grad_outs(shape, wire, split):
    if split:
        return [(wire, BF, FAR)] * 2, [pltpu.VMEM(shape, F32)]
    return [(shape, F32)], []


def expert_out_grads(facts, blocks, kept, act, after, split):
    count, width = kept.shape
    ff = act.shape[1]
    outs, scratch = grad_outs((ff, width), (ff // 2, width), split)
    return kernel_call(
        functools.partial(expert_out_grad_kernel, split, len(after)),
        "expert_out_grads",
        [((count, width), BF, FAR), *outs],
        [facts, *blocks, kept, act, *after],
        [SM] + [VM] * 8 + [VH, VH] + [AFTER] * len(after),
        scratch,
        cost=4,
    )


def expert_in_grads(facts, rows, grad_pre, after, split):
    width = rows.shape[1]
    ff = grad_pre.shape[1]
    outs, scratch = grad_outs((width, ff), (ff // 2, width), split)
    return kernel_call(
        functools.partial(expert_in_grad_kernel, split, len(after)),
        "expert_in_grads",
        outs,
        [facts, rows, grad_pre, *after],
        [SM, VH, VM] + [AFTER] * len(after),
        scratch,
        cost=4,
    )


def owner_kernel(facts, *refs):
    grad_in, grad_out = refs[-2:]
    rows = grad_in.shape[1]
    width = grad_out.shape[2]
    for place, step in enumerate(SPLIT_ORDER):
        at = jnp.bitwise_xor(facts[MINE], step)
        grad_out[at] = refs[place][...].astype(F32)
        piece = refs[4 + place]
        for side in range(2):
            spot = slice(side * rows, (side + 1) * rows)
            grad_in[at, :, side * width : (side + 1) * width] = piece[spot, :].astype(F32)


def owner_grads(facts, pieces, after, in_shape, out_shape):
    return kernel_call(
        owner_kernel,
        "owner_grads",
        [(in_shape, F32), (out_shape, F32)],
        [facts, *pieces, *after],
        [SM] + [VM] * len(pieces) + [AFTER] * len(after),
        cost=4,
    )


def attn_grad_kernel(attn_in, grad_proj, mixed, low, *refs):
    own, other = refs[-2:]
    width = attn_in.shape[1]
    cols = own.shape[1]
    for at, target in ((0, own), (1, other)):
        for part in range(3):
            target[part * width : (part + 1) * width, :] = dot_tn(
                attn_in[...], grad_proj[at, part]
            ).astype(BF)
        for side in range(2):
            spot = 3 * width + side * cols
            target[spot : spot + cols, :] = dot_tn(
                mixed[:, at * cols : (at + 1) * cols], low[:, side * cols : (side + 1) * cols]
            ).astype(BF)


def attn_grads(attn_in, grad_proj, mixed, low, after):
    pack, width = attn_in.shape
    cols = grad_proj.shape[3]
    return kernel_call(
        attn_grad_kernel,
        "attn_grads",
        [((3 * width + 2 * cols, cols), BF)] * 2,
        [attn_in, grad_proj, mixed, low, *after],
        [VH, VM, VH, VM] + [AFTER] * len(after),
        cost=3,
    )


def attn_split_kernel(facts, own, came, *refs):
    sends, keeps = refs[-4:-2], refs[-2:]
    cols = own.shape[1]
    width = 2 * cols
    shard = width // 8
    count = 4 * shard
    for at, step in enumerate(SPLIT_ORDER):
        owner = jnp.bitwise_xor(facts[MINE], step) * 2
        for rep, target, first in (
            (1 - facts[REP], sends[at // 2], at % 2 * count),
            (facts[REP], keeps[at // 2], at % 2 * count),
        ):
            for source, rows, spot in attn_rows(width, shard):
                where = pl.ds(pl.multiple_of(source + (owner + rep) * rows, rows), rows)
                target[first + spot : first + spot + rows, :] = (
                    own[where, :].astype(F32) + came[where, :].astype(F32)
                ).astype(BF)


def sum_kernel(steps, keep, came, *outs):
    outs = outs[-len(steps) :]
    count = outs[0].shape[0]
    for at, out in enumerate(outs):
        rows = slice(at * count, (at + 1) * count)
        both = keep[rows, :].astype(F32) + came[rows, :].astype(F32)
        out[...] = both.astype(out.dtype)


def sum_pieces(steps, keep, came, after=()):
    count = keep.shape[0] // len(steps)
    kinds = [F32 if step == 0 else BF for step in steps]
    return kernel_call(
        functools.partial(sum_kernel, steps),
        "sum_pieces",
        [((count, keep.shape[1]), kind) for kind in kinds],
        [keep, came, *after],
        [VH] * 2 + [AFTER] * len(after),
        cost=0,
    )


def attn_rows(width, shard):
    out = shard // 2
    return (
        (0, shard, 0),
        (width, shard, shard),
        (2 * width, shard, 2 * shard),
        (3 * width, out, 3 * shard),
        (3 * width + width // 2, out, 3 * shard + out),
    )


def attn_split(facts, own, came, after):
    rows, cols = own.shape
    return kernel_call(
        attn_split_kernel,
        "attn_split",
        [((rows // 4, cols), BF, FAR)] * 4,
        [facts, own, came, *after],
        [SM, VM, VM] + [AFTER] * len(after),
        cost=3,
    )


def solution(mesh):
    shape = mesh.shape
    n_pipe, n_dp, n_t = shape["pipe"], shape["dp"], shape["tensor"]
    axes = ("pipe", "dp", "tensor")
    plane = ("dp", "tensor")
    n_dev = n_dp * n_t

    def local(
        inputs,
        cotangent,
        dealing,
        routes,
        slot_order,
        doc_lengths,
        attn_weight,
        attn_out_weight,
        expert_in_weight,
        expert_out_weight,
        norm_gains,
        router_weight,
    ):
        dev_rows, width = inputs.shape
        experts = expert_in_weight.shape[1]
        reps = n_dp // experts
        paired = reps == 2
        pack = dev_rows
        cap = pack // experts
        per = dev_rows // n_dev
        shard, cols = attn_weight.shape[1], attn_weight.shape[3]
        ff = expert_in_weight.shape[3]
        in_rows, out_rows = expert_in_weight.shape[2], expert_out_weight.shape[2]
        pipe = lax.axis_index("pipe")
        dp = lax.axis_index("dp")
        core = lax.axis_index("tensor")
        mine = dp // reps
        rep = dp % reps
        lengths = lax.dynamic_index_in_dim(doc_lengths, core, 0, keepdims=False)
        zero = jnp.int32(0)
        facts = jnp.stack([pipe, mine, rep, core, lengths[0], zero, zero, zero]).astype(jnp.int32)

        def moved(value, rule):
            pairs = []
            for a in range(n_pipe):
                for b in range(experts):
                    for c in range(reps):
                        for d in range(n_t):
                            to = rule(a, b, c, d)
                            if to is not None:
                                flat = [
                                    ((w * experts + x) * reps + y) * n_t + z
                                    for w, x, y, z in ((a, b, c, d), to)
                                ]
                                pairs.append(tuple(flat))
            return lax.ppermute(value, axes, pairs)

        def swap_core(value):
            return moved(value, lambda a, b, c, d: (a, b, c, 1 - d))

        def swap_rep(value):
            return moved(value, lambda a, b, c, d: (a, b, 1 - c, d))

        def across(step):
            return lambda a, b, c, d: (a, b ^ step, c, d)

        def up(step):
            return lambda a, b, c, d: (1, b ^ step, c, d) if a == 0 else None

        def down(step):
            return lambda a, b, c, d: (0, b ^ step, c, d) if a == 1 else None

        order = (2, 3, 1)

        def exchange(blocks):
            out = {0: blocks[0]}
            for step in order:
                out[step] = moved(blocks[step], across(step))
            return [out[step] for step in range(experts)]

        def crossed(blocks, way):
            out = {}
            for step in (*order, 0):
                out[step] = moved(blocks[step], way(step))
            return [out[step] for step in range(experts)]

        def with_other(blocks):
            out = {}
            for step in (0, 1, 2, 3):
                out[step] = swap_core(blocks[step])
            return list(blocks) + [out[step] for step in range(experts)]

        def pick(blocks, step):
            return lax.dynamic_index_in_dim(blocks, mine ^ step, 0, keepdims=False)

        rep_groups = [[b * reps + c for c in range(reps)] for b in range(experts)]

        payload, send_hot = kernel_call(
            functools.partial(send_kernel, per),
            "send",
            [((dev_rows, width + EXTRA), BF), ((dev_rows, dev_rows), BF)],
            [
                facts,
                inputs,
                cotangent,
                dealing.reshape(1, dev_rows),
                routes.reshape(1, dev_rows),
                slot_order.reshape(1, dev_rows),
                router_weight[0].T,
                norm_gains[0],
            ],
            [SM] + [VM] * 7,
            cost=2,
        )
        dealt = lax.all_to_all(payload, plane, split_axis=0, concat_axis=0, tiled=True)
        params = dealt[:, width:].reshape(n_dev, per, 4, 32)[:, :, :3]
        params = jnp.swapaxes(params, 1, 2).reshape(width, 32)
        params = jnp.pad(params, ((0, 0), (0, EXTRA - 32)))
        both = lax.all_gather(dealt, "tensor", axis=0, tiled=True)
        own_rows, slots, onehot, place = kernel_call(
            deal_kernel,
            "deal",
            [
                ((pack, width), BF, FAR),
                ((pack, pack), BF, FAR),
                ((pack, EXTRA), F32, FAR),
                ((2 * pack, pack), BF, FAR),
            ],
            [facts, both],
            [SM, VM],
            cost=1.5,
        )
        plan = (slots, onehot)

        out_shard = attn_out_weight[0]
        attn_shape = (4 * width, cols)

        def expert_places(way, step):
            def owner_of(numbers):
                owner = jnp.bitwise_xor(numbers[MINE], step) * 2
                return owner + (numbers[REP] if way == 0 else 1 - numbers[REP])

            def spots_in(numbers):
                at = pl.multiple_of(owner_of(numbers) * in_rows, in_rows)
                return [(0, at, in_rows, 0, width), (in_rows, at, in_rows, width, width)]

            def spots_out(numbers):
                at = pl.multiple_of(owner_of(numbers) * out_rows, out_rows)
                return [(2 * in_rows, at, out_rows, 0, width)]

            return spots_in, spots_out

        if paired:
            w_in_raw, w_out_raw = expert_in_weight[0], expert_out_weight[0]
            attn_bundle = pack_attn(jnp.swapaxes(attn_weight[0], 0, 1), out_shard)
            near, far = {}, {}
            (near[0],) = pack_expert(facts, w_in_raw, w_out_raw, (0,), (attn_bundle,))
            far[0] = swap_rep(near[0])
            attn_near = exchange([attn_bundle] * experts)
            attn_near = stack_pieces(
                facts, [each.reshape(8, shard // 2, cols) for each in attn_near],
                [payload, far[0]],
            )
            first, bundle = pack_expert(facts, w_in_raw, w_out_raw, (1, 2), (attn_near,))
            near[1] = moved(first, across(1))
            attn_far = swap_rep(attn_near)
            near[2] = moved(bundle, across(2))
            (bundle,) = pack_expert(facts, w_in_raw, w_out_raw, (3,), (near[2],))
            attn_own = kernel_call(
                gather_kernel,
                "gather_attn",
                [((4 * experts, 4, shard // 2, cols), BF)],
                [facts, attn_near, attn_far, bundle],
                [SM, HB, HB, AFTER],
                [pltpu.SemaphoreType.DMA((22,))],
                room=12,
                hbm_outs=True,
            )[0].reshape(attn_shape)
            near[3] = moved(bundle, across(3))
            for step in (1, 2, 3):
                far[step] = swap_rep(near[step])
            pieces = [each[step] for each in (near, far) for step in range(experts)]
            ready = ()
            both_places = [
                expert_places(way, step) for way in range(2) for step in range(experts)
            ]
            places = ([each[0] for each in both_places], [each[1] for each in both_places])
        else:
            attn_bundle = jnp.concatenate(
                [attn_weight[0, :, part] for part in range(3)]
                + [out_shard[:, :cols], out_shard[:, cols:]],
                axis=0,
            )
            every = lax.all_gather(attn_bundle, "dp", axis=0)
            attn_own = jnp.concatenate(
                [
                    every[:, spot : spot + rows].reshape(-1, cols)
                    for _, rows, spot in attn_rows(width, shard)
                ],
                axis=0,
            )

            def assembled(blocks):
                got = exchange([pick(blocks, step) for step in range(experts)])
                got = jnp.stack(got)
                got = jnp.stack([pick(got, owner) for owner in range(experts)])
                got = lax.all_gather(got, "dp", axis_index_groups=rep_groups)
                return jnp.swapaxes(got, 0, 1)

            ready = ()
            pieces = [
                assembled(expert_in_weight[0]).reshape(width, ff),
                assembled(expert_out_weight[0]).reshape(ff, width),
            ]
            places = (
                [lambda numbers: [(0, 0, width, 0, ff)], lambda numbers: []],
                [lambda numbers: [], lambda numbers: [(0, 0, ff, 0, width)]],
            )
        attn_other = swap_core(attn_own)
        weights = (attn_own, attn_other, params)

        def expert_forward(blocks, name, keep, after=()):
            *kept, own, other = expert_call(name, keep, facts, blocks, pieces, places, width, ff)
            folded = fold(own, swap_core(other), "fold_" + name, after)
            return kept, own, other, folded

        def expert_backward(blocks, saved, name, after=()):
            grad_pre, own, other, *rows = expert_back_call(
                name, facts, blocks, saved, pieces, places, width, ff
            )
            return grad_pre, rows, fold(own, swap_core(other), "fold_" + name, after)

        def sent_back(merge, rows, extra, after):
            own, other = sent_rows(facts, merge, rows, extra, place, width, after)
            return own, other

        out = attn_forward(facts, own_rows, weights, plan, None, ready)
        mid_up = moved(out[0], lambda a, b, c, d: (1, b, c, d) if a == 0 else None)
        blocks = with_other(exchange(out[1:5]))
        _, _, _, expert_slots = expert_forward(
            blocks, "expert_first", False, (mid_up,)
        )
        from_first = crossed(expert_slots, up)

        out = attn_forward(facts, own_rows, weights, plan, (mid_up, *from_first))
        mid, attn_in, proj, mixed, mlp_in, probs = out[:6]
        stream = out[10]
        blocks = with_other(exchange(out[6:10]))
        kept_blocks = exchange(out[11:15])
        (slope, act, rows), own_out, other_out, expert_slots = expert_forward(blocks, "expert_second", True)
        expert_saved = (slope, own_out, other_out)

        saved = (stream, mid, proj, mlp_in, probs)
        kept_own = joined_rows(kept_blocks, (other_out,))
        _, (kept_rows,), grad_slots = expert_backward(
            [kept_own, swap_core(kept_own)], expert_saved, "expert_back_first"
        )
        back = attn_backward(
            facts, own_rows, [mid_up], exchange(grad_slots), saved, weights, plan, True
        )
        grad_down = moved(back[0], lambda a, b, c, d: (0, b, c, d) if a == 1 else None)
        expert_slots = exchange(expert_slots)
        out_back = sent_back(True, mid, (slots, *expert_slots), (back[1],))

        grads = with_other(crossed(back[1:5], down))
        grad_rows, *out_wire = expert_out_grads(
            facts, grads, kept_rows, act, (out_back[0],), paired
        )
        grad_pre, _, grad_slots = expert_backward(
            [grad_rows], expert_saved, "expert_back_second"
        )
        in_wire = expert_in_grads(facts, rows, grad_pre, [grad_slots[2]], paired)
        after = []
        if paired:
            out_sums = sum_pieces(
                SPLIT_ORDER, out_wire[1], swap_rep(out_wire[0]), [in_wire[1]]
            )
            after = [out_sums[0]]
        layer_grad, grad_proj, low, tiny = attn_backward(
            facts,
            grad_down,
            [own_rows, *after],
            exchange(grad_slots),
            saved,
            weights,
            plan,
            False,
        )

        if paired:
            out_near = [
                moved(each, across(step)) if step else each
                for step, each in zip(SPLIT_ORDER, out_sums, strict=True)
            ]
            came_in = swap_rep(in_wire[0])
            marker = [came_in, *out_near[:2]]
        else:

            def rep_scatter(each):
                return lax.psum_scatter(
                    each, "dp", axis_index_groups=rep_groups, scatter_dimension=0
                )

            def to_owner(grad, rows_each):
                each = grad.reshape(experts, reps, rows_each, -1).astype(BF)
                summed = rep_scatter(jnp.swapaxes(each, 0, 1))
                got = exchange([pick(summed, step) for step in range(experts)])
                got = jnp.stack(got)
                return jnp.stack([pick(got, owner) for owner in range(experts)]).astype(F32)

            marker = []
            (grad_w_in,), (grad_w_out,) = in_wire, out_wire
            grad_expert_in = to_owner(grad_w_in, in_rows)
            grad_expert_out = to_owner(grad_w_out, out_rows)

        grad_own, grad_other = attn_grads(attn_in, grad_proj, mixed, low, marker)
        came = swap_core(grad_other)
        if paired:
            in_sums = sum_pieces(SPLIT_ORDER, in_wire[1], came_in, [grad_own])
            in_near = [
                moved(each, across(step)) if step else each
                for step, each in zip(SPLIT_ORDER, in_sums, strict=True)
            ]
            out = attn_split(facts, grad_own, came, (in_sums[0],))
            after = (out[2],)
        else:
            after = ()
        grad_back = sent_back(False, layer_grad, (), after)
        tiny = jnp.swapaxes(tiny[:, :32].reshape(n_dev, 3, per, 32), 1, 2)
        tiny = jnp.pad(tiny.reshape(dev_rows, 96), ((0, 0), (0, EXTRA - 96)))
        theirs = swap_core(jnp.concatenate([out_back[1], grad_back[1]], axis=1))
        both = jnp.concatenate([out_back[0], grad_back[0]], axis=1) + theirs
        payload = jnp.concatenate([both, tiny], axis=1)
        if paired:
            total = {}
            first = sum_pieces(SPLIT_ORDER[:2], out[2], swap_rep(out[0]), [payload])
            last = swap_rep(ordered(out[1], (first[0],)))
            last = sum_pieces(SPLIT_ORDER[2:], out[3], last, [first[1]])
            for step, each in zip(SPLIT_ORDER, [*first, *last], strict=True):
                total[step] = moved(each, across(step)) if step else each
            grad_expert_in, grad_expert_out = owner_grads(
                facts,
                [*out_near, *in_near],
                (total[0],),
                expert_in_weight.shape[1:],
                expert_out_weight.shape[1:],
            )
            grad_attn, grad_attn_out = kernel_call(
                finish_kernel,
                "finish_attn",
                [((3, shard, cols), F32), ((shard // 2, width), F32)],
                [total[step] for step in range(experts)],
                [VM] * 4,
            )
        else:
            full = grad_own.astype(F32) + came.astype(F32)
            pieces_of = [
                full[source : source + rows * n_dp].reshape(n_dp, rows, cols)
                for source, rows, _ in attn_rows(width, shard)
            ]
            full = jnp.concatenate(pieces_of, axis=1).astype(BF)
            full = full.reshape((experts, reps) + full.shape[1:])
            full = rep_scatter(jnp.swapaxes(full, 0, 1))
            got = exchange([pick(full, step) for step in range(experts)])
            total = sum(each.astype(F32) for each in got)
            grad_attn = total[: 3 * shard].reshape(3, shard, cols)
            rows = shard // 2
            grad_attn_out = jnp.concatenate(
                [total[3 * shard : 3 * shard + rows], total[3 * shard + rows :]], axis=1
            )
        both = lax.all_to_all(payload, plane, split_axis=0, concat_axis=0, tiled=True)
        activations, input_grads, tiny = kernel_call(
            restore_kernel,
            "restore",
            [((dev_rows, width), BF), ((dev_rows, width), BF), ((per, EXTRA), F32)],
            [send_hot, both],
            [VM] * 2,
            cost=2,
        )
        tiny = tiny.reshape(per, 4, 32)[:, :3]
        tiny = jnp.swapaxes(tiny, 0, 1).reshape(3 * per, 32)
        grad_router = (tiny[:, :experts] + tiny[:, experts : 2 * experts])[None]
        grad_gains = (tiny[:, 8:10] + tiny[:, 10:12]).T[None]

        return (
            activations[None],
            input_grads[None],
            jnp.swapaxes(grad_attn, 0, 1)[None],
            grad_attn_out[None],
            grad_expert_in[None],
            grad_expert_out[None],
            grad_gains,
            grad_router,
        )

    in_specs = (
        P(("dp", "tensor"), None),
        P(("dp", "tensor"), None),
        P(("dp", "tensor")),
        P(("dp", "tensor"), None),
        P(("dp", "tensor")),
        P("dp", None),
        P("pipe", "dp", None, "tensor"),
        P("pipe", ("tensor", "dp"), None),
        P("pipe", None, "dp", "tensor"),
        P("pipe", None, ("tensor", "dp"), None),
        P("pipe", None, ("dp", "tensor")),
        P("pipe", ("dp", "tensor"), None),
    )
    out_specs = (
        P("pipe", ("dp", "tensor"), None),
        P("pipe", ("dp", "tensor"), None),
        P("pipe", "dp", None, "tensor"),
        P("pipe", ("tensor", "dp"), None),
        P("pipe", None, "dp", "tensor"),
        P("pipe", None, ("tensor", "dp"), None),
        P("pipe", None, ("dp", "tensor")),
        P("pipe", ("dp", "tensor"), None),
    )
    return jax.shard_map(local, mesh=mesh, in_specs=in_specs, out_specs=out_specs, check_vma=False)
```

```python
import functools

import jax
import jax.numpy as jnp
from jax import lax
from jax.experimental import pallas as pl
from jax.experimental.pallas import tpu as pltpu
from jax.sharding import PartitionSpec as P

HEAD_DIM = 64
EPSILON = 1e-06
NEGATIVE = -1e30
EXACT = lax.Precision.HIGHEST
EXTRA = 128
BF = jnp.bfloat16
F32 = jnp.float32
VM = pl.BlockSpec(memory_space=pltpu.VMEM)
SM = pl.BlockSpec(memory_space=pltpu.SMEM)
HB = pl.BlockSpec(memory_space=pltpu.HBM)
AFTER = pl.BlockSpec(memory_space=pl.ANY)
RAW = 2
VH = pl.BlockSpec(memory_space=pltpu.VMEM)
FAR = True
PIPE, MINE, REP, CORE, SPLIT = range(5)


def dot32(a, b):
    return jnp.dot(a, b, preferred_element_type=F32)


def dot_nt(a, b):
    return lax.dot_general(a, b, (((1,), (1,)), ((), ())), preferred_element_type=F32)


def dot_tn(a, b):
    return lax.dot_general(a, b, (((0,), (0,)), ((), ())), preferred_element_type=F32)


def split3(value):
    high = value.astype(BF)
    rest = value - high.astype(F32)
    mid = rest.astype(BF)
    return high, mid, (rest - mid.astype(F32)).astype(BF)


def parts_nt(a, b):
    return sum(dot_nt(a, part) for part in split3(b))


def norm_scale(x):
    return lax.rsqrt(jnp.mean(x * x, axis=-1, keepdims=True) + EPSILON)


def norm_back(x, scale, gain, grad):
    weighted = grad * gain
    grad_x = scale * weighted - x * (scale * scale * scale) * jnp.mean(
        x * weighted, axis=-1, keepdims=True
    )
    return grad_x, jnp.sum(grad * (x * scale), axis=0, keepdims=True)


def pinned(value):
    return pltpu.with_memory_space_constraint(value, pltpu.HBM)


def kernel_call(body, name, outs, ins, specs, scratch=(), cost=1, room=24, hbm_outs=False):
    ins = [
        pinned(each) if spec is HB or spec is VH else each
        for each, spec in zip(ins, specs, strict=True)
    ]
    far = [hbm_outs or len(each) > 2 for each in outs]
    return pl.pallas_call(
        body,
        name=name,
        out_shape=[
            (pltpu.HBM if away else jax.ShapeDtypeStruct)(each[0], each[1])
            for each, away in zip(outs, far, strict=True)
        ],
        in_specs=specs,
        out_specs=[HB if each[2:] == (RAW,) else VM for each in outs],
        scratch_shapes=list(scratch),
        compiler_params=pltpu.CompilerParams(vmem_limit_bytes=room << 20),
        cost_estimate=pl.CostEstimate(
            flops=int(cost * 1.1e9), bytes_accessed=0, transcendentals=0
        ),
    )(*ins)


def eye(count):
    rows = lax.broadcasted_iota(jnp.int32, (count, count), 0)
    return (rows == lax.broadcasted_iota(jnp.int32, (count, count), 1)).astype(F32).astype(BF)


def send_kernel(per, facts, inputs, cotangent, dealing, routes, order, router, gains, out, hot_out):
    rows, width = inputs.shape
    place = dealing[...]
    target = place >> 8
    numbers = [place & 255, routes[...], order[...] >> 8, order[...] & 255, target]
    numbers = [each.astype(F32) for each in numbers]
    numbers = jnp.concatenate(numbers + [jnp.zeros((EXTRA - 5, rows), F32)], axis=0)
    columns = dot_nt(eye(rows), numbers.astype(BF))
    targets = target.astype(F32)
    before = lax.broadcasted_iota(jnp.int32, (rows, rows), 0)
    after = lax.broadcasted_iota(jnp.int32, (rows, rows), 1)
    ahead = (columns[:, 4:5] == targets) & (before < after)
    slot = targets * per + jnp.sum(ahead.astype(F32), axis=0, keepdims=True)
    hot = (before.astype(F32) == slot).astype(F32).astype(BF)
    hot_out[...] = hot
    chosen = jnp.where(facts[PIPE] == 0, inputs[...], cotangent[...])
    out[:, :width] = dot32(hot, chosen).astype(BF)
    lane = lax.broadcasted_iota(jnp.int32, (rows, EXTRA), 1)
    tail = dot32(hot, jnp.where(lane < 4, columns, 0.0).astype(BF))
    parts = []
    for values in (router[...], gains[...]):
        high = values.astype(BF).astype(F32)
        mid = (values - high).astype(BF).astype(F32)
        parts += [high, mid, values - high - mid]
    count = gains.shape[1]
    blank = jnp.zeros((4, count), F32)
    block = jnp.concatenate([blank] + parts + [jnp.zeros((10, count), F32)], axis=0)
    block = dot_nt(eye(count), block.astype(BF))
    groups = [block[at * per : (at + 1) * per, :] for at in range(3)]
    block = jnp.concatenate(groups + [jnp.zeros((per, 32), F32)], axis=1)
    block = jnp.concatenate([block] * (rows // per), axis=0)
    out[:, width:] = (tail + block).astype(BF)


def deal_kernel(facts, both, own_rows, slots, onehot, place):
    width = own_rows.shape[1]
    pack = own_rows.shape[0]
    total = both.shape[0]
    half = pack // 2
    core = facts[CORE].astype(F32)
    numbers = both[:, width:]
    spot = numbers[:, 0:1].astype(F32)
    source = (lax.broadcasted_iota(jnp.int32, (total, 1), 0) >= pack).astype(F32)
    upper = (spot >= half).astype(F32)
    where = jnp.where(upper == core, source * half + spot - upper * half, -1.0)
    spots = lax.broadcasted_iota(jnp.int32, (total, pack), 1).astype(F32)
    hot = (spots == where).astype(F32).astype(BF)
    place[...] = hot
    own_rows[...] = dot_tn(hot, both[:, :width]).astype(BF)
    mine = dot_tn(hot, numbers)
    across = dot_nt(eye(EXTRA), mine.astype(BF))
    expert_col, expert_row = mine[:, 1:2], across[1:2, :]
    order_col = mine[:, 2:3] * 256.0 + mine[:, 3:4]
    order_row = across[2:3, :] * 256.0 + across[3:4, :]
    ahead = (expert_col == expert_row) & (order_col < order_row)
    rank = jnp.sum(ahead.astype(F32), axis=0, keepdims=True).astype(jnp.int32)
    experts = 4
    cap = pack // experts
    block = jnp.bitwise_xor(expert_row.astype(jnp.int32), facts[MINE])
    slot = jnp.where(rank < cap, block * cap + rank, -1)
    slots[...] = (lax.broadcasted_iota(jnp.int32, (pack, pack), 0) == slot).astype(F32).astype(BF)
    onehot[...] = (
        lax.broadcasted_iota(jnp.int32, (pack, EXTRA), 1) == expert_col.astype(jnp.int32)
    ).astype(F32)


def mask_of(facts, first, rows, columns):
    query = lax.broadcasted_iota(jnp.int32, (rows, columns), 0) + first
    key = lax.broadcasted_iota(jnp.int32, (rows, columns), 1)
    split = facts[SPLIT]
    return ((query < split) == (key < split)) & (key <= query)


def turned_mask(facts, first, rows, columns):
    key = lax.broadcasted_iota(jnp.int32, (rows, columns), 0) + first
    query = lax.broadcasted_iota(jnp.int32, (rows, columns), 1) + first
    split = facts[SPLIT]
    return ((query < split) == (key < split)) & (key <= query)


def stacked(refs):
    return jnp.concatenate([ref[...] for ref in refs], axis=0)


def flipped(params):
    flat = dot_nt(eye(EXTRA), params[...])
    return flat[16:18] + flat[18:20] + flat[20:22]


def weight_copies(sources, scratch, sems, width, cols):
    copies = []
    for at in range(2):
        each = []
        for start, rows in (*((part * width, width) for part in range(3)), (3 * width, 2 * cols)):
            spot = pl.ds(start, rows)
            each.append(
                pltpu.make_async_copy(
                    sources[at].at[spot], scratch.at[at, spot], sems.at[4 * at + len(each)]
                )
            )
        copies.append(each)
    return copies


def gate_of(up):
    return jnp.sum(up[:, up.shape[1] - EXTRA :].astype(F32), axis=-1, keepdims=True)


def attn_kernel(second, dropped, facts, *refs):
    refs = list(refs)
    weights, sems = refs[-2:] if second else refs[-5:-3]
    refs = refs[:-2] if second else refs[:-5] + refs[-3:]
    own_rows = refs.pop(0)
    if second:
        up = refs.pop(0)
        slots_in = [refs.pop(0) for _ in range(4)]
    attn_own, attn_other, params, slots, onehot = (refs.pop(0) for _ in range(5))
    refs = refs[dropped:]
    if second:
        mid, attn_in, proj, mixed, mlp_in, probs = (refs.pop(0) for _ in range(6))
    else:
        send_up = refs.pop(0)
        proj, mixed, mid = refs[4:]
    blocks = [refs.pop(0) for _ in range(4)]
    pack, width = own_rows.shape
    cols = attn_own.shape[1]
    cap = pack // 4
    copies = weight_copies((attn_own, attn_other), weights, sems, width, cols)
    for each in copies:
        for copy in each:
            copy.start()
    gains = flipped(params)
    hot = slots[...]
    if second:
        stream = refs.pop(0)
        grads = [refs.pop(0) for _ in range(4)]
        came = up[:, :width].astype(F32) + gate_of(up) * dot_tn(hot, stacked(slots_in))
        rows = jnp.where(facts[PIPE] == 0, own_rows[...], came.astype(BF))
        stream[...] = rows
    else:
        rows = own_rows[...]
    x = rows.astype(F32)
    normed = (x * norm_scale(x) * gains[0:1, :]).astype(BF)
    if second:
        attn_in[...] = normed
    half = pack // 2
    upper = mask_of(facts, 0, half, half)
    lower = mask_of(facts, half, half, pack)
    lane = lax.broadcasted_iota(jnp.int32, (pack, EXTRA), 1)
    totals = jnp.zeros((pack, EXTRA), F32)
    for at in range(2):
        for part in range(3):
            copies[at][part].wait()
            proj[at, part] = dot32(
                normed, weights[at, part * width : (part + 1) * width, :]
            ).astype(BF)
        for pair in range(cols // EXTRA):
            lanes = slice(pair * EXTRA, (pair + 1) * EXTRA)
            query = proj[at, 0, :, lanes] * jnp.asarray(HEAD_DIM ** (-0.5), BF)
            key, value = proj[at, 1, :, lanes], proj[at, 2, :, lanes]
            parts = []
            for side in range(2):
                chosen = jnp.where((lane >= HEAD_DIM) == (side == 1), query, 0)
                head = 8 + (at * cols + pair * EXTRA) // HEAD_DIM + side
                results = []
                for first, count, allowed in ((0, half, upper), (half, pack, lower)):
                    scores = dot_nt(chosen[first : first + half, :], key[:count, :])
                    scores = jnp.where(allowed, scores, NEGATIVE)
                    peak = jnp.max(scores, axis=-1, keepdims=True)
                    share = jnp.exp(scores - peak)
                    total = jnp.sum(share, axis=-1, keepdims=True)
                    results.append(
                        (dot32(share.astype(BF), value[:count, :]) * (1.0 / total), peak + jnp.log(total))
                    )
                parts.append(jnp.concatenate([each[0] for each in results], axis=0))
                if second:
                    level = jnp.concatenate([each[1] for each in results], axis=0)
                    totals = jnp.where(lane == head, level, totals)
            spot = at * cols + pair * EXTRA
            mixed[:, spot : spot + EXTRA] = jnp.where(lane < HEAD_DIM, *parts).astype(BF)
    base = 3 * width
    copies[0][3].wait()
    copies[1][3].wait()
    for side in range(2):
        rows_at = slice(base + side * cols, base + (side + 1) * cols)
        lanes = slice(side * cols, (side + 1) * cols)
        mid[:, lanes] = (
            x[:, lanes]
            + dot32(mixed[:, :cols], weights[0, rows_at, :])
            + dot32(mixed[:, cols:], weights[1, rows_at, :])
        )
    m = mid[:, :width]
    low = (m * norm_scale(m) * gains[1:2, :]).astype(BF)
    if second:
        mlp_in[...] = low
    logits = dot32(low, params[...])
    lane = lax.broadcasted_iota(jnp.int32, logits.shape, 1)
    logits = sum(pltpu.roll(logits, EXTRA - 4 * at, 1) for at in (1, 2, 3))
    logits = jnp.where(lane < 4, logits, NEGATIVE)
    rel = jnp.exp(logits - jnp.max(logits, axis=-1, keepdims=True))
    share = rel / jnp.sum(rel, axis=-1, keepdims=True)
    if second:
        probs[...] = share + totals
    gate = jnp.sum(share * onehot[...], axis=-1, keepdims=True)
    if second:
        mid[:, width:] = jnp.broadcast_to(gate, (pack, EXTRA))
    else:
        send_up[:, :width] = m.astype(BF)
        high = gate.astype(BF).astype(F32)
        middle = (gate - high).astype(BF).astype(F32)
        parts = jnp.where(lane == 1, middle, jnp.where(lane == 2, gate - high - middle, 0.0))
        send_up[:, width:] = jnp.where(lane == 0, high, parts).astype(BF)
    for step in range(4):
        blocks[step][...] = dot32(hot[step * cap : (step + 1) * cap, :], low).astype(BF)
    if second:
        weighted = (gate * own_rows[...].astype(F32)).astype(BF)
        for step in range(4):
            grads[step][...] = dot32(hot[step * cap : (step + 1) * cap, :], weighted).astype(BF)


def attn_forward(facts, own_rows, weights, plan, came=None, after=()):
    attn_own, attn_other, params = weights
    slots, onehot = plan
    pack, width = own_rows.shape
    cols = attn_own.shape[1]
    cap = pack // 4
    second = came is not None
    ins = [facts, own_rows] + (list(came) if second else [])
    specs = [SM, VH] + ([VH] if second else []) + [VM] * (len(ins) - (3 if second else 2))
    specs += [HB] * 2 + [VH] * 3 + [AFTER] * len(after)
    ins += [attn_own, attn_other, params, slots, onehot, *after]
    if second:
        outs = [
            ((pack, width + EXTRA), F32, FAR),
            ((pack, width), BF, FAR),
            ((2, 3, pack, cols), BF, FAR),
            ((pack, width), BF, FAR),
            ((pack, width), BF, FAR),
            ((pack, EXTRA), F32, FAR),
        ]
    else:
        outs = [((pack, width + EXTRA), BF, FAR)]
    outs += [((cap, width), BF)] * 4
    if second:
        outs += [((pack, width), BF, FAR)] + [((cap, width), BF)] * 4
    return kernel_call(
        functools.partial(attn_kernel, second, len(after)),
        "attn_second" if second else "attn_first",
        outs,
        ins,
        specs,
        [pltpu.VMEM((2, 3 * width + 2 * cols, cols), BF), pltpu.SemaphoreType.DMA((8,))]
        + ([] if second else [
            pltpu.VMEM((2, 3, pack, cols), BF),
            pltpu.VMEM((pack, width), BF),
            pltpu.VMEM((pack, width), F32),
        ]),
        cost=8,
    )


def attn_back_kernel(first, dropped, facts, *refs):
    refs = list(refs)
    weights, sems = refs[-2:]
    refs = refs[:-2]
    grad_out = refs.pop(0)
    if first:
        up = refs.pop(0)
    else:
        own_rows = refs.pop(0)
        refs = refs[dropped:]
    grad_slots = [refs.pop(0) for _ in range(4)]
    stream, mid, proj, mlp_in, probs, mixed = (refs.pop(0) for _ in range(6))
    attn_own, attn_other, params, slots, onehot = (refs.pop(0) for _ in range(5))
    grad_stream = refs.pop(0)
    if first:
        blocks = [refs.pop(0) for _ in range(4)]
        grad_proj = refs.pop(0)
    else:
        grad_proj, grad_low, tiny = (refs.pop(0) for _ in range(3))
    pack, width = stream.shape
    cols = attn_own.shape[1]
    cap = pack // 4
    copies = weight_copies((attn_own, attn_other), weights, sems, width, cols)
    for part in (3, 0, 1, 2):
        for each in copies:
            each[part].start()
    gains = flipped(params)
    hot = slots[...]
    rows = grad_out[...]
    if not first:
        rows = jnp.where(facts[PIPE] == 0, rows, own_rows[...])
    g = rows.astype(F32)
    slot_rows = stacked(grad_slots)
    at_tokens = dot_tn(hot, slot_rows[:, width:])
    lane = lax.broadcasted_iota(jnp.int32, (pack, EXTRA), 1)
    shares = jnp.where(lane < 4, probs[...], 0.0)
    grad_logits = (at_tokens[:, 0:1] + at_tokens[:, 1:2]) * (onehot[...] - shares)
    m = mid[:, :width]
    wide = sum(pltpu.roll(grad_logits, 4 * at, 1) for at in (1, 2, 3))
    grad_mlp = dot_tn(hot, slot_rows[:, :width]) + sum(
        dot_nt(part, params[...]) for part in split3(wide)
    )
    grad_norm, gain_two = norm_back(m, norm_scale(m), gains[1:2, :], grad_mlp)
    grad_mid = g + grad_norm
    low = grad_mid.astype(BF)
    base = 3 * width
    copies[0][3].wait()
    copies[1][3].wait()
    grad_mixed = jnp.concatenate(
        [
            (
                dot_nt(low[:, :cols], weights[at, base : base + cols, :])
                + dot_nt(low[:, cols:], weights[at, base + cols : base + 2 * cols, :])
            ).astype(BF)
            for at in range(2)
        ],
        axis=1,
    )
    heads = lax.broadcasted_iota(jnp.int32, (EXTRA, width), 0)
    heads = heads == lax.broadcasted_iota(jnp.int32, (EXTRA, width), 1) // HEAD_DIM + 8
    inner = parts_nt(heads.astype(F32).astype(BF), grad_mixed.astype(F32) * mixed[...].astype(F32))
    levels = parts_nt(eye(EXTRA), probs[...])
    half = pack // 2
    blocks_of = (
        (0, pack, turned_mask(facts, 0, half, pack)),
        (half, half, turned_mask(facts, half, half, half)),
    )
    grad_in = jnp.zeros((pack, width), F32)
    for at in range(2):
        for pair in range(cols // EXTRA):
            lanes = slice(pair * EXTRA, (pair + 1) * EXTRA)
            spot = at * cols + pair * EXTRA
            scale = jnp.asarray(HEAD_DIM ** (-0.5), BF)
            query = proj[at, 0, :, lanes] * scale
            key, value = proj[at, 1, :, lanes], proj[at, 2, :, lanes]
            grad_pair = grad_mixed[:, spot : spot + EXTRA]
            grad_query = jnp.zeros((pack, EXTRA), F32)
            grad_key = [jnp.zeros((half, EXTRA), F32) for _ in range(2)]
            grad_value = [jnp.zeros((half, EXTRA), F32) for _ in range(2)]
            for side in range(2):
                keep = (lane >= HEAD_DIM) == (side == 1)
                query_one = jnp.where(keep, query, 0)
                key_one = jnp.where(keep, key, 0)
                grad_one = jnp.where(keep, grad_pair, 0)
                head = 8 + spot // HEAD_DIM + side
                for at_block, (begin, count, allowed) in enumerate(blocks_of):
                    rows_at = slice(begin, begin + half)
                    after = slice(begin, begin + count)
                    scores = dot_nt(key[rows_at, :], query_one[after, :])
                    share = jnp.exp(scores - levels[head : head + 1, after])
                    share = jnp.where(allowed, share, 0.0)
                    grad_share = dot_nt(value[rows_at, :], grad_one[after, :])
                    grad_scores = share * (grad_share - inner[head : head + 1, after])
                    grad_scores = grad_scores.astype(BF)
                    grad_key[at_block] += dot32(grad_scores, query_one[after, :])
                    grad_value[at_block] += dot32(share.astype(BF), grad_one[after, :])
                    more = dot_tn(grad_scores, key_one[rows_at, :])
                    if begin:
                        more = jnp.concatenate([jnp.zeros((half, EXTRA), F32), more], axis=0)
                    grad_query += more
            grad_proj[at, 0, :, lanes] = (grad_query * HEAD_DIM ** (-0.5)).astype(BF)
            for at_block in range(2):
                rows_at = slice(at_block * half, (at_block + 1) * half)
                grad_proj[at, 1, rows_at, lanes] = grad_key[at_block].astype(BF)
                grad_proj[at, 2, rows_at, lanes] = grad_value[at_block].astype(BF)
        for part in range(3):
            copies[at][part].wait()
            grad_in += dot_nt(
                grad_proj[at, part], weights[at, part * width : (part + 1) * width, :]
            )
    x = stream[...].astype(F32)
    grad_norm, gain_one = norm_back(x, norm_scale(x), gains[0:1, :], grad_in)
    result = (grad_mid + grad_norm).astype(BF)
    grad_stream[...] = result
    if first:
        weighted = (gate_of(up) * result.astype(F32)).astype(BF)
        for step in range(4):
            blocks[step][...] = dot32(hot[step * cap : (step + 1) * cap, :], weighted).astype(BF)
    else:
        grad_low[...] = low
        high = grad_logits.astype(BF)
        rest = (grad_logits - high.astype(F32)).astype(BF)
        lane = lax.broadcasted_iota(jnp.int32, (width, EXTRA), 1)
        both = dot_tn(mlp_in[...], high) + dot_tn(mlp_in[...], rest)
        both = jnp.where(lane < 4, both, 0.0)
        high = both.astype(BF).astype(F32)
        flat = [gain_one.astype(BF).astype(F32), gain_two.astype(BF).astype(F32)]
        flat += [gain_one - flat[0], gain_two - flat[1]]
        flat = jnp.concatenate(flat + [jnp.zeros((12, width), F32)], axis=0).astype(BF)
        spot = lax.broadcasted_iota(jnp.int32, (16, EXTRA), 0) + 8
        spot = spot == lax.broadcasted_iota(jnp.int32, (16, EXTRA), 1)
        turned = dot_tn(flat, spot.astype(F32).astype(BF))
        tiny[...] = (high + pltpu.roll(both - high, 4, 1) + turned).astype(BF)


def attn_backward(facts, grad_out, extra, grad_slots, saved, weights, plan, first):
    attn_own, attn_other, params = weights
    slots, onehot = plan
    stream, mid, proj, mlp_in, probs, mixed = saved
    pack, width = stream.shape
    cols = attn_own.shape[1]
    cap = pack // 4
    ins = [facts, grad_out, *extra, *grad_slots, stream, mid, proj, mlp_in, probs, mixed]
    specs = [SM, VH if first else VM, VH] + [AFTER] * (len(extra) - 1)
    specs += [VM] * 4 + [VH] * 6 + [HB] * 2 + [VH] * 3
    ins += [attn_own, attn_other, params, slots, onehot]
    outs = [((pack, width), BF)]
    if first:
        outs += [((cap, width), BF)] * 4
    outs += [((2, 3, pack, cols), BF)]
    if not first:
        outs += [((pack, width), BF), ((width, EXTRA), BF)]
    return kernel_call(
        functools.partial(attn_back_kernel, first, len(extra) - 1),
        "attn_back_first" if first else "attn_back_second",
        outs,
        ins,
        specs,
        [pltpu.VMEM((2, 3 * width + 2 * cols, cols), BF), pltpu.SemaphoreType.DMA((8,))],
        cost=13,
    )


def gelu_both(u):
    square = u * u
    t = jnp.tanh(0.7978845608028654 * u * (1.0 + 0.044715 * square))
    half = 0.5 * (1.0 + t)
    inner = 0.7978845608028654 * (1.0 + 3.0 * 0.044715 * square)
    return half + 0.5 * u * (1.0 - t * t) * inner, half * u


def bring(facts, pieces, places, scratch, sems):
    copies = []
    for piece, spots in zip(pieces, places, strict=True):
        for source, target, rows, column, columns in spots(facts):
            copies.append(
                pltpu.make_async_copy(
                    piece.at[pl.ds(source, rows), pl.ds(0, columns)],
                    scratch.at[pl.ds(target, rows), pl.ds(column, columns)],
                    sems.at[len(copies)],
                )
            )
    for copy in copies:
        copy.start()
    return copies


TILE = 256


def expert_kernel(keep, places_in, places_out, facts, *refs):
    refs = list(refs)
    blocks = [refs.pop(0) for _ in range(8)]
    pieces = [refs.pop(0) for _ in range(len(places_in))]
    if keep:
        targets = [refs.pop(0) for _ in range(3)]
        own, other, w_in, w_out, sems_in, sems_out, act, rows, pre, sems = refs
    else:
        own, other, w_in, w_out, sems_in, sems_out, act, rows = refs
    arriving = bring(facts, pieces, places_in, w_in, sems_in)
    later = bring(facts, pieces, places_out, w_out, sems_out)
    cap = blocks[0].shape[0]
    for at, block in enumerate(blocks):
        rows[at * cap : (at + 1) * cap, :] = block[...]
    ff = w_in.shape[1]
    width = w_in.shape[0]
    if keep:
        leaving = pltpu.make_async_copy(rows, targets[2], sems.at[2, 0])
        leaving.start()

    def tile_copies(tile):
        lanes = pl.ds(pl.multiple_of(tile * TILE, TILE), TILE)
        return [
            pltpu.make_async_copy(
                source.at[:, lanes], targets[at].at[:, lanes], sems.at[at, tile]
            )
            for at, source in enumerate((pre, act))
        ]

    for copy in arriving:
        copy.wait()

    @pl.loop(0, ff // TILE, unroll=1)
    def _(tile):
        lanes = pl.ds(pl.multiple_of(tile * TILE, TILE), TILE)
        value = dot32(rows[...], w_in[:, lanes])
        slope, result = gelu_both(value)
        act[:, lanes] = result.astype(BF)
        if keep:
            pre[:, lanes] = slope.astype(BF)
            for copy in tile_copies(tile):
                copy.start()

    for copy in later:
        copy.wait()
    count = 4 * cap

    @pl.loop(0, width // TILE, unroll=1)
    def _(tile):
        lanes = pl.ds(pl.multiple_of(tile * TILE, TILE), TILE)
        value = dot32(act[...], w_out[:, lanes])
        own[:, lanes] = value[:count]
        other[:, lanes] = value[count:].astype(BF)

    if keep:
        leaving.wait()

        @pl.loop(0, ff // TILE, unroll=1)
        def _(tile):
            for copy in tile_copies(tile):
                copy.wait()


def halves(value, shape):
    high = value.astype(BF).astype(F32)
    lane = lax.broadcasted_iota(jnp.int32, shape, 1)
    return jnp.where(lane == 0, high, jnp.where(lane == 1, value - high, 0.0))


def expert_back_kernel(chosen, places_in, places_out, facts, *refs):
    refs = list(refs)
    blocks = [refs.pop(0) for _ in range(1 if chosen else 2)]
    pre, own_out, other_out = (refs.pop(0) for _ in range(3))
    pieces = [refs.pop(0) for _ in range(len(places_in))]
    grad_pre, own, other = (refs.pop(0) for _ in range(3))
    rows = blocks[0] if chosen else refs.pop(0)
    w_in, w_out, sems_in, sems_out = refs
    arriving = bring(facts, pieces, places_out, w_out, sems_out)
    later = bring(facts, pieces, places_in, w_in, sems_in)
    if not chosen:
        half = rows.shape[0] // 2
        for at, block in enumerate(blocks):
            rows[at * half : (at + 1) * half, :] = block[...]
    for copy in arriving:
        copy.wait()
    ff = w_in.shape[1]
    width = w_in.shape[0]
    count = rows.shape[0] // 2

    @pl.loop(0, ff // TILE, unroll=True)
    def _(tile):
        lanes = pl.ds(pl.multiple_of(tile * TILE, TILE), TILE)
        value = dot_nt(rows[...], w_out[lanes, :])
        grad_pre[:, lanes] = (value * pre[:, lanes].astype(F32)).astype(BF)

    for copy in later:
        copy.wait()

    @pl.loop(0, width // TILE, unroll=True)
    def _(tile):
        lanes = pl.ds(pl.multiple_of(tile * TILE, TILE), TILE)
        value = dot_nt(grad_pre[...], w_in[lanes, :])
        own[:, lanes] = value[:count]
        other[:, lanes] = value[count:].astype(BF)

    pull = jnp.sum(rows[:count, :].astype(F32) * own_out[...], axis=-1, keepdims=True)
    own[:, width:] = halves(pull, (count, EXTRA))
    pull = jnp.sum(
        rows[count:, :].astype(F32) * other_out[...].astype(F32), axis=-1, keepdims=True
    )
    other[:, width:] = halves(pull, (count, EXTRA)).astype(BF)


def expert_scratch(width, ff, places):
    numbers = jnp.zeros((8,), jnp.int32)
    sizes = [sum(len(spots(numbers)) for spots in each) for each in places]
    return (
        [pltpu.VMEM((width, ff), BF), pltpu.VMEM((ff, width), BF)],
        [pltpu.SemaphoreType.DMA((size,)) for size in sizes],
    )


def expert_call(name, keep, facts, blocks, pieces, places, width, ff):
    count = 4 * blocks[0].shape[0]
    ins = [facts, *blocks, *pieces]
    kept = [((2 * count, ff), BF, RAW)] * 2 + [((2 * count, width), BF, RAW)] if keep else []
    buffers, sems = expert_scratch(width, ff, places)
    scratch = [*buffers, *sems]
    scratch += [pltpu.VMEM((2 * count, ff), BF), pltpu.VMEM((2 * count, width), BF)]
    if keep:
        scratch.append(pltpu.VMEM((2 * count, ff), BF))
        scratch.append(pltpu.SemaphoreType.DMA((3, ff // TILE)))
    return kernel_call(
        functools.partial(expert_kernel, keep, *places),
        name,
        kept + [((count, width), F32), ((count, width), BF)],
        ins,
        [SM] + [VM] * 8 + [HB] * len(pieces),
        scratch,
        cost=7,
    )


def expert_back_call(name, facts, blocks, saved, pieces, places, width, ff):
    chosen = len(blocks) == 1
    count = blocks[0].shape[0] * len(blocks) // 2
    wide = width + EXTRA
    ins = [facts, *blocks, *saved, *pieces]
    buffers, sems = expert_scratch(width, ff, places)
    outs = [((2 * count, ff), BF), ((count, wide), F32), ((count, wide), BF)]
    if not chosen:
        outs.append(((2 * count, width), BF, FAR))
    return kernel_call(
        functools.partial(expert_back_kernel, chosen, *places),
        name,
        outs,
        ins,
        [SM] + ([VH] if chosen else [VM] * 2) + [VH, VM, VM] + [HB] * len(pieces),
        [*buffers, *sems],
        cost=8,
    )


def fold_kernel(own, other, *blocks):
    blocks = blocks[-4:]
    cap = blocks[0].shape[0]
    width = own.shape[1] // TILE * TILE
    for step, block in enumerate(blocks):
        rows = slice(step * cap, (step + 1) * cap)
        block[:, :width] = (own[rows, :width] + other[rows, :width].astype(F32)).astype(BF)
        if own.shape[1] > width:
            both = own[rows, width:] + other[rows, width:].astype(F32)
            block[:, width:] = halves(both[:, 0:1] + both[:, 1:2], (cap, EXTRA)).astype(BF)


def fold(own, other, name, after=()):
    count, width = own.shape
    cap = count // 4
    return kernel_call(
        fold_kernel, name, [((cap, width), BF)] * 4, [own, other, *after], [VM, VM] + [AFTER] * len(after)
    )


def return_kernel(merge, *refs):
    refs = list(refs)
    rows = refs.pop(0)
    if merge:
        hot = refs.pop(0)
        slots_in = [refs.pop(0) for _ in range(4)]
        width = slots_in[0].shape[1]
        values = rows[:, :width] + rows[:, width : width + 1] * dot_tn(hot[...], stacked(slots_in))
        values = values.astype(BF)
    else:
        values = rows[...]
    place, facts = refs[:2]
    own, other = refs[-2:]
    pack = own.shape[0]
    core = facts[CORE]
    own[...] = dot32(place[pl.ds(pl.multiple_of(core * pack, pack), pack), :], values).astype(BF)
    other[...] = dot32(
        place[pl.ds(pl.multiple_of((1 - core) * pack, pack), pack), :], values
    ).astype(BF)


def sent_rows(facts, merge, rows, extra, place, width, after):
    pack = place.shape[1]
    ins = [rows, *extra, place, facts, *after]
    outs = [((pack, width), BF)] * 2
    return kernel_call(
        functools.partial(return_kernel, merge),
        "return_merged" if merge else "return_rows",
        outs,
        ins,
        ([VH, VH] + [VM] * 4 if merge else [VM]) + [VH, SM] + [AFTER] * len(after),
        cost=1,
    )


def run_copies(moves, sems):
    copies = [
        pltpu.make_async_copy(source, target, sems.at[at])
        for at, (source, target) in enumerate(moves)
    ]
    for copy in copies:
        copy.start()
    for copy in copies:
        copy.wait()


def rows_kernel(*refs):
    cap = refs[0].shape[0]
    out = refs[-1]
    for at, ref in enumerate(refs[:4]):
        out[at * cap : (at + 1) * cap, :] = ref[...]


def joined_rows(blocks, after):
    cap, width = blocks[0].shape
    return kernel_call(
        rows_kernel,
        "join_rows",
        [((4 * cap, width), BF)],
        [*blocks, *after],
        [VM] * 4 + [AFTER] * len(after),
    )[0]


def ordered_kernel(*refs):
    del refs


def ordered(value, after):
    return pl.pallas_call(
        ordered_kernel,
        name="ordered",
        out_shape=pltpu.HBM(value.shape, value.dtype),
        in_specs=[HB] + [AFTER] * len(after),
        out_specs=HB,
        input_output_aliases={0: 0},
        compiler_params=pltpu.CompilerParams(vmem_limit_bytes=1 << 20),
        cost_estimate=pl.CostEstimate(flops=0, bytes_accessed=0, transcendentals=0),
    )(pinned(value), *after)


def restore_kernel(hot, back, activations, grads, tiny):
    width = activations.shape[1]
    activations[...] = dot_tn(hot[...], back[:, :width]).astype(BF)
    grads[...] = dot_tn(hot[...], back[:, width : 2 * width]).astype(BF)
    rows = tiny.shape[0]
    total = jnp.zeros(tiny.shape, F32)
    for at in range(back.shape[0] // rows):
        total += back[at * rows : (at + 1) * rows, 2 * width :].astype(F32)
    tiny[...] = total


def finish_kernel(*refs):
    pieces, attn, attn_out = refs[:4], refs[4], refs[5]
    _, shard, cols = attn.shape
    total = sum(piece[...].astype(F32) for piece in pieces)
    for part in range(3):
        attn[part] = total[part * shard : (part + 1) * shard, :]
    rows = attn_out.shape[0]
    for side in range(2):
        spot = 3 * shard + side * rows
        attn_out[:, side * cols : (side + 1) * cols] = total[spot : spot + rows, :]


def stack_kernel(count, facts, *refs):
    pieces, out, sems = refs[:count], refs[-2], refs[-1]
    run_copies(
        [
            (piece, out.at[jnp.bitwise_xor(facts[MINE], step)])
            for step, piece in enumerate(pieces)
        ],
        sems,
    )


def stack_pieces(facts, pieces, after):
    count = len(pieces)
    return kernel_call(
        functools.partial(stack_kernel, count),
        "stack_pieces",
        [((count, *pieces[0].shape), BF)],
        [facts, *pieces, *after],
        [SM] + [HB] * count + [AFTER] * len(after),
        [pltpu.SemaphoreType.DMA((count,))],
        room=12,
        hbm_outs=True,
    )[0]


def gather_kernel(facts, near, far, *refs):
    out, sems = refs[-2:]
    groups = near.shape[0]
    moves = []
    for rep, source in ((facts[REP], near), (1 - facts[REP], far)):
        for part in range(3):
            moves.append(
                (
                    source.at[:, pl.ds(2 * part, 2)],
                    out.at[pl.ds(part * groups, groups), pl.ds(2 * rep, 2)],
                )
            )
        for side in range(2):
            for group in range(groups):
                moves.append(
                    (
                        source.at[group, 6 + side],
                        out.at[3 * groups + 2 * side + group // 2, group % 2 * 2 + rep],
                    )
                )
    run_copies(moves, sems)


def pack_attn_kernel(attn, attn_out, bundle, sems):
    parts, shard, cols = attn.shape
    rows = attn_out.shape[0]
    moves = [(attn.at[part], bundle.at[pl.ds(part * shard, shard)]) for part in range(parts)]
    for side in range(2):
        moves.append(
            (
                attn_out.at[:, pl.ds(side * cols, cols)],
                bundle.at[pl.ds(parts * shard + side * rows, rows)],
            )
        )
    run_copies(moves, sems)


def pack_attn(attn, attn_out):
    parts, shard, cols = attn.shape
    rows = attn_out.shape[0]
    return kernel_call(
        pack_attn_kernel,
        "pack_attn",
        [((parts * shard + 2 * rows, cols), BF)],
        [attn, attn_out],
        [HB] * 2,
        [pltpu.SemaphoreType.DMA((parts + 2,))],
        room=12,
        hbm_outs=True,
    )[0]


def pack_expert_kernel(steps, facts, w_in, w_out, *refs):
    blocks, sems = refs[-1 - len(steps) : -1], refs[-1]
    in_rows, out_rows, width = w_in.shape[1], w_out.shape[1], w_out.shape[2]
    moves = []
    for step, block in zip(steps, blocks, strict=True):
        at = jnp.bitwise_xor(facts[MINE], step)
        for side in range(2):
            moves.append(
                (
                    w_in.at[at, :, pl.ds(side * width, width)],
                    block.at[pl.ds(side * in_rows, in_rows)],
                )
            )
        moves.append((w_out.at[at], block.at[pl.ds(2 * in_rows, out_rows)]))
    run_copies(moves, sems)


def pack_expert(facts, w_in, w_out, steps, after=()):
    block = (2 * w_in.shape[1] + w_out.shape[1], w_out.shape[2])
    return kernel_call(
        functools.partial(pack_expert_kernel, steps),
        "pack_expert",
        [(block, BF)] * len(steps),
        [facts, w_in, w_out, *after],
        [SM, HB, HB] + [AFTER] * len(after),
        [pltpu.SemaphoreType.DMA((3 * len(steps),))],
        room=12,
        hbm_outs=True,
    )


SPLIT_ORDER = (2, 3, 1, 0)


def expert_out_grad_kernel(split, dropped, facts, *refs):
    blocks, refs = refs[:8], refs[8:]
    kept, act = refs[:2]
    refs = refs[2 + dropped :]
    rows, refs = refs[0], refs[1:]
    cap = blocks[0].shape[0]
    for at, block in enumerate(blocks):
        spot = slice(at * cap, (at + 1) * cap)
        rows[spot, :] = jnp.where(facts[PIPE] == 0, block[...], kept[spot, :])
    ff = act.shape[1]
    grad = refs[-1]

    @pl.loop(0, ff // TILE, unroll=True)
    def _(tile):
        lanes = pl.ds(pl.multiple_of(tile * TILE, TILE), TILE)
        grad[lanes, :] = dot_tn(act[:, lanes], rows[...])

    if split:
        count = ff // 8
        for at, step in enumerate(SPLIT_ORDER):
            owner = jnp.bitwise_xor(facts[MINE], step) * 2
            to = slice(at * count, (at + 1) * count)
            for rep, target in ((1 - facts[REP], refs[0]), (facts[REP], refs[1])):
                spot = pl.ds(pl.multiple_of((owner + rep) * count, count), count)
                target[to, :] = grad[spot, :].astype(BF)


def expert_in_grad_kernel(split, dropped, facts, rows, grad_pre, *refs):
    refs = refs[dropped:]
    ff = grad_pre.shape[1]
    width = rows.shape[1]
    grad = refs[-1]

    @pl.loop(0, ff // TILE, unroll=True)
    def _(tile):
        lanes = pl.ds(pl.multiple_of(tile * TILE, TILE), TILE)
        grad[:, lanes] = dot_tn(rows[...], grad_pre[:, lanes])

    if split:
        count = width // 8
        for at, step in enumerate(SPLIT_ORDER):
            owner = jnp.bitwise_xor(facts[MINE], step) * 2
            first = at * 2 * count
            for rep, target in ((1 - facts[REP], refs[0]), (facts[REP], refs[1])):
                spot = pl.ds(pl.multiple_of((owner + rep) * count, count), count)
                target[first : first + count, :] = grad[spot, :width].astype(BF)
                target[first + count : first + 2 * count, :] = grad[spot, width:].astype(BF)


def grad_outs(shape, wire, split):
    if split:
        return [(wire, BF, FAR)] * 2, [pltpu.VMEM(shape, F32)]
    return [(shape, F32)], []


def expert_out_grads(facts, blocks, kept, act, after, split):
    count, width = kept.shape
    ff = act.shape[1]
    outs, scratch = grad_outs((ff, width), (ff // 2, width), split)
    return kernel_call(
        functools.partial(expert_out_grad_kernel, split, len(after)),
        "expert_out_grads",
        [((count, width), BF, FAR), *outs],
        [facts, *blocks, kept, act, *after],
        [SM] + [VM] * 8 + [VH, VH] + [AFTER] * len(after),
        scratch,
        cost=4,
    )


def expert_in_grads(facts, rows, grad_pre, after, split):
    width = rows.shape[1]
    ff = grad_pre.shape[1]
    outs, scratch = grad_outs((width, ff), (ff // 2, width), split)
    return kernel_call(
        functools.partial(expert_in_grad_kernel, split, len(after)),
        "expert_in_grads",
        outs,
        [facts, rows, grad_pre, *after],
        [SM, VH, VM] + [AFTER] * len(after),
        scratch,
        cost=4,
    )


def owner_kernel(facts, *refs):
    grad_in, grad_out = refs[-2:]
    rows = grad_in.shape[1]
    width = grad_out.shape[2]
    for place, step in enumerate(SPLIT_ORDER):
        at = jnp.bitwise_xor(facts[MINE], step)
        grad_out[at] = refs[place][...].astype(F32)
        piece = refs[4 + place]
        for side in range(2):
            spot = slice(side * rows, (side + 1) * rows)
            grad_in[at, :, side * width : (side + 1) * width] = piece[spot, :].astype(F32)


def owner_grads(facts, pieces, after, in_shape, out_shape):
    return kernel_call(
        owner_kernel,
        "owner_grads",
        [(in_shape, F32), (out_shape, F32)],
        [facts, *pieces, *after],
        [SM] + [VM] * len(pieces) + [AFTER] * len(after),
        cost=4,
    )


def attn_grad_kernel(attn_in, grad_proj, mixed, low, *refs):
    own, other = refs[-2:]
    width = attn_in.shape[1]
    cols = own.shape[1]
    for at, target in ((0, own), (1, other)):
        for part in range(3):
            target[part * width : (part + 1) * width, :] = dot_tn(
                attn_in[...], grad_proj[at, part]
            ).astype(BF)
        for side in range(2):
            spot = 3 * width + side * cols
            target[spot : spot + cols, :] = dot_tn(
                mixed[:, at * cols : (at + 1) * cols], low[:, side * cols : (side + 1) * cols]
            ).astype(BF)


def attn_grads(attn_in, grad_proj, mixed, low, after):
    pack, width = attn_in.shape
    cols = grad_proj.shape[3]
    return kernel_call(
        attn_grad_kernel,
        "attn_grads",
        [((3 * width + 2 * cols, cols), BF)] * 2,
        [attn_in, grad_proj, mixed, low, *after],
        [VH, VM, VH, VM] + [AFTER] * len(after),
        cost=3,
    )


def attn_split_kernel(facts, own, came, *refs):
    sends, keeps = refs[-4:-2], refs[-2:]
    cols = own.shape[1]
    width = 2 * cols
    shard = width // 8
    count = 4 * shard
    for at, step in enumerate(SPLIT_ORDER):
        owner = jnp.bitwise_xor(facts[MINE], step) * 2
        for rep, target, first in (
            (1 - facts[REP], sends[at // 2], at % 2 * count),
            (facts[REP], keeps[at // 2], at % 2 * count),
        ):
            for source, rows, spot in attn_rows(width, shard):
                where = pl.ds(pl.multiple_of(source + (owner + rep) * rows, rows), rows)
                target[first + spot : first + spot + rows, :] = (
                    own[where, :].astype(F32) + came[where, :].astype(F32)
                ).astype(BF)


def sum_kernel(steps, keep, came, *outs):
    outs = outs[-len(steps) :]
    count = outs[0].shape[0]
    for at, out in enumerate(outs):
        rows = slice(at * count, (at + 1) * count)
        both = keep[rows, :].astype(F32) + came[rows, :].astype(F32)
        out[...] = both.astype(out.dtype)


def sum_pieces(steps, keep, came, after=()):
    count = keep.shape[0] // len(steps)
    kinds = [F32 if step == 0 else BF for step in steps]
    return kernel_call(
        functools.partial(sum_kernel, steps),
        "sum_pieces",
        [((count, keep.shape[1]), kind) for kind in kinds],
        [keep, came, *after],
        [VH] * 2 + [AFTER] * len(after),
        cost=0,
    )


def attn_rows(width, shard):
    out = shard // 2
    return (
        (0, shard, 0),
        (width, shard, shard),
        (2 * width, shard, 2 * shard),
        (3 * width, out, 3 * shard),
        (3 * width + width // 2, out, 3 * shard + out),
    )


def attn_split(facts, own, came, after):
    rows, cols = own.shape
    return kernel_call(
        attn_split_kernel,
        "attn_split",
        [((rows // 4, cols), BF, FAR)] * 4,
        [facts, own, came, *after],
        [SM, VM, VM] + [AFTER] * len(after),
        cost=3,
    )


def solution(mesh):
    shape = mesh.shape
    n_pipe, n_dp, n_t = shape["pipe"], shape["dp"], shape["tensor"]
    axes = ("pipe", "dp", "tensor")
    plane = ("dp", "tensor")
    n_dev = n_dp * n_t

    def local(
        inputs,
        cotangent,
        dealing,
        routes,
        slot_order,
        doc_lengths,
        attn_weight,
        attn_out_weight,
        expert_in_weight,
        expert_out_weight,
        norm_gains,
        router_weight,
    ):
        dev_rows, width = inputs.shape
        experts = expert_in_weight.shape[1]
        reps = n_dp // experts
        paired = reps == 2
        pack = dev_rows
        cap = pack // experts
        per = dev_rows // n_dev
        shard, cols = attn_weight.shape[1], attn_weight.shape[3]
        ff = expert_in_weight.shape[3]
        in_rows, out_rows = expert_in_weight.shape[2], expert_out_weight.shape[2]
        pipe = lax.axis_index("pipe")
        dp = lax.axis_index("dp")
        core = lax.axis_index("tensor")
        mine = dp // reps
        rep = dp % reps
        lengths = lax.dynamic_index_in_dim(doc_lengths, core, 0, keepdims=False)
        zero = jnp.int32(0)
        facts = jnp.stack([pipe, mine, rep, core, lengths[0], zero, zero, zero]).astype(jnp.int32)

        def moved(value, rule):
            pairs = []
            for a in range(n_pipe):
                for b in range(experts):
                    for c in range(reps):
                        for d in range(n_t):
                            to = rule(a, b, c, d)
                            if to is not None:
                                flat = [
                                    ((w * experts + x) * reps + y) * n_t + z
                                    for w, x, y, z in ((a, b, c, d), to)
                                ]
                                pairs.append(tuple(flat))
            return lax.ppermute(value, axes, pairs)

        def swap_core(value):
            return moved(value, lambda a, b, c, d: (a, b, c, 1 - d))

        def swap_rep(value):
            return moved(value, lambda a, b, c, d: (a, b, 1 - c, d))

        def across(step):
            return lambda a, b, c, d: (a, b ^ step, c, d)

        def up(step):
            return lambda a, b, c, d: (1, b ^ step, c, d) if a == 0 else None

        def down(step):
            return lambda a, b, c, d: (0, b ^ step, c, d) if a == 1 else None

        order = (2, 3, 1)

        def exchange(blocks):
            out = {0: blocks[0]}
            for step in order:
                out[step] = moved(blocks[step], across(step))
            return [out[step] for step in range(experts)]

        def crossed(blocks, way):
            out = {}
            for step in (*order, 0):
                out[step] = moved(blocks[step], way(step))
            return [out[step] for step in range(experts)]

        def with_other(blocks):
            out = {}
            for step in (0, 1, 2, 3):
                out[step] = swap_core(blocks[step])
            return list(blocks) + [out[step] for step in range(experts)]

        def pick(blocks, step):
            return lax.dynamic_index_in_dim(blocks, mine ^ step, 0, keepdims=False)

        rep_groups = [[b * reps + c for c in range(reps)] for b in range(experts)]

        payload, send_hot = kernel_call(
            functools.partial(send_kernel, per),
            "send",
            [((dev_rows, width + EXTRA), BF), ((dev_rows, dev_rows), BF)],
            [
                facts,
                inputs,
                cotangent,
                dealing.reshape(1, dev_rows),
                routes.reshape(1, dev_rows),
                slot_order.reshape(1, dev_rows),
                router_weight[0].T,
                norm_gains[0],
            ],
            [SM] + [VM] * 7,
            cost=2,
        )
        dealt = lax.all_to_all(payload, plane, split_axis=0, concat_axis=0, tiled=True)
        params = dealt[:, width:].reshape(n_dev, per, 4, 32)[:, :, :3]
        params = jnp.swapaxes(params, 1, 2).reshape(width, 32)
        params = jnp.pad(params, ((0, 0), (0, EXTRA - 32)))
        both = lax.all_gather(dealt, "tensor", axis=0, tiled=True)
        own_rows, slots, onehot, place = kernel_call(
            deal_kernel,
            "deal",
            [
                ((pack, width), BF, FAR),
                ((pack, pack), BF, FAR),
                ((pack, EXTRA), F32, FAR),
                ((2 * pack, pack), BF, FAR),
            ],
            [facts, both],
            [SM, VM],
            cost=1.5,
        )
        plan = (slots, onehot)

        out_shard = attn_out_weight[0]
        attn_shape = (4 * width, cols)

        def expert_places(way, step):
            def owner_of(numbers):
                owner = jnp.bitwise_xor(numbers[MINE], step) * 2
                return owner + (numbers[REP] if way == 0 else 1 - numbers[REP])

            def spots_in(numbers):
                at = pl.multiple_of(owner_of(numbers) * in_rows, in_rows)
                return [(0, at, in_rows, 0, width), (in_rows, at, in_rows, width, width)]

            def spots_out(numbers):
                at = pl.multiple_of(owner_of(numbers) * out_rows, out_rows)
                return [(2 * in_rows, at, out_rows, 0, width)]

            return spots_in, spots_out

        if paired:
            w_in_raw, w_out_raw = expert_in_weight[0], expert_out_weight[0]
            attn_bundle = pack_attn(jnp.swapaxes(attn_weight[0], 0, 1), out_shard)
            near, far = {}, {}
            near[0], first, bundle = pack_expert(
                facts, w_in_raw, w_out_raw, (0, 1, 2), (attn_bundle,)
            )
            far[0] = swap_rep(near[0])
            attn_near = exchange([attn_bundle] * experts)
            attn_near = stack_pieces(
                facts, [each.reshape(8, shard // 2, cols) for each in attn_near],
                [payload, far[0]],
            )
            near[1] = moved(first, across(1))
            attn_far = swap_rep(attn_near)
            near[2] = moved(bundle, across(2))
            (bundle,) = pack_expert(facts, w_in_raw, w_out_raw, (3,), (near[2],))
            attn_own = kernel_call(
                gather_kernel,
                "gather_attn",
                [((4 * experts, 4, shard // 2, cols), BF)],
                [facts, attn_near, attn_far, bundle, dealt, near[1]],
                [SM, HB, HB, AFTER, AFTER, AFTER],
                [pltpu.SemaphoreType.DMA((22,))],
                room=12,
                hbm_outs=True,
            )[0].reshape(attn_shape)
            near[3] = moved(bundle, across(3))
            for step in (1, 2):
                far[step] = swap_rep(near[step])
            ready = ()
            both_places = [
                expert_places(way, step) for way in range(2) for step in range(experts)
            ]
            places = ([each[0] for each in both_places], [each[1] for each in both_places])
        else:
            attn_bundle = jnp.concatenate(
                [attn_weight[0, :, part] for part in range(3)]
                + [out_shard[:, :cols], out_shard[:, cols:]],
                axis=0,
            )
            every = lax.all_gather(attn_bundle, "dp", axis=0)
            attn_own = jnp.concatenate(
                [
                    every[:, spot : spot + rows].reshape(-1, cols)
                    for _, rows, spot in attn_rows(width, shard)
                ],
                axis=0,
            )

            def assembled(blocks):
                got = exchange([pick(blocks, step) for step in range(experts)])
                got = jnp.stack(got)
                got = jnp.stack([pick(got, owner) for owner in range(experts)])
                got = lax.all_gather(got, "dp", axis_index_groups=rep_groups)
                return jnp.swapaxes(got, 0, 1)

            ready = ()
            pieces = [
                assembled(expert_in_weight[0]).reshape(width, ff),
                assembled(expert_out_weight[0]).reshape(ff, width),
            ]
            places = (
                [lambda numbers: [(0, 0, width, 0, ff)], lambda numbers: []],
                [lambda numbers: [], lambda numbers: [(0, 0, ff, 0, width)]],
            )
        attn_other = swap_core(attn_own)
        weights = (attn_own, attn_other, params)

        def expert_forward(blocks, name, keep, after=()):
            *kept, own, other = expert_call(name, keep, facts, blocks, pieces, places, width, ff)
            folded = fold(own, swap_core(other), "fold_" + name, after)
            return kept, own, other, folded

        def expert_backward(blocks, saved, name, after=()):
            grad_pre, own, other, *rows = expert_back_call(
                name, facts, blocks, saved, pieces, places, width, ff
            )
            return grad_pre, rows, fold(own, swap_core(other), "fold_" + name, after)

        def sent_back(merge, rows, extra, after):
            own, other = sent_rows(facts, merge, rows, extra, place, width, after)
            return own, other

        out = attn_forward(facts, own_rows, weights, plan, None, ready)
        if paired:
            near[3] = ordered(near[3], (out[1],))
            far[3] = swap_rep(near[3])
            pieces = [each[step] for each in (near, far) for step in range(experts)]
        mid_up = moved(out[0], lambda a, b, c, d: (1, b, c, d) if a == 0 else None)
        blocks = with_other(exchange(out[1:5]))
        _, _, _, expert_slots = expert_forward(
            blocks, "expert_first", False, (mid_up,)
        )
        from_first = crossed(expert_slots, up)

        out = attn_forward(facts, own_rows, weights, plan, (mid_up, *from_first))
        mid, attn_in, proj, mixed, mlp_in, probs = out[:6]
        stream = out[10]
        blocks = with_other(exchange(out[6:10]))
        kept_blocks = exchange(out[11:15])
        (slope, act, rows), own_out, other_out, expert_slots = expert_forward(blocks, "expert_second", True)
        expert_saved = (slope, own_out, other_out)

        saved = (stream, mid, proj, mlp_in, probs, mixed)
        kept_own = joined_rows(kept_blocks, (other_out,))
        _, (kept_rows,), grad_slots = expert_backward(
            [kept_own, swap_core(kept_own)], expert_saved, "expert_back_first"
        )
        back = attn_backward(
            facts, own_rows, [mid_up], exchange(grad_slots), saved, weights, plan, True
        )
        expert_slots = exchange(expert_slots)
        if paired:
            back = list(back)
            back[1 + order[0]] = ordered(back[1 + order[0]], expert_slots[1:])
        grad_down = moved(back[0], lambda a, b, c, d: (0, b, c, d) if a == 1 else None)
        out_back = sent_back(True, mid, (slots, *expert_slots), (back[1],))

        grads = with_other(crossed(back[1:5], down))
        grad_rows, *out_wire = expert_out_grads(
            facts, grads, kept_rows, act, (out_back[0],), paired
        )
        grad_pre, _, grad_slots = expert_backward(
            [grad_rows], expert_saved, "expert_back_second"
        )
        in_wire = expert_in_grads(facts, rows, grad_pre, [grad_slots[2]], paired)
        after = []
        if paired:
            out_sums = sum_pieces(
                SPLIT_ORDER, out_wire[1], swap_rep(out_wire[0]), [in_wire[1]]
            )
            after = [out_sums[0]]
        layer_grad, grad_proj, low, tiny = attn_backward(
            facts,
            grad_down,
            [own_rows, *after],
            exchange(grad_slots),
            saved,
            weights,
            plan,
            False,
        )

        if paired:
            out_near = [
                moved(each, across(step)) if step else each
                for step, each in zip(SPLIT_ORDER, out_sums, strict=True)
            ]
            came_in = swap_rep(in_wire[0])
            marker = [came_in, *out_near[:2]]
        else:

            def rep_scatter(each):
                return lax.psum_scatter(
                    each, "dp", axis_index_groups=rep_groups, scatter_dimension=0
                )

            def to_owner(grad, rows_each):
                each = grad.reshape(experts, reps, rows_each, -1).astype(BF)
                summed = rep_scatter(jnp.swapaxes(each, 0, 1))
                got = exchange([pick(summed, step) for step in range(experts)])
                got = jnp.stack(got)
                return jnp.stack([pick(got, owner) for owner in range(experts)]).astype(F32)

            marker = []
            (grad_w_in,), (grad_w_out,) = in_wire, out_wire
            grad_expert_in = to_owner(grad_w_in, in_rows)
            grad_expert_out = to_owner(grad_w_out, out_rows)

        grad_own, grad_other = attn_grads(attn_in, grad_proj, mixed, low, marker)
        came = swap_core(grad_other)
        if paired:
            in_sums = sum_pieces(SPLIT_ORDER, in_wire[1], came_in, [grad_own])
            in_near = [
                moved(each, across(step)) if step else each
                for step, each in zip(SPLIT_ORDER, in_sums, strict=True)
            ]
            out = attn_split(facts, grad_own, came, (in_sums[0],))
            after = (out[2],)
        else:
            after = ()
        grad_back = sent_back(False, layer_grad, (), after)
        tiny = jnp.swapaxes(tiny[:, :32].reshape(n_dev, 3, per, 32), 1, 2)
        tiny = jnp.pad(tiny.reshape(dev_rows, 96), ((0, 0), (0, EXTRA - 96)))
        theirs = swap_core(jnp.concatenate([out_back[1], grad_back[1]], axis=1))
        both = jnp.concatenate([out_back[0], grad_back[0]], axis=1) + theirs
        payload = jnp.concatenate([both, tiny], axis=1)
        if paired:
            total = {}
            first = sum_pieces(SPLIT_ORDER[:2], out[2], swap_rep(out[0]), [payload])
            last = swap_rep(ordered(out[1], (first[0],)))
            last = sum_pieces(SPLIT_ORDER[2:], out[3], last, [first[1]])
            for step, each in zip(SPLIT_ORDER, [*first, *last], strict=True):
                total[step] = moved(each, across(step)) if step else each
            grad_expert_in, grad_expert_out = owner_grads(
                facts,
                [*out_near, *in_near],
                (total[0],),
                expert_in_weight.shape[1:],
                expert_out_weight.shape[1:],
            )
            grad_attn, grad_attn_out = kernel_call(
                finish_kernel,
                "finish_attn",
                [((3, shard, cols), F32), ((shard // 2, width), F32)],
                [total[step] for step in range(experts)],
                [VM] * 4,
            )
        else:
            full = grad_own.astype(F32) + came.astype(F32)
            pieces_of = [
                full[source : source + rows * n_dp].reshape(n_dp, rows, cols)
                for source, rows, _ in attn_rows(width, shard)
            ]
            full = jnp.concatenate(pieces_of, axis=1).astype(BF)
            full = full.reshape((experts, reps) + full.shape[1:])
            full = rep_scatter(jnp.swapaxes(full, 0, 1))
            got = exchange([pick(full, step) for step in range(experts)])
            total = sum(each.astype(F32) for each in got)
            grad_attn = total[: 3 * shard].reshape(3, shard, cols)
            rows = shard // 2
            grad_attn_out = jnp.concatenate(
                [total[3 * shard : 3 * shard + rows], total[3 * shard + rows :]], axis=1
            )
        both = lax.all_to_all(payload, plane, split_axis=0, concat_axis=0, tiled=True)
        activations, input_grads, tiny = kernel_call(
            restore_kernel,
            "restore",
            [((dev_rows, width), BF), ((dev_rows, width), BF), ((per, EXTRA), F32)],
            [send_hot, both],
            [VM] * 2,
            cost=2,
        )
        tiny = tiny.reshape(per, 4, 32)[:, :3]
        tiny = jnp.swapaxes(tiny, 0, 1).reshape(3 * per, 32)
        grad_router = (tiny[:, :experts] + tiny[:, experts : 2 * experts])[None]
        grad_gains = (tiny[:, 8:10] + tiny[:, 10:12]).T[None]

        return (
            activations[None],
            input_grads[None],
            jnp.swapaxes(grad_attn, 0, 1)[None],
            grad_attn_out[None],
            grad_expert_in[None],
            grad_expert_out[None],
            grad_gains,
            grad_router,
        )

    in_specs = (
        P(("dp", "tensor"), None),
        P(("dp", "tensor"), None),
        P(("dp", "tensor")),
        P(("dp", "tensor"), None),
        P(("dp", "tensor")),
        P("dp", None),
        P("pipe", "dp", None, "tensor"),
        P("pipe", ("tensor", "dp"), None),
        P("pipe", None, "dp", "tensor"),
        P("pipe", None, ("tensor", "dp"), None),
        P("pipe", None, ("dp", "tensor")),
        P("pipe", ("dp", "tensor"), None),
    )
    out_specs = (
        P("pipe", ("dp", "tensor"), None),
        P("pipe", ("dp", "tensor"), None),
        P("pipe", "dp", None, "tensor"),
        P("pipe", ("tensor", "dp"), None),
        P("pipe", None, "dp", "tensor"),
        P("pipe", None, ("tensor", "dp"), None),
        P("pipe", None, ("dp", "tensor")),
        P("pipe", ("dp", "tensor"), None),
    )
    return jax.shard_map(local, mesh=mesh, in_specs=in_specs, out_specs=out_specs, check_vma=False)
```

```python
import functools

import jax
import jax.numpy as jnp
from jax import lax
from jax.experimental import pallas as pl
from jax.experimental.pallas import tpu as pltpu
from jax.sharding import PartitionSpec as P

HEAD_DIM = 64
EPSILON = 1e-06
NEGATIVE = -1e30
EXACT = lax.Precision.HIGHEST
EXTRA = 128
BF = jnp.bfloat16
F32 = jnp.float32
VM = pl.BlockSpec(memory_space=pltpu.VMEM)
SM = pl.BlockSpec(memory_space=pltpu.SMEM)
HB = pl.BlockSpec(memory_space=pltpu.HBM)
AFTER = pl.BlockSpec(memory_space=pl.ANY)
RAW = 2
VH = pl.BlockSpec(memory_space=pltpu.VMEM)
FAR = True
PIPE, MINE, REP, CORE, SPLIT = range(5)


def dot32(a, b):
    return jnp.dot(a, b, preferred_element_type=F32)


def dot_nt(a, b):
    return lax.dot_general(a, b, (((1,), (1,)), ((), ())), preferred_element_type=F32)


def dot_tn(a, b):
    return lax.dot_general(a, b, (((0,), (0,)), ((), ())), preferred_element_type=F32)


def split3(value):
    high = value.astype(BF)
    rest = value - high.astype(F32)
    mid = rest.astype(BF)
    return high, mid, (rest - mid.astype(F32)).astype(BF)


def parts_nt(a, b):
    return sum(dot_nt(a, part) for part in split3(b))


def norm_scale(x):
    return lax.rsqrt(jnp.mean(x * x, axis=-1, keepdims=True) + EPSILON)


def norm_back(x, scale, gain, grad):
    weighted = grad * gain
    grad_x = scale * weighted - x * (scale * scale * scale) * jnp.mean(
        x * weighted, axis=-1, keepdims=True
    )
    return grad_x, jnp.sum(grad * (x * scale), axis=0, keepdims=True)


def pinned(value):
    return pltpu.with_memory_space_constraint(value, pltpu.HBM)


def kernel_call(body, name, outs, ins, specs, scratch=(), cost=1, room=24, hbm_outs=False):
    ins = [
        pinned(each) if spec is HB or spec is VH else each
        for each, spec in zip(ins, specs, strict=True)
    ]
    far = [hbm_outs or len(each) > 2 for each in outs]
    return pl.pallas_call(
        body,
        name=name,
        out_shape=[
            (pltpu.HBM if away else jax.ShapeDtypeStruct)(each[0], each[1])
            for each, away in zip(outs, far, strict=True)
        ],
        in_specs=specs,
        out_specs=[HB if each[2:] == (RAW,) else VM for each in outs],
        scratch_shapes=list(scratch),
        compiler_params=pltpu.CompilerParams(vmem_limit_bytes=room << 20),
        cost_estimate=pl.CostEstimate(
            flops=int(cost * 1.1e9), bytes_accessed=0, transcendentals=0
        ),
    )(*ins)


def eye(count):
    rows = lax.broadcasted_iota(jnp.int32, (count, count), 0)
    return (rows == lax.broadcasted_iota(jnp.int32, (count, count), 1)).astype(F32).astype(BF)


def send_kernel(per, facts, inputs, cotangent, dealing, routes, order, router, gains, out, hot_out):
    rows, width = inputs.shape
    place = dealing[...]
    target = place >> 8
    numbers = [place & 255, routes[...], order[...] >> 8, order[...] & 255, target]
    numbers = [each.astype(F32) for each in numbers]
    numbers = jnp.concatenate(numbers + [jnp.zeros((EXTRA - 5, rows), F32)], axis=0)
    columns = dot_nt(eye(rows), numbers.astype(BF))
    targets = target.astype(F32)
    before = lax.broadcasted_iota(jnp.int32, (rows, rows), 0)
    after = lax.broadcasted_iota(jnp.int32, (rows, rows), 1)
    ahead = (columns[:, 4:5] == targets) & (before < after)
    slot = targets * per + jnp.sum(ahead.astype(F32), axis=0, keepdims=True)
    hot = (before.astype(F32) == slot).astype(F32).astype(BF)
    hot_out[...] = hot
    chosen = jnp.where(facts[PIPE] == 0, inputs[...], cotangent[...])
    out[:, :width] = dot32(hot, chosen).astype(BF)
    lane = lax.broadcasted_iota(jnp.int32, (rows, EXTRA), 1)
    tail = dot32(hot, jnp.where(lane < 4, columns, 0.0).astype(BF))
    parts = []
    for values in (router[...], gains[...]):
        high = values.astype(BF).astype(F32)
        mid = (values - high).astype(BF).astype(F32)
        parts += [high, mid, values - high - mid]
    count = gains.shape[1]
    blank = jnp.zeros((4, count), F32)
    block = jnp.concatenate([blank] + parts + [jnp.zeros((10, count), F32)], axis=0)
    block = dot_nt(eye(count), block.astype(BF))
    groups = [block[at * per : (at + 1) * per, :] for at in range(3)]
    block = jnp.concatenate(groups + [jnp.zeros((per, 32), F32)], axis=1)
    block = jnp.concatenate([block] * (rows // per), axis=0)
    out[:, width:] = (tail + block).astype(BF)


def deal_kernel(facts, both, own_rows, slots, onehot, place):
    width = own_rows.shape[1]
    pack = own_rows.shape[0]
    total = both.shape[0]
    half = pack // 2
    core = facts[CORE].astype(F32)
    numbers = both[:, width:]
    spot = numbers[:, 0:1].astype(F32)
    source = (lax.broadcasted_iota(jnp.int32, (total, 1), 0) >= pack).astype(F32)
    upper = (spot >= half).astype(F32)
    where = jnp.where(upper == core, source * half + spot - upper * half, -1.0)
    spots = lax.broadcasted_iota(jnp.int32, (total, pack), 1).astype(F32)
    hot = (spots == where).astype(F32).astype(BF)
    place[...] = hot
    own_rows[...] = dot_tn(hot, both[:, :width]).astype(BF)
    mine = dot_tn(hot, numbers)
    across = dot_nt(eye(EXTRA), mine.astype(BF))
    expert_col, expert_row = mine[:, 1:2], across[1:2, :]
    order_col = mine[:, 2:3] * 256.0 + mine[:, 3:4]
    order_row = across[2:3, :] * 256.0 + across[3:4, :]
    ahead = (expert_col == expert_row) & (order_col < order_row)
    rank = jnp.sum(ahead.astype(F32), axis=0, keepdims=True).astype(jnp.int32)
    experts = 4
    cap = pack // experts
    block = jnp.bitwise_xor(expert_row.astype(jnp.int32), facts[MINE])
    slot = jnp.where(rank < cap, block * cap + rank, -1)
    slots[...] = (lax.broadcasted_iota(jnp.int32, (pack, pack), 0) == slot).astype(F32).astype(BF)
    onehot[...] = (
        lax.broadcasted_iota(jnp.int32, (pack, EXTRA), 1) == expert_col.astype(jnp.int32)
    ).astype(F32)


def mask_of(facts, first, rows, columns):
    query = lax.broadcasted_iota(jnp.int32, (rows, columns), 0) + first
    key = lax.broadcasted_iota(jnp.int32, (rows, columns), 1)
    split = facts[SPLIT]
    return ((query < split) == (key < split)) & (key <= query)


def turned_mask(facts, first, rows, columns):
    key = lax.broadcasted_iota(jnp.int32, (rows, columns), 0) + first
    query = lax.broadcasted_iota(jnp.int32, (rows, columns), 1) + first
    split = facts[SPLIT]
    return ((query < split) == (key < split)) & (key <= query)


def stacked(refs):
    return jnp.concatenate([ref[...] for ref in refs], axis=0)


def flipped(params):
    flat = dot_nt(eye(EXTRA), params[...])
    return flat[16:18] + flat[18:20] + flat[20:22]


def weight_copies(sources, scratch, sems, width, cols):
    copies = []
    for at in range(2):
        each = []
        for start, rows in (*((part * width, width) for part in range(3)), (3 * width, 2 * cols)):
            spot = pl.ds(start, rows)
            each.append(
                pltpu.make_async_copy(
                    sources[at].at[spot], scratch.at[at, spot], sems.at[4 * at + len(each)]
                )
            )
        copies.append(each)
    return copies


def gate_of(up):
    return jnp.sum(up[:, up.shape[1] - EXTRA :].astype(F32), axis=-1, keepdims=True)


def attn_kernel(second, dropped, facts, *refs):
    refs = list(refs)
    weights, sems = refs[-2:] if second else refs[-5:-3]
    refs = refs[:-2] if second else refs[:-5] + refs[-3:]
    own_rows = refs.pop(0)
    if second:
        up = refs.pop(0)
        slots_in = [refs.pop(0) for _ in range(4)]
    attn_own, attn_other, params, slots, onehot = (refs.pop(0) for _ in range(5))
    refs = refs[dropped:]
    if second:
        mid, attn_in, proj, mixed, mlp_in, probs = (refs.pop(0) for _ in range(6))
    else:
        send_up = refs.pop(0)
        proj, mixed, mid = refs[4:]
    blocks = [refs.pop(0) for _ in range(4)]
    pack, width = own_rows.shape
    cols = attn_own.shape[1]
    cap = pack // 4
    copies = weight_copies((attn_own, attn_other), weights, sems, width, cols)
    for each in copies:
        for copy in each:
            copy.start()
    gains = flipped(params)
    hot = slots[...]
    if second:
        stream = refs.pop(0)
        grads = [refs.pop(0) for _ in range(4)]
        came = up[:, :width].astype(F32) + gate_of(up) * dot_tn(hot, stacked(slots_in))
        rows = jnp.where(facts[PIPE] == 0, own_rows[...], came.astype(BF))
        stream[...] = rows
    else:
        rows = own_rows[...]
    x = rows.astype(F32)
    normed = (x * norm_scale(x) * gains[0:1, :]).astype(BF)
    if second:
        attn_in[...] = normed
    half = pack // 2
    upper = mask_of(facts, 0, half, half)
    lower = mask_of(facts, half, half, pack)
    lane = lax.broadcasted_iota(jnp.int32, (pack, EXTRA), 1)
    totals = jnp.zeros((pack, EXTRA), F32)
    for at in range(2):
        for part in range(3):
            copies[at][part].wait()
            proj[at, part] = dot32(
                normed, weights[at, part * width : (part + 1) * width, :]
            ).astype(BF)
        for pair in range(cols // EXTRA):
            lanes = slice(pair * EXTRA, (pair + 1) * EXTRA)
            query = proj[at, 0, :, lanes] * jnp.asarray(HEAD_DIM ** (-0.5), BF)
            key, value = proj[at, 1, :, lanes], proj[at, 2, :, lanes]
            parts = []
            for side in range(2):
                chosen = jnp.where((lane >= HEAD_DIM) == (side == 1), query, 0)
                head = 8 + (at * cols + pair * EXTRA) // HEAD_DIM + side
                results = []
                for first, count, allowed in ((0, half, upper), (half, pack, lower)):
                    scores = dot_nt(chosen[first : first + half, :], key[:count, :])
                    scores = jnp.where(allowed, scores, NEGATIVE)
                    peak = jnp.max(scores, axis=-1, keepdims=True)
                    share = jnp.exp(scores - peak)
                    total = jnp.sum(share, axis=-1, keepdims=True)
                    results.append(
                        (dot32(share.astype(BF), value[:count, :]) * (1.0 / total), peak + jnp.log(total))
                    )
                parts.append(jnp.concatenate([each[0] for each in results], axis=0))
                if second:
                    level = jnp.concatenate([each[1] for each in results], axis=0)
                    totals = jnp.where(lane == head, level, totals)
            spot = at * cols + pair * EXTRA
            mixed[:, spot : spot + EXTRA] = jnp.where(lane < HEAD_DIM, *parts).astype(BF)
    base = 3 * width
    copies[0][3].wait()
    copies[1][3].wait()
    for side in range(2):
        rows_at = slice(base + side * cols, base + (side + 1) * cols)
        lanes = slice(side * cols, (side + 1) * cols)
        mid[:, lanes] = (
            x[:, lanes]
            + dot32(mixed[:, :cols], weights[0, rows_at, :])
            + dot32(mixed[:, cols:], weights[1, rows_at, :])
        )
    m = mid[:, :width]
    low = (m * norm_scale(m) * gains[1:2, :]).astype(BF)
    if second:
        mlp_in[...] = low
    logits = dot32(low, params[...])
    lane = lax.broadcasted_iota(jnp.int32, logits.shape, 1)
    logits = sum(pltpu.roll(logits, EXTRA - 4 * at, 1) for at in (1, 2, 3))
    logits = jnp.where(lane < 4, logits, NEGATIVE)
    rel = jnp.exp(logits - jnp.max(logits, axis=-1, keepdims=True))
    share = rel / jnp.sum(rel, axis=-1, keepdims=True)
    if second:
        probs[...] = share + totals
    gate = jnp.sum(share * onehot[...], axis=-1, keepdims=True)
    if second:
        mid[:, width:] = jnp.broadcast_to(gate, (pack, EXTRA))
    else:
        send_up[:, :width] = m.astype(BF)
        high = gate.astype(BF).astype(F32)
        middle = (gate - high).astype(BF).astype(F32)
        parts = jnp.where(lane == 1, middle, jnp.where(lane == 2, gate - high - middle, 0.0))
        send_up[:, width:] = jnp.where(lane == 0, high, parts).astype(BF)
    for step in range(4):
        blocks[step][...] = dot32(hot[step * cap : (step + 1) * cap, :], low).astype(BF)
    if second:
        weighted = (gate * own_rows[...].astype(F32)).astype(BF)
        for step in range(4):
            grads[step][...] = dot32(hot[step * cap : (step + 1) * cap, :], weighted).astype(BF)


def attn_forward(facts, own_rows, weights, plan, came=None, after=()):
    attn_own, attn_other, params = weights
    slots, onehot = plan
    pack, width = own_rows.shape
    cols = attn_own.shape[1]
    cap = pack // 4
    second = came is not None
    ins = [facts, own_rows] + (list(came) if second else [])
    specs = [SM, VH] + ([VH] if second else []) + [VM] * (len(ins) - (3 if second else 2))
    specs += [HB] * 2 + [VH] * 3 + [AFTER] * len(after)
    ins += [attn_own, attn_other, params, slots, onehot, *after]
    if second:
        outs = [
            ((pack, width + EXTRA), F32, FAR),
            ((pack, width), BF, FAR),
            ((2, 3, pack, cols), BF, FAR),
            ((pack, width), BF, FAR),
            ((pack, width), BF, FAR),
            ((pack, EXTRA), F32, FAR),
        ]
    else:
        outs = [((pack, width + EXTRA), BF, FAR)]
    outs += [((cap, width), BF)] * 4
    if second:
        outs += [((pack, width), BF, FAR)] + [((cap, width), BF)] * 4
    return kernel_call(
        functools.partial(attn_kernel, second, len(after)),
        "attn_second" if second else "attn_first",
        outs,
        ins,
        specs,
        [pltpu.VMEM((2, 3 * width + 2 * cols, cols), BF), pltpu.SemaphoreType.DMA((8,))]
        + ([] if second else [
            pltpu.VMEM((2, 3, pack, cols), BF),
            pltpu.VMEM((pack, width), BF),
            pltpu.VMEM((pack, width), F32),
        ]),
        cost=8,
    )


def attn_back_kernel(first, dropped, facts, *refs):
    refs = list(refs)
    weights, sems = refs[-2:]
    refs = refs[:-2]
    grad_out = refs.pop(0)
    if first:
        up = refs.pop(0)
    else:
        own_rows = refs.pop(0)
        refs = refs[dropped:]
    grad_slots = [refs.pop(0) for _ in range(4)]
    stream, mid, proj, mlp_in, probs, mixed = (refs.pop(0) for _ in range(6))
    attn_own, attn_other, params, slots, onehot = (refs.pop(0) for _ in range(5))
    grad_stream = refs.pop(0)
    if first:
        blocks = [refs.pop(0) for _ in range(4)]
        grad_proj = refs.pop(0)
    else:
        grad_proj, grad_low, tiny = (refs.pop(0) for _ in range(3))
    pack, width = stream.shape
    cols = attn_own.shape[1]
    cap = pack // 4
    copies = weight_copies((attn_own, attn_other), weights, sems, width, cols)
    for part in (3, 0, 1, 2):
        for each in copies:
            each[part].start()
    gains = flipped(params)
    hot = slots[...]
    rows = grad_out[...]
    if not first:
        rows = jnp.where(facts[PIPE] == 0, rows, own_rows[...])
    g = rows.astype(F32)
    slot_rows = stacked(grad_slots)
    at_tokens = dot_tn(hot, slot_rows[:, width:])
    lane = lax.broadcasted_iota(jnp.int32, (pack, EXTRA), 1)
    shares = jnp.where(lane < 4, probs[...], 0.0)
    grad_logits = (at_tokens[:, 0:1] + at_tokens[:, 1:2]) * (onehot[...] - shares)
    m = mid[:, :width]
    wide = sum(pltpu.roll(grad_logits, 4 * at, 1) for at in (1, 2, 3))
    grad_mlp = dot_tn(hot, slot_rows[:, :width]) + sum(
        dot_nt(part, params[...]) for part in split3(wide)
    )
    grad_norm, gain_two = norm_back(m, norm_scale(m), gains[1:2, :], grad_mlp)
    grad_mid = g + grad_norm
    low = grad_mid.astype(BF)
    base = 3 * width
    copies[0][3].wait()
    copies[1][3].wait()
    grad_mixed = jnp.concatenate(
        [
            (
                dot_nt(low[:, :cols], weights[at, base : base + cols, :])
                + dot_nt(low[:, cols:], weights[at, base + cols : base + 2 * cols, :])
            ).astype(BF)
            for at in range(2)
        ],
        axis=1,
    )
    heads = lax.broadcasted_iota(jnp.int32, (EXTRA, width), 0)
    heads = heads == lax.broadcasted_iota(jnp.int32, (EXTRA, width), 1) // HEAD_DIM + 8
    inner = parts_nt(heads.astype(F32).astype(BF), grad_mixed.astype(F32) * mixed[...].astype(F32))
    levels = parts_nt(eye(EXTRA), probs[...])
    half = pack // 2
    blocks_of = (
        (0, pack, turned_mask(facts, 0, half, pack)),
        (half, half, turned_mask(facts, half, half, half)),
    )
    grad_in = jnp.zeros((pack, width), F32)
    for at in range(2):
        for pair in range(cols // EXTRA):
            lanes = slice(pair * EXTRA, (pair + 1) * EXTRA)
            spot = at * cols + pair * EXTRA
            scale = jnp.asarray(HEAD_DIM ** (-0.5), BF)
            query = proj[at, 0, :, lanes] * scale
            key, value = proj[at, 1, :, lanes], proj[at, 2, :, lanes]
            grad_pair = grad_mixed[:, spot : spot + EXTRA]
            grad_query = jnp.zeros((pack, EXTRA), F32)
            grad_key = [jnp.zeros((half, EXTRA), F32) for _ in range(2)]
            grad_value = [jnp.zeros((half, EXTRA), F32) for _ in range(2)]
            for side in range(2):
                keep = (lane >= HEAD_DIM) == (side == 1)
                query_one = jnp.where(keep, query, 0)
                key_one = jnp.where(keep, key, 0)
                grad_one = jnp.where(keep, grad_pair, 0)
                head = 8 + spot // HEAD_DIM + side
                for at_block, (begin, count, allowed) in enumerate(blocks_of):
                    rows_at = slice(begin, begin + half)
                    after = slice(begin, begin + count)
                    scores = dot_nt(key[rows_at, :], query_one[after, :])
                    share = jnp.exp(scores - levels[head : head + 1, after])
                    share = jnp.where(allowed, share, 0.0)
                    grad_share = dot_nt(value[rows_at, :], grad_one[after, :])
                    grad_scores = share * (grad_share - inner[head : head + 1, after])
                    grad_scores = grad_scores.astype(BF)
                    grad_key[at_block] += dot32(grad_scores, query_one[after, :])
                    grad_value[at_block] += dot32(share.astype(BF), grad_one[after, :])
                    more = dot_tn(grad_scores, key_one[rows_at, :])
                    if begin:
                        more = jnp.concatenate([jnp.zeros((half, EXTRA), F32), more], axis=0)
                    grad_query += more
            grad_proj[at, 0, :, lanes] = (grad_query * HEAD_DIM ** (-0.5)).astype(BF)
            for at_block in range(2):
                rows_at = slice(at_block * half, (at_block + 1) * half)
                grad_proj[at, 1, rows_at, lanes] = grad_key[at_block].astype(BF)
                grad_proj[at, 2, rows_at, lanes] = grad_value[at_block].astype(BF)
        for part in range(3):
            copies[at][part].wait()
            grad_in += dot_nt(
                grad_proj[at, part], weights[at, part * width : (part + 1) * width, :]
            )
    x = stream[...].astype(F32)
    grad_norm, gain_one = norm_back(x, norm_scale(x), gains[0:1, :], grad_in)
    result = (grad_mid + grad_norm).astype(BF)
    grad_stream[...] = result
    if first:
        weighted = (gate_of(up) * result.astype(F32)).astype(BF)
        for step in range(4):
            blocks[step][...] = dot32(hot[step * cap : (step + 1) * cap, :], weighted).astype(BF)
    else:
        grad_low[...] = low
        high = grad_logits.astype(BF)
        rest = (grad_logits - high.astype(F32)).astype(BF)
        lane = lax.broadcasted_iota(jnp.int32, (width, EXTRA), 1)
        both = dot_tn(mlp_in[...], high) + dot_tn(mlp_in[...], rest)
        both = jnp.where(lane < 4, both, 0.0)
        high = both.astype(BF).astype(F32)
        flat = [gain_one.astype(BF).astype(F32), gain_two.astype(BF).astype(F32)]
        flat += [gain_one - flat[0], gain_two - flat[1]]
        flat = jnp.concatenate(flat + [jnp.zeros((12, width), F32)], axis=0).astype(BF)
        spot = lax.broadcasted_iota(jnp.int32, (16, EXTRA), 0) + 8
        spot = spot == lax.broadcasted_iota(jnp.int32, (16, EXTRA), 1)
        turned = dot_tn(flat, spot.astype(F32).astype(BF))
        tiny[...] = (high + pltpu.roll(both - high, 4, 1) + turned).astype(BF)


def attn_backward(facts, grad_out, extra, grad_slots, saved, weights, plan, first):
    attn_own, attn_other, params = weights
    slots, onehot = plan
    stream, mid, proj, mlp_in, probs, mixed = saved
    pack, width = stream.shape
    cols = attn_own.shape[1]
    cap = pack // 4
    ins = [facts, grad_out, *extra, *grad_slots, stream, mid, proj, mlp_in, probs, mixed]
    specs = [SM, VH if first else VM, VH] + [AFTER] * (len(extra) - 1)
    specs += [VM] * 4 + [VH] * 6 + [HB] * 2 + [VH] * 3
    ins += [attn_own, attn_other, params, slots, onehot]
    outs = [((pack, width), BF)]
    if first:
        outs += [((cap, width), BF)] * 4
    outs += [((2, 3, pack, cols), BF)]
    if not first:
        outs += [((pack, width), BF), ((width, EXTRA), BF)]
    return kernel_call(
        functools.partial(attn_back_kernel, first, len(extra) - 1),
        "attn_back_first" if first else "attn_back_second",
        outs,
        ins,
        specs,
        [pltpu.VMEM((2, 3 * width + 2 * cols, cols), BF), pltpu.SemaphoreType.DMA((8,))],
        cost=13,
    )


def gelu_both(u):
    square = u * u
    t = jnp.tanh(0.7978845608028654 * u * (1.0 + 0.044715 * square))
    half = 0.5 * (1.0 + t)
    inner = 0.7978845608028654 * (1.0 + 3.0 * 0.044715 * square)
    return half + 0.5 * u * (1.0 - t * t) * inner, half * u


def bring(facts, pieces, places, scratch, sems):
    copies = []
    for piece, spots in zip(pieces, places, strict=True):
        for source, target, rows, column, columns in spots(facts):
            copies.append(
                pltpu.make_async_copy(
                    piece.at[pl.ds(source, rows), pl.ds(0, columns)],
                    scratch.at[pl.ds(target, rows), pl.ds(column, columns)],
                    sems.at[len(copies)],
                )
            )
    for copy in copies:
        copy.start()
    return copies


TILE = 256


def expert_kernel(keep, places_in, places_out, facts, *refs):
    refs = list(refs)
    blocks = [refs.pop(0) for _ in range(8)]
    pieces = [refs.pop(0) for _ in range(len(places_in))]
    if keep:
        targets = [refs.pop(0) for _ in range(3)]
        own, other, w_in, w_out, sems_in, sems_out, act, rows, pre, sems = refs
    else:
        own, other, w_in, w_out, sems_in, sems_out, act, rows = refs
    arriving = bring(facts, pieces, places_in, w_in, sems_in)
    later = bring(facts, pieces, places_out, w_out, sems_out)
    cap = blocks[0].shape[0]
    for at, block in enumerate(blocks):
        rows[at * cap : (at + 1) * cap, :] = block[...]
    ff = w_in.shape[1]
    width = w_in.shape[0]
    if keep:
        leaving = pltpu.make_async_copy(rows, targets[2], sems.at[2, 0])
        leaving.start()

    def tile_copies(tile):
        lanes = pl.ds(pl.multiple_of(tile * TILE, TILE), TILE)
        return [
            pltpu.make_async_copy(
                source.at[:, lanes], targets[at].at[:, lanes], sems.at[at, tile]
            )
            for at, source in enumerate((pre, act))
        ]

    for copy in arriving:
        copy.wait()

    @pl.loop(0, ff // TILE, unroll=1)
    def _(tile):
        lanes = pl.ds(pl.multiple_of(tile * TILE, TILE), TILE)
        value = dot32(rows[...], w_in[:, lanes])
        slope, result = gelu_both(value)
        act[:, lanes] = result.astype(BF)
        if keep:
            pre[:, lanes] = slope.astype(BF)
            for copy in tile_copies(tile):
                copy.start()

    for copy in later:
        copy.wait()
    count = 4 * cap

    @pl.loop(0, width // TILE, unroll=1)
    def _(tile):
        lanes = pl.ds(pl.multiple_of(tile * TILE, TILE), TILE)
        value = dot32(act[...], w_out[:, lanes])
        own[:, lanes] = value[:count]
        other[:, lanes] = value[count:].astype(BF)

    if keep:
        leaving.wait()

        @pl.loop(0, ff // TILE, unroll=1)
        def _(tile):
            for copy in tile_copies(tile):
                copy.wait()


def halves(value, shape):
    high = value.astype(BF).astype(F32)
    lane = lax.broadcasted_iota(jnp.int32, shape, 1)
    return jnp.where(lane == 0, high, jnp.where(lane == 1, value - high, 0.0))


def expert_back_kernel(chosen, places_in, places_out, facts, *refs):
    refs = list(refs)
    blocks = [refs.pop(0) for _ in range(1 if chosen else 2)]
    pre, own_out, other_out = (refs.pop(0) for _ in range(3))
    pieces = [refs.pop(0) for _ in range(len(places_in))]
    grad_pre, own, other = (refs.pop(0) for _ in range(3))
    rows = blocks[0] if chosen else refs.pop(0)
    w_in, w_out, sems_in, sems_out = refs
    arriving = bring(facts, pieces, places_out, w_out, sems_out)
    later = bring(facts, pieces, places_in, w_in, sems_in)
    if not chosen:
        half = rows.shape[0] // 2
        for at, block in enumerate(blocks):
            rows[at * half : (at + 1) * half, :] = block[...]
    for copy in arriving:
        copy.wait()
    ff = w_in.shape[1]
    width = w_in.shape[0]
    count = rows.shape[0] // 2

    @pl.loop(0, ff // TILE, unroll=True)
    def _(tile):
        lanes = pl.ds(pl.multiple_of(tile * TILE, TILE), TILE)
        value = dot_nt(rows[...], w_out[lanes, :])
        grad_pre[:, lanes] = (value * pre[:, lanes].astype(F32)).astype(BF)

    for copy in later:
        copy.wait()

    @pl.loop(0, width // TILE, unroll=True)
    def _(tile):
        lanes = pl.ds(pl.multiple_of(tile * TILE, TILE), TILE)
        value = dot_nt(grad_pre[...], w_in[lanes, :])
        own[:, lanes] = value[:count]
        other[:, lanes] = value[count:].astype(BF)

    pull = jnp.sum(rows[:count, :].astype(F32) * own_out[...], axis=-1, keepdims=True)
    own[:, width:] = halves(pull, (count, EXTRA))
    pull = jnp.sum(
        rows[count:, :].astype(F32) * other_out[...].astype(F32), axis=-1, keepdims=True
    )
    other[:, width:] = halves(pull, (count, EXTRA)).astype(BF)


def expert_scratch(width, ff, places):
    numbers = jnp.zeros((8,), jnp.int32)
    sizes = [sum(len(spots(numbers)) for spots in each) for each in places]
    return (
        [pltpu.VMEM((width, ff), BF), pltpu.VMEM((ff, width), BF)],
        [pltpu.SemaphoreType.DMA((size,)) for size in sizes],
    )


def expert_call(name, keep, facts, blocks, pieces, places, width, ff):
    count = 4 * blocks[0].shape[0]
    ins = [facts, *blocks, *pieces]
    kept = [((2 * count, ff), BF, RAW)] * 2 + [((2 * count, width), BF, RAW)] if keep else []
    buffers, sems = expert_scratch(width, ff, places)
    scratch = [*buffers, *sems]
    scratch += [pltpu.VMEM((2 * count, ff), BF), pltpu.VMEM((2 * count, width), BF)]
    if keep:
        scratch.append(pltpu.VMEM((2 * count, ff), BF))
        scratch.append(pltpu.SemaphoreType.DMA((3, ff // TILE)))
    return kernel_call(
        functools.partial(expert_kernel, keep, *places),
        name,
        kept + [((count, width), F32), ((count, width), BF)],
        ins,
        [SM] + [VM] * 8 + [HB] * len(pieces),
        scratch,
        cost=7,
    )


def expert_back_call(name, facts, blocks, saved, pieces, places, width, ff):
    chosen = len(blocks) == 1
    count = blocks[0].shape[0] * len(blocks) // 2
    wide = width + EXTRA
    ins = [facts, *blocks, *saved, *pieces]
    buffers, sems = expert_scratch(width, ff, places)
    outs = [((2 * count, ff), BF), ((count, wide), F32), ((count, wide), BF)]
    if not chosen:
        outs.append(((2 * count, width), BF, FAR))
    return kernel_call(
        functools.partial(expert_back_kernel, chosen, *places),
        name,
        outs,
        ins,
        [SM] + ([VH] if chosen else [VM] * 2) + [VH, VM, VM] + [HB] * len(pieces),
        [*buffers, *sems],
        cost=8,
    )


def fold_kernel(own, other, *blocks):
    blocks = blocks[-4:]
    cap = blocks[0].shape[0]
    width = own.shape[1] // TILE * TILE
    for step, block in enumerate(blocks):
        rows = slice(step * cap, (step + 1) * cap)
        block[:, :width] = (own[rows, :width] + other[rows, :width].astype(F32)).astype(BF)
        if own.shape[1] > width:
            both = own[rows, width:] + other[rows, width:].astype(F32)
            block[:, width:] = halves(both[:, 0:1] + both[:, 1:2], (cap, EXTRA)).astype(BF)


def fold(own, other, name, after=()):
    count, width = own.shape
    cap = count // 4
    return kernel_call(
        fold_kernel, name, [((cap, width), BF)] * 4, [own, other, *after], [VM, VM] + [AFTER] * len(after)
    )


def return_kernel(merge, *refs):
    refs = list(refs)
    rows = refs.pop(0)
    if merge:
        hot = refs.pop(0)
        slots_in = [refs.pop(0) for _ in range(4)]
        width = slots_in[0].shape[1]
        values = rows[:, :width] + rows[:, width : width + 1] * dot_tn(hot[...], stacked(slots_in))
        values = values.astype(BF)
    else:
        values = rows[...]
    place, facts = refs[:2]
    own, other = refs[-2:]
    pack = own.shape[0]
    core = facts[CORE]
    own[...] = dot32(place[pl.ds(pl.multiple_of(core * pack, pack), pack), :], values).astype(BF)
    other[...] = dot32(
        place[pl.ds(pl.multiple_of((1 - core) * pack, pack), pack), :], values
    ).astype(BF)


def sent_rows(facts, merge, rows, extra, place, width, after):
    pack = place.shape[1]
    ins = [rows, *extra, place, facts, *after]
    outs = [((pack, width), BF)] * 2
    return kernel_call(
        functools.partial(return_kernel, merge),
        "return_merged" if merge else "return_rows",
        outs,
        ins,
        ([VH, VH] + [VM] * 4 if merge else [VM]) + [VH, SM] + [AFTER] * len(after),
        cost=1,
    )


def run_copies(moves, sems):
    copies = [
        pltpu.make_async_copy(source, target, sems.at[at])
        for at, (source, target) in enumerate(moves)
    ]
    for copy in copies:
        copy.start()
    for copy in copies:
        copy.wait()


def rows_kernel(*refs):
    cap = refs[0].shape[0]
    out = refs[-1]
    for at, ref in enumerate(refs[:4]):
        out[at * cap : (at + 1) * cap, :] = ref[...]


def joined_rows(blocks, after):
    cap, width = blocks[0].shape
    return kernel_call(
        rows_kernel,
        "join_rows",
        [((4 * cap, width), BF)],
        [*blocks, *after],
        [VM] * 4 + [AFTER] * len(after),
    )[0]


def ordered_kernel(*refs):
    del refs


def ordered(value, after):
    return pl.pallas_call(
        ordered_kernel,
        name="ordered",
        out_shape=pltpu.HBM(value.shape, value.dtype),
        in_specs=[HB] + [AFTER] * len(after),
        out_specs=HB,
        input_output_aliases={0: 0},
        compiler_params=pltpu.CompilerParams(vmem_limit_bytes=1 << 20),
        cost_estimate=pl.CostEstimate(flops=0, bytes_accessed=0, transcendentals=0),
    )(pinned(value), *after)


def restore_kernel(hot, back, activations, grads, tiny):
    width = activations.shape[1]
    activations[...] = dot_tn(hot[...], back[:, :width]).astype(BF)
    grads[...] = dot_tn(hot[...], back[:, width : 2 * width]).astype(BF)
    rows = tiny.shape[0]
    total = jnp.zeros(tiny.shape, F32)
    for at in range(back.shape[0] // rows):
        total += back[at * rows : (at + 1) * rows, 2 * width :].astype(F32)
    tiny[...] = total


def finish_kernel(*refs):
    pieces, attn, attn_out = refs[:4], refs[4], refs[5]
    _, shard, cols = attn.shape
    total = sum(piece[...].astype(F32) for piece in pieces)
    for part in range(3):
        attn[part] = total[part * shard : (part + 1) * shard, :]
    rows = attn_out.shape[0]
    for side in range(2):
        spot = 3 * shard + side * rows
        attn_out[:, side * cols : (side + 1) * cols] = total[spot : spot + rows, :]


def stack_kernel(count, facts, *refs):
    pieces, out, sems = refs[:count], refs[-2], refs[-1]
    run_copies(
        [
            (piece, out.at[jnp.bitwise_xor(facts[MINE], step)])
            for step, piece in enumerate(pieces)
        ],
        sems,
    )


def stack_pieces(facts, pieces, after):
    count = len(pieces)
    return kernel_call(
        functools.partial(stack_kernel, count),
        "stack_pieces",
        [((count, *pieces[0].shape), BF)],
        [facts, *pieces, *after],
        [SM] + [HB] * count + [AFTER] * len(after),
        [pltpu.SemaphoreType.DMA((count,))],
        room=12,
        hbm_outs=True,
    )[0]


def gather_kernel(facts, near, far, *refs):
    out, sems = refs[-2:]
    groups = near.shape[0]
    moves = []
    for rep, source in ((facts[REP], near), (1 - facts[REP], far)):
        for part in range(3):
            moves.append(
                (
                    source.at[:, pl.ds(2 * part, 2)],
                    out.at[pl.ds(part * groups, groups), pl.ds(2 * rep, 2)],
                )
            )
        for side in range(2):
            for group in range(groups):
                moves.append(
                    (
                        source.at[group, 6 + side],
                        out.at[3 * groups + 2 * side + group // 2, group % 2 * 2 + rep],
                    )
                )
    run_copies(moves, sems)


def pack_attn_kernel(attn, attn_out, bundle, sems):
    parts, shard, cols = attn.shape
    rows = attn_out.shape[0]
    moves = [(attn.at[part], bundle.at[pl.ds(part * shard, shard)]) for part in range(parts)]
    for side in range(2):
        moves.append(
            (
                attn_out.at[:, pl.ds(side * cols, cols)],
                bundle.at[pl.ds(parts * shard + side * rows, rows)],
            )
        )
    run_copies(moves, sems)


def pack_attn(attn, attn_out):
    parts, shard, cols = attn.shape
    rows = attn_out.shape[0]
    return kernel_call(
        pack_attn_kernel,
        "pack_attn",
        [((parts * shard + 2 * rows, cols), BF)],
        [attn, attn_out],
        [HB] * 2,
        [pltpu.SemaphoreType.DMA((parts + 2,))],
        room=12,
        hbm_outs=True,
    )[0]


def pack_expert_kernel(steps, facts, w_in, w_out, *refs):
    blocks, sems = refs[-1 - len(steps) : -1], refs[-1]
    in_rows, out_rows, width = w_in.shape[1], w_out.shape[1], w_out.shape[2]
    moves = []
    for step, block in zip(steps, blocks, strict=True):
        at = jnp.bitwise_xor(facts[MINE], step)
        for side in range(2):
            moves.append(
                (
                    w_in.at[at, :, pl.ds(side * width, width)],
                    block.at[pl.ds(side * in_rows, in_rows)],
                )
            )
        moves.append((w_out.at[at], block.at[pl.ds(2 * in_rows, out_rows)]))
    run_copies(moves, sems)


def pack_expert(facts, w_in, w_out, steps, after=()):
    block = (2 * w_in.shape[1] + w_out.shape[1], w_out.shape[2])
    return kernel_call(
        functools.partial(pack_expert_kernel, steps),
        "pack_expert",
        [(block, BF)] * len(steps),
        [facts, w_in, w_out, *after],
        [SM, HB, HB] + [AFTER] * len(after),
        [pltpu.SemaphoreType.DMA((3 * len(steps),))],
        room=12,
        hbm_outs=True,
    )


SPLIT_ORDER = (2, 3, 1, 0)


def expert_out_grad_kernel(split, dropped, facts, *refs):
    blocks, refs = refs[:8], refs[8:]
    kept, act = refs[:2]
    refs = refs[2 + dropped :]
    rows, refs = refs[0], refs[1:]
    cap = blocks[0].shape[0]
    for at, block in enumerate(blocks):
        spot = slice(at * cap, (at + 1) * cap)
        rows[spot, :] = jnp.where(facts[PIPE] == 0, block[...], kept[spot, :])
    ff = act.shape[1]
    grad = refs[-1]

    @pl.loop(0, ff // TILE, unroll=True)
    def _(tile):
        lanes = pl.ds(pl.multiple_of(tile * TILE, TILE), TILE)
        grad[lanes, :] = dot_tn(act[:, lanes], rows[...])

    if split:
        count = ff // 8
        for at, step in enumerate(SPLIT_ORDER):
            owner = jnp.bitwise_xor(facts[MINE], step) * 2
            to = slice(at % 2 * count, (at % 2 + 1) * count)
            for rep, target in ((1 - facts[REP], refs[at // 2]), (facts[REP], refs[2 + at // 2])):
                spot = pl.ds(pl.multiple_of((owner + rep) * count, count), count)
                target[to, :] = grad[spot, :].astype(BF)


def expert_in_grad_kernel(split, dropped, facts, rows, grad_pre, *refs):
    refs = refs[dropped:]
    ff = grad_pre.shape[1]
    width = rows.shape[1]
    grad = refs[-1]

    @pl.loop(0, ff // TILE, unroll=True)
    def _(tile):
        lanes = pl.ds(pl.multiple_of(tile * TILE, TILE), TILE)
        grad[:, lanes] = dot_tn(rows[...], grad_pre[:, lanes])

    if split:
        count = width // 8
        for at, step in enumerate(SPLIT_ORDER):
            owner = jnp.bitwise_xor(facts[MINE], step) * 2
            first = at * 2 * count
            for rep, target in ((1 - facts[REP], refs[0]), (facts[REP], refs[1])):
                spot = pl.ds(pl.multiple_of((owner + rep) * count, count), count)
                target[first : first + count, :] = grad[spot, :width].astype(BF)
                target[first + count : first + 2 * count, :] = grad[spot, width:].astype(BF)


def grad_outs(shape, wire, split, count):
    if split:
        return [(wire, BF, FAR)] * count, [pltpu.VMEM(shape, F32)]
    return [(shape, F32)], []


def expert_out_grads(facts, blocks, kept, act, after, split):
    count, width = kept.shape
    ff = act.shape[1]
    outs, scratch = grad_outs((ff, width), (ff // 4, width), split, 4)
    return kernel_call(
        functools.partial(expert_out_grad_kernel, split, len(after)),
        "expert_out_grads",
        [((count, width), BF, FAR), *outs],
        [facts, *blocks, kept, act, *after],
        [SM] + [VM] * 8 + [VH, VH] + [AFTER] * len(after),
        scratch,
        cost=4,
    )


def expert_in_grads(facts, rows, grad_pre, after, split):
    width = rows.shape[1]
    ff = grad_pre.shape[1]
    outs, scratch = grad_outs((width, ff), (ff // 2, width), split, 2)
    return kernel_call(
        functools.partial(expert_in_grad_kernel, split, len(after)),
        "expert_in_grads",
        outs,
        [facts, rows, grad_pre, *after],
        [SM, VH, VM] + [AFTER] * len(after),
        scratch,
        cost=4,
    )


def owner_kernel(facts, *refs):
    grad_in, grad_out = refs[-2:]
    rows = grad_in.shape[1]
    width = grad_out.shape[2]
    for place, step in enumerate(SPLIT_ORDER):
        at = jnp.bitwise_xor(facts[MINE], step)
        grad_out[at] = refs[place][...].astype(F32)
        piece = refs[4 + place]
        for side in range(2):
            spot = slice(side * rows, (side + 1) * rows)
            grad_in[at, :, side * width : (side + 1) * width] = piece[spot, :].astype(F32)


def owner_grads(facts, pieces, after, in_shape, out_shape):
    return kernel_call(
        owner_kernel,
        "owner_grads",
        [(in_shape, F32), (out_shape, F32)],
        [facts, *pieces, *after],
        [SM] + [VM] * len(pieces) + [AFTER] * len(after),
        cost=4,
    )


def attn_grad_kernel(attn_in, grad_proj, mixed, low, *refs):
    own, other = refs[-2:]
    width = attn_in.shape[1]
    cols = own.shape[1]
    for at, target in ((0, own), (1, other)):
        for part in range(3):
            target[part * width : (part + 1) * width, :] = dot_tn(
                attn_in[...], grad_proj[at, part]
            ).astype(BF)
        for side in range(2):
            spot = 3 * width + side * cols
            target[spot : spot + cols, :] = dot_tn(
                mixed[:, at * cols : (at + 1) * cols], low[:, side * cols : (side + 1) * cols]
            ).astype(BF)


def attn_grads(attn_in, grad_proj, mixed, low, after):
    pack, width = attn_in.shape
    cols = grad_proj.shape[3]
    return kernel_call(
        attn_grad_kernel,
        "attn_grads",
        [((3 * width + 2 * cols, cols), BF)] * 2,
        [attn_in, grad_proj, mixed, low, *after],
        [VH, VM, VH, VM] + [AFTER] * len(after),
        cost=3,
    )


def attn_split_kernel(facts, own, came, *refs):
    sends, keeps = refs[-4:-2], refs[-2:]
    cols = own.shape[1]
    width = 2 * cols
    shard = width // 8
    count = 4 * shard
    for at, step in enumerate(SPLIT_ORDER):
        owner = jnp.bitwise_xor(facts[MINE], step) * 2
        for rep, target, first in (
            (1 - facts[REP], sends[at // 2], at % 2 * count),
            (facts[REP], keeps[at // 2], at % 2 * count),
        ):
            for source, rows, spot in attn_rows(width, shard):
                where = pl.ds(pl.multiple_of(source + (owner + rep) * rows, rows), rows)
                target[first + spot : first + spot + rows, :] = (
                    own[where, :].astype(F32) + came[where, :].astype(F32)
                ).astype(BF)


def sum_kernel(steps, keep, came, *outs):
    outs = outs[-len(steps) :]
    count = outs[0].shape[0]
    for at, out in enumerate(outs):
        rows = slice(at * count, (at + 1) * count)
        both = keep[rows, :].astype(F32) + came[rows, :].astype(F32)
        out[...] = both.astype(out.dtype)


def sum_pieces(steps, keep, came, after=()):
    count = keep.shape[0] // len(steps)
    kinds = [F32 if step == 0 else BF for step in steps]
    return kernel_call(
        functools.partial(sum_kernel, steps),
        "sum_pieces",
        [((count, keep.shape[1]), kind) for kind in kinds],
        [keep, came, *after],
        [VH] * 2 + [AFTER] * len(after),
        cost=0,
    )


def attn_rows(width, shard):
    out = shard // 2
    return (
        (0, shard, 0),
        (width, shard, shard),
        (2 * width, shard, 2 * shard),
        (3 * width, out, 3 * shard),
        (3 * width + width // 2, out, 3 * shard + out),
    )


def attn_split(facts, own, came, after):
    rows, cols = own.shape
    return kernel_call(
        attn_split_kernel,
        "attn_split",
        [((rows // 4, cols), BF, FAR)] * 4,
        [facts, own, came, *after],
        [SM, VM, VM] + [AFTER] * len(after),
        cost=3,
    )


def solution(mesh):
    shape = mesh.shape
    n_pipe, n_dp, n_t = shape["pipe"], shape["dp"], shape["tensor"]
    axes = ("pipe", "dp", "tensor")
    plane = ("dp", "tensor")
    n_dev = n_dp * n_t

    def local(
        inputs,
        cotangent,
        dealing,
        routes,
        slot_order,
        doc_lengths,
        attn_weight,
        attn_out_weight,
        expert_in_weight,
        expert_out_weight,
        norm_gains,
        router_weight,
    ):
        dev_rows, width = inputs.shape
        experts = expert_in_weight.shape[1]
        reps = n_dp // experts
        paired = reps == 2
        pack = dev_rows
        cap = pack // experts
        per = dev_rows // n_dev
        shard, cols = attn_weight.shape[1], attn_weight.shape[3]
        ff = expert_in_weight.shape[3]
        in_rows, out_rows = expert_in_weight.shape[2], expert_out_weight.shape[2]
        pipe = lax.axis_index("pipe")
        dp = lax.axis_index("dp")
        core = lax.axis_index("tensor")
        mine = dp // reps
        rep = dp % reps
        lengths = lax.dynamic_index_in_dim(doc_lengths, core, 0, keepdims=False)
        zero = jnp.int32(0)
        facts = jnp.stack([pipe, mine, rep, core, lengths[0], zero, zero, zero]).astype(jnp.int32)

        def moved(value, rule):
            pairs = []
            for a in range(n_pipe):
                for b in range(experts):
                    for c in range(reps):
                        for d in range(n_t):
                            to = rule(a, b, c, d)
                            if to is not None:
                                flat = [
                                    ((w * experts + x) * reps + y) * n_t + z
                                    for w, x, y, z in ((a, b, c, d), to)
                                ]
                                pairs.append(tuple(flat))
            return lax.ppermute(value, axes, pairs)

        def swap_core(value):
            return moved(value, lambda a, b, c, d: (a, b, c, 1 - d))

        def swap_rep(value):
            return moved(value, lambda a, b, c, d: (a, b, 1 - c, d))

        def across(step):
            return lambda a, b, c, d: (a, b ^ step, c, d)

        def up(step):
            return lambda a, b, c, d: (1, b ^ step, c, d) if a == 0 else None

        def down(step):
            return lambda a, b, c, d: (0, b ^ step, c, d) if a == 1 else None

        order = (2, 3, 1)

        def exchange(blocks):
            out = {0: blocks[0]}
            for step in order:
                out[step] = moved(blocks[step], across(step))
            return [out[step] for step in range(experts)]

        def crossed(blocks, way):
            out = {}
            for step in (*order, 0):
                out[step] = moved(blocks[step], way(step))
            return [out[step] for step in range(experts)]

        def with_other(blocks):
            out = {}
            for step in (0, 1, 2, 3):
                out[step] = swap_core(blocks[step])
            return list(blocks) + [out[step] for step in range(experts)]

        def pick(blocks, step):
            return lax.dynamic_index_in_dim(blocks, mine ^ step, 0, keepdims=False)

        rep_groups = [[b * reps + c for c in range(reps)] for b in range(experts)]

        payload, send_hot = kernel_call(
            functools.partial(send_kernel, per),
            "send",
            [((dev_rows, width + EXTRA), BF), ((dev_rows, dev_rows), BF)],
            [
                facts,
                inputs,
                cotangent,
                dealing.reshape(1, dev_rows),
                routes.reshape(1, dev_rows),
                slot_order.reshape(1, dev_rows),
                router_weight[0].T,
                norm_gains[0],
            ],
            [SM] + [VM] * 7,
            cost=2,
        )
        dealt = lax.all_to_all(payload, plane, split_axis=0, concat_axis=0, tiled=True)
        params = dealt[:, width:].reshape(n_dev, per, 4, 32)[:, :, :3]
        params = jnp.swapaxes(params, 1, 2).reshape(width, 32)
        params = jnp.pad(params, ((0, 0), (0, EXTRA - 32)))
        both = lax.all_gather(dealt, "tensor", axis=0, tiled=True)
        own_rows, slots, onehot, place = kernel_call(
            deal_kernel,
            "deal",
            [
                ((pack, width), BF, FAR),
                ((pack, pack), BF, FAR),
                ((pack, EXTRA), F32, FAR),
                ((2 * pack, pack), BF, FAR),
            ],
            [facts, both],
            [SM, VM],
            cost=1.5,
        )
        plan = (slots, onehot)

        out_shard = attn_out_weight[0]
        attn_shape = (4 * width, cols)

        def expert_places(way, step):
            def owner_of(numbers):
                owner = jnp.bitwise_xor(numbers[MINE], step) * 2
                return owner + (numbers[REP] if way == 0 else 1 - numbers[REP])

            def spots_in(numbers):
                at = pl.multiple_of(owner_of(numbers) * in_rows, in_rows)
                return [(0, at, in_rows, 0, width), (in_rows, at, in_rows, width, width)]

            def spots_out(numbers):
                at = pl.multiple_of(owner_of(numbers) * out_rows, out_rows)
                return [(2 * in_rows, at, out_rows, 0, width)]

            return spots_in, spots_out

        if paired:
            w_in_raw, w_out_raw = expert_in_weight[0], expert_out_weight[0]
            attn_bundle = pack_attn(jnp.swapaxes(attn_weight[0], 0, 1), out_shard)
            near, far = {}, {}
            near[0], first, bundle = pack_expert(
                facts, w_in_raw, w_out_raw, (0, 1, 2), (attn_bundle,)
            )
            far[0] = swap_rep(near[0])
            attn_near = exchange([attn_bundle] * experts)
            attn_near = stack_pieces(
                facts, [each.reshape(8, shard // 2, cols) for each in attn_near],
                [payload, far[0]],
            )
            near[1] = moved(first, across(1))
            attn_far = swap_rep(attn_near)
            near[2] = moved(bundle, across(2))
            (bundle,) = pack_expert(facts, w_in_raw, w_out_raw, (3,), (near[2],))
            attn_own = kernel_call(
                gather_kernel,
                "gather_attn",
                [((4 * experts, 4, shard // 2, cols), BF)],
                [facts, attn_near, attn_far, bundle, dealt, near[1]],
                [SM, HB, HB, AFTER, AFTER, AFTER],
                [pltpu.SemaphoreType.DMA((22,))],
                room=12,
                hbm_outs=True,
            )[0].reshape(attn_shape)
            near[3] = moved(bundle, across(3))
            for step in (1, 2):
                far[step] = swap_rep(near[step])
            ready = ()
            both_places = [
                expert_places(way, step) for way in range(2) for step in range(experts)
            ]
            places = ([each[0] for each in both_places], [each[1] for each in both_places])
        else:
            attn_bundle = jnp.concatenate(
                [attn_weight[0, :, part] for part in range(3)]
                + [out_shard[:, :cols], out_shard[:, cols:]],
                axis=0,
            )
            every = lax.all_gather(attn_bundle, "dp", axis=0)
            attn_own = jnp.concatenate(
                [
                    every[:, spot : spot + rows].reshape(-1, cols)
                    for _, rows, spot in attn_rows(width, shard)
                ],
                axis=0,
            )

            def assembled(blocks):
                got = exchange([pick(blocks, step) for step in range(experts)])
                got = jnp.stack(got)
                got = jnp.stack([pick(got, owner) for owner in range(experts)])
                got = lax.all_gather(got, "dp", axis_index_groups=rep_groups)
                return jnp.swapaxes(got, 0, 1)

            ready = ()
            pieces = [
                assembled(expert_in_weight[0]).reshape(width, ff),
                assembled(expert_out_weight[0]).reshape(ff, width),
            ]
            places = (
                [lambda numbers: [(0, 0, width, 0, ff)], lambda numbers: []],
                [lambda numbers: [], lambda numbers: [(0, 0, ff, 0, width)]],
            )
        attn_other = swap_core(attn_own)
        weights = (attn_own, attn_other, params)

        def expert_forward(blocks, name, keep, after=()):
            *kept, own, other = expert_call(name, keep, facts, blocks, pieces, places, width, ff)
            folded = fold(own, swap_core(other), "fold_" + name, after)
            return kept, own, other, folded

        def expert_backward(blocks, saved, name, after=()):
            grad_pre, own, other, *rows = expert_back_call(
                name, facts, blocks, saved, pieces, places, width, ff
            )
            return grad_pre, rows, fold(own, swap_core(other), "fold_" + name, after)

        def sent_back(merge, rows, extra, after):
            own, other = sent_rows(facts, merge, rows, extra, place, width, after)
            return own, other

        out = attn_forward(facts, own_rows, weights, plan, None, ready)
        if paired:
            near[3] = ordered(near[3], (out[1],))
            far[3] = swap_rep(near[3])
            pieces = [each[step] for each in (near, far) for step in range(experts)]
        mid_up = moved(out[0], lambda a, b, c, d: (1, b, c, d) if a == 0 else None)
        blocks = with_other(exchange(out[1:5]))
        _, _, _, expert_slots = expert_forward(
            blocks, "expert_first", False, (mid_up,)
        )
        from_first = crossed(expert_slots, up)

        out = attn_forward(facts, own_rows, weights, plan, (mid_up, *from_first))
        mid, attn_in, proj, mixed, mlp_in, probs = out[:6]
        stream = out[10]
        blocks = with_other(exchange(out[6:10]))
        kept_blocks = exchange(out[11:15])
        (slope, act, rows), own_out, other_out, expert_slots = expert_forward(blocks, "expert_second", True)
        expert_saved = (slope, own_out, other_out)

        saved = (stream, mid, proj, mlp_in, probs, mixed)
        kept_own = joined_rows(kept_blocks, (other_out,))
        _, (kept_rows,), grad_slots = expert_backward(
            [kept_own, swap_core(kept_own)], expert_saved, "expert_back_first"
        )
        back = attn_backward(
            facts, own_rows, [mid_up], exchange(grad_slots), saved, weights, plan, True
        )
        expert_slots = exchange(expert_slots)
        if paired:
            back = list(back)
            back[1 + order[0]] = ordered(back[1 + order[0]], expert_slots[1:])
        grad_down = moved(back[0], lambda a, b, c, d: (0, b, c, d) if a == 1 else None)
        out_back = sent_back(True, mid, (slots, *expert_slots), (back[1],))

        grads = with_other(crossed(back[1:5], down))
        grad_rows, *out_wire = expert_out_grads(
            facts, grads, kept_rows, act, (out_back[0],), paired
        )
        grad_pre, _, grad_slots = expert_backward(
            [grad_rows], expert_saved, "expert_back_second"
        )
        out_came = [swap_rep(out_wire[0])] if paired else []
        in_wire = expert_in_grads(facts, rows, grad_pre, [grad_slots[2], *out_came], paired)
        after = []
        if paired:
            out_sums = sum_pieces(
                SPLIT_ORDER[:2], out_wire[2], out_came[0], [in_wire[1]]
            )
            after = [out_sums[0]]
        layer_grad, grad_proj, low, tiny = attn_backward(
            facts,
            grad_down,
            [own_rows, *after],
            exchange(grad_slots),
            saved,
            weights,
            plan,
            False,
        )

        if paired:
            out_near = [
                moved(each, across(step)) if step else each
                for step, each in zip(SPLIT_ORDER[:2], out_sums, strict=True)
            ]
            came_in = swap_rep(in_wire[0])
            came_last = swap_rep(out_wire[1])
            marker = [came_last, came_in, *out_near]
        else:

            def rep_scatter(each):
                return lax.psum_scatter(
                    each, "dp", axis_index_groups=rep_groups, scatter_dimension=0
                )

            def to_owner(grad, rows_each):
                each = grad.reshape(experts, reps, rows_each, -1).astype(BF)
                summed = rep_scatter(jnp.swapaxes(each, 0, 1))
                got = exchange([pick(summed, step) for step in range(experts)])
                got = jnp.stack(got)
                return jnp.stack([pick(got, owner) for owner in range(experts)]).astype(F32)

            marker = []
            (grad_w_in,), (grad_w_out,) = in_wire, out_wire
            grad_expert_in = to_owner(grad_w_in, in_rows)
            grad_expert_out = to_owner(grad_w_out, out_rows)

        grad_own, grad_other = attn_grads(attn_in, grad_proj, mixed, low, marker)
        came = swap_core(grad_other)
        if paired:
            in_sums = sum_pieces(SPLIT_ORDER, in_wire[1], came_in, [grad_own])
            in_near = [
                moved(each, across(step)) if step else each
                for step, each in zip(SPLIT_ORDER, in_sums, strict=True)
            ]
            out = attn_split(facts, grad_own, came, (in_sums[0],))
            last = sum_pieces(SPLIT_ORDER[2:], out_wire[3], came_last, [out[2]])
            out_near += [moved(last[0], across(1)), last[1]]
            after = (last[1],)
        else:
            after = ()
        grad_back = sent_back(False, layer_grad, (), after)
        tiny = jnp.swapaxes(tiny[:, :32].reshape(n_dev, 3, per, 32), 1, 2)
        tiny = jnp.pad(tiny.reshape(dev_rows, 96), ((0, 0), (0, EXTRA - 96)))
        theirs = swap_core(jnp.concatenate([out_back[1], grad_back[1]], axis=1))
        both = jnp.concatenate([out_back[0], grad_back[0]], axis=1) + theirs
        payload = jnp.concatenate([both, tiny], axis=1)
        if paired:
            total = {}
            first = sum_pieces(SPLIT_ORDER[:2], out[2], swap_rep(out[0]), [payload])
            last = swap_rep(ordered(out[1], (first[0],)))
            last = sum_pieces(SPLIT_ORDER[2:], out[3], last, [first[1]])
            for step, each in zip(SPLIT_ORDER, [*first, *last], strict=True):
                total[step] = moved(each, across(step)) if step else each
            grad_expert_in, grad_expert_out = owner_grads(
                facts,
                [*out_near, *in_near],
                (total[0],),
                expert_in_weight.shape[1:],
                expert_out_weight.shape[1:],
            )
            grad_attn, grad_attn_out = kernel_call(
                finish_kernel,
                "finish_attn",
                [((3, shard, cols), F32), ((shard // 2, width), F32)],
                [total[step] for step in range(experts)],
                [VM] * 4,
            )
        else:
            full = grad_own.astype(F32) + came.astype(F32)
            pieces_of = [
                full[source : source + rows * n_dp].reshape(n_dp, rows, cols)
                for source, rows, _ in attn_rows(width, shard)
            ]
            full = jnp.concatenate(pieces_of, axis=1).astype(BF)
            full = full.reshape((experts, reps) + full.shape[1:])
            full = rep_scatter(jnp.swapaxes(full, 0, 1))
            got = exchange([pick(full, step) for step in range(experts)])
            total = sum(each.astype(F32) for each in got)
            grad_attn = total[: 3 * shard].reshape(3, shard, cols)
            rows = shard // 2
            grad_attn_out = jnp.concatenate(
                [total[3 * shard : 3 * shard + rows], total[3 * shard + rows :]], axis=1
            )
        both = lax.all_to_all(payload, plane, split_axis=0, concat_axis=0, tiled=True)
        activations, input_grads, tiny = kernel_call(
            restore_kernel,
            "restore",
            [((dev_rows, width), BF), ((dev_rows, width), BF), ((per, EXTRA), F32)],
            [send_hot, both],
            [VM] * 2,
            cost=2,
        )
        tiny = tiny.reshape(per, 4, 32)[:, :3]
        tiny = jnp.swapaxes(tiny, 0, 1).reshape(3 * per, 32)
        grad_router = (tiny[:, :experts] + tiny[:, experts : 2 * experts])[None]
        grad_gains = (tiny[:, 8:10] + tiny[:, 10:12]).T[None]

        return (
            activations[None],
            input_grads[None],
            jnp.swapaxes(grad_attn, 0, 1)[None],
            grad_attn_out[None],
            grad_expert_in[None],
            grad_expert_out[None],
            grad_gains,
            grad_router,
        )

    in_specs = (
        P(("dp", "tensor"), None),
        P(("dp", "tensor"), None),
        P(("dp", "tensor")),
        P(("dp", "tensor"), None),
        P(("dp", "tensor")),
        P("dp", None),
        P("pipe", "dp", None, "tensor"),
        P("pipe", ("tensor", "dp"), None),
        P("pipe", None, "dp", "tensor"),
        P("pipe", None, ("tensor", "dp"), None),
        P("pipe", None, ("dp", "tensor")),
        P("pipe", ("dp", "tensor"), None),
    )
    out_specs = (
        P("pipe", ("dp", "tensor"), None),
        P("pipe", ("dp", "tensor"), None),
        P("pipe", "dp", None, "tensor"),
        P("pipe", ("tensor", "dp"), None),
        P("pipe", None, "dp", "tensor"),
        P("pipe", None, ("tensor", "dp"), None),
        P("pipe", None, ("dp", "tensor")),
        P("pipe", ("dp", "tensor"), None),
    )
    return jax.shard_map(local, mesh=mesh, in_specs=in_specs, out_specs=out_specs, check_vma=False)
```

```python
import functools

import jax
import jax.numpy as jnp
from jax import lax
from jax.experimental import pallas as pl
from jax.experimental.pallas import tpu as pltpu
from jax.sharding import PartitionSpec as P

HEAD_DIM = 64
EPSILON = 1e-06
NEGATIVE = -1e30
EXACT = lax.Precision.HIGHEST
EXTRA = 128
BF = jnp.bfloat16
F32 = jnp.float32
VM = pl.BlockSpec(memory_space=pltpu.VMEM)
SM = pl.BlockSpec(memory_space=pltpu.SMEM)
HB = pl.BlockSpec(memory_space=pltpu.HBM)
AFTER = pl.BlockSpec(memory_space=pl.ANY)
RAW = 2
VH = pl.BlockSpec(memory_space=pltpu.VMEM)
FAR = True
PIPE, MINE, REP, CORE, SPLIT = range(5)


def dot32(a, b):
    return jnp.dot(a, b, preferred_element_type=F32)


def dot_nt(a, b):
    return lax.dot_general(a, b, (((1,), (1,)), ((), ())), preferred_element_type=F32)


def dot_tn(a, b):
    return lax.dot_general(a, b, (((0,), (0,)), ((), ())), preferred_element_type=F32)


def split3(value):
    high = value.astype(BF)
    rest = value - high.astype(F32)
    mid = rest.astype(BF)
    return high, mid, (rest - mid.astype(F32)).astype(BF)


def parts_nt(a, b):
    return sum(dot_nt(a, part) for part in split3(b))


def norm_scale(x):
    return lax.rsqrt(jnp.mean(x * x, axis=-1, keepdims=True) + EPSILON)


def norm_back(x, scale, gain, grad):
    weighted = grad * gain
    grad_x = scale * weighted - x * (scale * scale * scale) * jnp.mean(
        x * weighted, axis=-1, keepdims=True
    )
    return grad_x, jnp.sum(grad * (x * scale), axis=0, keepdims=True)


def pinned(value):
    return pltpu.with_memory_space_constraint(value, pltpu.HBM)


def kernel_call(body, name, outs, ins, specs, scratch=(), cost=1, room=24, hbm_outs=False):
    ins = [
        pinned(each) if spec is HB or spec is VH else each
        for each, spec in zip(ins, specs, strict=True)
    ]
    far = [hbm_outs or len(each) > 2 for each in outs]
    return pl.pallas_call(
        body,
        name=name,
        out_shape=[
            (pltpu.HBM if away else jax.ShapeDtypeStruct)(each[0], each[1])
            for each, away in zip(outs, far, strict=True)
        ],
        in_specs=specs,
        out_specs=[HB if each[2:] == (RAW,) else VM for each in outs],
        scratch_shapes=list(scratch),
        compiler_params=pltpu.CompilerParams(vmem_limit_bytes=room << 20),
        cost_estimate=pl.CostEstimate(
            flops=int(cost * 1.1e9), bytes_accessed=0, transcendentals=0
        ),
    )(*ins)


def eye(count):
    rows = lax.broadcasted_iota(jnp.int32, (count, count), 0)
    return (rows == lax.broadcasted_iota(jnp.int32, (count, count), 1)).astype(F32).astype(BF)


def send_kernel(per, facts, inputs, cotangent, dealing, routes, order, router, gains, out, hot_out):
    rows, width = inputs.shape
    place = dealing[...]
    target = place >> 8
    numbers = [place & 255, routes[...], order[...] >> 8, order[...] & 255, target]
    numbers = [each.astype(F32) for each in numbers]
    numbers = jnp.concatenate(numbers + [jnp.zeros((EXTRA - 5, rows), F32)], axis=0)
    columns = dot_nt(eye(rows), numbers.astype(BF))
    targets = target.astype(F32)
    before = lax.broadcasted_iota(jnp.int32, (rows, rows), 0)
    after = lax.broadcasted_iota(jnp.int32, (rows, rows), 1)
    ahead = (columns[:, 4:5] == targets) & (before < after)
    slot = targets * per + jnp.sum(ahead.astype(F32), axis=0, keepdims=True)
    hot = (before.astype(F32) == slot).astype(F32).astype(BF)
    hot_out[...] = hot
    chosen = jnp.where(facts[PIPE] == 0, inputs[...], cotangent[...])
    out[:, :width] = dot32(hot, chosen).astype(BF)
    lane = lax.broadcasted_iota(jnp.int32, (rows, EXTRA), 1)
    tail = dot32(hot, jnp.where(lane < 4, columns, 0.0).astype(BF))
    parts = []
    for values in (router[...], gains[...]):
        high = values.astype(BF).astype(F32)
        mid = (values - high).astype(BF).astype(F32)
        parts += [high, mid, values - high - mid]
    count = gains.shape[1]
    blank = jnp.zeros((4, count), F32)
    block = jnp.concatenate([blank] + parts + [jnp.zeros((10, count), F32)], axis=0)
    block = dot_nt(eye(count), block.astype(BF))
    groups = [block[at * per : (at + 1) * per, :] for at in range(3)]
    block = jnp.concatenate(groups + [jnp.zeros((per, 32), F32)], axis=1)
    block = jnp.concatenate([block] * (rows // per), axis=0)
    out[:, width:] = (tail + block).astype(BF)


def deal_kernel(facts, both, own_rows, slots, onehot, place):
    width = own_rows.shape[1]
    pack = own_rows.shape[0]
    total = both.shape[0]
    half = pack // 2
    core = facts[CORE].astype(F32)
    numbers = both[:, width:]
    spot = numbers[:, 0:1].astype(F32)
    source = (lax.broadcasted_iota(jnp.int32, (total, 1), 0) >= pack).astype(F32)
    upper = (spot >= half).astype(F32)
    where = jnp.where(upper == core, source * half + spot - upper * half, -1.0)
    spots = lax.broadcasted_iota(jnp.int32, (total, pack), 1).astype(F32)
    hot = (spots == where).astype(F32).astype(BF)
    place[...] = hot
    own_rows[...] = dot_tn(hot, both[:, :width]).astype(BF)
    mine = dot_tn(hot, numbers)
    across = dot_nt(eye(EXTRA), mine.astype(BF))
    expert_col, expert_row = mine[:, 1:2], across[1:2, :]
    order_col = mine[:, 2:3] * 256.0 + mine[:, 3:4]
    order_row = across[2:3, :] * 256.0 + across[3:4, :]
    ahead = (expert_col == expert_row) & (order_col < order_row)
    rank = jnp.sum(ahead.astype(F32), axis=0, keepdims=True).astype(jnp.int32)
    experts = 4
    cap = pack // experts
    block = jnp.bitwise_xor(expert_row.astype(jnp.int32), facts[MINE])
    slot = jnp.where(rank < cap, block * cap + rank, -1)
    slots[...] = (lax.broadcasted_iota(jnp.int32, (pack, pack), 0) == slot).astype(F32).astype(BF)
    onehot[...] = (
        lax.broadcasted_iota(jnp.int32, (pack, EXTRA), 1) == expert_col.astype(jnp.int32)
    ).astype(F32)


def mask_of(facts, first, rows, columns):
    query = lax.broadcasted_iota(jnp.int32, (rows, columns), 0) + first
    key = lax.broadcasted_iota(jnp.int32, (rows, columns), 1)
    split = facts[SPLIT]
    return ((query < split) == (key < split)) & (key <= query)


def turned_mask(facts, first, rows, columns):
    key = lax.broadcasted_iota(jnp.int32, (rows, columns), 0) + first
    query = lax.broadcasted_iota(jnp.int32, (rows, columns), 1) + first
    split = facts[SPLIT]
    return ((query < split) == (key < split)) & (key <= query)


def stacked(refs):
    return jnp.concatenate([ref[...] for ref in refs], axis=0)


def flipped(params):
    flat = dot_nt(eye(EXTRA), params[...])
    return flat[16:18] + flat[18:20] + flat[20:22]


def weight_copies(sources, scratch, sems, width, cols):
    copies = []
    for at in range(2):
        each = []
        for start, rows in (*((part * width, width) for part in range(3)), (3 * width, 2 * cols)):
            spot = pl.ds(start, rows)
            each.append(
                pltpu.make_async_copy(
                    sources[at].at[spot], scratch.at[at, spot], sems.at[4 * at + len(each)]
                )
            )
        copies.append(each)
    return copies


def gate_of(up):
    return jnp.sum(up[:, up.shape[1] - EXTRA :].astype(F32), axis=-1, keepdims=True)


def attn_kernel(second, dropped, facts, *refs):
    refs = list(refs)
    weights, sems = refs[-2:] if second else refs[-5:-3]
    refs = refs[:-2] if second else refs[:-5] + refs[-3:]
    own_rows = refs.pop(0)
    if second:
        up = refs.pop(0)
        slots_in = [refs.pop(0) for _ in range(4)]
    attn_own, attn_other, params, slots, onehot = (refs.pop(0) for _ in range(5))
    refs = refs[dropped:]
    if second:
        mid, attn_in, proj, mixed, mlp_in, probs = (refs.pop(0) for _ in range(6))
    else:
        send_up = refs.pop(0)
        proj, mixed, mid = refs[4:]
    blocks = [refs.pop(0) for _ in range(4)]
    pack, width = own_rows.shape
    cols = attn_own.shape[1]
    cap = pack // 4
    copies = weight_copies((attn_own, attn_other), weights, sems, width, cols)
    for each in copies:
        for copy in each:
            copy.start()
    gains = flipped(params)
    hot = slots[...]
    if second:
        stream = refs.pop(0)
        grads = [refs.pop(0) for _ in range(4)]
        came = up[:, :width].astype(F32) + gate_of(up) * dot_tn(hot, stacked(slots_in))
        rows = jnp.where(facts[PIPE] == 0, own_rows[...], came.astype(BF))
        stream[...] = rows
    else:
        rows = own_rows[...]
    x = rows.astype(F32)
    normed = (x * norm_scale(x) * gains[0:1, :]).astype(BF)
    if second:
        attn_in[...] = normed
    half = pack // 2
    upper = mask_of(facts, 0, half, half)
    lower = mask_of(facts, half, half, pack)
    lane = lax.broadcasted_iota(jnp.int32, (pack, EXTRA), 1)
    totals = jnp.zeros((pack, EXTRA), F32)
    for at in range(2):
        for part in range(3):
            copies[at][part].wait()
            proj[at, part] = dot32(
                normed, weights[at, part * width : (part + 1) * width, :]
            ).astype(BF)
        for pair in range(cols // EXTRA):
            lanes = slice(pair * EXTRA, (pair + 1) * EXTRA)
            query = proj[at, 0, :, lanes] * jnp.asarray(HEAD_DIM ** (-0.5), BF)
            key, value = proj[at, 1, :, lanes], proj[at, 2, :, lanes]
            parts = []
            for side in range(2):
                chosen = jnp.where((lane >= HEAD_DIM) == (side == 1), query, 0)
                head = 8 + (at * cols + pair * EXTRA) // HEAD_DIM + side
                results = []
                for first, count, allowed in ((0, half, upper), (half, pack, lower)):
                    scores = dot_nt(chosen[first : first + half, :], key[:count, :])
                    scores = jnp.where(allowed, scores, NEGATIVE)
                    peak = jnp.max(scores, axis=-1, keepdims=True)
                    share = jnp.exp(scores - peak)
                    total = jnp.sum(share, axis=-1, keepdims=True)
                    results.append(
                        (dot32(share.astype(BF), value[:count, :]) * (1.0 / total), peak + jnp.log(total))
                    )
                parts.append(jnp.concatenate([each[0] for each in results], axis=0))
                if second:
                    level = jnp.concatenate([each[1] for each in results], axis=0)
                    totals = jnp.where(lane == head, level, totals)
            spot = at * cols + pair * EXTRA
            mixed[:, spot : spot + EXTRA] = jnp.where(lane < HEAD_DIM, *parts).astype(BF)
    base = 3 * width
    copies[0][3].wait()
    copies[1][3].wait()
    for side in range(2):
        rows_at = slice(base + side * cols, base + (side + 1) * cols)
        lanes = slice(side * cols, (side + 1) * cols)
        mid[:, lanes] = (
            x[:, lanes]
            + dot32(mixed[:, :cols], weights[0, rows_at, :])
            + dot32(mixed[:, cols:], weights[1, rows_at, :])
        )
    m = mid[:, :width]
    low = (m * norm_scale(m) * gains[1:2, :]).astype(BF)
    if second:
        mlp_in[...] = low
    logits = dot32(low, params[...])
    lane = lax.broadcasted_iota(jnp.int32, logits.shape, 1)
    logits = sum(pltpu.roll(logits, EXTRA - 4 * at, 1) for at in (1, 2, 3))
    logits = jnp.where(lane < 4, logits, NEGATIVE)
    rel = jnp.exp(logits - jnp.max(logits, axis=-1, keepdims=True))
    share = rel / jnp.sum(rel, axis=-1, keepdims=True)
    if second:
        probs[...] = share + totals
    gate = jnp.sum(share * onehot[...], axis=-1, keepdims=True)
    if second:
        mid[:, width:] = jnp.broadcast_to(gate, (pack, EXTRA))
    else:
        send_up[:, :width] = m.astype(BF)
        high = gate.astype(BF).astype(F32)
        middle = (gate - high).astype(BF).astype(F32)
        parts = jnp.where(lane == 1, middle, jnp.where(lane == 2, gate - high - middle, 0.0))
        send_up[:, width:] = jnp.where(lane == 0, high, parts).astype(BF)
    for step in range(4):
        blocks[step][...] = dot32(hot[step * cap : (step + 1) * cap, :], low).astype(BF)
    if second:
        weighted = (gate * own_rows[...].astype(F32)).astype(BF)
        for step in range(4):
            grads[step][...] = dot32(hot[step * cap : (step + 1) * cap, :], weighted).astype(BF)


def attn_forward(facts, own_rows, weights, plan, came=None, after=()):
    attn_own, attn_other, params = weights
    slots, onehot = plan
    pack, width = own_rows.shape
    cols = attn_own.shape[1]
    cap = pack // 4
    second = came is not None
    ins = [facts, own_rows] + (list(came) if second else [])
    specs = [SM, VH] + ([VH] if second else []) + [VM] * (len(ins) - (3 if second else 2))
    specs += [HB] * 2 + [VH] * 3 + [AFTER] * len(after)
    ins += [attn_own, attn_other, params, slots, onehot, *after]
    if second:
        outs = [
            ((pack, width + EXTRA), F32, FAR),
            ((pack, width), BF, FAR),
            ((2, 3, pack, cols), BF, FAR),
            ((pack, width), BF, FAR),
            ((pack, width), BF, FAR),
            ((pack, EXTRA), F32, FAR),
        ]
    else:
        outs = [((pack, width + EXTRA), BF, FAR)]
    outs += [((cap, width), BF)] * 4
    if second:
        outs += [((pack, width), BF, FAR)] + [((cap, width), BF)] * 4
    return kernel_call(
        functools.partial(attn_kernel, second, len(after)),
        "attn_second" if second else "attn_first",
        outs,
        ins,
        specs,
        [pltpu.VMEM((2, 3 * width + 2 * cols, cols), BF), pltpu.SemaphoreType.DMA((8,))]
        + ([] if second else [
            pltpu.VMEM((2, 3, pack, cols), BF),
            pltpu.VMEM((pack, width), BF),
            pltpu.VMEM((pack, width), F32),
        ]),
        cost=8,
    )


def attn_back_kernel(first, dropped, facts, *refs):
    refs = list(refs)
    weights, sems = refs[-2:]
    refs = refs[:-2]
    grad_out = refs.pop(0)
    if first:
        up = refs.pop(0)
    else:
        own_rows = refs.pop(0)
        refs = refs[dropped:]
    grad_slots = [refs.pop(0) for _ in range(4)]
    stream, mid, proj, mlp_in, probs, mixed = (refs.pop(0) for _ in range(6))
    attn_own, attn_other, params, slots, onehot = (refs.pop(0) for _ in range(5))
    grad_stream = refs.pop(0)
    if first:
        blocks = [refs.pop(0) for _ in range(4)]
        grad_proj = refs.pop(0)
    else:
        grad_proj, grad_low, tiny = (refs.pop(0) for _ in range(3))
    pack, width = stream.shape
    cols = attn_own.shape[1]
    cap = pack // 4
    copies = weight_copies((attn_own, attn_other), weights, sems, width, cols)
    for part in (3, 0, 1, 2):
        for each in copies:
            each[part].start()
    gains = flipped(params)
    hot = slots[...]
    rows = grad_out[...]
    if not first:
        rows = jnp.where(facts[PIPE] == 0, rows, own_rows[...])
    g = rows.astype(F32)
    slot_rows = stacked(grad_slots)
    at_tokens = dot_tn(hot, slot_rows[:, width:])
    lane = lax.broadcasted_iota(jnp.int32, (pack, EXTRA), 1)
    shares = jnp.where(lane < 4, probs[...], 0.0)
    grad_logits = (at_tokens[:, 0:1] + at_tokens[:, 1:2]) * (onehot[...] - shares)
    m = mid[:, :width]
    wide = sum(pltpu.roll(grad_logits, 4 * at, 1) for at in (1, 2, 3))
    grad_mlp = dot_tn(hot, slot_rows[:, :width]) + sum(
        dot_nt(part, params[...]) for part in split3(wide)
    )
    grad_norm, gain_two = norm_back(m, norm_scale(m), gains[1:2, :], grad_mlp)
    grad_mid = g + grad_norm
    low = grad_mid.astype(BF)
    base = 3 * width
    copies[0][3].wait()
    copies[1][3].wait()
    grad_mixed = jnp.concatenate(
        [
            (
                dot_nt(low[:, :cols], weights[at, base : base + cols, :])
                + dot_nt(low[:, cols:], weights[at, base + cols : base + 2 * cols, :])
            ).astype(BF)
            for at in range(2)
        ],
        axis=1,
    )
    heads = lax.broadcasted_iota(jnp.int32, (EXTRA, width), 0)
    heads = heads == lax.broadcasted_iota(jnp.int32, (EXTRA, width), 1) // HEAD_DIM + 8
    inner = parts_nt(heads.astype(F32).astype(BF), grad_mixed.astype(F32) * mixed[...].astype(F32))
    levels = parts_nt(eye(EXTRA), probs[...])
    half = pack // 2
    blocks_of = (
        (0, pack, turned_mask(facts, 0, half, pack)),
        (half, half, turned_mask(facts, half, half, half)),
    )
    grad_in = jnp.zeros((pack, width), F32)
    for at in range(2):
        for pair in range(cols // EXTRA):
            lanes = slice(pair * EXTRA, (pair + 1) * EXTRA)
            spot = at * cols + pair * EXTRA
            scale = jnp.asarray(HEAD_DIM ** (-0.5), BF)
            query = proj[at, 0, :, lanes] * scale
            key, value = proj[at, 1, :, lanes], proj[at, 2, :, lanes]
            grad_pair = grad_mixed[:, spot : spot + EXTRA]
            grad_query = jnp.zeros((pack, EXTRA), F32)
            grad_key = [jnp.zeros((half, EXTRA), F32) for _ in range(2)]
            grad_value = [jnp.zeros((half, EXTRA), F32) for _ in range(2)]
            for side in range(2):
                keep = (lane >= HEAD_DIM) == (side == 1)
                query_one = jnp.where(keep, query, 0)
                key_one = jnp.where(keep, key, 0)
                grad_one = jnp.where(keep, grad_pair, 0)
                head = 8 + spot // HEAD_DIM + side
                for at_block, (begin, count, allowed) in enumerate(blocks_of):
                    rows_at = slice(begin, begin + half)
                    after = slice(begin, begin + count)
                    scores = dot_nt(key[rows_at, :], query_one[after, :])
                    share = jnp.exp(scores - levels[head : head + 1, after])
                    share = jnp.where(allowed, share, 0.0)
                    grad_share = dot_nt(value[rows_at, :], grad_one[after, :])
                    grad_scores = share * (grad_share - inner[head : head + 1, after])
                    grad_scores = grad_scores.astype(BF)
                    grad_key[at_block] += dot32(grad_scores, query_one[after, :])
                    grad_value[at_block] += dot32(share.astype(BF), grad_one[after, :])
                    more = dot_tn(grad_scores, key_one[rows_at, :])
                    if begin:
                        more = jnp.concatenate([jnp.zeros((half, EXTRA), F32), more], axis=0)
                    grad_query += more
            grad_proj[at, 0, :, lanes] = (grad_query * HEAD_DIM ** (-0.5)).astype(BF)
            for at_block in range(2):
                rows_at = slice(at_block * half, (at_block + 1) * half)
                grad_proj[at, 1, rows_at, lanes] = grad_key[at_block].astype(BF)
                grad_proj[at, 2, rows_at, lanes] = grad_value[at_block].astype(BF)
        for part in range(3):
            copies[at][part].wait()
            grad_in += dot_nt(
                grad_proj[at, part], weights[at, part * width : (part + 1) * width, :]
            )
    x = stream[...].astype(F32)
    grad_norm, gain_one = norm_back(x, norm_scale(x), gains[0:1, :], grad_in)
    result = (grad_mid + grad_norm).astype(BF)
    grad_stream[...] = result
    if first:
        weighted = (gate_of(up) * result.astype(F32)).astype(BF)
        for step in range(4):
            blocks[step][...] = dot32(hot[step * cap : (step + 1) * cap, :], weighted).astype(BF)
    else:
        grad_low[...] = low
        high = grad_logits.astype(BF)
        rest = (grad_logits - high.astype(F32)).astype(BF)
        lane = lax.broadcasted_iota(jnp.int32, (width, EXTRA), 1)
        both = dot_tn(mlp_in[...], high) + dot_tn(mlp_in[...], rest)
        both = jnp.where(lane < 4, both, 0.0)
        high = both.astype(BF).astype(F32)
        flat = [gain_one.astype(BF).astype(F32), gain_two.astype(BF).astype(F32)]
        flat += [gain_one - flat[0], gain_two - flat[1]]
        flat = jnp.concatenate(flat + [jnp.zeros((12, width), F32)], axis=0).astype(BF)
        spot = lax.broadcasted_iota(jnp.int32, (16, EXTRA), 0) + 8
        spot = spot == lax.broadcasted_iota(jnp.int32, (16, EXTRA), 1)
        turned = dot_tn(flat, spot.astype(F32).astype(BF))
        tiny[...] = (high + pltpu.roll(both - high, 4, 1) + turned).astype(BF)


def attn_backward(facts, grad_out, extra, grad_slots, saved, weights, plan, first):
    attn_own, attn_other, params = weights
    slots, onehot = plan
    stream, mid, proj, mlp_in, probs, mixed = saved
    pack, width = stream.shape
    cols = attn_own.shape[1]
    cap = pack // 4
    ins = [facts, grad_out, *extra, *grad_slots, stream, mid, proj, mlp_in, probs, mixed]
    specs = [SM, VH if first else VM, VH] + [AFTER] * (len(extra) - 1)
    specs += [VM] * 4 + [VH] * 6 + [HB] * 2 + [VH] * 3
    ins += [attn_own, attn_other, params, slots, onehot]
    outs = [((pack, width), BF)]
    if first:
        outs += [((cap, width), BF)] * 4
    outs += [((2, 3, pack, cols), BF)]
    if not first:
        outs += [((pack, width), BF), ((width, EXTRA), BF)]
    return kernel_call(
        functools.partial(attn_back_kernel, first, len(extra) - 1),
        "attn_back_first" if first else "attn_back_second",
        outs,
        ins,
        specs,
        [pltpu.VMEM((2, 3 * width + 2 * cols, cols), BF), pltpu.SemaphoreType.DMA((8,))],
        cost=13,
    )


def gelu_both(u):
    square = u * u
    t = jnp.tanh(0.7978845608028654 * u * (1.0 + 0.044715 * square))
    half = 0.5 * (1.0 + t)
    inner = 0.7978845608028654 * (1.0 + 3.0 * 0.044715 * square)
    return half + 0.5 * u * (1.0 - t * t) * inner, half * u


def bring(facts, pieces, places, scratch, sems):
    copies = []
    for piece, spots in zip(pieces, places, strict=True):
        for source, target, rows, column, columns in spots(facts):
            copies.append(
                pltpu.make_async_copy(
                    piece.at[pl.ds(source, rows), pl.ds(0, columns)],
                    scratch.at[pl.ds(target, rows), pl.ds(column, columns)],
                    sems.at[len(copies)],
                )
            )
    for copy in copies:
        copy.start()
    return copies


TILE = 256


def expert_kernel(keep, places_in, places_out, facts, *refs):
    refs = list(refs)
    blocks = [refs.pop(0) for _ in range(8)]
    pieces = [refs.pop(0) for _ in range(len(places_in))]
    if keep:
        targets = [refs.pop(0) for _ in range(3)]
        own, other, w_in, w_out, sems_in, sems_out, act, rows, pre, sems = refs
    else:
        own, other, w_in, w_out, sems_in, sems_out, act, rows = refs
    arriving = bring(facts, pieces, places_in, w_in, sems_in)
    later = bring(facts, pieces, places_out, w_out, sems_out)
    cap = blocks[0].shape[0]
    for at, block in enumerate(blocks):
        rows[at * cap : (at + 1) * cap, :] = block[...]
    ff = w_in.shape[1]
    width = w_in.shape[0]
    if keep:
        leaving = pltpu.make_async_copy(rows, targets[2], sems.at[2, 0])
        leaving.start()

    def tile_copies(tile):
        lanes = pl.ds(pl.multiple_of(tile * TILE, TILE), TILE)
        return [
            pltpu.make_async_copy(
                source.at[:, lanes], targets[at].at[:, lanes], sems.at[at, tile]
            )
            for at, source in enumerate((pre, act))
        ]

    for copy in arriving:
        copy.wait()

    @pl.loop(0, ff // TILE, unroll=2)
    def _(tile):
        lanes = pl.ds(pl.multiple_of(tile * TILE, TILE), TILE)
        value = dot32(rows[...], w_in[:, lanes])
        slope, result = gelu_both(value)
        act[:, lanes] = result.astype(BF)
        if keep:
            pre[:, lanes] = slope.astype(BF)
            for copy in tile_copies(tile):
                copy.start()

    for copy in later:
        copy.wait()
    count = 4 * cap

    @pl.loop(0, width // TILE, unroll=1)
    def _(tile):
        lanes = pl.ds(pl.multiple_of(tile * TILE, TILE), TILE)
        value = dot32(act[...], w_out[:, lanes])
        own[:, lanes] = value[:count]
        other[:, lanes] = value[count:].astype(BF)

    if keep:
        leaving.wait()

        @pl.loop(0, ff // TILE, unroll=2)
        def _(tile):
            for copy in tile_copies(tile):
                copy.wait()


def halves(value, shape):
    high = value.astype(BF).astype(F32)
    lane = lax.broadcasted_iota(jnp.int32, shape, 1)
    return jnp.where(lane == 0, high, jnp.where(lane == 1, value - high, 0.0))


def expert_back_kernel(chosen, places_in, places_out, facts, *refs):
    refs = list(refs)
    blocks = [refs.pop(0) for _ in range(1 if chosen else 2)]
    pre, own_out, other_out = (refs.pop(0) for _ in range(3))
    pieces = [refs.pop(0) for _ in range(len(places_in))]
    grad_pre, own, other = (refs.pop(0) for _ in range(3))
    rows = blocks[0] if chosen else refs.pop(0)
    w_in, w_out, sems_in, sems_out = refs
    arriving = bring(facts, pieces, places_out, w_out, sems_out)
    later = bring(facts, pieces, places_in, w_in, sems_in)
    if not chosen:
        half = rows.shape[0] // 2
        for at, block in enumerate(blocks):
            rows[at * half : (at + 1) * half, :] = block[...]
    for copy in arriving:
        copy.wait()
    ff = w_in.shape[1]
    width = w_in.shape[0]
    count = rows.shape[0] // 2

    @pl.loop(0, ff // TILE, unroll=True)
    def _(tile):
        lanes = pl.ds(pl.multiple_of(tile * TILE, TILE), TILE)
        value = dot_nt(rows[...], w_out[lanes, :])
        grad_pre[:, lanes] = (value * pre[:, lanes].astype(F32)).astype(BF)

    for copy in later:
        copy.wait()

    @pl.loop(0, width // TILE, unroll=True)
    def _(tile):
        lanes = pl.ds(pl.multiple_of(tile * TILE, TILE), TILE)
        value = dot_nt(grad_pre[...], w_in[lanes, :])
        own[:, lanes] = value[:count]
        other[:, lanes] = value[count:].astype(BF)

    pull = jnp.sum(rows[:count, :].astype(F32) * own_out[...], axis=-1, keepdims=True)
    own[:, width:] = halves(pull, (count, EXTRA))
    pull = jnp.sum(
        rows[count:, :].astype(F32) * other_out[...].astype(F32), axis=-1, keepdims=True
    )
    other[:, width:] = halves(pull, (count, EXTRA)).astype(BF)


def expert_scratch(width, ff, places):
    numbers = jnp.zeros((8,), jnp.int32)
    sizes = [sum(len(spots(numbers)) for spots in each) for each in places]
    return (
        [pltpu.VMEM((width, ff), BF), pltpu.VMEM((ff, width), BF)],
        [pltpu.SemaphoreType.DMA((size,)) for size in sizes],
    )


def expert_call(name, keep, facts, blocks, pieces, places, width, ff):
    count = 4 * blocks[0].shape[0]
    ins = [facts, *blocks, *pieces]
    kept = [((2 * count, ff), BF, RAW)] * 2 + [((2 * count, width), BF, RAW)] if keep else []
    buffers, sems = expert_scratch(width, ff, places)
    scratch = [*buffers, *sems]
    scratch += [pltpu.VMEM((2 * count, ff), BF), pltpu.VMEM((2 * count, width), BF)]
    if keep:
        scratch.append(pltpu.VMEM((2 * count, ff), BF))
        scratch.append(pltpu.SemaphoreType.DMA((3, ff // TILE)))
    return kernel_call(
        functools.partial(expert_kernel, keep, *places),
        name,
        kept + [((count, width), F32), ((count, width), BF)],
        ins,
        [SM] + [VM] * 8 + [HB] * len(pieces),
        scratch,
        cost=7,
    )


def expert_back_call(name, facts, blocks, saved, pieces, places, width, ff):
    chosen = len(blocks) == 1
    count = blocks[0].shape[0] * len(blocks) // 2
    wide = width + EXTRA
    ins = [facts, *blocks, *saved, *pieces]
    buffers, sems = expert_scratch(width, ff, places)
    outs = [((2 * count, ff), BF), ((count, wide), F32), ((count, wide), BF)]
    if not chosen:
        outs.append(((2 * count, width), BF, FAR))
    return kernel_call(
        functools.partial(expert_back_kernel, chosen, *places),
        name,
        outs,
        ins,
        [SM] + ([VH] if chosen else [VM] * 2) + [VH, VM, VM] + [HB] * len(pieces),
        [*buffers, *sems],
        cost=8,
    )


def fold_kernel(own, other, *blocks):
    blocks = blocks[-4:]
    cap = blocks[0].shape[0]
    width = own.shape[1] // TILE * TILE
    for step, block in enumerate(blocks):
        rows = slice(step * cap, (step + 1) * cap)
        block[:, :width] = (own[rows, :width] + other[rows, :width].astype(F32)).astype(BF)
        if own.shape[1] > width:
            both = own[rows, width:] + other[rows, width:].astype(F32)
            block[:, width:] = halves(both[:, 0:1] + both[:, 1:2], (cap, EXTRA)).astype(BF)


def fold(own, other, name, after=()):
    count, width = own.shape
    cap = count // 4
    return kernel_call(
        fold_kernel, name, [((cap, width), BF)] * 4, [own, other, *after], [VM, VM] + [AFTER] * len(after)
    )


def return_kernel(merge, *refs):
    refs = list(refs)
    rows = refs.pop(0)
    if merge:
        hot = refs.pop(0)
        slots_in = [refs.pop(0) for _ in range(4)]
        width = slots_in[0].shape[1]
        values = rows[:, :width] + rows[:, width : width + 1] * dot_tn(hot[...], stacked(slots_in))
        values = values.astype(BF)
    else:
        values = rows[...]
    place, facts = refs[:2]
    own, other = refs[-2:]
    pack = own.shape[0]
    core = facts[CORE]
    own[...] = dot32(place[pl.ds(pl.multiple_of(core * pack, pack), pack), :], values).astype(BF)
    other[...] = dot32(
        place[pl.ds(pl.multiple_of((1 - core) * pack, pack), pack), :], values
    ).astype(BF)


def sent_rows(facts, merge, rows, extra, place, width, after):
    pack = place.shape[1]
    ins = [rows, *extra, place, facts, *after]
    outs = [((pack, width), BF)] * 2
    return kernel_call(
        functools.partial(return_kernel, merge),
        "return_merged" if merge else "return_rows",
        outs,
        ins,
        ([VH, VH] + [VM] * 4 if merge else [VM]) + [VH, SM] + [AFTER] * len(after),
        cost=1,
    )


def run_copies(moves, sems):
    copies = [
        pltpu.make_async_copy(source, target, sems.at[at])
        for at, (source, target) in enumerate(moves)
    ]
    for copy in copies:
        copy.start()
    for copy in copies:
        copy.wait()


def rows_kernel(*refs):
    cap = refs[0].shape[0]
    out = refs[-1]
    for at, ref in enumerate(refs[:4]):
        out[at * cap : (at + 1) * cap, :] = ref[...]


def joined_rows(blocks, after):
    cap, width = blocks[0].shape
    return kernel_call(
        rows_kernel,
        "join_rows",
        [((4 * cap, width), BF)],
        [*blocks, *after],
        [VM] * 4 + [AFTER] * len(after),
    )[0]


def ordered_kernel(*refs):
    del refs


def ordered(value, after):
    return pl.pallas_call(
        ordered_kernel,
        name="ordered",
        out_shape=pltpu.HBM(value.shape, value.dtype),
        in_specs=[HB] + [AFTER] * len(after),
        out_specs=HB,
        input_output_aliases={0: 0},
        compiler_params=pltpu.CompilerParams(vmem_limit_bytes=1 << 20),
        cost_estimate=pl.CostEstimate(flops=0, bytes_accessed=0, transcendentals=0),
    )(pinned(value), *after)


def restore_kernel(hot, back, activations, grads, tiny):
    width = activations.shape[1]
    activations[...] = dot_tn(hot[...], back[:, :width]).astype(BF)
    grads[...] = dot_tn(hot[...], back[:, width : 2 * width]).astype(BF)
    rows = tiny.shape[0]
    total = jnp.zeros(tiny.shape, F32)
    for at in range(back.shape[0] // rows):
        total += back[at * rows : (at + 1) * rows, 2 * width :].astype(F32)
    tiny[...] = total


def finish_kernel(*refs):
    pieces, attn, attn_out = refs[:4], refs[4], refs[5]
    _, shard, cols = attn.shape
    total = sum(piece[...].astype(F32) for piece in pieces)
    for part in range(3):
        attn[part] = total[part * shard : (part + 1) * shard, :]
    rows = attn_out.shape[0]
    for side in range(2):
        spot = 3 * shard + side * rows
        attn_out[:, side * cols : (side + 1) * cols] = total[spot : spot + rows, :]


def stack_kernel(count, facts, *refs):
    pieces, out, sems = refs[:count], refs[-2], refs[-1]
    run_copies(
        [
            (piece, out.at[jnp.bitwise_xor(facts[MINE], step)])
            for step, piece in enumerate(pieces)
        ],
        sems,
    )


def stack_pieces(facts, pieces, after):
    count = len(pieces)
    return kernel_call(
        functools.partial(stack_kernel, count),
        "stack_pieces",
        [((count, *pieces[0].shape), BF)],
        [facts, *pieces, *after],
        [SM] + [HB] * count + [AFTER] * len(after),
        [pltpu.SemaphoreType.DMA((count,))],
        room=12,
        hbm_outs=True,
    )[0]


def gather_kernel(facts, near, far, *refs):
    out, sems = refs[-2:]
    groups = near.shape[0]
    moves = []
    for rep, source in ((facts[REP], near), (1 - facts[REP], far)):
        for part in range(3):
            moves.append(
                (
                    source.at[:, pl.ds(2 * part, 2)],
                    out.at[pl.ds(part * groups, groups), pl.ds(2 * rep, 2)],
                )
            )
        for side in range(2):
            for group in range(groups):
                moves.append(
                    (
                        source.at[group, 6 + side],
                        out.at[3 * groups + 2 * side + group // 2, group % 2 * 2 + rep],
                    )
                )
    run_copies(moves, sems)


def pack_attn_kernel(attn, attn_out, bundle, sems):
    parts, shard, cols = attn.shape
    rows = attn_out.shape[0]
    moves = [(attn.at[part], bundle.at[pl.ds(part * shard, shard)]) for part in range(parts)]
    for side in range(2):
        moves.append(
            (
                attn_out.at[:, pl.ds(side * cols, cols)],
                bundle.at[pl.ds(parts * shard + side * rows, rows)],
            )
        )
    run_copies(moves, sems)


def pack_attn(attn, attn_out):
    parts, shard, cols = attn.shape
    rows = attn_out.shape[0]
    return kernel_call(
        pack_attn_kernel,
        "pack_attn",
        [((parts * shard + 2 * rows, cols), BF)],
        [attn, attn_out],
        [HB] * 2,
        [pltpu.SemaphoreType.DMA((parts + 2,))],
        room=12,
        hbm_outs=True,
    )[0]


def pack_expert_kernel(steps, facts, w_in, w_out, *refs):
    blocks, sems = refs[-1 - len(steps) : -1], refs[-1]
    in_rows, out_rows, width = w_in.shape[1], w_out.shape[1], w_out.shape[2]
    moves = []
    for step, block in zip(steps, blocks, strict=True):
        at = jnp.bitwise_xor(facts[MINE], step)
        for side in range(2):
            moves.append(
                (
                    w_in.at[at, :, pl.ds(side * width, width)],
                    block.at[pl.ds(side * in_rows, in_rows)],
                )
            )
        moves.append((w_out.at[at], block.at[pl.ds(2 * in_rows, out_rows)]))
    run_copies(moves, sems)


def pack_expert(facts, w_in, w_out, steps, after=()):
    block = (2 * w_in.shape[1] + w_out.shape[1], w_out.shape[2])
    return kernel_call(
        functools.partial(pack_expert_kernel, steps),
        "pack_expert",
        [(block, BF)] * len(steps),
        [facts, w_in, w_out, *after],
        [SM, HB, HB] + [AFTER] * len(after),
        [pltpu.SemaphoreType.DMA((3 * len(steps),))],
        room=12,
        hbm_outs=True,
    )


SPLIT_ORDER = (2, 3, 1, 0)


def expert_out_grad_kernel(split, dropped, facts, *refs):
    blocks, refs = refs[:8], refs[8:]
    kept, act = refs[:2]
    refs = refs[2 + dropped :]
    rows, refs = refs[0], refs[1:]
    cap = blocks[0].shape[0]
    for at, block in enumerate(blocks):
        spot = slice(at * cap, (at + 1) * cap)
        rows[spot, :] = jnp.where(facts[PIPE] == 0, block[...], kept[spot, :])
    ff = act.shape[1]
    grad = refs[-1]

    @pl.loop(0, ff // TILE, unroll=True)
    def _(tile):
        lanes = pl.ds(pl.multiple_of(tile * TILE, TILE), TILE)
        grad[lanes, :] = dot_tn(act[:, lanes], rows[...])

    if split:
        count = ff // 8
        for at, step in enumerate(SPLIT_ORDER):
            owner = jnp.bitwise_xor(facts[MINE], step) * 2
            to = slice(at % 2 * count, (at % 2 + 1) * count)
            for rep, target in ((1 - facts[REP], refs[at // 2]), (facts[REP], refs[2 + at // 2])):
                spot = pl.ds(pl.multiple_of((owner + rep) * count, count), count)
                target[to, :] = grad[spot, :].astype(BF)


def expert_in_grad_kernel(split, dropped, facts, rows, grad_pre, *refs):
    refs = refs[dropped:]
    ff = grad_pre.shape[1]
    width = rows.shape[1]
    grad = refs[-1]

    @pl.loop(0, ff // TILE, unroll=True)
    def _(tile):
        lanes = pl.ds(pl.multiple_of(tile * TILE, TILE), TILE)
        grad[:, lanes] = dot_tn(rows[...], grad_pre[:, lanes])

    if split:
        count = width // 8
        for at, step in enumerate(SPLIT_ORDER):
            owner = jnp.bitwise_xor(facts[MINE], step) * 2
            first = at * 2 * count
            for rep, target in ((1 - facts[REP], refs[0]), (facts[REP], refs[1])):
                spot = pl.ds(pl.multiple_of((owner + rep) * count, count), count)
                target[first : first + count, :] = grad[spot, :width].astype(BF)
                target[first + count : first + 2 * count, :] = grad[spot, width:].astype(BF)


def grad_outs(shape, wire, split, count):
    if split:
        return [(wire, BF, FAR)] * count, [pltpu.VMEM(shape, F32)]
    return [(shape, F32)], []


def expert_out_grads(facts, blocks, kept, act, after, split):
    count, width = kept.shape
    ff = act.shape[1]
    outs, scratch = grad_outs((ff, width), (ff // 4, width), split, 4)
    return kernel_call(
        functools.partial(expert_out_grad_kernel, split, len(after)),
        "expert_out_grads",
        [((count, width), BF, FAR), *outs],
        [facts, *blocks, kept, act, *after],
        [SM] + [VM] * 8 + [VH, VH] + [AFTER] * len(after),
        scratch,
        cost=4,
    )


def expert_in_grads(facts, rows, grad_pre, after, split):
    width = rows.shape[1]
    ff = grad_pre.shape[1]
    outs, scratch = grad_outs((width, ff), (ff // 2, width), split, 2)
    return kernel_call(
        functools.partial(expert_in_grad_kernel, split, len(after)),
        "expert_in_grads",
        outs,
        [facts, rows, grad_pre, *after],
        [SM, VH, VM] + [AFTER] * len(after),
        scratch,
        cost=4,
    )


def owner_kernel(facts, *refs):
    grad_in, grad_out = refs[-2:]
    rows = grad_in.shape[1]
    width = grad_out.shape[2]
    for place, step in enumerate(SPLIT_ORDER):
        at = jnp.bitwise_xor(facts[MINE], step)
        grad_out[at] = refs[place][...].astype(F32)
        piece = refs[4 + place]
        for side in range(2):
            spot = slice(side * rows, (side + 1) * rows)
            grad_in[at, :, side * width : (side + 1) * width] = piece[spot, :].astype(F32)


def owner_grads(facts, pieces, after, in_shape, out_shape):
    return kernel_call(
        owner_kernel,
        "owner_grads",
        [(in_shape, F32), (out_shape, F32)],
        [facts, *pieces, *after],
        [SM] + [VM] * len(pieces) + [AFTER] * len(after),
        cost=4,
    )


def attn_grad_kernel(attn_in, grad_proj, mixed, low, *refs):
    own, other = refs[-2:]
    width = attn_in.shape[1]
    cols = own.shape[1]
    for at, target in ((0, own), (1, other)):
        for part in range(3):
            target[part * width : (part + 1) * width, :] = dot_tn(
                attn_in[...], grad_proj[at, part]
            ).astype(BF)
        for side in range(2):
            spot = 3 * width + side * cols
            target[spot : spot + cols, :] = dot_tn(
                mixed[:, at * cols : (at + 1) * cols], low[:, side * cols : (side + 1) * cols]
            ).astype(BF)


def attn_grads(attn_in, grad_proj, mixed, low, after):
    pack, width = attn_in.shape
    cols = grad_proj.shape[3]
    return kernel_call(
        attn_grad_kernel,
        "attn_grads",
        [((3 * width + 2 * cols, cols), BF)] * 2,
        [attn_in, grad_proj, mixed, low, *after],
        [VH, VM, VH, VM] + [AFTER] * len(after),
        cost=3,
    )


def attn_split_kernel(facts, own, came, *refs):
    sends, keeps = refs[-4:-2], refs[-2:]
    cols = own.shape[1]
    width = 2 * cols
    shard = width // 8
    count = 4 * shard
    for at, step in enumerate(SPLIT_ORDER):
        owner = jnp.bitwise_xor(facts[MINE], step) * 2
        for rep, target, first in (
            (1 - facts[REP], sends[at // 2], at % 2 * count),
            (facts[REP], keeps[at // 2], at % 2 * count),
        ):
            for source, rows, spot in attn_rows(width, shard):
                where = pl.ds(pl.multiple_of(source + (owner + rep) * rows, rows), rows)
                target[first + spot : first + spot + rows, :] = (
                    own[where, :].astype(F32) + came[where, :].astype(F32)
                ).astype(BF)


def sum_kernel(steps, keep, came, *outs):
    outs = outs[-len(steps) :]
    count = outs[0].shape[0]
    for at, out in enumerate(outs):
        rows = slice(at * count, (at + 1) * count)
        both = keep[rows, :].astype(F32) + came[rows, :].astype(F32)
        out[...] = both.astype(out.dtype)


def sum_pieces(steps, keep, came, after=()):
    count = keep.shape[0] // len(steps)
    kinds = [F32 if step == 0 else BF for step in steps]
    return kernel_call(
        functools.partial(sum_kernel, steps),
        "sum_pieces",
        [((count, keep.shape[1]), kind) for kind in kinds],
        [keep, came, *after],
        [VH] * 2 + [AFTER] * len(after),
        cost=0,
    )


def attn_rows(width, shard):
    out = shard // 2
    return (
        (0, shard, 0),
        (width, shard, shard),
        (2 * width, shard, 2 * shard),
        (3 * width, out, 3 * shard),
        (3 * width + width // 2, out, 3 * shard + out),
    )


def attn_split(facts, own, came, after):
    rows, cols = own.shape
    return kernel_call(
        attn_split_kernel,
        "attn_split",
        [((rows // 4, cols), BF, FAR)] * 4,
        [facts, own, came, *after],
        [SM, VM, VM] + [AFTER] * len(after),
        cost=3,
    )


def solution(mesh):
    shape = mesh.shape
    n_pipe, n_dp, n_t = shape["pipe"], shape["dp"], shape["tensor"]
    axes = ("pipe", "dp", "tensor")
    plane = ("dp", "tensor")
    n_dev = n_dp * n_t

    def local(
        inputs,
        cotangent,
        dealing,
        routes,
        slot_order,
        doc_lengths,
        attn_weight,
        attn_out_weight,
        expert_in_weight,
        expert_out_weight,
        norm_gains,
        router_weight,
    ):
        dev_rows, width = inputs.shape
        experts = expert_in_weight.shape[1]
        reps = n_dp // experts
        paired = reps == 2
        pack = dev_rows
        cap = pack // experts
        per = dev_rows // n_dev
        shard, cols = attn_weight.shape[1], attn_weight.shape[3]
        ff = expert_in_weight.shape[3]
        in_rows, out_rows = expert_in_weight.shape[2], expert_out_weight.shape[2]
        pipe = lax.axis_index("pipe")
        dp = lax.axis_index("dp")
        core = lax.axis_index("tensor")
        mine = dp // reps
        rep = dp % reps
        lengths = lax.dynamic_index_in_dim(doc_lengths, core, 0, keepdims=False)
        zero = jnp.int32(0)
        facts = jnp.stack([pipe, mine, rep, core, lengths[0], zero, zero, zero]).astype(jnp.int32)

        def moved(value, rule):
            pairs = []
            for a in range(n_pipe):
                for b in range(experts):
                    for c in range(reps):
                        for d in range(n_t):
                            to = rule(a, b, c, d)
                            if to is not None:
                                flat = [
                                    ((w * experts + x) * reps + y) * n_t + z
                                    for w, x, y, z in ((a, b, c, d), to)
                                ]
                                pairs.append(tuple(flat))
            return lax.ppermute(value, axes, pairs)

        def swap_core(value):
            return moved(value, lambda a, b, c, d: (a, b, c, 1 - d))

        def swap_rep(value):
            return moved(value, lambda a, b, c, d: (a, b, 1 - c, d))

        def across(step):
            return lambda a, b, c, d: (a, b ^ step, c, d)

        def up(step):
            return lambda a, b, c, d: (1, b ^ step, c, d) if a == 0 else None

        def down(step):
            return lambda a, b, c, d: (0, b ^ step, c, d) if a == 1 else None

        order = (2, 3, 1)

        def exchange(blocks):
            out = {0: blocks[0]}
            for step in order:
                out[step] = moved(blocks[step], across(step))
            return [out[step] for step in range(experts)]

        def crossed(blocks, way):
            out = {}
            for step in (*order, 0):
                out[step] = moved(blocks[step], way(step))
            return [out[step] for step in range(experts)]

        def with_other(blocks):
            out = {}
            for step in (0, 1, 2, 3):
                out[step] = swap_core(blocks[step])
            return list(blocks) + [out[step] for step in range(experts)]

        def pick(blocks, step):
            return lax.dynamic_index_in_dim(blocks, mine ^ step, 0, keepdims=False)

        rep_groups = [[b * reps + c for c in range(reps)] for b in range(experts)]

        payload, send_hot = kernel_call(
            functools.partial(send_kernel, per),
            "send",
            [((dev_rows, width + EXTRA), BF), ((dev_rows, dev_rows), BF)],
            [
                facts,
                inputs,
                cotangent,
                dealing.reshape(1, dev_rows),
                routes.reshape(1, dev_rows),
                slot_order.reshape(1, dev_rows),
                router_weight[0].T,
                norm_gains[0],
            ],
            [SM] + [VM] * 7,
            cost=2,
        )
        dealt = lax.all_to_all(payload, plane, split_axis=0, concat_axis=0, tiled=True)
        params = dealt[:, width:].reshape(n_dev, per, 4, 32)[:, :, :3]
        params = jnp.swapaxes(params, 1, 2).reshape(width, 32)
        params = jnp.pad(params, ((0, 0), (0, EXTRA - 32)))
        both = lax.all_gather(dealt, "tensor", axis=0, tiled=True)
        own_rows, slots, onehot, place = kernel_call(
            deal_kernel,
            "deal",
            [
                ((pack, width), BF, FAR),
                ((pack, pack), BF, FAR),
                ((pack, EXTRA), F32, FAR),
                ((2 * pack, pack), BF, FAR),
            ],
            [facts, both],
            [SM, VM],
            cost=1.5,
        )
        plan = (slots, onehot)

        out_shard = attn_out_weight[0]
        attn_shape = (4 * width, cols)

        def expert_places(way, step):
            def owner_of(numbers):
                owner = jnp.bitwise_xor(numbers[MINE], step) * 2
                return owner + (numbers[REP] if way == 0 else 1 - numbers[REP])

            def spots_in(numbers):
                at = pl.multiple_of(owner_of(numbers) * in_rows, in_rows)
                return [(0, at, in_rows, 0, width), (in_rows, at, in_rows, width, width)]

            def spots_out(numbers):
                at = pl.multiple_of(owner_of(numbers) * out_rows, out_rows)
                return [(2 * in_rows, at, out_rows, 0, width)]

            return spots_in, spots_out

        if paired:
            w_in_raw, w_out_raw = expert_in_weight[0], expert_out_weight[0]
            attn_bundle = pack_attn(jnp.swapaxes(attn_weight[0], 0, 1), out_shard)
            near, far = {}, {}
            near[0], first, bundle = pack_expert(
                facts, w_in_raw, w_out_raw, (0, 1, 2), (attn_bundle,)
            )
            far[0] = swap_rep(near[0])
            attn_near = exchange([attn_bundle] * experts)
            attn_near = stack_pieces(
                facts, [each.reshape(8, shard // 2, cols) for each in attn_near],
                [payload, far[0]],
            )
            near[1] = moved(first, across(1))
            attn_far = swap_rep(attn_near)
            near[2] = moved(bundle, across(2))
            (bundle,) = pack_expert(facts, w_in_raw, w_out_raw, (3,), (near[2],))
            attn_own = kernel_call(
                gather_kernel,
                "gather_attn",
                [((4 * experts, 4, shard // 2, cols), BF)],
                [facts, attn_near, attn_far, bundle, dealt, near[1]],
                [SM, HB, HB, AFTER, AFTER, AFTER],
                [pltpu.SemaphoreType.DMA((22,))],
                room=12,
                hbm_outs=True,
            )[0].reshape(attn_shape)
            near[3] = moved(bundle, across(3))
            for step in (1, 2):
                far[step] = swap_rep(near[step])
            ready = ()
            both_places = [
                expert_places(way, step) for way in range(2) for step in range(experts)
            ]
            places = ([each[0] for each in both_places], [each[1] for each in both_places])
        else:
            attn_bundle = jnp.concatenate(
                [attn_weight[0, :, part] for part in range(3)]
                + [out_shard[:, :cols], out_shard[:, cols:]],
                axis=0,
            )
            every = lax.all_gather(attn_bundle, "dp", axis=0)
            attn_own = jnp.concatenate(
                [
                    every[:, spot : spot + rows].reshape(-1, cols)
                    for _, rows, spot in attn_rows(width, shard)
                ],
                axis=0,
            )

            def assembled(blocks):
                got = exchange([pick(blocks, step) for step in range(experts)])
                got = jnp.stack(got)
                got = jnp.stack([pick(got, owner) for owner in range(experts)])
                got = lax.all_gather(got, "dp", axis_index_groups=rep_groups)
                return jnp.swapaxes(got, 0, 1)

            ready = ()
            pieces = [
                assembled(expert_in_weight[0]).reshape(width, ff),
                assembled(expert_out_weight[0]).reshape(ff, width),
            ]
            places = (
                [lambda numbers: [(0, 0, width, 0, ff)], lambda numbers: []],
                [lambda numbers: [], lambda numbers: [(0, 0, ff, 0, width)]],
            )
        attn_other = swap_core(attn_own)
        weights = (attn_own, attn_other, params)

        def expert_forward(blocks, name, keep, after=()):
            *kept, own, other = expert_call(name, keep, facts, blocks, pieces, places, width, ff)
            folded = fold(own, swap_core(other), "fold_" + name, after)
            return kept, own, other, folded

        def expert_backward(blocks, saved, name, after=()):
            grad_pre, own, other, *rows = expert_back_call(
                name, facts, blocks, saved, pieces, places, width, ff
            )
            return grad_pre, rows, fold(own, swap_core(other), "fold_" + name, after)

        def sent_back(merge, rows, extra, after):
            own, other = sent_rows(facts, merge, rows, extra, place, width, after)
            return own, other

        out = attn_forward(facts, own_rows, weights, plan, None, ready)
        if paired:
            near[3] = ordered(near[3], (out[1],))
            far[3] = swap_rep(near[3])
            pieces = [each[step] for each in (near, far) for step in range(experts)]
        mid_up = moved(out[0], lambda a, b, c, d: (1, b, c, d) if a == 0 else None)
        blocks = with_other(exchange(out[1:5]))
        _, _, _, expert_slots = expert_forward(
            blocks, "expert_first", False, (mid_up,)
        )
        from_first = crossed(expert_slots, up)

        out = attn_forward(facts, own_rows, weights, plan, (mid_up, *from_first))
        mid, attn_in, proj, mixed, mlp_in, probs = out[:6]
        stream = out[10]
        blocks = with_other(exchange(out[6:10]))
        kept_blocks = exchange(out[11:15])
        (slope, act, rows), own_out, other_out, expert_slots = expert_forward(blocks, "expert_second", True)
        expert_saved = (slope, own_out, other_out)

        saved = (stream, mid, proj, mlp_in, probs, mixed)
        kept_own = joined_rows(kept_blocks, (other_out,))
        _, (kept_rows,), grad_slots = expert_backward(
            [kept_own, swap_core(kept_own)], expert_saved, "expert_back_first"
        )
        back = attn_backward(
            facts, own_rows, [mid_up], exchange(grad_slots), saved, weights, plan, True
        )
        expert_slots = exchange(expert_slots)
        if paired:
            back = list(back)
            back[1 + order[0]] = ordered(back[1 + order[0]], expert_slots[1:])
        grad_down = moved(back[0], lambda a, b, c, d: (0, b, c, d) if a == 1 else None)
        out_back = sent_back(True, mid, (slots, *expert_slots), (back[1],))

        grads = with_other(crossed(back[1:5], down))
        grad_rows, *out_wire = expert_out_grads(
            facts, grads, kept_rows, act, (out_back[0],), paired
        )
        grad_pre, _, grad_slots = expert_backward(
            [grad_rows], expert_saved, "expert_back_second"
        )
        out_came = [swap_rep(out_wire[0])] if paired else []
        in_wire = expert_in_grads(facts, rows, grad_pre, [grad_slots[2], *out_came], paired)
        after = []
        if paired:
            out_sums = sum_pieces(
                SPLIT_ORDER[:2], out_wire[2], out_came[0], [in_wire[1]]
            )
            after = [out_sums[0]]
        layer_grad, grad_proj, low, tiny = attn_backward(
            facts,
            grad_down,
            [own_rows, *after],
            exchange(grad_slots),
            saved,
            weights,
            plan,
            False,
        )

        if paired:
            out_near = [
                moved(each, across(step)) if step else each
                for step, each in zip(SPLIT_ORDER[:2], out_sums, strict=True)
            ]
            came_in = swap_rep(in_wire[0])
            came_last = swap_rep(out_wire[1])
            marker = [came_last, came_in, *out_near]
        else:

            def rep_scatter(each):
                return lax.psum_scatter(
                    each, "dp", axis_index_groups=rep_groups, scatter_dimension=0
                )

            def to_owner(grad, rows_each):
                each = grad.reshape(experts, reps, rows_each, -1).astype(BF)
                summed = rep_scatter(jnp.swapaxes(each, 0, 1))
                got = exchange([pick(summed, step) for step in range(experts)])
                got = jnp.stack(got)
                return jnp.stack([pick(got, owner) for owner in range(experts)]).astype(F32)

            marker = []
            (grad_w_in,), (grad_w_out,) = in_wire, out_wire
            grad_expert_in = to_owner(grad_w_in, in_rows)
            grad_expert_out = to_owner(grad_w_out, out_rows)

        grad_own, grad_other = attn_grads(attn_in, grad_proj, mixed, low, marker)
        came = swap_core(grad_other)
        if paired:
            in_sums = sum_pieces(SPLIT_ORDER, in_wire[1], came_in, [grad_own])
            in_near = [
                moved(each, across(step)) if step else each
                for step, each in zip(SPLIT_ORDER, in_sums, strict=True)
            ]
            out = attn_split(facts, grad_own, came, (in_sums[0],))
            last = sum_pieces(SPLIT_ORDER[2:], out_wire[3], came_last, [out[2]])
            out_near += [moved(last[0], across(1)), last[1]]
            after = (last[1],)
        else:
            after = ()
        grad_back = sent_back(False, layer_grad, (), after)
        tiny = jnp.swapaxes(tiny[:, :32].reshape(n_dev, 3, per, 32), 1, 2)
        tiny = jnp.pad(tiny.reshape(dev_rows, 96), ((0, 0), (0, EXTRA - 96)))
        theirs = swap_core(jnp.concatenate([out_back[1], grad_back[1]], axis=1))
        both = jnp.concatenate([out_back[0], grad_back[0]], axis=1) + theirs
        payload = jnp.concatenate([both, tiny], axis=1)
        if paired:
            total = {}
            first = sum_pieces(SPLIT_ORDER[:2], out[2], swap_rep(out[0]), [payload])
            last = swap_rep(ordered(out[1], (first[0],)))
            last = sum_pieces(SPLIT_ORDER[2:], out[3], last, [first[1]])
            for step, each in zip(SPLIT_ORDER, [*first, *last], strict=True):
                total[step] = moved(each, across(step)) if step else each
            grad_expert_in, grad_expert_out = owner_grads(
                facts,
                [*out_near, *in_near],
                (total[0],),
                expert_in_weight.shape[1:],
                expert_out_weight.shape[1:],
            )
            grad_attn, grad_attn_out = kernel_call(
                finish_kernel,
                "finish_attn",
                [((3, shard, cols), F32), ((shard // 2, width), F32)],
                [total[step] for step in range(experts)],
                [VM] * 4,
            )
        else:
            full = grad_own.astype(F32) + came.astype(F32)
            pieces_of = [
                full[source : source + rows * n_dp].reshape(n_dp, rows, cols)
                for source, rows, _ in attn_rows(width, shard)
            ]
            full = jnp.concatenate(pieces_of, axis=1).astype(BF)
            full = full.reshape((experts, reps) + full.shape[1:])
            full = rep_scatter(jnp.swapaxes(full, 0, 1))
            got = exchange([pick(full, step) for step in range(experts)])
            total = sum(each.astype(F32) for each in got)
            grad_attn = total[: 3 * shard].reshape(3, shard, cols)
            rows = shard // 2
            grad_attn_out = jnp.concatenate(
                [total[3 * shard : 3 * shard + rows], total[3 * shard + rows :]], axis=1
            )
        both = lax.all_to_all(payload, plane, split_axis=0, concat_axis=0, tiled=True)
        activations, input_grads, tiny = kernel_call(
            restore_kernel,
            "restore",
            [((dev_rows, width), BF), ((dev_rows, width), BF), ((per, EXTRA), F32)],
            [send_hot, both],
            [VM] * 2,
            cost=2,
        )
        tiny = tiny.reshape(per, 4, 32)[:, :3]
        tiny = jnp.swapaxes(tiny, 0, 1).reshape(3 * per, 32)
        grad_router = (tiny[:, :experts] + tiny[:, experts : 2 * experts])[None]
        grad_gains = (tiny[:, 8:10] + tiny[:, 10:12]).T[None]

        return (
            activations[None],
            input_grads[None],
            jnp.swapaxes(grad_attn, 0, 1)[None],
            grad_attn_out[None],
            grad_expert_in[None],
            grad_expert_out[None],
            grad_gains,
            grad_router,
        )

    in_specs = (
        P(("dp", "tensor"), None),
        P(("dp", "tensor"), None),
        P(("dp", "tensor")),
        P(("dp", "tensor"), None),
        P(("dp", "tensor")),
        P("dp", None),
        P("pipe", "dp", None, "tensor"),
        P("pipe", ("tensor", "dp"), None),
        P("pipe", None, "dp", "tensor"),
        P("pipe", None, ("tensor", "dp"), None),
        P("pipe", None, ("dp", "tensor")),
        P("pipe", ("dp", "tensor"), None),
    )
    out_specs = (
        P("pipe", ("dp", "tensor"), None),
        P("pipe", ("dp", "tensor"), None),
        P("pipe", "dp", None, "tensor"),
        P("pipe", ("tensor", "dp"), None),
        P("pipe", None, "dp", "tensor"),
        P("pipe", None, ("tensor", "dp"), None),
        P("pipe", None, ("dp", "tensor")),
        P("pipe", ("dp", "tensor"), None),
    )
    return jax.shard_map(local, mesh=mesh, in_specs=in_specs, out_specs=out_specs, check_vma=False)
```

```python
import functools

import jax
import jax.numpy as jnp
from jax import lax
from jax.experimental import pallas as pl
from jax.experimental.pallas import tpu as pltpu
from jax.sharding import PartitionSpec as P

HEAD_DIM = 64
EPSILON = 1e-06
NEGATIVE = -1e30
EXACT = lax.Precision.HIGHEST
EXTRA = 128
BF = jnp.bfloat16
F32 = jnp.float32
VM = pl.BlockSpec(memory_space=pltpu.VMEM)
SM = pl.BlockSpec(memory_space=pltpu.SMEM)
HB = pl.BlockSpec(memory_space=pltpu.HBM)
AFTER = pl.BlockSpec(memory_space=pl.ANY)
RAW = 2
VH = pl.BlockSpec(memory_space=pltpu.VMEM)
FAR = True
PIPE, MINE, REP, CORE, SPLIT = range(5)


def dot32(a, b):
    return jnp.dot(a, b, preferred_element_type=F32)


def dot_nt(a, b):
    return lax.dot_general(a, b, (((1,), (1,)), ((), ())), preferred_element_type=F32)


def dot_tn(a, b):
    return lax.dot_general(a, b, (((0,), (0,)), ((), ())), preferred_element_type=F32)


def split3(value):
    high = value.astype(BF)
    rest = value - high.astype(F32)
    mid = rest.astype(BF)
    return high, mid, (rest - mid.astype(F32)).astype(BF)


def parts_nt(a, b):
    return sum(dot_nt(a, part) for part in split3(b))


def norm_scale(x):
    return lax.rsqrt(jnp.mean(x * x, axis=-1, keepdims=True) + EPSILON)


def norm_back(x, scale, gain, grad):
    weighted = grad * gain
    grad_x = scale * weighted - x * (scale * scale * scale) * jnp.mean(
        x * weighted, axis=-1, keepdims=True
    )
    return grad_x, jnp.sum(grad * (x * scale), axis=0, keepdims=True)


def pinned(value):
    return pltpu.with_memory_space_constraint(value, pltpu.HBM)


def kernel_call(body, name, outs, ins, specs, scratch=(), cost=1, room=24, hbm_outs=False):
    ins = [
        pinned(each) if spec is HB or spec is VH else each
        for each, spec in zip(ins, specs, strict=True)
    ]
    far = [hbm_outs or len(each) > 2 for each in outs]
    return pl.pallas_call(
        body,
        name=name,
        out_shape=[
            (pltpu.HBM if away else jax.ShapeDtypeStruct)(each[0], each[1])
            for each, away in zip(outs, far, strict=True)
        ],
        in_specs=specs,
        out_specs=[HB if each[2:] == (RAW,) else VM for each in outs],
        scratch_shapes=list(scratch),
        compiler_params=pltpu.CompilerParams(vmem_limit_bytes=room << 20),
        cost_estimate=pl.CostEstimate(
            flops=int(cost * 1.1e9), bytes_accessed=0, transcendentals=0
        ),
    )(*ins)


def eye(count):
    rows = lax.broadcasted_iota(jnp.int32, (count, count), 0)
    return (rows == lax.broadcasted_iota(jnp.int32, (count, count), 1)).astype(F32).astype(BF)


def send_kernel(per, facts, inputs, cotangent, dealing, routes, order, router, gains, out, hot_out):
    rows, width = inputs.shape
    place = dealing[...]
    target = place >> 8
    numbers = [place & 255, routes[...], order[...] >> 8, order[...] & 255, target]
    numbers = [each.astype(F32) for each in numbers]
    numbers = jnp.concatenate(numbers + [jnp.zeros((EXTRA - 5, rows), F32)], axis=0)
    columns = dot_nt(eye(rows), numbers.astype(BF))
    targets = target.astype(F32)
    before = lax.broadcasted_iota(jnp.int32, (rows, rows), 0)
    after = lax.broadcasted_iota(jnp.int32, (rows, rows), 1)
    ahead = (columns[:, 4:5] == targets) & (before < after)
    slot = targets * per + jnp.sum(ahead.astype(F32), axis=0, keepdims=True)
    hot = (before.astype(F32) == slot).astype(F32).astype(BF)
    hot_out[...] = hot
    chosen = jnp.where(facts[PIPE] == 0, inputs[...], cotangent[...])
    out[:, :width] = dot32(hot, chosen).astype(BF)
    lane = lax.broadcasted_iota(jnp.int32, (rows, EXTRA), 1)
    tail = dot32(hot, jnp.where(lane < 4, columns, 0.0).astype(BF))
    parts = []
    for values in (router[...], gains[...]):
        high = values.astype(BF).astype(F32)
        mid = (values - high).astype(BF).astype(F32)
        parts += [high, mid, values - high - mid]
    count = gains.shape[1]
    blank = jnp.zeros((4, count), F32)
    block = jnp.concatenate([blank] + parts + [jnp.zeros((10, count), F32)], axis=0)
    block = dot_nt(eye(count), block.astype(BF))
    groups = [block[at * per : (at + 1) * per, :] for at in range(3)]
    block = jnp.concatenate(groups + [jnp.zeros((per, 32), F32)], axis=1)
    block = jnp.concatenate([block] * (rows // per), axis=0)
    out[:, width:] = (tail + block).astype(BF)


def deal_kernel(facts, both, own_rows, slots, onehot, place):
    width = own_rows.shape[1]
    pack = own_rows.shape[0]
    total = both.shape[0]
    half = pack // 2
    core = facts[CORE].astype(F32)
    numbers = both[:, width:]
    spot = numbers[:, 0:1].astype(F32)
    source = (lax.broadcasted_iota(jnp.int32, (total, 1), 0) >= pack).astype(F32)
    upper = (spot >= half).astype(F32)
    where = jnp.where(upper == core, source * half + spot - upper * half, -1.0)
    spots = lax.broadcasted_iota(jnp.int32, (total, pack), 1).astype(F32)
    hot = (spots == where).astype(F32).astype(BF)
    place[...] = hot
    own_rows[...] = dot_tn(hot, both[:, :width]).astype(BF)
    mine = dot_tn(hot, numbers)
    across = dot_nt(eye(EXTRA), mine.astype(BF))
    expert_col, expert_row = mine[:, 1:2], across[1:2, :]
    order_col = mine[:, 2:3] * 256.0 + mine[:, 3:4]
    order_row = across[2:3, :] * 256.0 + across[3:4, :]
    ahead = (expert_col == expert_row) & (order_col < order_row)
    rank = jnp.sum(ahead.astype(F32), axis=0, keepdims=True).astype(jnp.int32)
    experts = 4
    cap = pack // experts
    block = jnp.bitwise_xor(expert_row.astype(jnp.int32), facts[MINE])
    slot = jnp.where(rank < cap, block * cap + rank, -1)
    slots[...] = (lax.broadcasted_iota(jnp.int32, (pack, pack), 0) == slot).astype(F32).astype(BF)
    onehot[...] = (
        lax.broadcasted_iota(jnp.int32, (pack, EXTRA), 1) == expert_col.astype(jnp.int32)
    ).astype(F32)


def mask_of(facts, first, rows, columns):
    query = lax.broadcasted_iota(jnp.int32, (rows, columns), 0) + first
    key = lax.broadcasted_iota(jnp.int32, (rows, columns), 1)
    split = facts[SPLIT]
    return ((query < split) == (key < split)) & (key <= query)


def turned_mask(facts, first, rows, columns):
    key = lax.broadcasted_iota(jnp.int32, (rows, columns), 0) + first
    query = lax.broadcasted_iota(jnp.int32, (rows, columns), 1) + first
    split = facts[SPLIT]
    return ((query < split) == (key < split)) & (key <= query)


def stacked(refs):
    return jnp.concatenate([ref[...] for ref in refs], axis=0)


def flipped(params):
    flat = dot_nt(eye(EXTRA), params[...])
    return flat[16:18] + flat[18:20] + flat[20:22]


def weight_copies(sources, scratch, sems, width, cols):
    copies = []
    for at in range(2):
        each = []
        for start, rows in (*((part * width, width) for part in range(3)), (3 * width, 2 * cols)):
            spot = pl.ds(start, rows)
            each.append(
                pltpu.make_async_copy(
                    sources[at].at[spot], scratch.at[at, spot], sems.at[4 * at + len(each)]
                )
            )
        copies.append(each)
    return copies


def gate_of(up):
    return jnp.sum(up[:, up.shape[1] - EXTRA :].astype(F32), axis=-1, keepdims=True)


def attn_kernel(second, dropped, facts, *refs):
    refs = list(refs)
    weights, sems = refs[-2:] if second else refs[-5:-3]
    refs = refs[:-2] if second else refs[:-5] + refs[-3:]
    own_rows = refs.pop(0)
    if second:
        up = refs.pop(0)
        slots_in = [refs.pop(0) for _ in range(4)]
    attn_own, attn_other, params, slots, onehot = (refs.pop(0) for _ in range(5))
    refs = refs[dropped:]
    if second:
        mid, attn_in, proj, mixed, mlp_in, probs = (refs.pop(0) for _ in range(6))
    else:
        send_up = refs.pop(0)
        proj, mixed, mid = refs[4:]
    blocks = [refs.pop(0) for _ in range(4)]
    pack, width = own_rows.shape
    cols = attn_own.shape[1]
    cap = pack // 4
    copies = weight_copies((attn_own, attn_other), weights, sems, width, cols)
    for each in copies:
        for copy in each:
            copy.start()
    gains = flipped(params)
    hot = slots[...]
    if second:
        stream = refs.pop(0)
        grads = [refs.pop(0) for _ in range(4)]
        came = up[:, :width].astype(F32) + gate_of(up) * dot_tn(hot, stacked(slots_in))
        rows = jnp.where(facts[PIPE] == 0, own_rows[...], came.astype(BF))
        stream[...] = rows
    else:
        rows = own_rows[...]
    x = rows.astype(F32)
    normed = (x * norm_scale(x) * gains[0:1, :]).astype(BF)
    if second:
        attn_in[...] = normed
    half = pack // 2
    upper = mask_of(facts, 0, half, half)
    lower = mask_of(facts, half, half, pack)
    lane = lax.broadcasted_iota(jnp.int32, (pack, EXTRA), 1)
    totals = jnp.zeros((pack, EXTRA), F32)
    for at in range(2):
        for part in range(3):
            copies[at][part].wait()
            proj[at, part] = dot32(
                normed, weights[at, part * width : (part + 1) * width, :]
            ).astype(BF)
        for pair in range(cols // EXTRA):
            lanes = slice(pair * EXTRA, (pair + 1) * EXTRA)
            query = proj[at, 0, :, lanes] * jnp.asarray(HEAD_DIM ** (-0.5), BF)
            key, value = proj[at, 1, :, lanes], proj[at, 2, :, lanes]
            parts = []
            for side in range(2):
                chosen = jnp.where((lane >= HEAD_DIM) == (side == 1), query, 0)
                head = 8 + (at * cols + pair * EXTRA) // HEAD_DIM + side
                results = []
                for first, count, allowed in ((0, half, upper), (half, pack, lower)):
                    scores = dot_nt(chosen[first : first + half, :], key[:count, :])
                    scores = jnp.where(allowed, scores, NEGATIVE)
                    peak = jnp.max(scores, axis=-1, keepdims=True)
                    share = jnp.exp(scores - peak)
                    total = jnp.sum(share, axis=-1, keepdims=True)
                    results.append(
                        (dot32(share.astype(BF), value[:count, :]) * (1.0 / total), peak + jnp.log(total))
                    )
                parts.append(jnp.concatenate([each[0] for each in results], axis=0))
                if second:
                    level = jnp.concatenate([each[1] for each in results], axis=0)
                    totals = jnp.where(lane == head, level, totals)
            spot = at * cols + pair * EXTRA
            mixed[:, spot : spot + EXTRA] = jnp.where(lane < HEAD_DIM, *parts).astype(BF)
    base = 3 * width
    copies[0][3].wait()
    copies[1][3].wait()
    for side in range(2):
        rows_at = slice(base + side * cols, base + (side + 1) * cols)
        lanes = slice(side * cols, (side + 1) * cols)
        mid[:, lanes] = (
            x[:, lanes]
            + dot32(mixed[:, :cols], weights[0, rows_at, :])
            + dot32(mixed[:, cols:], weights[1, rows_at, :])
        )
    m = mid[:, :width]
    low = (m * norm_scale(m) * gains[1:2, :]).astype(BF)
    if second:
        mlp_in[...] = low
    logits = dot32(low, params[...])
    lane = lax.broadcasted_iota(jnp.int32, logits.shape, 1)
    logits = sum(pltpu.roll(logits, EXTRA - 4 * at, 1) for at in (1, 2, 3))
    logits = jnp.where(lane < 4, logits, NEGATIVE)
    rel = jnp.exp(logits - jnp.max(logits, axis=-1, keepdims=True))
    share = rel / jnp.sum(rel, axis=-1, keepdims=True)
    if second:
        probs[...] = share + totals
    gate = jnp.sum(share * onehot[...], axis=-1, keepdims=True)
    if second:
        mid[:, width:] = jnp.broadcast_to(gate, (pack, EXTRA))
    else:
        send_up[:, :width] = m.astype(BF)
        high = gate.astype(BF).astype(F32)
        middle = (gate - high).astype(BF).astype(F32)
        parts = jnp.where(lane == 1, middle, jnp.where(lane == 2, gate - high - middle, 0.0))
        send_up[:, width:] = jnp.where(lane == 0, high, parts).astype(BF)
    for step in range(4):
        blocks[step][...] = dot32(hot[step * cap : (step + 1) * cap, :], low).astype(BF)
    if second:
        weighted = (gate * own_rows[...].astype(F32)).astype(BF)
        for step in range(4):
            grads[step][...] = dot32(hot[step * cap : (step + 1) * cap, :], weighted).astype(BF)


def attn_forward(facts, own_rows, weights, plan, came=None, after=()):
    attn_own, attn_other, params = weights
    slots, onehot = plan
    pack, width = own_rows.shape
    cols = attn_own.shape[1]
    cap = pack // 4
    second = came is not None
    ins = [facts, own_rows] + (list(came) if second else [])
    specs = [SM, VH] + ([VH] if second else []) + [VM] * (len(ins) - (3 if second else 2))
    specs += [HB] * 2 + [VH] * 3 + [AFTER] * len(after)
    ins += [attn_own, attn_other, params, slots, onehot, *after]
    if second:
        outs = [
            ((pack, width + EXTRA), F32, FAR),
            ((pack, width), BF, FAR),
            ((2, 3, pack, cols), BF, FAR),
            ((pack, width), BF, FAR),
            ((pack, width), BF, FAR),
            ((pack, EXTRA), F32, FAR),
        ]
    else:
        outs = [((pack, width + EXTRA), BF, FAR)]
    outs += [((cap, width), BF)] * 4
    if second:
        outs += [((pack, width), BF, FAR)] + [((cap, width), BF)] * 4
    return kernel_call(
        functools.partial(attn_kernel, second, len(after)),
        "attn_second" if second else "attn_first",
        outs,
        ins,
        specs,
        [pltpu.VMEM((2, 3 * width + 2 * cols, cols), BF), pltpu.SemaphoreType.DMA((8,))]
        + ([] if second else [
            pltpu.VMEM((2, 3, pack, cols), BF),
            pltpu.VMEM((pack, width), BF),
            pltpu.VMEM((pack, width), F32),
        ]),
        cost=8,
    )


def attn_back_kernel(first, dropped, facts, *refs):
    refs = list(refs)
    weights, sems = refs[-2:]
    refs = refs[:-2]
    grad_out = refs.pop(0)
    if first:
        up = refs.pop(0)
    else:
        own_rows = refs.pop(0)
        refs = refs[dropped:]
    grad_slots = [refs.pop(0) for _ in range(4)]
    stream, mid, proj, mlp_in, probs, mixed = (refs.pop(0) for _ in range(6))
    attn_own, attn_other, params, slots, onehot = (refs.pop(0) for _ in range(5))
    grad_stream = refs.pop(0)
    if first:
        blocks = [refs.pop(0) for _ in range(4)]
        grad_proj = refs.pop(0)
    else:
        grad_proj, grad_low, tiny = (refs.pop(0) for _ in range(3))
    pack, width = stream.shape
    cols = attn_own.shape[1]
    cap = pack // 4
    copies = weight_copies((attn_own, attn_other), weights, sems, width, cols)
    for part in (3, 0, 1, 2):
        for each in copies:
            each[part].start()
    gains = flipped(params)
    hot = slots[...]
    rows = grad_out[...]
    if not first:
        rows = jnp.where(facts[PIPE] == 0, rows, own_rows[...])
    g = rows.astype(F32)
    slot_rows = stacked(grad_slots)
    at_tokens = dot_tn(hot, slot_rows[:, width:])
    lane = lax.broadcasted_iota(jnp.int32, (pack, EXTRA), 1)
    shares = jnp.where(lane < 4, probs[...], 0.0)
    grad_logits = (at_tokens[:, 0:1] + at_tokens[:, 1:2]) * (onehot[...] - shares)
    m = mid[:, :width]
    wide = sum(pltpu.roll(grad_logits, 4 * at, 1) for at in (1, 2, 3))
    grad_mlp = dot_tn(hot, slot_rows[:, :width]) + sum(
        dot_nt(part, params[...]) for part in split3(wide)
    )
    grad_norm, gain_two = norm_back(m, norm_scale(m), gains[1:2, :], grad_mlp)
    grad_mid = g + grad_norm
    low = grad_mid.astype(BF)
    base = 3 * width
    copies[0][3].wait()
    copies[1][3].wait()
    grad_mixed = jnp.concatenate(
        [
            (
                dot_nt(low[:, :cols], weights[at, base : base + cols, :])
                + dot_nt(low[:, cols:], weights[at, base + cols : base + 2 * cols, :])
            ).astype(BF)
            for at in range(2)
        ],
        axis=1,
    )
    heads = lax.broadcasted_iota(jnp.int32, (EXTRA, width), 0)
    heads = heads == lax.broadcasted_iota(jnp.int32, (EXTRA, width), 1) // HEAD_DIM + 8
    inner = parts_nt(heads.astype(F32).astype(BF), grad_mixed.astype(F32) * mixed[...].astype(F32))
    levels = parts_nt(eye(EXTRA), probs[...])
    half = pack // 2
    blocks_of = (
        (0, pack, turned_mask(facts, 0, half, pack)),
        (half, half, turned_mask(facts, half, half, half)),
    )
    grad_in = jnp.zeros((pack, width), F32)
    for at in range(2):
        for pair in range(cols // EXTRA):
            lanes = slice(pair * EXTRA, (pair + 1) * EXTRA)
            spot = at * cols + pair * EXTRA
            scale = jnp.asarray(HEAD_DIM ** (-0.5), BF)
            query = proj[at, 0, :, lanes] * scale
            key, value = proj[at, 1, :, lanes], proj[at, 2, :, lanes]
            grad_pair = grad_mixed[:, spot : spot + EXTRA]
            grad_query = jnp.zeros((pack, EXTRA), F32)
            grad_key = [jnp.zeros((half, EXTRA), F32) for _ in range(2)]
            grad_value = [jnp.zeros((half, EXTRA), F32) for _ in range(2)]
            for side in range(2):
                keep = (lane >= HEAD_DIM) == (side == 1)
                query_one = jnp.where(keep, query, 0)
                key_one = jnp.where(keep, key, 0)
                grad_one = jnp.where(keep, grad_pair, 0)
                head = 8 + spot // HEAD_DIM + side
                for at_block, (begin, count, allowed) in enumerate(blocks_of):
                    rows_at = slice(begin, begin + half)
                    after = slice(begin, begin + count)
                    scores = dot_nt(key[rows_at, :], query_one[after, :])
                    share = jnp.exp(scores - levels[head : head + 1, after])
                    share = jnp.where(allowed, share, 0.0)
                    grad_share = dot_nt(value[rows_at, :], grad_one[after, :])
                    grad_scores = share * (grad_share - inner[head : head + 1, after])
                    grad_scores = grad_scores.astype(BF)
                    grad_key[at_block] += dot32(grad_scores, query_one[after, :])
                    grad_value[at_block] += dot32(share.astype(BF), grad_one[after, :])
                    more = dot_tn(grad_scores, key_one[rows_at, :])
                    if begin:
                        more = jnp.concatenate([jnp.zeros((half, EXTRA), F32), more], axis=0)
                    grad_query += more
            grad_proj[at, 0, :, lanes] = (grad_query * HEAD_DIM ** (-0.5)).astype(BF)
            for at_block in range(2):
                rows_at = slice(at_block * half, (at_block + 1) * half)
                grad_proj[at, 1, rows_at, lanes] = grad_key[at_block].astype(BF)
                grad_proj[at, 2, rows_at, lanes] = grad_value[at_block].astype(BF)
        for part in range(3):
            copies[at][part].wait()
            grad_in += dot_nt(
                grad_proj[at, part], weights[at, part * width : (part + 1) * width, :]
            )
    x = stream[...].astype(F32)
    grad_norm, gain_one = norm_back(x, norm_scale(x), gains[0:1, :], grad_in)
    result = (grad_mid + grad_norm).astype(BF)
    grad_stream[...] = result
    if first:
        weighted = (gate_of(up) * result.astype(F32)).astype(BF)
        for step in range(4):
            blocks[step][...] = dot32(hot[step * cap : (step + 1) * cap, :], weighted).astype(BF)
    else:
        grad_low[...] = low
        high = grad_logits.astype(BF)
        rest = (grad_logits - high.astype(F32)).astype(BF)
        lane = lax.broadcasted_iota(jnp.int32, (width, EXTRA), 1)
        both = dot_tn(mlp_in[...], high) + dot_tn(mlp_in[...], rest)
        both = jnp.where(lane < 4, both, 0.0)
        high = both.astype(BF).astype(F32)
        flat = [gain_one.astype(BF).astype(F32), gain_two.astype(BF).astype(F32)]
        flat += [gain_one - flat[0], gain_two - flat[1]]
        flat = jnp.concatenate(flat + [jnp.zeros((12, width), F32)], axis=0).astype(BF)
        spot = lax.broadcasted_iota(jnp.int32, (16, EXTRA), 0) + 8
        spot = spot == lax.broadcasted_iota(jnp.int32, (16, EXTRA), 1)
        turned = dot_tn(flat, spot.astype(F32).astype(BF))
        tiny[...] = (high + pltpu.roll(both - high, 4, 1) + turned).astype(BF)


def attn_backward(facts, grad_out, extra, grad_slots, saved, weights, plan, first):
    attn_own, attn_other, params = weights
    slots, onehot = plan
    stream, mid, proj, mlp_in, probs, mixed = saved
    pack, width = stream.shape
    cols = attn_own.shape[1]
    cap = pack // 4
    ins = [facts, grad_out, *extra, *grad_slots, stream, mid, proj, mlp_in, probs, mixed]
    specs = [SM, VH if first else VM, VH] + [AFTER] * (len(extra) - 1)
    specs += [VM] * 4 + [VH] * 6 + [HB] * 2 + [VH] * 3
    ins += [attn_own, attn_other, params, slots, onehot]
    outs = [((pack, width), BF)]
    if first:
        outs += [((cap, width), BF)] * 4
    outs += [((2, 3, pack, cols), BF)]
    if not first:
        outs += [((pack, width), BF), ((width, EXTRA), BF)]
    return kernel_call(
        functools.partial(attn_back_kernel, first, len(extra) - 1),
        "attn_back_first" if first else "attn_back_second",
        outs,
        ins,
        specs,
        [pltpu.VMEM((2, 3 * width + 2 * cols, cols), BF), pltpu.SemaphoreType.DMA((8,))],
        cost=13,
    )


def gelu_both(u):
    square = u * u
    t = jnp.tanh(0.7978845608028654 * u * (1.0 + 0.044715 * square))
    half = 0.5 * (1.0 + t)
    inner = 0.7978845608028654 * (1.0 + 3.0 * 0.044715 * square)
    return half + 0.5 * u * (1.0 - t * t) * inner, half * u


def bring(facts, pieces, places, scratch, sems):
    copies = []
    for piece, spots in zip(pieces, places, strict=True):
        for source, target, rows, column, columns in spots(facts):
            copies.append(
                pltpu.make_async_copy(
                    piece.at[pl.ds(source, rows), pl.ds(0, columns)],
                    scratch.at[pl.ds(target, rows), pl.ds(column, columns)],
                    sems.at[len(copies)],
                )
            )
    for copy in copies:
        copy.start()
    return copies


TILE = 256


def expert_kernel(keep, places_in, places_out, facts, *refs):
    refs = list(refs)
    blocks = [refs.pop(0) for _ in range(8)]
    pieces = [refs.pop(0) for _ in range(len(places_in))]
    if keep:
        targets = [refs.pop(0) for _ in range(3)]
        own, other, w_in, w_out, sems_in, sems_out, act, rows, pre, sems = refs
    else:
        own, other, w_in, w_out, sems_in, sems_out, act, rows = refs
    arriving = bring(facts, pieces, places_in, w_in, sems_in)
    later = bring(facts, pieces, places_out, w_out, sems_out)
    cap = blocks[0].shape[0]
    for at, block in enumerate(blocks):
        rows[at * cap : (at + 1) * cap, :] = block[...]
    ff = w_in.shape[1]
    width = w_in.shape[0]
    if keep:
        leaving = pltpu.make_async_copy(rows, targets[2], sems.at[2, 0])
        leaving.start()

    def tile_copies(tile):
        lanes = pl.ds(pl.multiple_of(tile * TILE, TILE), TILE)
        return [
            pltpu.make_async_copy(
                source.at[:, lanes], targets[at].at[:, lanes], sems.at[at, tile]
            )
            for at, source in enumerate((pre, act))
        ]

    for copy in arriving:
        copy.wait()

    @pl.loop(0, ff // TILE, unroll=1)
    def _(tile):
        lanes = pl.ds(pl.multiple_of(tile * TILE, TILE), TILE)
        value = dot32(rows[...], w_in[:, lanes])
        slope, result = gelu_both(value)
        act[:, lanes] = result.astype(BF)
        if keep:
            pre[:, lanes] = slope.astype(BF)
            for copy in tile_copies(tile):
                copy.start()

    for copy in later:
        copy.wait()
    count = 4 * cap

    @pl.loop(0, width // TILE, unroll=1)
    def _(tile):
        lanes = pl.ds(pl.multiple_of(tile * TILE, TILE), TILE)
        value = dot32(act[...], w_out[:, lanes])
        own[:, lanes] = value[:count]
        other[:, lanes] = value[count:].astype(BF)

    if keep:
        leaving.wait()

        @pl.loop(0, ff // TILE, unroll=1)
        def _(tile):
            for copy in tile_copies(tile):
                copy.wait()


def halves(value, shape):
    high = value.astype(BF).astype(F32)
    lane = lax.broadcasted_iota(jnp.int32, shape, 1)
    return jnp.where(lane == 0, high, jnp.where(lane == 1, value - high, 0.0))


def expert_back_kernel(chosen, places_in, places_out, facts, *refs):
    refs = list(refs)
    blocks = [refs.pop(0) for _ in range(1 if chosen else 2)]
    pre, own_out, other_out = (refs.pop(0) for _ in range(3))
    pieces = [refs.pop(0) for _ in range(len(places_in))]
    grad_pre, own, other = (refs.pop(0) for _ in range(3))
    rows = blocks[0] if chosen else refs.pop(0)
    w_in, w_out, sems_in, sems_out = refs
    arriving = bring(facts, pieces, places_out, w_out, sems_out)
    later = bring(facts, pieces, places_in, w_in, sems_in)
    if not chosen:
        half = rows.shape[0] // 2
        for at, block in enumerate(blocks):
            rows[at * half : (at + 1) * half, :] = block[...]
    for copy in arriving:
        copy.wait()
    ff = w_in.shape[1]
    width = w_in.shape[0]
    count = rows.shape[0] // 2

    @pl.loop(0, ff // TILE, unroll=True)
    def _(tile):
        lanes = pl.ds(pl.multiple_of(tile * TILE, TILE), TILE)
        value = dot_nt(rows[...], w_out[lanes, :])
        grad_pre[:, lanes] = (value * pre[:, lanes].astype(F32)).astype(BF)

    for copy in later:
        copy.wait()

    @pl.loop(0, width // TILE, unroll=True)
    def _(tile):
        lanes = pl.ds(pl.multiple_of(tile * TILE, TILE), TILE)
        value = dot_nt(grad_pre[...], w_in[lanes, :])
        own[:, lanes] = value[:count]
        other[:, lanes] = value[count:].astype(BF)

    pull = jnp.sum(rows[:count, :].astype(F32) * own_out[...], axis=-1, keepdims=True)
    own[:, width:] = halves(pull, (count, EXTRA))
    pull = jnp.sum(
        rows[count:, :].astype(F32) * other_out[...].astype(F32), axis=-1, keepdims=True
    )
    other[:, width:] = halves(pull, (count, EXTRA)).astype(BF)


def expert_scratch(width, ff, places):
    numbers = jnp.zeros((8,), jnp.int32)
    sizes = [sum(len(spots(numbers)) for spots in each) for each in places]
    return (
        [pltpu.VMEM((width, ff), BF), pltpu.VMEM((ff, width), BF)],
        [pltpu.SemaphoreType.DMA((size,)) for size in sizes],
    )


def expert_call(name, keep, facts, blocks, pieces, places, width, ff):
    count = 4 * blocks[0].shape[0]
    ins = [facts, *blocks, *pieces]
    kept = [((2 * count, ff), BF, RAW)] * 2 + [((2 * count, width), BF, RAW)] if keep else []
    buffers, sems = expert_scratch(width, ff, places)
    scratch = [*buffers, *sems]
    scratch += [pltpu.VMEM((2 * count, ff), BF), pltpu.VMEM((2 * count, width), BF)]
    if keep:
        scratch.append(pltpu.VMEM((2 * count, ff), BF))
        scratch.append(pltpu.SemaphoreType.DMA((3, ff // TILE)))
    return kernel_call(
        functools.partial(expert_kernel, keep, *places),
        name,
        kept + [((count, width), F32), ((count, width), BF)],
        ins,
        [SM] + [VM] * 8 + [HB] * len(pieces),
        scratch,
        cost=7,
    )


def expert_back_call(name, facts, blocks, saved, pieces, places, width, ff):
    chosen = len(blocks) == 1
    count = blocks[0].shape[0] * len(blocks) // 2
    wide = width + EXTRA
    ins = [facts, *blocks, *saved, *pieces]
    buffers, sems = expert_scratch(width, ff, places)
    outs = [((2 * count, ff), BF), ((count, wide), F32), ((count, wide), BF)]
    if not chosen:
        outs.append(((2 * count, width), BF, FAR))
    return kernel_call(
        functools.partial(expert_back_kernel, chosen, *places),
        name,
        outs,
        ins,
        [SM] + ([VH] if chosen else [VM] * 2) + [VH, VM, VM] + [HB] * len(pieces),
        [*buffers, *sems],
        cost=8,
    )


def fold_kernel(own, other, *blocks):
    blocks = blocks[-4:]
    cap = blocks[0].shape[0]
    width = own.shape[1] // TILE * TILE
    for step, block in enumerate(blocks):
        rows = slice(step * cap, (step + 1) * cap)
        block[:, :width] = (own[rows, :width] + other[rows, :width].astype(F32)).astype(BF)
        if own.shape[1] > width:
            both = own[rows, width:] + other[rows, width:].astype(F32)
            block[:, width:] = halves(both[:, 0:1] + both[:, 1:2], (cap, EXTRA)).astype(BF)


def fold(own, other, name, after=()):
    count, width = own.shape
    cap = count // 4
    return kernel_call(
        fold_kernel, name, [((cap, width), BF)] * 4, [own, other, *after], [VM, VM] + [AFTER] * len(after)
    )


def return_kernel(merge, *refs):
    refs = list(refs)
    rows = refs.pop(0)
    if merge:
        hot = refs.pop(0)
        slots_in = [refs.pop(0) for _ in range(4)]
        width = slots_in[0].shape[1]
        values = rows[:, :width] + rows[:, width : width + 1] * dot_tn(hot[...], stacked(slots_in))
        values = values.astype(BF)
    else:
        values = rows[...]
    place, facts = refs[:2]
    own, other = refs[-2:]
    pack = own.shape[0]
    core = facts[CORE]
    own[...] = dot32(place[pl.ds(pl.multiple_of(core * pack, pack), pack), :], values).astype(BF)
    other[...] = dot32(
        place[pl.ds(pl.multiple_of((1 - core) * pack, pack), pack), :], values
    ).astype(BF)


def sent_rows(facts, merge, rows, extra, place, width, after):
    pack = place.shape[1]
    ins = [rows, *extra, place, facts, *after]
    outs = [((pack, width), BF)] * 2
    return kernel_call(
        functools.partial(return_kernel, merge),
        "return_merged" if merge else "return_rows",
        outs,
        ins,
        ([VH, VH] + [VM] * 4 if merge else [VM]) + [VH, SM] + [AFTER] * len(after),
        cost=1,
    )


def run_copies(moves, sems):
    copies = [
        pltpu.make_async_copy(source, target, sems.at[at])
        for at, (source, target) in enumerate(moves)
    ]
    for copy in copies:
        copy.start()
    for copy in copies:
        copy.wait()


def rows_kernel(*refs):
    cap = refs[0].shape[0]
    out = refs[-1]
    for at, ref in enumerate(refs[:4]):
        out[at * cap : (at + 1) * cap, :] = ref[...]


def joined_rows(blocks, after):
    cap, width = blocks[0].shape
    return kernel_call(
        rows_kernel,
        "join_rows",
        [((4 * cap, width), BF)],
        [*blocks, *after],
        [VM] * 4 + [AFTER] * len(after),
    )[0]


def ordered_kernel(*refs):
    del refs


def ordered(value, after):
    return pl.pallas_call(
        ordered_kernel,
        name="ordered",
        out_shape=pltpu.HBM(value.shape, value.dtype),
        in_specs=[HB] + [AFTER] * len(after),
        out_specs=HB,
        input_output_aliases={0: 0},
        compiler_params=pltpu.CompilerParams(vmem_limit_bytes=1 << 20),
        cost_estimate=pl.CostEstimate(flops=0, bytes_accessed=0, transcendentals=0),
    )(pinned(value), *after)


def restore_kernel(hot, back, activations, grads, tiny):
    width = activations.shape[1]
    activations[...] = dot_tn(hot[...], back[:, :width]).astype(BF)
    grads[...] = dot_tn(hot[...], back[:, width : 2 * width]).astype(BF)
    rows = tiny.shape[0]
    total = jnp.zeros(tiny.shape, F32)
    for at in range(back.shape[0] // rows):
        total += back[at * rows : (at + 1) * rows, 2 * width :].astype(F32)
    tiny[...] = total


def finish_kernel(*refs):
    pieces, attn, attn_out = refs[:4], refs[4], refs[5]
    _, shard, cols = attn.shape
    total = sum(piece[...].astype(F32) for piece in pieces)
    for part in range(3):
        attn[part] = total[part * shard : (part + 1) * shard, :]
    rows = attn_out.shape[0]
    for side in range(2):
        spot = 3 * shard + side * rows
        attn_out[:, side * cols : (side + 1) * cols] = total[spot : spot + rows, :]


def stack_kernel(count, facts, *refs):
    pieces, out, sems = refs[:count], refs[-2], refs[-1]
    run_copies(
        [
            (piece, out.at[jnp.bitwise_xor(facts[MINE], step)])
            for step, piece in enumerate(pieces)
        ],
        sems,
    )


def stack_pieces(facts, pieces, after):
    count = len(pieces)
    return kernel_call(
        functools.partial(stack_kernel, count),
        "stack_pieces",
        [((count, *pieces[0].shape), BF)],
        [facts, *pieces, *after],
        [SM] + [HB] * count + [AFTER] * len(after),
        [pltpu.SemaphoreType.DMA((count,))],
        room=12,
        hbm_outs=True,
    )[0]


def gather_kernel(facts, near, far, *refs):
    out, sems = refs[-2:]
    groups = near.shape[0]
    moves = []
    for rep, source in ((facts[REP], near), (1 - facts[REP], far)):
        for part in range(3):
            moves.append(
                (
                    source.at[:, pl.ds(2 * part, 2)],
                    out.at[pl.ds(part * groups, groups), pl.ds(2 * rep, 2)],
                )
            )
        for side in range(2):
            for group in range(groups):
                moves.append(
                    (
                        source.at[group, 6 + side],
                        out.at[3 * groups + 2 * side + group // 2, group % 2 * 2 + rep],
                    )
                )
    run_copies(moves, sems)


def pack_attn_kernel(attn, attn_out, bundle, sems):
    parts, shard, cols = attn.shape
    rows = attn_out.shape[0]
    moves = [(attn.at[part], bundle.at[pl.ds(part * shard, shard)]) for part in range(parts)]
    for side in range(2):
        moves.append(
            (
                attn_out.at[:, pl.ds(side * cols, cols)],
                bundle.at[pl.ds(parts * shard + side * rows, rows)],
            )
        )
    run_copies(moves, sems)


def pack_attn(attn, attn_out):
    parts, shard, cols = attn.shape
    rows = attn_out.shape[0]
    return kernel_call(
        pack_attn_kernel,
        "pack_attn",
        [((parts * shard + 2 * rows, cols), BF)],
        [attn, attn_out],
        [HB] * 2,
        [pltpu.SemaphoreType.DMA((parts + 2,))],
        room=12,
        hbm_outs=True,
    )[0]


def pack_expert_kernel(steps, facts, w_in, w_out, *refs):
    blocks, sems = refs[-1 - len(steps) : -1], refs[-1]
    in_rows, out_rows, width = w_in.shape[1], w_out.shape[1], w_out.shape[2]
    moves = []
    for step, block in zip(steps, blocks, strict=True):
        at = jnp.bitwise_xor(facts[MINE], step)
        for side in range(2):
            moves.append(
                (
                    w_in.at[at, :, pl.ds(side * width, width)],
                    block.at[pl.ds(side * in_rows, in_rows)],
                )
            )
        moves.append((w_out.at[at], block.at[pl.ds(2 * in_rows, out_rows)]))
    run_copies(moves, sems)


def pack_expert(facts, w_in, w_out, steps, after=()):
    block = (2 * w_in.shape[1] + w_out.shape[1], w_out.shape[2])
    return kernel_call(
        functools.partial(pack_expert_kernel, steps),
        "pack_expert",
        [(block, BF)] * len(steps),
        [facts, w_in, w_out, *after],
        [SM, HB, HB] + [AFTER] * len(after),
        [pltpu.SemaphoreType.DMA((3 * len(steps),))],
        room=12,
        hbm_outs=True,
    )


SPLIT_ORDER = (2, 3, 1, 0)


def expert_out_grad_kernel(split, dropped, facts, *refs):
    blocks, refs = refs[:8], refs[8:]
    kept, act = refs[:2]
    refs = refs[2 + dropped :]
    rows, refs = refs[0], refs[1:]
    cap = blocks[0].shape[0]
    for at, block in enumerate(blocks):
        spot = slice(at * cap, (at + 1) * cap)
        rows[spot, :] = jnp.where(facts[PIPE] == 0, block[...], kept[spot, :])
    ff = act.shape[1]
    grad = refs[-1]

    @pl.loop(0, ff // TILE, unroll=True)
    def _(tile):
        lanes = pl.ds(pl.multiple_of(tile * TILE, TILE), TILE)
        grad[lanes, :] = dot_tn(act[:, lanes], rows[...])

    if split:
        count = ff // 8
        for at, step in enumerate(SPLIT_ORDER):
            owner = jnp.bitwise_xor(facts[MINE], step) * 2
            to = slice(at % 2 * count, (at % 2 + 1) * count)
            for rep, target in ((1 - facts[REP], refs[at // 2]), (facts[REP], refs[2 + at // 2])):
                spot = pl.ds(pl.multiple_of((owner + rep) * count, count), count)
                target[to, :] = grad[spot, :].astype(BF)


def expert_in_grad_kernel(split, dropped, facts, rows, grad_pre, *refs):
    refs = refs[dropped:]
    ff = grad_pre.shape[1]
    width = rows.shape[1]
    grad = refs[-1]

    @pl.loop(0, ff // TILE, unroll=True)
    def _(tile):
        lanes = pl.ds(pl.multiple_of(tile * TILE, TILE), TILE)
        grad[:, lanes] = dot_tn(rows[...], grad_pre[:, lanes])

    if split:
        count = width // 8
        for at, step in enumerate(SPLIT_ORDER):
            owner = jnp.bitwise_xor(facts[MINE], step) * 2
            first = at * 2 * count
            for rep, target in ((1 - facts[REP], refs[0]), (facts[REP], refs[1])):
                spot = pl.ds(pl.multiple_of((owner + rep) * count, count), count)
                target[first : first + count, :] = grad[spot, :width].astype(BF)
                target[first + count : first + 2 * count, :] = grad[spot, width:].astype(BF)


def grad_outs(shape, wire, split, count):
    if split:
        return [(wire, BF, FAR)] * count, [pltpu.VMEM(shape, F32)]
    return [(shape, F32)], []


def expert_out_grads(facts, blocks, kept, act, after, split):
    count, width = kept.shape
    ff = act.shape[1]
    outs, scratch = grad_outs((ff, width), (ff // 4, width), split, 4)
    return kernel_call(
        functools.partial(expert_out_grad_kernel, split, len(after)),
        "expert_out_grads",
        [((count, width), BF, FAR), *outs],
        [facts, *blocks, kept, act, *after],
        [SM] + [VM] * 8 + [VH, VH] + [AFTER] * len(after),
        scratch,
        cost=4,
    )


def expert_in_grads(facts, rows, grad_pre, after, split):
    width = rows.shape[1]
    ff = grad_pre.shape[1]
    outs, scratch = grad_outs((width, ff), (ff // 2, width), split, 2)
    return kernel_call(
        functools.partial(expert_in_grad_kernel, split, len(after)),
        "expert_in_grads",
        outs,
        [facts, rows, grad_pre, *after],
        [SM, VH, VM] + [AFTER] * len(after),
        scratch,
        cost=4,
    )


def owner_kernel(facts, *refs):
    grad_in, grad_out = refs[-2:]
    rows = grad_in.shape[1]
    width = grad_out.shape[2]
    for place, step in enumerate(SPLIT_ORDER):
        at = jnp.bitwise_xor(facts[MINE], step)
        grad_out[at] = refs[place][...].astype(F32)
        piece = refs[4 + place]
        for side in range(2):
            spot = slice(side * rows, (side + 1) * rows)
            grad_in[at, :, side * width : (side + 1) * width] = piece[spot, :].astype(F32)


def owner_grads(facts, pieces, after, in_shape, out_shape):
    return kernel_call(
        owner_kernel,
        "owner_grads",
        [(in_shape, F32), (out_shape, F32)],
        [facts, *pieces, *after],
        [SM] + [VM] * len(pieces) + [AFTER] * len(after),
        cost=4,
    )


def attn_grad_kernel(attn_in, grad_proj, mixed, low, *refs):
    own, other = refs[-2:]
    width = attn_in.shape[1]
    cols = own.shape[1]
    for at, target in ((0, own), (1, other)):
        for part in range(3):
            target[part * width : (part + 1) * width, :] = dot_tn(
                attn_in[...], grad_proj[at, part]
            ).astype(BF)
        for side in range(2):
            spot = 3 * width + side * cols
            target[spot : spot + cols, :] = dot_tn(
                mixed[:, at * cols : (at + 1) * cols], low[:, side * cols : (side + 1) * cols]
            ).astype(BF)


def attn_grads(attn_in, grad_proj, mixed, low, after):
    pack, width = attn_in.shape
    cols = grad_proj.shape[3]
    return kernel_call(
        attn_grad_kernel,
        "attn_grads",
        [((3 * width + 2 * cols, cols), BF)] * 2,
        [attn_in, grad_proj, mixed, low, *after],
        [VH, VM, VH, VM] + [AFTER] * len(after),
        cost=3,
    )


def attn_split_kernel(facts, own, came, *refs):
    sends, keeps = refs[-4:-2], refs[-2:]
    cols = own.shape[1]
    width = 2 * cols
    shard = width // 8
    count = 4 * shard
    for at, step in enumerate(SPLIT_ORDER):
        owner = jnp.bitwise_xor(facts[MINE], step) * 2
        for rep, target, first in (
            (1 - facts[REP], sends[at // 2], at % 2 * count),
            (facts[REP], keeps[at // 2], at % 2 * count),
        ):
            for source, rows, spot in attn_rows(width, shard):
                where = pl.ds(pl.multiple_of(source + (owner + rep) * rows, rows), rows)
                target[first + spot : first + spot + rows, :] = (
                    own[where, :].astype(F32) + came[where, :].astype(F32)
                ).astype(BF)


def sum_kernel(steps, keep, came, *outs):
    outs = outs[-len(steps) :]
    count = outs[0].shape[0]
    for at, out in enumerate(outs):
        rows = slice(at * count, (at + 1) * count)
        both = keep[rows, :].astype(F32) + came[rows, :].astype(F32)
        out[...] = both.astype(out.dtype)


def sum_pieces(steps, keep, came, after=()):
    count = keep.shape[0] // len(steps)
    kinds = [F32 if step == 0 else BF for step in steps]
    return kernel_call(
        functools.partial(sum_kernel, steps),
        "sum_pieces",
        [((count, keep.shape[1]), kind) for kind in kinds],
        [keep, came, *after],
        [VH] * 2 + [AFTER] * len(after),
        cost=0,
    )


def attn_rows(width, shard):
    out = shard // 2
    return (
        (0, shard, 0),
        (width, shard, shard),
        (2 * width, shard, 2 * shard),
        (3 * width, out, 3 * shard),
        (3 * width + width // 2, out, 3 * shard + out),
    )


def attn_split(facts, own, came, after):
    rows, cols = own.shape
    return kernel_call(
        attn_split_kernel,
        "attn_split",
        [((rows // 4, cols), BF, FAR)] * 4,
        [facts, own, came, *after],
        [SM, VM, VM] + [AFTER] * len(after),
        cost=3,
    )


def solution(mesh):
    shape = mesh.shape
    n_pipe, n_dp, n_t = shape["pipe"], shape["dp"], shape["tensor"]
    axes = ("pipe", "dp", "tensor")
    plane = ("dp", "tensor")
    n_dev = n_dp * n_t

    def local(
        inputs,
        cotangent,
        dealing,
        routes,
        slot_order,
        doc_lengths,
        attn_weight,
        attn_out_weight,
        expert_in_weight,
        expert_out_weight,
        norm_gains,
        router_weight,
    ):
        dev_rows, width = inputs.shape
        experts = expert_in_weight.shape[1]
        reps = n_dp // experts
        paired = reps == 2
        pack = dev_rows
        cap = pack // experts
        per = dev_rows // n_dev
        shard, cols = attn_weight.shape[1], attn_weight.shape[3]
        ff = expert_in_weight.shape[3]
        in_rows, out_rows = expert_in_weight.shape[2], expert_out_weight.shape[2]
        pipe = lax.axis_index("pipe")
        dp = lax.axis_index("dp")
        core = lax.axis_index("tensor")
        mine = dp // reps
        rep = dp % reps
        lengths = lax.dynamic_index_in_dim(doc_lengths, core, 0, keepdims=False)
        zero = jnp.int32(0)
        facts = jnp.stack([pipe, mine, rep, core, lengths[0], zero, zero, zero]).astype(jnp.int32)

        def moved(value, rule):
            pairs = []
            for a in range(n_pipe):
                for b in range(experts):
                    for c in range(reps):
                        for d in range(n_t):
                            to = rule(a, b, c, d)
                            if to is not None:
                                flat = [
                                    ((w * experts + x) * reps + y) * n_t + z
                                    for w, x, y, z in ((a, b, c, d), to)
                                ]
                                pairs.append(tuple(flat))
            return lax.ppermute(value, axes, pairs)

        def swap_core(value):
            return moved(value, lambda a, b, c, d: (a, b, c, 1 - d))

        def swap_rep(value):
            return moved(value, lambda a, b, c, d: (a, b, 1 - c, d))

        def across(step):
            return lambda a, b, c, d: (a, b ^ step, c, d)

        def up(step):
            return lambda a, b, c, d: (1, b ^ step, c, d) if a == 0 else None

        def down(step):
            return lambda a, b, c, d: (0, b ^ step, c, d) if a == 1 else None

        order = (3, 2, 1)

        def exchange(blocks):
            out = {0: blocks[0]}
            for step in order:
                out[step] = moved(blocks[step], across(step))
            return [out[step] for step in range(experts)]

        def crossed(blocks, way):
            out = {}
            for step in (*order, 0):
                out[step] = moved(blocks[step], way(step))
            return [out[step] for step in range(experts)]

        def with_other(blocks):
            out = {}
            for step in (0, 1, 2, 3):
                out[step] = swap_core(blocks[step])
            return list(blocks) + [out[step] for step in range(experts)]

        def pick(blocks, step):
            return lax.dynamic_index_in_dim(blocks, mine ^ step, 0, keepdims=False)

        rep_groups = [[b * reps + c for c in range(reps)] for b in range(experts)]

        payload, send_hot = kernel_call(
            functools.partial(send_kernel, per),
            "send",
            [((dev_rows, width + EXTRA), BF), ((dev_rows, dev_rows), BF)],
            [
                facts,
                inputs,
                cotangent,
                dealing.reshape(1, dev_rows),
                routes.reshape(1, dev_rows),
                slot_order.reshape(1, dev_rows),
                router_weight[0].T,
                norm_gains[0],
            ],
            [SM] + [VM] * 7,
            cost=2,
        )
        dealt = lax.all_to_all(payload, plane, split_axis=0, concat_axis=0, tiled=True)
        params = dealt[:, width:].reshape(n_dev, per, 4, 32)[:, :, :3]
        params = jnp.swapaxes(params, 1, 2).reshape(width, 32)
        params = jnp.pad(params, ((0, 0), (0, EXTRA - 32)))
        both = lax.all_gather(dealt, "tensor", axis=0, tiled=True)
        own_rows, slots, onehot, place = kernel_call(
            deal_kernel,
            "deal",
            [
                ((pack, width), BF, FAR),
                ((pack, pack), BF, FAR),
                ((pack, EXTRA), F32, FAR),
                ((2 * pack, pack), BF, FAR),
            ],
            [facts, both],
            [SM, VM],
            cost=1.5,
        )
        plan = (slots, onehot)

        out_shard = attn_out_weight[0]
        attn_shape = (4 * width, cols)

        def expert_places(way, step):
            def owner_of(numbers):
                owner = jnp.bitwise_xor(numbers[MINE], step) * 2
                return owner + (numbers[REP] if way == 0 else 1 - numbers[REP])

            def spots_in(numbers):
                at = pl.multiple_of(owner_of(numbers) * in_rows, in_rows)
                return [(0, at, in_rows, 0, width), (in_rows, at, in_rows, width, width)]

            def spots_out(numbers):
                at = pl.multiple_of(owner_of(numbers) * out_rows, out_rows)
                return [(2 * in_rows, at, out_rows, 0, width)]

            return spots_in, spots_out

        if paired:
            w_in_raw, w_out_raw = expert_in_weight[0], expert_out_weight[0]
            attn_bundle = pack_attn(jnp.swapaxes(attn_weight[0], 0, 1), out_shard)
            near, far = {}, {}
            near[0], first, bundle = pack_expert(
                facts, w_in_raw, w_out_raw, (0, 1, 2), (attn_bundle,)
            )
            far[0] = swap_rep(near[0])
            attn_near = exchange([attn_bundle] * experts)
            attn_near = stack_pieces(
                facts, [each.reshape(8, shard // 2, cols) for each in attn_near],
                [payload, far[0]],
            )
            near[1] = moved(first, across(1))
            attn_far = swap_rep(attn_near)
            near[2] = moved(bundle, across(2))
            (bundle,) = pack_expert(facts, w_in_raw, w_out_raw, (3,), (near[2],))
            attn_own = kernel_call(
                gather_kernel,
                "gather_attn",
                [((4 * experts, 4, shard // 2, cols), BF)],
                [facts, attn_near, attn_far, bundle, dealt, near[1]],
                [SM, HB, HB, AFTER, AFTER, AFTER],
                [pltpu.SemaphoreType.DMA((22,))],
                room=12,
                hbm_outs=True,
            )[0].reshape(attn_shape)
            near[3] = moved(bundle, across(3))
            for step in (1, 2):
                far[step] = swap_rep(near[step])
            ready = ()
            both_places = [
                expert_places(way, step) for way in range(2) for step in range(experts)
            ]
            places = ([each[0] for each in both_places], [each[1] for each in both_places])
        else:
            attn_bundle = jnp.concatenate(
                [attn_weight[0, :, part] for part in range(3)]
                + [out_shard[:, :cols], out_shard[:, cols:]],
                axis=0,
            )
            every = lax.all_gather(attn_bundle, "dp", axis=0)
            attn_own = jnp.concatenate(
                [
                    every[:, spot : spot + rows].reshape(-1, cols)
                    for _, rows, spot in attn_rows(width, shard)
                ],
                axis=0,
            )

            def assembled(blocks):
                got = exchange([pick(blocks, step) for step in range(experts)])
                got = jnp.stack(got)
                got = jnp.stack([pick(got, owner) for owner in range(experts)])
                got = lax.all_gather(got, "dp", axis_index_groups=rep_groups)
                return jnp.swapaxes(got, 0, 1)

            ready = ()
            pieces = [
                assembled(expert_in_weight[0]).reshape(width, ff),
                assembled(expert_out_weight[0]).reshape(ff, width),
            ]
            places = (
                [lambda numbers: [(0, 0, width, 0, ff)], lambda numbers: []],
                [lambda numbers: [], lambda numbers: [(0, 0, ff, 0, width)]],
            )
        attn_other = swap_core(attn_own)
        weights = (attn_own, attn_other, params)

        def expert_forward(blocks, name, keep, after=()):
            *kept, own, other = expert_call(name, keep, facts, blocks, pieces, places, width, ff)
            folded = fold(own, swap_core(other), "fold_" + name, after)
            return kept, own, other, folded

        def expert_backward(blocks, saved, name, after=()):
            grad_pre, own, other, *rows = expert_back_call(
                name, facts, blocks, saved, pieces, places, width, ff
            )
            return grad_pre, rows, fold(own, swap_core(other), "fold_" + name, after)

        def sent_back(merge, rows, extra, after):
            own, other = sent_rows(facts, merge, rows, extra, place, width, after)
            return own, other

        out = attn_forward(facts, own_rows, weights, plan, None, ready)
        if paired:
            near[3] = ordered(near[3], (out[1],))
            far[3] = swap_rep(near[3])
            pieces = [each[step] for each in (near, far) for step in range(experts)]
        mid_up = moved(out[0], lambda a, b, c, d: (1, b, c, d) if a == 0 else None)
        blocks = with_other(exchange(out[1:5]))
        _, _, _, expert_slots = expert_forward(
            blocks, "expert_first", False, (mid_up,)
        )
        from_first = crossed(expert_slots, up)

        out = attn_forward(facts, own_rows, weights, plan, (mid_up, *from_first))
        mid, attn_in, proj, mixed, mlp_in, probs = out[:6]
        stream = out[10]
        blocks = with_other(exchange(out[6:10]))
        kept_blocks = exchange(out[11:15])
        (slope, act, rows), own_out, other_out, expert_slots = expert_forward(blocks, "expert_second", True)
        expert_saved = (slope, own_out, other_out)

        saved = (stream, mid, proj, mlp_in, probs, mixed)
        kept_own = joined_rows(kept_blocks, (other_out,))
        _, (kept_rows,), grad_slots = expert_backward(
            [kept_own, swap_core(kept_own)], expert_saved, "expert_back_first"
        )
        back = attn_backward(
            facts, own_rows, [mid_up], exchange(grad_slots), saved, weights, plan, True
        )
        expert_slots = exchange(expert_slots)
        if paired:
            back = list(back)
            back[1 + order[0]] = ordered(back[1 + order[0]], expert_slots[1:])
        grad_down = moved(back[0], lambda a, b, c, d: (0, b, c, d) if a == 1 else None)
        out_back = sent_back(True, mid, (slots, *expert_slots), (back[1],))

        grads = with_other(crossed(back[1:5], down))
        grad_rows, *out_wire = expert_out_grads(
            facts, grads, kept_rows, act, (out_back[0],), paired
        )
        grad_pre, _, grad_slots = expert_backward(
            [grad_rows], expert_saved, "expert_back_second"
        )
        out_came = [swap_rep(out_wire[0])] if paired else []
        in_wire = expert_in_grads(facts, rows, grad_pre, [grad_slots[2], *out_came], paired)
        after = []
        if paired:
            out_sums = sum_pieces(
                SPLIT_ORDER[:2], out_wire[2], out_came[0], [in_wire[1]]
            )
            after = [out_sums[0]]
        layer_grad, grad_proj, low, tiny = attn_backward(
            facts,
            grad_down,
            [own_rows, *after],
            exchange(grad_slots),
            saved,
            weights,
            plan,
            False,
        )

        if paired:
            out_near = [
                moved(each, across(step)) if step else each
                for step, each in zip(SPLIT_ORDER[:2], out_sums, strict=True)
            ]
            came_in = swap_rep(in_wire[0])
            came_last = swap_rep(out_wire[1])
            marker = [came_last, came_in, *out_near]
        else:

            def rep_scatter(each):
                return lax.psum_scatter(
                    each, "dp", axis_index_groups=rep_groups, scatter_dimension=0
                )

            def to_owner(grad, rows_each):
                each = grad.reshape(experts, reps, rows_each, -1).astype(BF)
                summed = rep_scatter(jnp.swapaxes(each, 0, 1))
                got = exchange([pick(summed, step) for step in range(experts)])
                got = jnp.stack(got)
                return jnp.stack([pick(got, owner) for owner in range(experts)]).astype(F32)

            marker = []
            (grad_w_in,), (grad_w_out,) = in_wire, out_wire
            grad_expert_in = to_owner(grad_w_in, in_rows)
            grad_expert_out = to_owner(grad_w_out, out_rows)

        grad_own, grad_other = attn_grads(attn_in, grad_proj, mixed, low, marker)
        came = swap_core(grad_other)
        if paired:
            in_sums = sum_pieces(SPLIT_ORDER, in_wire[1], came_in, [grad_own])
            in_near = [
                moved(each, across(step)) if step else each
                for step, each in zip(SPLIT_ORDER, in_sums, strict=True)
            ]
            out = attn_split(facts, grad_own, came, (in_sums[0],))
            last = sum_pieces(SPLIT_ORDER[2:], out_wire[3], came_last, [out[2]])
            out_near += [moved(last[0], across(1)), last[1]]
            after = (last[1],)
        else:
            after = ()
        grad_back = sent_back(False, layer_grad, (), after)
        tiny = jnp.swapaxes(tiny[:, :32].reshape(n_dev, 3, per, 32), 1, 2)
        tiny = jnp.pad(tiny.reshape(dev_rows, 96), ((0, 0), (0, EXTRA - 96)))
        theirs = swap_core(jnp.concatenate([out_back[1], grad_back[1]], axis=1))
        both = jnp.concatenate([out_back[0], grad_back[0]], axis=1) + theirs
        payload = jnp.concatenate([both, tiny], axis=1)
        if paired:
            total = {}
            first = sum_pieces(SPLIT_ORDER[:2], out[2], swap_rep(out[0]), [payload])
            last = swap_rep(ordered(out[1], (first[0],)))
            last = sum_pieces(SPLIT_ORDER[2:], out[3], last, [first[1]])
            for step, each in zip(SPLIT_ORDER, [*first, *last], strict=True):
                total[step] = moved(each, across(step)) if step else each
            grad_expert_in, grad_expert_out = owner_grads(
                facts,
                [*out_near, *in_near],
                (total[0],),
                expert_in_weight.shape[1:],
                expert_out_weight.shape[1:],
            )
            grad_attn, grad_attn_out = kernel_call(
                finish_kernel,
                "finish_attn",
                [((3, shard, cols), F32), ((shard // 2, width), F32)],
                [total[step] for step in range(experts)],
                [VM] * 4,
            )
        else:
            full = grad_own.astype(F32) + came.astype(F32)
            pieces_of = [
                full[source : source + rows * n_dp].reshape(n_dp, rows, cols)
                for source, rows, _ in attn_rows(width, shard)
            ]
            full = jnp.concatenate(pieces_of, axis=1).astype(BF)
            full = full.reshape((experts, reps) + full.shape[1:])
            full = rep_scatter(jnp.swapaxes(full, 0, 1))
            got = exchange([pick(full, step) for step in range(experts)])
            total = sum(each.astype(F32) for each in got)
            grad_attn = total[: 3 * shard].reshape(3, shard, cols)
            rows = shard // 2
            grad_attn_out = jnp.concatenate(
                [total[3 * shard : 3 * shard + rows], total[3 * shard + rows :]], axis=1
            )
        both = lax.all_to_all(payload, plane, split_axis=0, concat_axis=0, tiled=True)
        activations, input_grads, tiny = kernel_call(
            restore_kernel,
            "restore",
            [((dev_rows, width), BF), ((dev_rows, width), BF), ((per, EXTRA), F32)],
            [send_hot, both],
            [VM] * 2,
            cost=2,
        )
        tiny = tiny.reshape(per, 4, 32)[:, :3]
        tiny = jnp.swapaxes(tiny, 0, 1).reshape(3 * per, 32)
        grad_router = (tiny[:, :experts] + tiny[:, experts : 2 * experts])[None]
        grad_gains = (tiny[:, 8:10] + tiny[:, 10:12]).T[None]

        return (
            activations[None],
            input_grads[None],
            jnp.swapaxes(grad_attn, 0, 1)[None],
            grad_attn_out[None],
            grad_expert_in[None],
            grad_expert_out[None],
            grad_gains,
            grad_router,
        )

    in_specs = (
        P(("dp", "tensor"), None),
        P(("dp", "tensor"), None),
        P(("dp", "tensor")),
        P(("dp", "tensor"), None),
        P(("dp", "tensor")),
        P("dp", None),
        P("pipe", "dp", None, "tensor"),
        P("pipe", ("tensor", "dp"), None),
        P("pipe", None, "dp", "tensor"),
        P("pipe", None, ("tensor", "dp"), None),
        P("pipe", None, ("dp", "tensor")),
        P("pipe", ("dp", "tensor"), None),
    )
    out_specs = (
        P("pipe", ("dp", "tensor"), None),
        P("pipe", ("dp", "tensor"), None),
        P("pipe", "dp", None, "tensor"),
        P("pipe", ("tensor", "dp"), None),
        P("pipe", None, "dp", "tensor"),
        P("pipe", None, ("tensor", "dp"), None),
        P("pipe", None, ("dp", "tensor")),
        P("pipe", ("dp", "tensor"), None),
    )
    return jax.shard_map(local, mesh=mesh, in_specs=in_specs, out_specs=out_specs, check_vma=False)
```
